32 devices in a mesh: crop: 2 (over y), row: 4 (over z), col: 4 (over x, core).
Axes of the slice: x: 2, y: 2, z: 4, core: 2. Of those that a mesh axis runs over, the one named last changes fastest.
Arguments:
- pair_tiles: bfloat16 [512, 256, 128], P(('crop', 'row'), 'col'), parts along dimension 0, may hold values from -6 to 6
- grad_out: bfloat16 [512, 256, 128], P(('crop', 'row'), 'col'), parts along dimension 0, may hold values from -6 to 6
- exponents: int32 [512, 256], P(('crop', 'row'), 'col'), parts along dimension 0, may hold values from -10 to -8
- token_mask: int32 [512], P('crop'), parts along dimension 0, may hold values from 0 to 1, as said below
- gain_in: float32 [128], replicated, may hold values from 0.1 to 1.9
- w_proj: bfloat16 [128, 512], replicated, may hold values from -0.5 to 0.5
- w_gate: bfloat16 [128, 128], replicated, may hold values from -0.5 to 0.5
- gain_out: float32 [128], replicated, may hold values from 0.1 to 1.9
- w_out: bfloat16 [128, 128], replicated, may hold values from -0.5 to 0.5
Outputs:
- d_pair: bfloat16 [512, 256, 128], P(('crop', 'row'), 'col'), parts along dimension 0
- d_wproj: float32 [256, 512], P('crop'), parts along dimension 0
- d_wgate: float32 [256, 128], P('crop'), parts along dimension 0
- d_wout: float32 [256, 128], P('crop'), parts along dimension 0
The draws below stay inside these ranges and needn't reach their ends.
There are 2 independent parts, one for each index of `crop`. The reference program is written for one: setup_inputs(seed, part) draws one part's arguments, and reference() takes and returns one part's arrays. A program takes and returns all parts, laid end to end along the dimension named above; an argument that names none is the same for every part. Nothing has to cross between parts.
Inputs may be any that keep to these rules, and one draw needn't show every extreme that they name: `token_mask`: 1 on a leading run of tokens and 0 after it; the run covers at least half of the 256 tokens.
All inputs are finite; a program needn't handle non-finite values.
Results may differ from the reference program's by a relative error of at most 0.015.
The reference program's roundings to bfloat16 on the way (of `normed`, `left`, `right`, `tnorm`, `d_outproj`, `d_tri`, `d_gatepre` and `d_proj`) count: a program that leaves them out, or rounds other values in their place, can miss the bound.
Values may be sent and summed in bfloat16 or wider, within the bound.
No kernel may reach another device: no remote copies, remote signals or barrier semaphores. Data moves between devices by JAX's collectives and lax.ppermute only.
A program may use at most 128 MiB of HBM per device.

```python
import jax
import jax.numpy as jnp
from jax import lax

CH = 128
CROP = 256
TI = 64


def draw_token_mask(key, part):
    key = jax.random.fold_in(key, 7)
    valid = jax.random.randint(key, (), CROP // 2, CROP + 1)
    return (jnp.arange(CROP) < valid).astype(jnp.int32)


def plant(entries, key, smallest, high):
    shape = entries.shape
    place = [jax.random.randint(jax.random.fold_in(key, axis), (), 0, shape[axis]) for axis in range(len(shape))]
    entries = entries.at[tuple(place)].set(smallest)
    longest = shape.index(max(shape))
    place[longest] = (place[longest] + 1) % shape[longest]
    return entries.at[tuple(place)].set(high)


def shard_levels(key, shape, cuts, smallest, largest):
    def one(axis_at, parts):
        draws = jax.random.uniform(jax.random.fold_in(jax.random.fold_in(key, 6), axis_at), (parts,), jnp.float32, smallest / len(cuts), largest / len(cuts))
        return jnp.repeat(jnp.exp(draws), shape[axis_at] // parts).reshape((-1,) + (1,) * (len(shape) - axis_at - 1))

    level = one(*cuts[0])
    for cut in cuts[1:]:
        level = level * one(*cut)
    return level


def noise(stream_key, extent, width, limit, pieces=(), held_as=jnp.bfloat16):
    array = width * jax.random.normal(stream_key, extent, jnp.float32)
    if pieces:
        array = array * shard_levels(stream_key, extent, pieces, -0.22, 0.18)
    return jnp.clip(array, -limit, limit).astype(held_as)


def setup_inputs(seed: int = 0, part: int = 0) -> dict:
    key_of = jax.random.split(jax.random.key(seed), 10)
    own_keys = jax.random.split(jax.random.fold_in(key_of[9], part), 10)
    return {
        "pair_tiles": noise(own_keys[0], (CROP, CROP, CH), 1.0, 6.0, ((0, 4), (1, 4))),
        "grad_out": noise(own_keys[1], (CROP, CROP, CH), 1.0, 6.0, ((0, 4), (1, 4))),
        "exponents": plant(jax.random.randint(own_keys[2], (CROP, CROP), -10, -7), jax.random.fold_in(own_keys[2], 1), -10, (-7) - 1).astype(jnp.int32),
        "token_mask": draw_token_mask(jax.random.fold_in(jax.random.fold_in(key_of[9], part), 71), part),
        "gain_in": jnp.clip(1.0 + 0.18 * jax.random.normal(key_of[4], (CH,), jnp.float32), 0.1, 1.9),
        "w_proj": noise(key_of[5], (CH, 4 * CH), CH ** -0.5, 0.5),
        "w_gate": noise(key_of[6], (CH, CH), CH ** -0.5, 0.5),
        "gain_out": jnp.clip(1.0 + 0.18 * jax.random.normal(key_of[7], (CH,), jnp.float32), 0.1, 1.9),
        "w_out": noise(key_of[8], (CH, CH), CH ** -0.5, 0.5),
    }


EPS = 1e-05

def layer_norm(values, gain):
    center = lax.optimization_barrier(jnp.mean(values, axis=-1, keepdims=True))
    spread = lax.optimization_barrier(jnp.mean((values - center) ** 2, axis=-1, keepdims=True))
    inverse = lax.rsqrt(spread + EPS)
    centred = (values - center) * inverse
    return (centred * gain, centred, inverse)

def norm_back(upstream, centred, inverse, gain):
    scaled = upstream * gain
    first = lax.optimization_barrier(jnp.mean(scaled, axis=-1, keepdims=True))
    second = lax.optimization_barrier(jnp.mean(scaled * centred, axis=-1, keepdims=True))
    return inverse * (scaled - first - centred * second)

def reference(pair_tiles, grad_out, exponents, token_mask, gain_in, w_proj, w_gate, gain_out, w_out):
    f32 = jnp.float32
    bf16 = jnp.bfloat16
    hi = lax.Precision.HIGHEST
    normed_f, centred, inverse = layer_norm(pair_tiles.astype(f32), gain_in)
    normed = normed_f.astype(bf16)
    flat = normed.reshape(-1, CH)
    projected = jnp.dot(flat, w_proj, preferred_element_type=f32).reshape(CROP, CROP, 4 * CH)
    gate_a = projected[..., :CH]
    value_a = projected[..., CH:2 * CH]
    gate_b = projected[..., 2 * CH:3 * CH]
    value_b = projected[..., 3 * CH:]
    maskf = token_mask.astype(f32)
    pair_mask = (maskf[:, None] * maskf[None, :])[..., None]
    sig_a = jax.nn.sigmoid(gate_a)
    sig_b = jax.nn.sigmoid(gate_b)
    left = (pair_mask * sig_a * value_a).astype(bf16)
    right_raw = pair_mask * sig_b * value_b
    bound = (448.0 * jnp.exp2(exponents.astype(f32)))[..., None]
    right = jnp.clip(right_raw, -bound, bound).astype(bf16)
    inside = (jnp.abs(right_raw) <= bound).astype(f32)
    tri = jnp.einsum('ikc,jkc->ijc', left.astype(f32), right.astype(f32), precision=hi)
    tnorm_f, tcentred, tinverse = layer_norm(tri, gain_out)
    tnorm = tnorm_f.astype(bf16)
    tflat = tnorm.reshape(-1, CH)
    opened = jax.nn.sigmoid(jnp.dot(flat, w_gate, preferred_element_type=f32)).reshape(CROP, CROP, CH)
    outproj = jnp.dot(tflat, w_out, preferred_element_type=f32).reshape(CROP, CROP, CH)
    upstream = grad_out.astype(f32)
    d_open = upstream * outproj
    d_outproj = (upstream * opened).astype(bf16).reshape(-1, CH)
    d_wout = jnp.dot(tflat.T, d_outproj, preferred_element_type=f32) / CROP
    d_tnorm = jnp.dot(d_outproj, w_out.T, preferred_element_type=f32).reshape(CROP, CROP, CH)
    d_tri = norm_back(d_tnorm, tcentred, tinverse, gain_out).astype(bf16)
    d_gatepre = (d_open * opened * (1.0 - opened)).astype(bf16).reshape(-1, CH)
    d_wgate = jnp.dot(flat.T, d_gatepre, preferred_element_type=f32) / CROP
    d_left = jnp.einsum('ijc,jkc->ikc', d_tri.astype(f32), right.astype(f32), precision=hi)
    tri_blocks = d_tri.reshape(CROP // TI, TI, CROP, CH)
    left_blocks = left.reshape(CROP // TI, TI, CROP, CH)

    def add_block(total, index):
        grads = lax.dynamic_index_in_dim(tri_blocks, index, 0, keepdims=False).astype(f32)
        lefts = lax.dynamic_index_in_dim(left_blocks, index, 0, keepdims=False).astype(f32)
        term = jnp.einsum('ijc,ikc->jkc', grads, lefts, precision=hi)
        return (total + term.astype(bf16).astype(f32), None)
    d_right, unused = lax.scan(add_block, jnp.zeros((CROP, CROP, CH), f32), jnp.arange(CROP // TI, dtype=jnp.int32))
    d_right = d_right * inside
    d_gate_a = d_left * pair_mask * value_a * sig_a * (1.0 - sig_a)
    d_value_a = d_left * pair_mask * sig_a
    d_gate_b = d_right * pair_mask * value_b * sig_b * (1.0 - sig_b)
    d_value_b = d_right * pair_mask * sig_b
    d_proj = jnp.concatenate([d_gate_a, d_value_a, d_gate_b, d_value_b], axis=-1).astype(bf16).reshape(-1, 4 * CH)
    d_wproj = jnp.dot(flat.T, d_proj, preferred_element_type=f32) / CROP
    d_normed = jnp.dot(d_proj, w_proj.T, preferred_element_type=f32) + jnp.dot(d_gatepre, w_gate.T, preferred_element_type=f32)
    d_pair = norm_back(d_normed.reshape(CROP, CROP, CH), centred, inverse, gain_in).astype(bf16)
    return (d_pair, d_wproj, d_wgate, d_wout)
```

```python
import functools

import jax
import jax.numpy as jnp
from jax import lax
from jax.experimental import pallas as pl
from jax.experimental.pallas import tpu as pltpu
from jax.sharding import PartitionSpec as P

EPS = 1e-05


def layer_norm(values, gain):
    center = jnp.mean(values, axis=-1, keepdims=True)
    spread = jnp.mean((values - center) ** 2, axis=-1, keepdims=True)
    inverse = lax.rsqrt(spread + EPS)
    centred = (values - center) * inverse
    return (centred * gain, centred, inverse)


def norm_back(upstream, centred, inverse, gain):
    scaled = upstream * gain
    first = jnp.mean(scaled, axis=-1, keepdims=True)
    second = jnp.mean(scaled * centred, axis=-1, keepdims=True)
    return inverse * (scaled - first - centred * second)


def plain(pair_tiles, grad_out, exponents, token_mask, gain_in, w_proj, w_gate, gain_out, w_out):
    f32 = jnp.float32
    bf16 = jnp.bfloat16
    rows, cols, width = pair_tiles.shape
    crop_len = token_mask.shape[0]
    row_at = lax.axis_index("row")
    col_at = lax.axis_index("col")
    maskf = token_mask.astype(f32)
    mask_rows = lax.dynamic_slice_in_dim(maskf, row_at * rows, rows)
    mask_cols = lax.dynamic_slice_in_dim(maskf, col_at * cols, cols)
    pair_mask = (mask_rows[:, None] * mask_cols[None, :])[..., None]
    normed_f, centred, inverse = layer_norm(pair_tiles.astype(f32), gain_in)
    normed = normed_f.astype(bf16)
    flat = normed.reshape(-1, width)
    projected = jnp.dot(flat, w_proj, preferred_element_type=f32).reshape(rows, cols, 4 * width)
    gate_a = projected[..., :width]
    value_a = projected[..., width : 2 * width]
    gate_b = projected[..., 2 * width : 3 * width]
    value_b = projected[..., 3 * width :]
    sig_a = jax.nn.sigmoid(gate_a)
    sig_b = jax.nn.sigmoid(gate_b)
    left = (pair_mask * sig_a * value_a).astype(bf16)
    right_raw = pair_mask * sig_b * value_b
    bound = (448.0 * jnp.exp2(exponents.astype(f32)))[..., None]
    right = jnp.clip(right_raw, -bound, bound).astype(bf16)
    inside = (jnp.abs(right_raw) <= bound).astype(f32)
    panel = lax.all_gather(right, "row", axis=0, tiled=True)
    tri_cols = lax.psum_scatter(
        jnp.einsum("jkc,ikc->jic", panel, left, preferred_element_type=f32).astype(jnp.bfloat16),
        "col",
        scatter_dimension=0,
        tiled=True,
    ).astype(jnp.float32)
    tri = jnp.transpose(tri_cols, (1, 0, 2))
    tnorm_f, tcentred, tinverse = layer_norm(tri, gain_out)
    tnorm = tnorm_f.astype(bf16)
    tflat = tnorm.reshape(-1, width)
    opened = jax.nn.sigmoid(jnp.dot(flat, w_gate, preferred_element_type=f32)).reshape(
        rows, cols, width
    )
    outproj = jnp.dot(tflat, w_out, preferred_element_type=f32).reshape(rows, cols, width)
    upstream = grad_out.astype(f32)
    d_open = upstream * outproj
    d_outproj = (upstream * opened).astype(bf16).reshape(-1, width)
    g_out = jnp.dot(tflat.T, d_outproj, preferred_element_type=f32)
    d_tnorm = jnp.dot(d_outproj, w_out.T, preferred_element_type=f32).reshape(rows, cols, width)
    d_tri = norm_back(d_tnorm, tcentred, tinverse, gain_out).astype(bf16)
    d_gatepre = (d_open * opened * (1.0 - opened)).astype(bf16).reshape(-1, width)
    g_gate = jnp.dot(flat.T, d_gatepre, preferred_element_type=f32)
    grad_full = lax.all_gather(d_tri, "col", axis=1, tiled=True)
    d_left = jnp.einsum("ijc,jkc->ikc", grad_full, panel, preferred_element_type=f32)
    d_right = (
        lax.psum_scatter(
            jnp.einsum("ijc,ikc->jkc", grad_full, left, preferred_element_type=f32).astype(
                jnp.bfloat16
            ),
            "row",
            scatter_dimension=0,
            tiled=True,
        ).astype(jnp.float32)
        * inside
    )
    d_gate_a = d_left * pair_mask * value_a * sig_a * (1.0 - sig_a)
    d_value_a = d_left * pair_mask * sig_a
    d_gate_b = d_right * pair_mask * value_b * sig_b * (1.0 - sig_b)
    d_value_b = d_right * pair_mask * sig_b
    d_proj = (
        jnp.concatenate([d_gate_a, d_value_a, d_gate_b, d_value_b], axis=-1)
        .astype(bf16)
        .reshape(-1, 4 * width)
    )
    g_proj = jnp.dot(flat.T, d_proj, preferred_element_type=f32)
    d_normed = jnp.dot(d_proj, w_proj.T, preferred_element_type=f32) + jnp.dot(
        d_gatepre, w_gate.T, preferred_element_type=f32
    )
    d_pair = norm_back(d_normed.reshape(rows, cols, width), centred, inverse, gain_in).astype(bf16)
    sum_proj, sum_gate, sum_out = lax.psum((g_proj, g_gate, g_out), ("row", "col"))
    return (d_pair, sum_proj / crop_len, sum_gate / crop_len, sum_out / crop_len)


SUB = 16
HALF = 64
WIDTH = 128
LANES = SUB * HALF
GROUP = 16
NT = (((1,), (1,)), ((), ()))
NN = (((1,), (0,)), ((), ()))
TN = (((0,), (0,)), ((), ()))
F32 = jnp.float32
BF16 = jnp.bfloat16


def mm(a, b, dims):
    return lax.dot_general(a, b, dims, preferred_element_type=F32)


def params():
    return pltpu.CompilerParams(vmem_limit_bytes=40 * 1024 * 1024)


def cost(flops, size, exps=0):
    return pl.CostEstimate(flops=flops, bytes_accessed=size, transcendentals=exps)


def first_half(rows):
    return lax.broadcasted_iota(jnp.int32, (rows, WIDTH), 1) < HALF


def swap_halves(a, b):
    first = first_half(HALF)
    return (
        jnp.where(first, a, pltpu.roll(b, HALF, 1)),
        jnp.where(first, pltpu.roll(a, HALF, 1), b),
    )


def eye():
    row = lax.broadcasted_iota(jnp.int32, (WIDTH, WIDTH), 0)
    lane = lax.broadcasted_iota(jnp.int32, (WIDTH, WIDTH), 1)
    return (row == lane).astype(F32).astype(BF16)


def to_channels(cells):
    return mm(eye(), cells, NT)


def to_cells(channels):
    return mm(channels, eye(), TN)


def stage_rows(channels, buf):
    for t in range(SUB // 2):
        part = channels[:, t * WIDTH : (t + 1) * WIDTH]
        one, two = swap_halves(part[:HALF], part[HALF:])
        buf[(2 * t) * HALF : (2 * t + 1) * HALF, :] = one
        buf[(2 * t + 1) * HALF : (2 * t + 2) * HALF, :] = two


def panel_row(buf, p):
    return buf[pl.ds(p, SUB, stride=HALF), :]


def channels_of(panels, buf, out):
    buf[...] = panels.reshape(LANES, WIDTH)
    for t in range(SUB // 2):
        one = buf[pl.ds(2 * t, HALF, stride=SUB), :]
        two = buf[pl.ds(2 * t + 1, HALF, stride=SUB), :]
        low, high = swap_halves(one, two)
        out[:HALF, t * WIDTH : (t + 1) * WIDTH] = low
        out[HALF:, t * WIDTH : (t + 1) * WIDTH] = high
    return out[...]


def norm_channels(values, gain):
    center = jnp.mean(values, axis=0, keepdims=True)
    spread = jnp.mean((values - center) ** 2, axis=0, keepdims=True)
    inverse = lax.rsqrt(spread + EPS)
    centred = (values - center) * inverse
    return centred * gain, centred, inverse


def norm_back_channels(upstream, centred, inverse, gain):
    scaled = upstream * gain
    first = jnp.mean(scaled, axis=0, keepdims=True)
    second = jnp.mean(scaled * centred, axis=0, keepdims=True)
    return inverse * (scaled - first - centred * second)


def right_kernel(x_ref, gain_ref, w_ref, mask_ref, bound_ref, out_ref, buf):
    values = to_channels(x_ref[...].reshape(LANES, WIDTH))
    normed = norm_channels(values, gain_ref[...])[0].astype(BF16)
    proj = mm(w_ref[...], normed, NN)
    raw = mask_ref[...] * jax.nn.sigmoid(proj[:WIDTH]) * proj[WIDTH:]
    bound = bound_ref[...]
    stage_rows(jnp.clip(raw, -bound, bound), buf)
    for p in range(HALF):
        out_ref[p] = panel_row(buf, p).astype(BF16)


def left_kernel(x_ref, gain_ref, w_ref, mask_ref, out_ref, buf):
    values = to_channels(x_ref[...].reshape(LANES, WIDTH))
    normed = norm_channels(values, gain_ref[...])[0].astype(BF16)
    proj = mm(w_ref[...], normed, NN)
    stage_rows(mask_ref[...] * jax.nn.sigmoid(proj[:WIDTH]) * proj[WIDTH:], buf)
    first = first_half(SUB)
    for p in range(HALF):
        row = panel_row(buf, p)
        out_ref[p, 0] = jnp.where(first, row, 0.0).astype(BF16)
        out_ref[p, 1] = jnp.where(first, 0.0, row).astype(BF16)


def tri_kernel(place_ref, r0, r1, r2, r3, left_ref, out_ref, panel_ref):
    slots = (r0, r1, r2, r3)
    place = [place_ref[m] for m in range(4)]
    for p in range(GROUP):
        right = jnp.concatenate([r[p] for r in slots], axis=0)
        left = left_ref[p].reshape(WIDTH, WIDTH)
        tri = mm(right, left, NT).astype(BF16)
        for m in range(4):
            out_ref[place[m], p] = tri[m * SUB : (m + 1) * SUB]
            panel_ref[place[m], p] = slots[m][p]


def mid_kernel(
    a_ref, b_ref, c_ref, x_ref, grad_ref, gain_in_ref, gain_out_ref, gate_t_ref, out_t_ref, out_w_ref,
    dtri_ref, dgate_ref, g_out_ref, g_gate_ref, buf, wide,
):
    tri = channels_of(
        a_ref[...].astype(F32) + b_ref[...].astype(F32) + c_ref[...].astype(F32), buf, wide
    )
    tnorm_f, tcentred, tinverse = norm_channels(tri, gain_out_ref[...])
    tnorm = tnorm_f.astype(BF16)

    def turned(ref):
        buf[...] = ref[...].astype(F32).reshape(LANES, WIDTH)
        rows = [buf[pl.ds(j, HALF, stride=SUB), :] for j in range(SUB)]
        return to_channels(jnp.concatenate(rows, axis=0).astype(BF16))

    normed = norm_channels(turned(x_ref), gain_in_ref[...])[0].astype(BF16)
    upstream = turned(grad_ref)
    opened = jax.nn.sigmoid(mm(gate_t_ref[...], normed, NN))
    outproj = mm(out_t_ref[...], tnorm, NN)
    d_open = upstream * outproj
    d_outproj = (upstream * opened).astype(BF16)
    g_out_ref[...] = mm(tnorm, d_outproj, NT)
    d_tnorm = mm(out_w_ref[...], d_outproj, NN)
    d_tri = norm_back_channels(d_tnorm, tcentred, tinverse, gain_out_ref[...])
    d_gatepre = (d_open * opened * (1.0 - opened)).astype(BF16)
    g_gate_ref[...] = mm(normed, d_gatepre, NT)
    stage_rows(d_tri, buf)
    for p in range(HALF):
        dtri_ref[p] = panel_row(buf, p).astype(BF16)
    buf[...] = to_cells(d_gatepre)
    for i in range(HALF):
        dgate_ref[i] = panel_row(buf, i).astype(BF16)


def dright_kernel(place_ref, d0, d1, d2, d3, left_ref, out_ref):
    blocks = (d0, d1, d2, d3)
    place = [place_ref[m] for m in range(4)]
    for p in range(GROUP):
        grads = jnp.concatenate([d[p] for d in blocks], axis=0)
        left = left_ref[p].reshape(WIDTH, WIDTH)
        part = mm(grads, left, NN).astype(BF16)
        for m in range(4):
            out_ref[place[m], p] = part[m * SUB : (m + 1) * SUB]


def dleft_kernel(*refs):
    out_ref = refs[-1]
    parts = (len(refs) - 1) // 5
    grad_refs, panel_refs = refs[: 4 * parts], refs[4 * parts : 5 * parts]
    first = first_half(HALF)
    for p in range(GROUP):
        grads = jnp.concatenate([d[p] for d in grad_refs], axis=0)
        right = jnp.concatenate([r[q, p] for r in panel_refs for q in range(4)], axis=0)
        both = mm(grads, right, TN)
        out_ref[p] = jnp.where(first, both[:HALF], both[HALF:])


def final_kernel(
    x_ref, dleft_ref, dr_a_ref, dr_b_ref, mask_ref, bound_ref, gain_ref, w_t_ref, w_ref, gate_ref,
    q0, q1, q2, q3, prev_ref, out_ref, g_ref, buf, wide,
):
    values = to_channels(x_ref[...].reshape(LANES, WIDTH))
    normed_f, centred, inverse = norm_channels(values, gain_ref[...])
    normed = normed_f.astype(BF16)
    mask = mask_ref[...]
    bound = bound_ref[...]

    gates = mm(w_t_ref[: 2 * WIDTH], normed, NN)
    sig = jax.nn.sigmoid(gates[:WIDTH])
    d_left = channels_of(dleft_ref[...], buf, wide)
    d_gate_a = (d_left * mask * gates[WIDTH:] * sig * (1.0 - sig)).astype(BF16)
    d_value_a = (d_left * mask * sig).astype(BF16)

    gates = mm(w_t_ref[2 * WIDTH :], normed, NN)
    sig = jax.nn.sigmoid(gates[:WIDTH])
    inside = jnp.abs(mask * sig * gates[WIDTH:]) <= bound
    d_right = channels_of(dr_a_ref[...].astype(F32) + dr_b_ref[0].astype(F32), buf, wide)
    d_right = jnp.where(inside, d_right, 0.0)
    d_gate_b = (d_right * mask * gates[WIDTH:] * sig * (1.0 - sig)).astype(BF16)
    d_value_b = (d_right * mask * sig).astype(BF16)

    d_proj = jnp.concatenate([d_gate_a, d_value_a, d_gate_b, d_value_b], axis=0)
    g_ref[...] = prev_ref[...] + mm(normed, d_proj, NT)
    d_gate = jnp.concatenate([q[...] for q in (q0, q1, q2, q3)], axis=1).reshape(LANES, WIDTH)
    d_normed = mm(w_ref[...], d_proj, NN) + mm(gate_ref[...], d_gate, NT)
    d_pair = norm_back_channels(d_normed, centred, inverse, gain_ref[...]).astype(BF16)
    out_ref[...] = to_cells(d_pair).astype(BF16).reshape(SUB, HALF, WIDTH)


def whole(array):
    return pl.BlockSpec(array.shape, lambda i: (0,) * array.ndim)


def block(shape, at):
    return pl.BlockSpec(shape, lambda i: at)


SMEM = pl.BlockSpec(memory_space=pltpu.SMEM)
BUF = pltpu.VMEM((LANES, WIDTH), F32)
WIDE = pltpu.VMEM((WIDTH, LANES), F32)
PANEL = jax.ShapeDtypeStruct((HALF, SUB, WIDTH), BF16)
PANEL_SPEC = pl.BlockSpec((GROUP, SUB, WIDTH), lambda i: (i, 0, 0))
FOUR = jax.ShapeDtypeStruct((4, HALF, SUB, WIDTH), BF16)
FOUR_SPEC = pl.BlockSpec((4, GROUP, SUB, WIDTH), lambda i: (0, i, 0, 0))
LEFT_SPEC = pl.BlockSpec((GROUP, 2, HALF, WIDTH), lambda i: (i, 0, 0, 0))


def right_part(s, pair, gain, w_b, mask, bound):
    return pl.pallas_call(
        right_kernel,
        grid=(1,),
        out_shape=PANEL,
        in_specs=[
            block((SUB, HALF, WIDTH), (s, 0, 0)), whole(gain), whole(w_b),
            block((1, LANES), (0, s)), block((1, LANES), (0, s)),
        ],
        out_specs=block((HALF, SUB, WIDTH), (0, 0, 0)),
        scratch_shapes=[BUF],
        compiler_params=params(),
        cost_estimate=cost(4 * LANES * WIDTH * WIDTH, 1 << 19, LANES * WIDTH),
        name="right_part",
    )(pair, gain, w_b, mask, bound)


def left_part(pair, gain, w_a, mask):
    return pl.pallas_call(
        left_kernel,
        grid=(HALF // SUB,),
        out_shape=jax.ShapeDtypeStruct((HALF, 2, HALF, WIDTH), BF16),
        in_specs=[
            pl.BlockSpec((SUB, HALF, WIDTH), lambda i: (i, 0, 0)), whole(gain), whole(w_a),
            pl.BlockSpec((1, LANES), lambda i: (0, i)),
        ],
        out_specs=pl.BlockSpec((HALF, 2, SUB, WIDTH), lambda i: (0, 0, i, 0)),
        scratch_shapes=[BUF],
        compiler_params=params(),
        cost_estimate=cost(16 * LANES * WIDTH * WIDTH, 3 << 20, 4 * LANES * WIDTH),
        name="left_part",
    )(pair, gain, w_a, mask)


def tri_part(place, slots, left):
    return pl.pallas_call(
        tri_kernel,
        grid=(HALF // GROUP,),
        out_shape=(FOUR, FOUR),
        in_specs=[SMEM] + [PANEL_SPEC] * 4 + [LEFT_SPEC],
        out_specs=(FOUR_SPEC, FOUR_SPEC),
        compiler_params=params(),
        cost_estimate=cost(2 * HALF * HALF * WIDTH * WIDTH, 5 << 20),
        name="tri_part",
    )(place, *slots, left)


def mid_part(s, parts, pair, grad, gain_in, gain_out, gate_t, out_t, w_out):
    square = jax.ShapeDtypeStruct((WIDTH, WIDTH), F32)
    columns = block((HALF, SUB, WIDTH), (0, s, 0))
    small = [gain_in, gain_out, gate_t, out_t, w_out]
    return pl.pallas_call(
        mid_kernel,
        grid=(1,),
        out_shape=(PANEL, PANEL, square, square),
        in_specs=[block((HALF, SUB, WIDTH), (0, 0, 0))] * 3 + [columns] * 2 + [whole(a) for a in small],
        out_specs=(
            block(PANEL.shape, (0, 0, 0)), block(PANEL.shape, (0, 0, 0)),
            block(square.shape, (0, 0)), block(square.shape, (0, 0)),
        ),
        scratch_shapes=[BUF, WIDE],
        compiler_params=params(),
        cost_estimate=cost(12 * LANES * WIDTH * WIDTH, 2 << 20, LANES * WIDTH),
        name="mid_part",
    )(*parts, pair, grad, *small)


def dright_part(place, blocks, left):
    return pl.pallas_call(
        dright_kernel,
        grid=(HALF // GROUP,),
        out_shape=FOUR,
        in_specs=[SMEM] + [PANEL_SPEC] * 4 + [LEFT_SPEC],
        out_specs=FOUR_SPEC,
        compiler_params=params(),
        cost_estimate=cost(2 * HALF * HALF * WIDTH * WIDTH, 4 << 20),
        name="dright_part",
    )(place, *blocks, left)


def dleft_part(grads, panels):
    return pl.pallas_call(
        dleft_kernel,
        grid=(HALF // GROUP,),
        out_shape=jax.ShapeDtypeStruct((HALF, HALF, WIDTH), F32),
        in_specs=[PANEL_SPEC] * len(grads) + [FOUR_SPEC] * len(panels),
        out_specs=pl.BlockSpec((GROUP, HALF, WIDTH), lambda i: (i, 0, 0)),
        compiler_params=params(),
        cost_estimate=cost(8 * HALF * HALF * WIDTH * WIDTH, 10 << 20),
        name="dleft_part",
    )(*grads, *panels)


def final_part(s, pair, dleft, dr_a, dr_b, mask, bound, gain, w_t, w_proj, w_gate, gates, so_far, into):
    small = [gain, w_t, w_proj, w_gate]
    in_specs = [
        block((SUB, HALF, WIDTH), (s, 0, 0)),
        block((HALF, SUB, WIDTH), (0, s, 0)),
        block((HALF, SUB, WIDTH), (0, 0, 0)),
        block((1, HALF, SUB, WIDTH), (0, 0, 0, 0)),
        block((1, LANES), (0, s)),
        block((1, LANES), (0, s)),
    ]
    in_specs += [whole(a) for a in small]
    in_specs += [block((SUB, SUB, WIDTH), (s, 0, 0))] * 4 + [whole(so_far)]
    operands = [pair, dleft, dr_a, dr_b, mask, bound, *small, *gates, so_far]
    aliases = {}
    body = final_kernel
    if into is not None:
        in_specs.append(pl.BlockSpec(memory_space=pl.ANY))
        aliases = {len(operands): 0}
        operands.append(into)

        def body(*refs):
            count = len(operands) - 1
            final_kernel(*refs[:count], *refs[count + 1 :])

    return pl.pallas_call(
        body,
        grid=(1,),
        out_shape=(
            jax.ShapeDtypeStruct((HALF, HALF, WIDTH), BF16),
            jax.ShapeDtypeStruct(so_far.shape, F32),
        ),
        in_specs=in_specs,
        out_specs=(block((SUB, HALF, WIDTH), (s, 0, 0)), block(so_far.shape, (0, 0))),
        scratch_shapes=[BUF, WIDE],
        input_output_aliases=aliases,
        compiler_params=params(),
        cost_estimate=cost(26 * LANES * WIDTH * WIDTH, 3 << 20, 2 * LANES * WIDTH),
        name="final_part",
    )(*operands)


def ring_order(count):
    return [0] + list(range(1, count, 2)) + list(reversed(range(2, count, 2)))


def blocked(pair_tiles, grad_out, exponents, token_mask, gain_in, w_proj, w_gate, gain_out, w_out):
    rows, cols, width = pair_tiles.shape
    crop_len = token_mask.shape[0]
    parts = rows // SUB
    z = lax.axis_index("row")
    q = lax.axis_index("col")
    core = q % 2

    order = ring_order(4)
    hops = [(order[k], order[(k + 1) % 4]) for k in range(4)]
    at = jnp.array([order.index(k) for k in range(4)], jnp.int32)
    across = [(k, k ^ 2) for k in range(4)]
    beside = [(k, k ^ 1) for k in range(4)]

    def forward(a):
        return lax.ppermute(a, "row", hops)

    def over_x(a):
        return lax.ppermute(a, "col", across)

    def over_core(a):
        return lax.ppermute(a, "col", beside)

    slot_block = jnp.array(order, jnp.int32)[(at[z] - jnp.arange(4)) % 4]
    other = slot_block ^ q
    slot_to_rel = (other % 2) * 2 + other // 2
    rel = jnp.arange(4)
    rel_block = q ^ ((rel % 2) * 2 + rel // 2)
    rel_to_slot = (at[z] - at[rel_block]) % 4

    maskf = token_mask.astype(F32)
    mask_rows = lax.dynamic_slice_in_dim(maskf, z * rows, rows)
    mask_cols = lax.dynamic_slice_in_dim(maskf, q * cols, cols)
    mask = (mask_rows[:, None] * mask_cols[None, :]).reshape(1, rows * cols)
    bound = (448.0 * jnp.exp2(exponents.astype(F32))).reshape(1, rows * cols)
    gain_in = gain_in.reshape(width, 1)
    gain_out = gain_out.reshape(width, 1)
    w_t = w_proj.T
    gate_t = w_gate.T
    out_t = w_out.T

    slots = []
    for s in range(parts):
        held = [right_part(s, pair_tiles, gain_in, w_t[2 * width :], mask, bound)]
        for _ in range(3):
            held.append(forward(held[-1]))
        slots.append(held)
    left = left_part(pair_tiles, gain_in, w_t[: 2 * width], mask)

    grads, panels, gates, drights = [], [], [], []
    g_out = g_gate = 0.0
    for s in range(parts):
        tri, panel = tri_part(slot_to_rel, slots[s], left)
        got = over_core(tri[2:])
        mine = over_x((tri[1].astype(F32) + got[1].astype(F32)).astype(BF16))
        d_tri, d_gate, part_out, part_gate = mid_part(
            s, (tri[0], got[0], mine), pair_tiles, grad_out, gain_in, gain_out, gate_t, out_t, w_out
        )
        g_out, g_gate = g_out + part_out, g_gate + part_gate
        far = over_x(d_tri)
        blocks = [d_tri, far, over_core(d_tri), over_core(far)]
        part = dright_part(rel_to_slot, blocks, left)
        total = part[1]
        for m in (2, 3):
            total = (forward(total).astype(F32) + part[m].astype(F32)).astype(BF16)
        drights.append((forward(total), part))
        grads += blocks
        panels.append(panel)
        gates.append(d_gate)
    d_left = dleft_part(grads, panels)

    d_pair = None
    g_proj = jnp.zeros((width, 4 * width), F32)
    for s in range(parts):
        d_pair, g_proj = final_part(
            s, pair_tiles, d_left, *drights[s], mask, bound, gain_in, w_t, w_proj, w_gate, gates, g_proj, d_pair
        )

    def summed(a):
        half = a.shape[0] // 2
        mine = lax.dynamic_slice_in_dim(a, core * half, half)
        mine = mine + over_core(lax.dynamic_slice_in_dim(a, (1 - core) * half, half))
        mine = mine + over_x(mine)
        for bit in (1, 2):
            mine = mine + lax.ppermute(mine, "row", [(k, k ^ bit) for k in range(4)])
        theirs = over_core(mine)
        low = jnp.where(core == 0, mine, theirs)
        high = jnp.where(core == 0, theirs, mine)
        return jnp.concatenate([low, high], axis=0) / crop_len

    early = summed(jnp.concatenate([g_out, g_gate], axis=0))
    return d_pair, summed(g_proj), early[width:], early[:width]


def local(pair_tiles, *rest, rows_over, cols_over):
    if pair_tiles.shape == (HALF, HALF, WIDTH) and rows_over == cols_over == 4:
        return blocked(pair_tiles, *rest)
    return plain(pair_tiles, *rest)


def solution(mesh):
    return jax.shard_map(
        functools.partial(local, rows_over=mesh.shape["row"], cols_over=mesh.shape["col"]),
        mesh=mesh,
        in_specs=(
            P(("crop", "row"), "col", None),
            P(("crop", "row"), "col", None),
            P(("crop", "row"), "col"),
            P("crop"),
            P(),
            P(),
            P(),
            P(),
            P(),
        ),
        out_specs=(
            P(("crop", "row"), "col", None),
            P("crop", None),
            P("crop", None),
            P("crop", None),
        ),
        check_vma=False,
    )
```

```python
import functools

import jax
import jax.numpy as jnp
from jax import lax
from jax.experimental import pallas as pl
from jax.experimental.pallas import tpu as pltpu
from jax.sharding import PartitionSpec as P

EPS = 1e-05


def layer_norm(values, gain):
    center = jnp.mean(values, axis=-1, keepdims=True)
    spread = jnp.mean((values - center) ** 2, axis=-1, keepdims=True)
    inverse = lax.rsqrt(spread + EPS)
    centred = (values - center) * inverse
    return (centred * gain, centred, inverse)


def norm_back(upstream, centred, inverse, gain):
    scaled = upstream * gain
    first = jnp.mean(scaled, axis=-1, keepdims=True)
    second = jnp.mean(scaled * centred, axis=-1, keepdims=True)
    return inverse * (scaled - first - centred * second)


def plain(pair_tiles, grad_out, exponents, token_mask, gain_in, w_proj, w_gate, gain_out, w_out):
    f32 = jnp.float32
    bf16 = jnp.bfloat16
    rows, cols, width = pair_tiles.shape
    crop_len = token_mask.shape[0]
    row_at = lax.axis_index("row")
    col_at = lax.axis_index("col")
    maskf = token_mask.astype(f32)
    mask_rows = lax.dynamic_slice_in_dim(maskf, row_at * rows, rows)
    mask_cols = lax.dynamic_slice_in_dim(maskf, col_at * cols, cols)
    pair_mask = (mask_rows[:, None] * mask_cols[None, :])[..., None]
    normed_f, centred, inverse = layer_norm(pair_tiles.astype(f32), gain_in)
    normed = normed_f.astype(bf16)
    flat = normed.reshape(-1, width)
    projected = jnp.dot(flat, w_proj, preferred_element_type=f32).reshape(rows, cols, 4 * width)
    gate_a = projected[..., :width]
    value_a = projected[..., width : 2 * width]
    gate_b = projected[..., 2 * width : 3 * width]
    value_b = projected[..., 3 * width :]
    sig_a = jax.nn.sigmoid(gate_a)
    sig_b = jax.nn.sigmoid(gate_b)
    left = (pair_mask * sig_a * value_a).astype(bf16)
    right_raw = pair_mask * sig_b * value_b
    bound = (448.0 * jnp.exp2(exponents.astype(f32)))[..., None]
    right = jnp.clip(right_raw, -bound, bound).astype(bf16)
    inside = (jnp.abs(right_raw) <= bound).astype(f32)
    panel = lax.all_gather(right, "row", axis=0, tiled=True)
    tri_cols = lax.psum_scatter(
        jnp.einsum("jkc,ikc->jic", panel, left, preferred_element_type=f32).astype(jnp.bfloat16),
        "col",
        scatter_dimension=0,
        tiled=True,
    ).astype(jnp.float32)
    tri = jnp.transpose(tri_cols, (1, 0, 2))
    tnorm_f, tcentred, tinverse = layer_norm(tri, gain_out)
    tnorm = tnorm_f.astype(bf16)
    tflat = tnorm.reshape(-1, width)
    opened = jax.nn.sigmoid(jnp.dot(flat, w_gate, preferred_element_type=f32)).reshape(
        rows, cols, width
    )
    outproj = jnp.dot(tflat, w_out, preferred_element_type=f32).reshape(rows, cols, width)
    upstream = grad_out.astype(f32)
    d_open = upstream * outproj
    d_outproj = (upstream * opened).astype(bf16).reshape(-1, width)
    g_out = jnp.dot(tflat.T, d_outproj, preferred_element_type=f32)
    d_tnorm = jnp.dot(d_outproj, w_out.T, preferred_element_type=f32).reshape(rows, cols, width)
    d_tri = norm_back(d_tnorm, tcentred, tinverse, gain_out).astype(bf16)
    d_gatepre = (d_open * opened * (1.0 - opened)).astype(bf16).reshape(-1, width)
    g_gate = jnp.dot(flat.T, d_gatepre, preferred_element_type=f32)
    grad_full = lax.all_gather(d_tri, "col", axis=1, tiled=True)
    d_left = jnp.einsum("ijc,jkc->ikc", grad_full, panel, preferred_element_type=f32)
    d_right = (
        lax.psum_scatter(
            jnp.einsum("ijc,ikc->jkc", grad_full, left, preferred_element_type=f32).astype(
                jnp.bfloat16
            ),
            "row",
            scatter_dimension=0,
            tiled=True,
        ).astype(jnp.float32)
        * inside
    )
    d_gate_a = d_left * pair_mask * value_a * sig_a * (1.0 - sig_a)
    d_value_a = d_left * pair_mask * sig_a
    d_gate_b = d_right * pair_mask * value_b * sig_b * (1.0 - sig_b)
    d_value_b = d_right * pair_mask * sig_b
    d_proj = (
        jnp.concatenate([d_gate_a, d_value_a, d_gate_b, d_value_b], axis=-1)
        .astype(bf16)
        .reshape(-1, 4 * width)
    )
    g_proj = jnp.dot(flat.T, d_proj, preferred_element_type=f32)
    d_normed = jnp.dot(d_proj, w_proj.T, preferred_element_type=f32) + jnp.dot(
        d_gatepre, w_gate.T, preferred_element_type=f32
    )
    d_pair = norm_back(d_normed.reshape(rows, cols, width), centred, inverse, gain_in).astype(bf16)
    sum_proj, sum_gate, sum_out = lax.psum((g_proj, g_gate, g_out), ("row", "col"))
    return (d_pair, sum_proj / crop_len, sum_gate / crop_len, sum_out / crop_len)


SUB = 16
HALF = 64
WIDTH = 128
LANES = SUB * HALF
GROUP = 16
NT = (((1,), (1,)), ((), ()))
NN = (((1,), (0,)), ((), ()))
TN = (((0,), (0,)), ((), ()))
F32 = jnp.float32
BF16 = jnp.bfloat16


def mm(a, b, dims):
    return lax.dot_general(a, b, dims, preferred_element_type=F32)


def params():
    return pltpu.CompilerParams(vmem_limit_bytes=40 * 1024 * 1024)


def cost(flops, size, exps=0):
    return pl.CostEstimate(flops=flops, bytes_accessed=size, transcendentals=exps)


def first_half(rows):
    return lax.broadcasted_iota(jnp.int32, (rows, WIDTH), 1) < HALF


def swap_halves(a, b):
    first = first_half(HALF)
    return (
        jnp.where(first, a, pltpu.roll(b, HALF, 1)),
        jnp.where(first, pltpu.roll(a, HALF, 1), b),
    )


def eye():
    row = lax.broadcasted_iota(jnp.int32, (WIDTH, WIDTH), 0)
    lane = lax.broadcasted_iota(jnp.int32, (WIDTH, WIDTH), 1)
    return (row == lane).astype(F32).astype(BF16)


def to_channels(cells):
    return mm(eye(), cells, NT)


def to_cells(channels):
    return mm(channels, eye(), TN)


def stage_rows(channels, buf):
    for t in range(SUB // 2):
        part = channels[:, t * WIDTH : (t + 1) * WIDTH]
        one, two = swap_halves(part[:HALF], part[HALF:])
        buf[(2 * t) * HALF : (2 * t + 1) * HALF, :] = one
        buf[(2 * t + 1) * HALF : (2 * t + 2) * HALF, :] = two


def panel_row(buf, p):
    return buf[pl.ds(p, SUB, stride=HALF), :]


def channels_of(panels, buf, out):
    buf[...] = panels.reshape(LANES, WIDTH)
    for t in range(SUB // 2):
        one = buf[pl.ds(2 * t, HALF, stride=SUB), :]
        two = buf[pl.ds(2 * t + 1, HALF, stride=SUB), :]
        low, high = swap_halves(one, two)
        out[:HALF, t * WIDTH : (t + 1) * WIDTH] = low
        out[HALF:, t * WIDTH : (t + 1) * WIDTH] = high
    return out[...]


def norm_channels(values, gain):
    center = jnp.mean(values, axis=0, keepdims=True)
    spread = jnp.mean((values - center) ** 2, axis=0, keepdims=True)
    inverse = lax.rsqrt(spread + EPS)
    centred = (values - center) * inverse
    return centred * gain, centred, inverse


def norm_back_channels(upstream, centred, inverse, gain):
    scaled = upstream * gain
    first = jnp.mean(scaled, axis=0, keepdims=True)
    second = jnp.mean(scaled * centred, axis=0, keepdims=True)
    return inverse * (scaled - first - centred * second)


def column(row):
    at = lax.broadcasted_iota(jnp.int32, (WIDTH, WIDTH), 0)
    lane = lax.broadcasted_iota(jnp.int32, (WIDTH, WIDTH), 1)
    return jnp.sum(jnp.where(at == lane, row, 0.0), axis=1, keepdims=True)


def mask_lanes(token_ref, s):
    valid = jnp.sum(token_ref[...].astype(F32), axis=1, keepdims=True)
    lane = lax.broadcasted_iota(jnp.int32, (1, LANES), 1)
    row = lane // HALF + (lax.axis_index("row") * HALF + s * SUB)
    col = lane % HALF + lax.axis_index("col") * HALF
    return (jnp.maximum(row, col).astype(F32) < valid).astype(F32)


def bound_lanes(exponent_ref):
    bound = 448.0 * jnp.exp2(exponent_ref[...].astype(F32))
    return jnp.concatenate([bound[i : i + 1] for i in range(SUB)], axis=1)


def normed_cells(x_ref, gain_ref):
    gain = column(gain_ref[...])
    normed, centred, inverse = norm_channels(to_channels(x_ref[...].reshape(LANES, WIDTH)), gain)
    return normed.astype(BF16), centred, inverse, gain


def right_kernel(s, x_ref, gain_ref, w_ref, token_ref, exponent_ref, out_ref, buf):
    normed = normed_cells(x_ref, gain_ref)[0]
    proj = mm(w_ref[...], normed, TN)
    raw = mask_lanes(token_ref, s) * jax.nn.sigmoid(proj[:WIDTH]) * proj[WIDTH:]
    bound = bound_lanes(exponent_ref)
    stage_rows(jnp.clip(raw, -bound, bound), buf)
    for p in range(HALF):
        out_ref[p] = panel_row(buf, p).astype(BF16)


def left_kernel(x_ref, gain_ref, w_ref, token_ref, out_ref, buf):
    normed = normed_cells(x_ref, gain_ref)[0]
    proj = mm(w_ref[...], normed, TN)
    mask = mask_lanes(token_ref, pl.program_id(0))
    stage_rows(mask * jax.nn.sigmoid(proj[:WIDTH]) * proj[WIDTH:], buf)
    first = first_half(SUB)
    for p in range(HALF):
        row = panel_row(buf, p)
        out_ref[p, 0] = jnp.where(first, row, 0.0).astype(BF16)
        out_ref[p, 1] = jnp.where(first, 0.0, row).astype(BF16)


def tri_kernel(own, up1, up2, up3, down1, down2, down3, left_ref, keep_ref, near_ref, send_ref, panel_ref):
    z, q = lax.axis_index("row"), lax.axis_index("col")
    for d in range(4):
        other = ((z + d) & 3) ^ q
        place = (other & 1) * 2 + (other >> 1)
        if d == 0:
            panel_ref[place] = own[...]
        else:
            panel_ref[place] = (up1, up2, up3)[d - 1][...] + (down1, down2, down3)[3 - d][...]
    for p in range(GROUP):
        right = jnp.concatenate([panel_ref[r, p] for r in range(4)], axis=0)
        tri = mm(right, left_ref[p].reshape(WIDTH, WIDTH), NT).astype(BF16)
        keep_ref[p] = tri[:SUB]
        near_ref[p] = tri[SUB : 2 * SUB]
        send_ref[0, p] = tri[2 * SUB : 3 * SUB]
        send_ref[1, p] = tri[3 * SUB :]


def mid_kernel(
    a_ref, b_ref, c_ref, x_ref, grad_ref, gain_in_ref, gain_out_ref, gate_ref, out_w_ref,
    dtri_ref, dgate_ref, g_out_ref, g_gate_ref, buf, wide,
):
    gain_out = column(gain_out_ref[...])
    tri = channels_of(
        a_ref[...].astype(F32) + b_ref[0].astype(F32) + c_ref[...].astype(F32), buf, wide
    )
    tnorm_f, tcentred, tinverse = norm_channels(tri, gain_out)
    tnorm = tnorm_f.astype(BF16)

    def turned(ref):
        buf[...] = ref[...].astype(F32).reshape(LANES, WIDTH)
        rows = [buf[pl.ds(j, HALF, stride=SUB), :] for j in range(SUB)]
        return to_channels(jnp.concatenate(rows, axis=0).astype(BF16))

    normed = norm_channels(turned(x_ref), column(gain_in_ref[...]))[0].astype(BF16)
    upstream = turned(grad_ref)
    opened = jax.nn.sigmoid(mm(gate_ref[...], normed, TN))
    outproj = mm(out_w_ref[...], tnorm, TN)
    d_open = upstream * outproj
    d_outproj = (upstream * opened).astype(BF16)
    g_out_ref[...] = mm(tnorm, d_outproj, NT)
    d_tnorm = mm(out_w_ref[...], d_outproj, NN)
    d_tri = norm_back_channels(d_tnorm, tcentred, tinverse, gain_out)
    d_gatepre = (d_open * opened * (1.0 - opened)).astype(BF16)
    g_gate_ref[...] = mm(normed, d_gatepre, NT)
    stage_rows(d_tri, buf)
    for p in range(HALF):
        dtri_ref[p] = panel_row(buf, p).astype(BF16)
    buf[...] = to_cells(d_gatepre)
    for i in range(HALF):
        dgate_ref[i] = panel_row(buf, i).astype(BF16)


def dright_kernel(d0, d1, d2, d3, left_ref, p0, p1, p2, p3, held):
    z, q = lax.axis_index("row"), lax.axis_index("col")
    for r, ref in enumerate((d0, d1, d2, d3)):
        slot = ((q ^ ((r % 2) * 2 + r // 2)) - z + 4) & 3
        held[slot] = ref[...]
    for p in range(GROUP):
        grads = jnp.concatenate([held[d, p] for d in range(4)], axis=0)
        part = mm(grads, left_ref[p].reshape(WIDTH, WIDTH), NN).astype(BF16)
        for d, ref in enumerate((p0, p1, p2, p3)):
            ref[p] = part[d * SUB : (d + 1) * SUB]


def dleft_kernel(*refs):
    out_ref = refs[-1]
    parts = (len(refs) - 1) // 5
    grad_refs, panel_refs = refs[: 4 * parts], refs[4 * parts : 5 * parts]
    first = first_half(HALF)
    for p in range(GROUP):
        grads = jnp.concatenate([d[p] for d in grad_refs], axis=0)
        right = jnp.concatenate([r[q, p] for r in panel_refs for q in range(4)], axis=0)
        both = mm(grads, right, TN)
        out_ref[p] = jnp.where(first, both[:HALF], both[HALF:])


def gate_grads(upstream, mask, sig, value):
    d_gate = (upstream * mask * value * sig * (1.0 - sig)).astype(BF16)
    d_value = (upstream * mask * sig).astype(BF16)
    return jnp.concatenate([d_gate, d_value], axis=0)


def final_a_kernel(
    x_ref, dleft_ref, token_ref, gain_ref, w_ref, gate_ref, q0, q1, q2, q3, out_ref, g_ref, buf, wide
):
    s = pl.program_id(0)
    normed = normed_cells(x_ref, gain_ref)[0]
    proj = mm(w_ref[...], normed, TN)
    d_left = channels_of(dleft_ref[...], buf, wide)
    d_proj = gate_grads(d_left, mask_lanes(token_ref, s), jax.nn.sigmoid(proj[:WIDTH]), proj[WIDTH:])
    d_gate = jnp.concatenate([q[...] for q in (q0, q1, q2, q3)], axis=1).reshape(LANES, WIDTH)
    out_ref[...] = mm(w_ref[...], d_proj, NN) + mm(gate_ref[...], d_gate, NT)

    @pl.when(s == 0)
    def start():
        g_ref[...] = jnp.zeros_like(g_ref)

    g_ref[...] += mm(normed, d_proj, NT)


def final_b_kernel(
    s, x_ref, part_ref, a_ref, b_ref, c_ref, token_ref, exponent_ref, gain_ref, w_ref, into_ref,
    out_ref, g_ref, buf, wide,
):
    normed, centred, inverse, gain = normed_cells(x_ref, gain_ref)
    proj = mm(w_ref[...], normed, TN)
    mask = mask_lanes(token_ref, s)
    sig = jax.nn.sigmoid(proj[:WIDTH])
    inside = jnp.abs(mask * sig * proj[WIDTH:]) <= bound_lanes(exponent_ref)
    d_right = channels_of(
        a_ref[...].astype(F32) + b_ref[...].astype(F32) + c_ref[...].astype(F32), buf, wide
    )
    d_proj = gate_grads(jnp.where(inside, d_right, 0.0), mask, sig, proj[WIDTH:])
    g_ref[...] = mm(normed, d_proj, NT)
    d_normed = part_ref[...] + mm(w_ref[...], d_proj, NN)
    d_pair = norm_back_channels(d_normed, centred, inverse, gain).astype(BF16)
    out_ref[...] = to_cells(d_pair).astype(BF16).reshape(SUB, HALF, WIDTH)


def whole(array):
    return pl.BlockSpec(array.shape, lambda i: (0,) * array.ndim)


def block(shape, at):
    return pl.BlockSpec(shape, lambda i: at)


BUF = pltpu.VMEM((LANES, WIDTH), F32)
WIDE = pltpu.VMEM((WIDTH, LANES), F32)
PANEL = jax.ShapeDtypeStruct((HALF, SUB, WIDTH), BF16)
PANEL_SPEC = pl.BlockSpec((GROUP, SUB, WIDTH), lambda i: (i, 0, 0))
FOUR = jax.ShapeDtypeStruct((4, HALF, SUB, WIDTH), BF16)
FOUR_SPEC = pl.BlockSpec((4, GROUP, SUB, WIDTH), lambda i: (0, i, 0, 0))
TWO = jax.ShapeDtypeStruct((2, HALF, SUB, WIDTH), BF16)
TWO_SPEC = pl.BlockSpec((2, GROUP, SUB, WIDTH), lambda i: (0, i, 0, 0))
LEFT_SPEC = pl.BlockSpec((GROUP, 2, HALF, WIDTH), lambda i: (i, 0, 0, 0))
WHOLE_PANEL = pl.BlockSpec(PANEL.shape, lambda i: (0, 0, 0))


def right_part(s, pair, gain, w_proj, tokens, exponents):
    return pl.pallas_call(
        functools.partial(right_kernel, s),
        grid=(1,),
        out_shape=PANEL,
        in_specs=[
            block((SUB, HALF, WIDTH), (s, 0, 0)), whole(gain), block((WIDTH, 2 * WIDTH), (0, 1)),
            whole(tokens), block((SUB, HALF), (s, 0)),
        ],
        out_specs=WHOLE_PANEL,
        scratch_shapes=[BUF],
        compiler_params=params(),
        cost_estimate=cost(4 * LANES * WIDTH * WIDTH, 1 << 19, LANES * WIDTH),
        name="right_part",
    )(pair, gain, w_proj, tokens, exponents)


def left_part(pair, gain, w_proj, tokens):
    return pl.pallas_call(
        left_kernel,
        grid=(HALF // SUB,),
        out_shape=jax.ShapeDtypeStruct((HALF, 2, HALF, WIDTH), BF16),
        in_specs=[
            pl.BlockSpec((SUB, HALF, WIDTH), lambda i: (i, 0, 0)), whole(gain),
            block((WIDTH, 2 * WIDTH), (0, 0)), whole(tokens),
        ],
        out_specs=pl.BlockSpec((HALF, 2, SUB, WIDTH), lambda i: (0, 0, i, 0)),
        scratch_shapes=[BUF],
        compiler_params=params(),
        cost_estimate=cost(16 * LANES * WIDTH * WIDTH, 3 << 20, 4 * LANES * WIDTH),
        name="left_part",
    )(pair, gain, w_proj, tokens)


def tri_part(slots, left):
    return pl.pallas_call(
        tri_kernel,
        grid=(HALF // GROUP,),
        out_shape=(PANEL, PANEL, TWO, FOUR),
        in_specs=[PANEL_SPEC] * 7 + [LEFT_SPEC],
        out_specs=(PANEL_SPEC, PANEL_SPEC, TWO_SPEC, FOUR_SPEC),
        compiler_params=params(),
        cost_estimate=cost(2 * HALF * HALF * WIDTH * WIDTH, 5 << 20),
        name="tri_part",
    )(*slots, left)


def mid_part(s, parts, pair, grad, gain_in, gain_out, w_gate, w_out):
    square = jax.ShapeDtypeStruct((WIDTH, WIDTH), F32)
    columns = block((HALF, SUB, WIDTH), (0, s, 0))
    small = [gain_in, gain_out, w_gate, w_out]
    return pl.pallas_call(
        mid_kernel,
        grid=(1,),
        out_shape=(PANEL, PANEL, square, square),
        in_specs=[WHOLE_PANEL, block((1, HALF, SUB, WIDTH), (0, 0, 0, 0)), WHOLE_PANEL]
        + [columns] * 2
        + [whole(a) for a in small],
        out_specs=(WHOLE_PANEL, WHOLE_PANEL, block(square.shape, (0, 0)), block(square.shape, (0, 0))),
        scratch_shapes=[BUF, WIDE],
        compiler_params=params(),
        cost_estimate=cost(12 * LANES * WIDTH * WIDTH, 2 << 20, LANES * WIDTH),
        name="mid_part",
    )(*parts, pair, grad, *small)


def dright_part(blocks, left):
    return pl.pallas_call(
        dright_kernel,
        grid=(HALF // GROUP,),
        out_shape=(PANEL,) * 4,
        in_specs=[PANEL_SPEC] * 4 + [LEFT_SPEC],
        out_specs=(PANEL_SPEC,) * 4,
        scratch_shapes=[pltpu.VMEM((4, GROUP, SUB, WIDTH), BF16)],
        compiler_params=params(),
        cost_estimate=cost(2 * HALF * HALF * WIDTH * WIDTH, 4 << 20),
        name="dright_part",
    )(*blocks, left)


def dleft_part(grads, panels):
    return pl.pallas_call(
        dleft_kernel,
        grid=(HALF // GROUP,),
        out_shape=jax.ShapeDtypeStruct((HALF, HALF, WIDTH), F32),
        in_specs=[PANEL_SPEC] * len(grads) + [FOUR_SPEC] * len(panels),
        out_specs=pl.BlockSpec((GROUP, HALF, WIDTH), lambda i: (i, 0, 0)),
        compiler_params=params(),
        cost_estimate=cost(8 * HALF * HALF * WIDTH * WIDTH, 10 << 20),
        name="dleft_part",
    )(*grads, *panels)


def final_a_part(pair, dleft, tokens, gain, w_proj, w_gate, gates):
    return pl.pallas_call(
        final_a_kernel,
        grid=(HALF // SUB,),
        out_shape=(
            jax.ShapeDtypeStruct((WIDTH, HALF * HALF), F32),
            jax.ShapeDtypeStruct((WIDTH, 2 * WIDTH), F32),
        ),
        in_specs=[
            pl.BlockSpec((SUB, HALF, WIDTH), lambda i: (i, 0, 0)),
            pl.BlockSpec((HALF, SUB, WIDTH), lambda i: (0, i, 0)),
            whole(tokens), whole(gain), block((WIDTH, 2 * WIDTH), (0, 0)), whole(w_gate),
        ]
        + [pl.BlockSpec((SUB, SUB, WIDTH), lambda i: (i, 0, 0))] * 4,
        out_specs=(
            pl.BlockSpec((WIDTH, LANES), lambda i: (0, i)),
            block((WIDTH, 2 * WIDTH), (0, 0)),
        ),
        scratch_shapes=[BUF, WIDE],
        compiler_params=params(),
        cost_estimate=cost(56 * LANES * WIDTH * WIDTH, 8 << 20, 4 * LANES * WIDTH),
        name="final_a_part",
    )(pair, dleft, tokens, gain, w_proj, w_gate, *gates)


def final_b_part(s, pair, part, sums, tokens, exponents, gain, w_proj, into):
    return pl.pallas_call(
        functools.partial(final_b_kernel, s),
        grid=(1,),
        out_shape=(
            jax.ShapeDtypeStruct((HALF, HALF, WIDTH), BF16),
            jax.ShapeDtypeStruct((WIDTH, 2 * WIDTH), F32),
        ),
        in_specs=[
            block((SUB, HALF, WIDTH), (s, 0, 0)),
            block((WIDTH, LANES), (0, s)),
            WHOLE_PANEL, WHOLE_PANEL, WHOLE_PANEL,
            whole(tokens), block((SUB, HALF), (s, 0)), whole(gain),
            block((WIDTH, 2 * WIDTH), (0, 1)),
            pl.BlockSpec(memory_space=pl.ANY),
        ],
        out_specs=(block((SUB, HALF, WIDTH), (s, 0, 0)), block((WIDTH, 2 * WIDTH), (0, 0))),
        scratch_shapes=[BUF, WIDE],
        input_output_aliases={9: 0} if into.shape == pair.shape else {},
        compiler_params=params(),
        cost_estimate=cost(14 * LANES * WIDTH * WIDTH, 2 << 20, LANES * WIDTH),
        name="final_b_part",
    )(pair, part, *sums, tokens, exponents, gain, w_proj, into)


def after(array, *others):
    return lax.optimization_barrier((array, *others))[0]


def blocked(pair_tiles, grad_out, exponents, token_mask, gain_in, w_proj, w_gate, gain_out, w_out):
    rows, cols, width = pair_tiles.shape
    crop_len = token_mask.shape[0]
    parts = rows // SUB
    core = lax.axis_index("col") % 2
    x_at = lax.axis_index("col") // 2
    tokens = token_mask.reshape(1, crop_len)
    gain_in = gain_in.reshape(1, width)
    gain_out = gain_out.reshape(1, width)

    def up(a, t):
        return lax.ppermute(a, "row", [(k, k + 1) for k in range(t - 1, 3)])

    def down(a, t):
        return lax.ppermute(a, "row", [(k, k - 1) for k in range(4 - t, 0, -1)])

    def sum_up(a, t):
        return lax.ppermute(a, "row", [(k, k + 1) for k in range(t)])

    def sum_down(a, t):
        return lax.ppermute(a, "row", [(k, k - 1) for k in range(3, 3 - t, -1)])

    def over_x(a):
        return lax.ppermute(a, "col", [(k, k ^ 2) for k in range(4)])

    def over_core(a):
        return lax.ppermute(a, "col", [(k, k ^ 1) for k in range(4)])

    def plus(a, b):
        return (a.astype(F32) + b.astype(F32)).astype(BF16)

    slots = []
    ready = ()
    for s in range(parts):
        own = after(right_part(s, pair_tiles, gain_in, w_proj, tokens, exponents), *ready)
        ups, downs = [own], [own]
        for t in (1, 2, 3):
            ups.append(up(ups[-1], t))
            downs.append(down(downs[-1], t))
        ready = (ups[2], downs[2])
        slots.append((own, *downs[1:], *ups[1:]))
    left = left_part(pair_tiles, gain_in, w_proj, tokens)

    grads, panels, gates, sums = [], [], [], []
    g_out = g_gate = 0.0
    for s in range(parts):
        keep, near, send, panel = tri_part(slots[s], left)
        got = over_core(send)
        mine = over_x(plus(near, got[1]))
        d_tri, d_gate, part_out, part_gate = mid_part(
            s, (keep, got, mine), pair_tiles, grad_out, gain_in, gain_out, w_gate, w_out
        )
        g_out, g_gate = g_out + part_out, g_gate + part_gate
        far = over_x(d_tri)
        blocks = [d_tri, far, over_core(d_tri), over_core(far)]
        part = dright_part(blocks, left)
        rise, fall = part[3], part[1]
        for t in (1, 2):
            rise = plus(sum_up(rise, t), part[3 - t])
            fall = plus(sum_down(fall, t), part[1 + t])
        sums.append((part[0], sum_up(rise, 3), sum_down(fall, 3)))
        grads += blocks
        panels.append(panel)
        gates.append(d_gate)
    d_left = dleft_part(grads, panels)
    partial, g_a = final_a_part(pair_tiles, d_left, tokens, gain_in, w_proj, w_gate, gates)

    d_pair = gain_in
    g_b = []
    for s in range(parts):
        d_pair, part_b = final_b_part(
            s, pair_tiles, partial, sums[s], tokens, exponents, gain_in, w_proj, d_pair
        )
        g_b.append(part_b)

    def exchange(a, send, at):
        half = a.shape[0] // 2
        return lax.dynamic_slice_in_dim(a, at * half, half) + send(
            lax.dynamic_slice_in_dim(a, (1 - at) * half, half)
        )

    def join(a, send, at):
        theirs = send(a)
        return jnp.concatenate([jnp.where(at == 0, a, theirs), jnp.where(at == 0, theirs, a)], axis=0)

    def over_rows(a):
        for bit in (1, 2):
            a = a + lax.ppermute(a, "row", [(k, k ^ bit) for k in range(4)])
        return a

    early = jnp.concatenate([g_out, g_gate, g_a, g_b[0] + g_b[1] + g_b[2]], axis=1)
    early = over_rows(exchange(exchange(early, over_core, core), over_x, x_at))
    early = join(join(early, over_x, x_at), over_core, core)
    late = exchange(g_b[3], over_core, core)
    late = join(over_rows(late + over_x(late)), over_core, core)
    g_proj = jnp.concatenate([early[:, 2 * width : 4 * width], early[:, 4 * width :] + late], axis=1)
    return d_pair, g_proj / crop_len, early[:, width : 2 * width] / crop_len, early[:, :width] / crop_len


def local(pair_tiles, *rest, rows_over, cols_over):
    if pair_tiles.shape == (HALF, HALF, WIDTH) and rows_over == cols_over == 4:
        return blocked(pair_tiles, *rest)
    return plain(pair_tiles, *rest)


def solution(mesh):
    return jax.shard_map(
        functools.partial(local, rows_over=mesh.shape["row"], cols_over=mesh.shape["col"]),
        mesh=mesh,
        in_specs=(
            P(("crop", "row"), "col", None),
            P(("crop", "row"), "col", None),
            P(("crop", "row"), "col"),
            P("crop"),
            P(),
            P(),
            P(),
            P(),
            P(),
        ),
        out_specs=(
            P(("crop", "row"), "col", None),
            P("crop", None),
            P("crop", None),
            P("crop", None),
        ),
        check_vma=False,
    )
```

```python
import functools

import jax
import jax.numpy as jnp
from jax import lax
from jax.experimental import pallas as pl
from jax.experimental.pallas import tpu as pltpu
from jax.sharding import PartitionSpec as P

EPS = 1e-05


def layer_norm(values, gain):
    center = jnp.mean(values, axis=-1, keepdims=True)
    spread = jnp.mean((values - center) ** 2, axis=-1, keepdims=True)
    inverse = lax.rsqrt(spread + EPS)
    centred = (values - center) * inverse
    return (centred * gain, centred, inverse)


def norm_back(upstream, centred, inverse, gain):
    scaled = upstream * gain
    first = jnp.mean(scaled, axis=-1, keepdims=True)
    second = jnp.mean(scaled * centred, axis=-1, keepdims=True)
    return inverse * (scaled - first - centred * second)


def plain(pair_tiles, grad_out, exponents, token_mask, gain_in, w_proj, w_gate, gain_out, w_out):
    f32 = jnp.float32
    bf16 = jnp.bfloat16
    rows, cols, width = pair_tiles.shape
    crop_len = token_mask.shape[0]
    row_at = lax.axis_index("row")
    col_at = lax.axis_index("col")
    maskf = token_mask.astype(f32)
    mask_rows = lax.dynamic_slice_in_dim(maskf, row_at * rows, rows)
    mask_cols = lax.dynamic_slice_in_dim(maskf, col_at * cols, cols)
    pair_mask = (mask_rows[:, None] * mask_cols[None, :])[..., None]
    normed_f, centred, inverse = layer_norm(pair_tiles.astype(f32), gain_in)
    normed = normed_f.astype(bf16)
    flat = normed.reshape(-1, width)
    projected = jnp.dot(flat, w_proj, preferred_element_type=f32).reshape(rows, cols, 4 * width)
    gate_a = projected[..., :width]
    value_a = projected[..., width : 2 * width]
    gate_b = projected[..., 2 * width : 3 * width]
    value_b = projected[..., 3 * width :]
    sig_a = jax.nn.sigmoid(gate_a)
    sig_b = jax.nn.sigmoid(gate_b)
    left = (pair_mask * sig_a * value_a).astype(bf16)
    right_raw = pair_mask * sig_b * value_b
    bound = (448.0 * jnp.exp2(exponents.astype(f32)))[..., None]
    right = jnp.clip(right_raw, -bound, bound).astype(bf16)
    inside = (jnp.abs(right_raw) <= bound).astype(f32)
    panel = lax.all_gather(right, "row", axis=0, tiled=True)
    tri_cols = lax.psum_scatter(
        jnp.einsum("jkc,ikc->jic", panel, left, preferred_element_type=f32).astype(jnp.bfloat16),
        "col",
        scatter_dimension=0,
        tiled=True,
    ).astype(jnp.float32)
    tri = jnp.transpose(tri_cols, (1, 0, 2))
    tnorm_f, tcentred, tinverse = layer_norm(tri, gain_out)
    tnorm = tnorm_f.astype(bf16)
    tflat = tnorm.reshape(-1, width)
    opened = jax.nn.sigmoid(jnp.dot(flat, w_gate, preferred_element_type=f32)).reshape(
        rows, cols, width
    )
    outproj = jnp.dot(tflat, w_out, preferred_element_type=f32).reshape(rows, cols, width)
    upstream = grad_out.astype(f32)
    d_open = upstream * outproj
    d_outproj = (upstream * opened).astype(bf16).reshape(-1, width)
    g_out = jnp.dot(tflat.T, d_outproj, preferred_element_type=f32)
    d_tnorm = jnp.dot(d_outproj, w_out.T, preferred_element_type=f32).reshape(rows, cols, width)
    d_tri = norm_back(d_tnorm, tcentred, tinverse, gain_out).astype(bf16)
    d_gatepre = (d_open * opened * (1.0 - opened)).astype(bf16).reshape(-1, width)
    g_gate = jnp.dot(flat.T, d_gatepre, preferred_element_type=f32)
    grad_full = lax.all_gather(d_tri, "col", axis=1, tiled=True)
    d_left = jnp.einsum("ijc,jkc->ikc", grad_full, panel, preferred_element_type=f32)
    d_right = (
        lax.psum_scatter(
            jnp.einsum("ijc,ikc->jkc", grad_full, left, preferred_element_type=f32).astype(
                jnp.bfloat16
            ),
            "row",
            scatter_dimension=0,
            tiled=True,
        ).astype(jnp.float32)
        * inside
    )
    d_gate_a = d_left * pair_mask * value_a * sig_a * (1.0 - sig_a)
    d_value_a = d_left * pair_mask * sig_a
    d_gate_b = d_right * pair_mask * value_b * sig_b * (1.0 - sig_b)
    d_value_b = d_right * pair_mask * sig_b
    d_proj = (
        jnp.concatenate([d_gate_a, d_value_a, d_gate_b, d_value_b], axis=-1)
        .astype(bf16)
        .reshape(-1, 4 * width)
    )
    g_proj = jnp.dot(flat.T, d_proj, preferred_element_type=f32)
    d_normed = jnp.dot(d_proj, w_proj.T, preferred_element_type=f32) + jnp.dot(
        d_gatepre, w_gate.T, preferred_element_type=f32
    )
    d_pair = norm_back(d_normed.reshape(rows, cols, width), centred, inverse, gain_in).astype(bf16)
    sum_proj, sum_gate, sum_out = lax.psum((g_proj, g_gate, g_out), ("row", "col"))
    return (d_pair, sum_proj / crop_len, sum_gate / crop_len, sum_out / crop_len)


SUB = 16
HALF = 64
WIDTH = 128
LANES = SUB * HALF
GROUP = 16
NT = (((1,), (1,)), ((), ()))
NN = (((1,), (0,)), ((), ()))
TN = (((0,), (0,)), ((), ()))
F32 = jnp.float32
BF16 = jnp.bfloat16


def mm(a, b, dims):
    return lax.dot_general(a, b, dims, preferred_element_type=F32)


def params():
    return pltpu.CompilerParams(vmem_limit_bytes=56 * 1024 * 1024)


def cost(flops, size, exps=0):
    return pl.CostEstimate(flops=flops, bytes_accessed=size, transcendentals=exps)


def first_half(rows):
    return lax.broadcasted_iota(jnp.int32, (rows, WIDTH), 1) < HALF


def swap_halves(a, b):
    first = first_half(HALF)
    return (
        jnp.where(first, a, pltpu.roll(b, HALF, 1)),
        jnp.where(first, pltpu.roll(a, HALF, 1), b),
    )


def eye():
    row = lax.broadcasted_iota(jnp.int32, (WIDTH, WIDTH), 0)
    lane = lax.broadcasted_iota(jnp.int32, (WIDTH, WIDTH), 1)
    return (row == lane).astype(F32).astype(BF16)


def to_channels(cells):
    return mm(eye(), cells, NT)


def to_cells(channels):
    return mm(channels, eye(), TN)


def stage_rows(channels, buf):
    for t in range(SUB // 2):
        part = channels[:, t * WIDTH : (t + 1) * WIDTH]
        one, two = swap_halves(part[:HALF], part[HALF:])
        buf[(2 * t) * HALF : (2 * t + 1) * HALF, :] = one
        buf[(2 * t + 1) * HALF : (2 * t + 2) * HALF, :] = two


def panel_row(buf, p):
    return buf[pl.ds(p, SUB, stride=HALF), :]


def channels_of(panels, buf, out):
    buf[...] = panels.reshape(LANES, WIDTH)
    for t in range(SUB // 2):
        one = buf[pl.ds(2 * t, HALF, stride=SUB), :]
        two = buf[pl.ds(2 * t + 1, HALF, stride=SUB), :]
        low, high = swap_halves(one, two)
        out[:HALF, t * WIDTH : (t + 1) * WIDTH] = low
        out[HALF:, t * WIDTH : (t + 1) * WIDTH] = high
    return out[...]


def norm_channels(values, gain):
    center = jnp.mean(values, axis=0, keepdims=True)
    spread = jnp.mean((values - center) ** 2, axis=0, keepdims=True)
    inverse = lax.rsqrt(spread + EPS)
    centred = (values - center) * inverse
    return centred * gain, centred, inverse


def norm_back_channels(upstream, centred, inverse, gain):
    scaled = upstream * gain
    first = jnp.mean(scaled, axis=0, keepdims=True)
    second = jnp.mean(scaled * centred, axis=0, keepdims=True)
    return inverse * (scaled - first - centred * second)


def column(row):
    at = lax.broadcasted_iota(jnp.int32, (WIDTH, WIDTH), 0)
    lane = lax.broadcasted_iota(jnp.int32, (WIDTH, WIDTH), 1)
    return jnp.sum(jnp.where(at == lane, row, 0.0), axis=1, keepdims=True)


def mask_lanes(token_ref, s):
    valid = jnp.sum(token_ref[...].astype(F32), axis=1, keepdims=True)
    lane = lax.broadcasted_iota(jnp.int32, (1, LANES), 1)
    row = lane // HALF + (lax.axis_index("row") * HALF + s * SUB)
    col = lane % HALF + lax.axis_index("col") * HALF
    return (jnp.maximum(row, col).astype(F32) < valid).astype(F32)


def bound_lanes(exponent_ref):
    bound = 448.0 * jnp.exp2(exponent_ref[...].astype(F32))
    return jnp.concatenate([bound[i : i + 1] for i in range(SUB)], axis=1)


def normed_cells(x_ref, gain_ref):
    gain = column(gain_ref[...])
    normed, centred, inverse = norm_channels(to_channels(x_ref[...].reshape(LANES, WIDTH)), gain)
    return normed.astype(BF16), centred, inverse, gain


def right_kernel(s, x_ref, gain_ref, w_ref, token_ref, exponent_ref, out_ref, buf):
    normed = normed_cells(x_ref, gain_ref)[0]
    proj = mm(w_ref[...], normed, TN)
    raw = mask_lanes(token_ref, s) * jax.nn.sigmoid(proj[:WIDTH]) * proj[WIDTH:]
    bound = bound_lanes(exponent_ref)
    stage_rows(jnp.clip(raw, -bound, bound), buf)
    for p in range(HALF):
        out_ref[p] = panel_row(buf, p).astype(BF16)


def left_kernel(x_ref, gain_ref, w_ref, token_ref, out_ref, buf):
    normed = normed_cells(x_ref, gain_ref)[0]
    proj = mm(w_ref[...], normed, TN)
    mask = mask_lanes(token_ref, pl.program_id(0))
    stage_rows(mask * jax.nn.sigmoid(proj[:WIDTH]) * proj[WIDTH:], buf)
    first = first_half(SUB)
    for p in range(HALF):
        row = panel_row(buf, p)
        out_ref[p, 0] = jnp.where(first, row, 0.0).astype(BF16)
        out_ref[p, 1] = jnp.where(first, 0.0, row).astype(BF16)


def tri_kernel(s0, s1, s2, s3, left_ref, keep_ref, near_ref, send_ref, panel_ref):
    z, q = lax.axis_index("row"), lax.axis_index("col")
    for e, ref in enumerate((s0, s1, s2, s3)):
        other = z ^ e ^ q
        panel_ref[(other & 1) * 2 + (other >> 1)] = ref[...]
    for p in range(GROUP):
        right = jnp.concatenate([panel_ref[r, p] for r in range(4)], axis=0)
        tri = mm(right, left_ref[p].reshape(WIDTH, WIDTH), NT).astype(BF16)
        keep_ref[p] = tri[:SUB]
        near_ref[p] = tri[SUB : 2 * SUB]
        send_ref[0, p] = tri[2 * SUB : 3 * SUB]
        send_ref[1, p] = tri[3 * SUB :]


def mid_kernel(
    a_ref, b_ref, c_ref, x_ref, grad_ref, gain_in_ref, gain_out_ref, gate_ref, out_w_ref,
    dtri_ref, dgate_ref, g_out_ref, g_gate_ref, buf, wide,
):
    gain_out = column(gain_out_ref[...])
    tri = channels_of(
        a_ref[...].astype(F32) + b_ref[0].astype(F32) + c_ref[...].astype(F32), buf, wide
    )
    tnorm_f, tcentred, tinverse = norm_channels(tri, gain_out)
    tnorm = tnorm_f.astype(BF16)

    def turned(ref):
        buf[...] = ref[...].astype(F32).reshape(LANES, WIDTH)
        rows = [buf[pl.ds(j, HALF, stride=SUB), :] for j in range(SUB)]
        return to_channels(jnp.concatenate(rows, axis=0).astype(BF16))

    normed = norm_channels(turned(x_ref), column(gain_in_ref[...]))[0].astype(BF16)
    upstream = turned(grad_ref)
    opened = jax.nn.sigmoid(mm(gate_ref[...], normed, TN))
    outproj = mm(out_w_ref[...], tnorm, TN)
    d_open = upstream * outproj
    d_outproj = (upstream * opened).astype(BF16)
    g_out_ref[...] = mm(tnorm, d_outproj, NT)
    d_tnorm = mm(out_w_ref[...], d_outproj, NN)
    d_tri = norm_back_channels(d_tnorm, tcentred, tinverse, gain_out)
    d_gatepre = (d_open * opened * (1.0 - opened)).astype(BF16)
    g_gate_ref[...] = mm(normed, d_gatepre, NT)
    stage_rows(d_tri, buf)
    for p in range(HALF):
        dtri_ref[p] = panel_row(buf, p).astype(BF16)
    buf[...] = to_cells(d_gatepre)
    for i in range(HALF):
        dgate_ref[i] = panel_row(buf, i).astype(BF16)


def dright_kernel(d0, d1, d2, d3, left_ref, p0, p13, p2, held):
    z, q = lax.axis_index("row"), lax.axis_index("col")
    for r, ref in enumerate((d0, d1, d2, d3)):
        held[q ^ z ^ ((r % 2) * 2 + r // 2)] = ref[...]
    for p in range(GROUP):
        grads = jnp.concatenate([held[d, p] for d in range(4)], axis=0)
        part = mm(grads, left_ref[p].reshape(WIDTH, WIDTH), NN).astype(BF16)
        p0[p] = part[:SUB]
        p13[0, p] = part[SUB : 2 * SUB]
        p2[p] = part[2 * SUB : 3 * SUB]
        p13[1, p] = part[3 * SUB :]


def dleft_kernel(*refs):
    out_ref = refs[-1]
    parts = (len(refs) - 1) // 5
    grad_refs, panel_refs = refs[: 4 * parts], refs[4 * parts : 5 * parts]
    first = first_half(HALF)
    for p in range(GROUP):
        grads = jnp.concatenate([d[p] for d in grad_refs], axis=0)
        right = jnp.concatenate([r[q, p] for r in panel_refs for q in range(4)], axis=0)
        both = mm(grads, right, TN)
        out_ref[p] = jnp.where(first, both[:HALF], both[HALF:])


def gate_grads(upstream, mask, sig, value):
    d_gate = (upstream * mask * value * sig * (1.0 - sig)).astype(BF16)
    d_value = (upstream * mask * sig).astype(BF16)
    return jnp.concatenate([d_gate, d_value], axis=0)


def final_a_kernel(
    x_ref, dleft_ref, token_ref, gain_ref, w_ref, gate_ref, q0, q1, q2, q3, out_ref, g_ref, buf, wide
):
    s = pl.program_id(0)
    normed = normed_cells(x_ref, gain_ref)[0]
    proj = mm(w_ref[...], normed, TN)
    d_left = channels_of(dleft_ref[...], buf, wide)
    d_proj = gate_grads(d_left, mask_lanes(token_ref, s), jax.nn.sigmoid(proj[:WIDTH]), proj[WIDTH:])
    d_gate = jnp.concatenate([q[...] for q in (q0, q1, q2, q3)], axis=1).reshape(LANES, WIDTH)
    out_ref[...] = mm(w_ref[...], d_proj, NN) + mm(gate_ref[...], d_gate, NT)

    @pl.when(s == 0)
    def start():
        g_ref[...] = jnp.zeros_like(g_ref)

    g_ref[...] += mm(normed, d_proj, NT)


def final_b_kernel(
    s, x_ref, part_ref, a_ref, b_ref, c_ref, token_ref, exponent_ref, gain_ref, w_ref, into_ref,
    out_ref, g_ref, buf, wide,
):
    normed, centred, inverse, gain = normed_cells(x_ref, gain_ref)
    proj = mm(w_ref[...], normed, TN)
    mask = mask_lanes(token_ref, s)
    sig = jax.nn.sigmoid(proj[:WIDTH])
    inside = jnp.abs(mask * sig * proj[WIDTH:]) <= bound_lanes(exponent_ref)
    d_right = channels_of(
        a_ref[...].astype(F32) + b_ref[0].astype(F32) + c_ref[...].astype(F32), buf, wide
    )
    d_proj = gate_grads(jnp.where(inside, d_right, 0.0), mask, sig, proj[WIDTH:])
    g_ref[...] = mm(normed, d_proj, NT)
    d_normed = part_ref[...] + mm(w_ref[...], d_proj, NN)
    d_pair = norm_back_channels(d_normed, centred, inverse, gain).astype(BF16)
    out_ref[...] = to_cells(d_pair).astype(BF16).reshape(SUB, HALF, WIDTH)


def whole(array):
    return pl.BlockSpec(array.shape, lambda i: (0,) * array.ndim)


def block(shape, at):
    return pl.BlockSpec(shape, lambda i: at)


BUF = pltpu.VMEM((LANES, WIDTH), F32)
WIDE = pltpu.VMEM((WIDTH, LANES), F32)
PANEL = jax.ShapeDtypeStruct((HALF, SUB, WIDTH), BF16)
PANEL_SPEC = pl.BlockSpec((GROUP, SUB, WIDTH), lambda i: (i, 0, 0))
FOUR = jax.ShapeDtypeStruct((4, HALF, SUB, WIDTH), BF16)
FOUR_SPEC = pl.BlockSpec((4, GROUP, SUB, WIDTH), lambda i: (0, i, 0, 0))
TWO = jax.ShapeDtypeStruct((2, HALF, SUB, WIDTH), BF16)
TWO_SPEC = pl.BlockSpec((2, GROUP, SUB, WIDTH), lambda i: (0, i, 0, 0))
LEFT_SPEC = pl.BlockSpec((GROUP, 2, HALF, WIDTH), lambda i: (i, 0, 0, 0))
WHOLE_PANEL = pl.BlockSpec(PANEL.shape, lambda i: (0, 0, 0))


def right_part(s, pair, gain, w_proj, tokens, exponents):
    return pl.pallas_call(
        functools.partial(right_kernel, s),
        grid=(1,),
        out_shape=PANEL,
        in_specs=[
            block((SUB, HALF, WIDTH), (s, 0, 0)), whole(gain), block((WIDTH, 2 * WIDTH), (0, 1)),
            whole(tokens), block((SUB, HALF), (s, 0)),
        ],
        out_specs=WHOLE_PANEL,
        scratch_shapes=[BUF],
        compiler_params=params(),
        cost_estimate=cost(4 * LANES * WIDTH * WIDTH, 1 << 19, LANES * WIDTH),
        name="right_part",
    )(pair, gain, w_proj, tokens, exponents)


def left_part(pair, gain, w_proj, tokens):
    return pl.pallas_call(
        left_kernel,
        grid=(HALF // SUB,),
        out_shape=jax.ShapeDtypeStruct((HALF, 2, HALF, WIDTH), BF16),
        in_specs=[
            pl.BlockSpec((SUB, HALF, WIDTH), lambda i: (i, 0, 0)), whole(gain),
            block((WIDTH, 2 * WIDTH), (0, 0)), whole(tokens),
        ],
        out_specs=pl.BlockSpec((HALF, 2, SUB, WIDTH), lambda i: (0, 0, i, 0)),
        scratch_shapes=[BUF],
        compiler_params=params(),
        cost_estimate=cost(16 * LANES * WIDTH * WIDTH, 3 << 20, 4 * LANES * WIDTH),
        name="left_part",
    )(pair, gain, w_proj, tokens)


def tri_part(slots, left):
    return pl.pallas_call(
        tri_kernel,
        grid=(HALF // GROUP,),
        out_shape=(PANEL, PANEL, TWO, FOUR),
        in_specs=[PANEL_SPEC] * 4 + [LEFT_SPEC],
        out_specs=(PANEL_SPEC, PANEL_SPEC, TWO_SPEC, FOUR_SPEC),
        compiler_params=params(),
        cost_estimate=cost(2 * HALF * HALF * WIDTH * WIDTH, 5 << 20),
        name="tri_part",
    )(*slots, left)


def mid_part(s, parts, pair, grad, gain_in, gain_out, w_gate, w_out):
    square = jax.ShapeDtypeStruct((WIDTH, WIDTH), F32)
    columns = block((HALF, SUB, WIDTH), (0, s, 0))
    small = [gain_in, gain_out, w_gate, w_out]
    return pl.pallas_call(
        mid_kernel,
        grid=(1,),
        out_shape=(PANEL, PANEL, square, square),
        in_specs=[WHOLE_PANEL, block((1, HALF, SUB, WIDTH), (0, 0, 0, 0)), WHOLE_PANEL]
        + [columns] * 2
        + [whole(a) for a in small],
        out_specs=(WHOLE_PANEL, WHOLE_PANEL, block(square.shape, (0, 0)), block(square.shape, (0, 0))),
        scratch_shapes=[BUF, WIDE],
        compiler_params=params(),
        cost_estimate=cost(12 * LANES * WIDTH * WIDTH, 2 << 20, LANES * WIDTH),
        name="mid_part",
    )(*parts, pair, grad, *small)


def dright_part(blocks, left):
    return pl.pallas_call(
        dright_kernel,
        grid=(HALF // GROUP,),
        out_shape=(PANEL, TWO, PANEL),
        in_specs=[PANEL_SPEC] * 4 + [LEFT_SPEC],
        out_specs=(PANEL_SPEC, TWO_SPEC, PANEL_SPEC),
        scratch_shapes=[pltpu.VMEM((4, GROUP, SUB, WIDTH), BF16)],
        compiler_params=params(),
        cost_estimate=cost(2 * HALF * HALF * WIDTH * WIDTH, 4 << 20),
        name="dright_part",
    )(*blocks, left)


def dleft_part(grads, panels):
    return pl.pallas_call(
        dleft_kernel,
        grid=(HALF // GROUP,),
        out_shape=jax.ShapeDtypeStruct((HALF, HALF, WIDTH), F32),
        in_specs=[PANEL_SPEC] * len(grads) + [FOUR_SPEC] * len(panels),
        out_specs=pl.BlockSpec((GROUP, HALF, WIDTH), lambda i: (i, 0, 0)),
        compiler_params=params(),
        cost_estimate=cost(8 * HALF * HALF * WIDTH * WIDTH, 10 << 20),
        name="dleft_part",
    )(*grads, *panels)


def final_a_part(pair, dleft, tokens, gain, w_proj, w_gate, gates):
    return pl.pallas_call(
        final_a_kernel,
        grid=(HALF // SUB,),
        out_shape=(
            jax.ShapeDtypeStruct((WIDTH, HALF * HALF), F32),
            jax.ShapeDtypeStruct((WIDTH, 2 * WIDTH), F32),
        ),
        in_specs=[
            pl.BlockSpec((SUB, HALF, WIDTH), lambda i: (i, 0, 0)),
            pl.BlockSpec((HALF, SUB, WIDTH), lambda i: (0, i, 0)),
            whole(tokens), whole(gain), block((WIDTH, 2 * WIDTH), (0, 0)), whole(w_gate),
        ]
        + [pl.BlockSpec((SUB, SUB, WIDTH), lambda i: (i, 0, 0))] * 4,
        out_specs=(
            pl.BlockSpec((WIDTH, LANES), lambda i: (0, i)),
            block((WIDTH, 2 * WIDTH), (0, 0)),
        ),
        scratch_shapes=[BUF, WIDE],
        compiler_params=params(),
        cost_estimate=cost(56 * LANES * WIDTH * WIDTH, 8 << 20, 4 * LANES * WIDTH),
        name="final_a_part",
    )(pair, dleft, tokens, gain, w_proj, w_gate, *gates)


def final_b_part(s, pair, part, sums, tokens, exponents, gain, w_proj, into):
    return pl.pallas_call(
        functools.partial(final_b_kernel, s),
        grid=(1,),
        out_shape=(
            jax.ShapeDtypeStruct((HALF, HALF, WIDTH), BF16),
            jax.ShapeDtypeStruct((WIDTH, 2 * WIDTH), F32),
        ),
        in_specs=[
            block((SUB, HALF, WIDTH), (s, 0, 0)),
            block((WIDTH, LANES), (0, s)),
            WHOLE_PANEL, block((1, HALF, SUB, WIDTH), (0, 0, 0, 0)), WHOLE_PANEL,
            whole(tokens), block((SUB, HALF), (s, 0)), whole(gain),
            block((WIDTH, 2 * WIDTH), (0, 1)),
            pl.BlockSpec(memory_space=pl.ANY),
        ],
        out_specs=(block((SUB, HALF, WIDTH), (s, 0, 0)), block((WIDTH, 2 * WIDTH), (0, 0))),
        scratch_shapes=[BUF, WIDE],
        input_output_aliases={9: 0} if into.shape == pair.shape else {},
        compiler_params=params(),
        cost_estimate=cost(14 * LANES * WIDTH * WIDTH, 2 << 20, LANES * WIDTH),
        name="final_b_part",
    )(pair, part, *sums, tokens, exponents, gain, w_proj, into)


def after(array, *others):
    return lax.optimization_barrier((array, *others))[0]


def blocked(pair_tiles, grad_out, exponents, token_mask, gain_in, w_proj, w_gate, gain_out, w_out):
    rows, cols, width = pair_tiles.shape
    crop_len = token_mask.shape[0]
    parts = rows // SUB
    core = lax.axis_index("col") % 2
    x_at = lax.axis_index("col") // 2
    tokens = token_mask.reshape(1, crop_len)
    gain_in = gain_in.reshape(1, width)
    gain_out = gain_out.reshape(1, width)

    def over_row(a, bit):
        return lax.ppermute(a, "row", [(k, k ^ bit) for k in range(4)])

    def over_x(a):
        return lax.ppermute(a, "col", [(k, k ^ 2) for k in range(4)])

    def over_core(a):
        return lax.ppermute(a, "col", [(k, k ^ 1) for k in range(4)])

    def plus(a, b):
        return (a.astype(F32) + b.astype(F32)).astype(BF16)

    slots = []
    ready = ()
    for s in range(parts):
        own = after(right_part(s, pair_tiles, gain_in, w_proj, tokens, exponents), *ready)
        far = over_row(own, 2)
        slots.append((own, over_row(own, 1), far, over_row(far, 1)))
        ready = (far,)
    left = left_part(pair_tiles, gain_in, w_proj, tokens)

    grads, panels, gates, sums = [], [], [], []
    g_out = g_gate = 0.0
    for s in range(parts):
        keep, near, send, panel = tri_part(slots[s], left)
        got = over_core(send)
        mine = over_x(plus(near, got[1]))
        d_tri, d_gate, part_out, part_gate = mid_part(
            s, (keep, got, mine), pair_tiles, grad_out, gain_in, gain_out, w_gate, w_out
        )
        g_out, g_gate = g_out + part_out, g_gate + part_gate
        far = over_x(d_tri)
        blocks = [d_tri, far, over_core(d_tri), over_core(far)]
        stay, pair, cross = dright_part(blocks, left)
        got = over_row(pair, 1)
        sums.append((stay, got, over_row(plus(cross, got[1]), 2)))
        grads += blocks
        panels.append(panel)
        gates.append(d_gate)
    d_left = dleft_part(grads, panels)
    partial, g_a = final_a_part(pair_tiles, d_left, tokens, gain_in, w_proj, w_gate, gates)

    d_pair = gain_in
    g_b = []
    for s in range(parts):
        d_pair, part_b = final_b_part(
            s, pair_tiles, partial, sums[s], tokens, exponents, gain_in, w_proj, d_pair
        )
        g_b.append(part_b)

    def exchange(a, send, at):
        half = a.shape[0] // 2
        return lax.dynamic_slice_in_dim(a, at * half, half) + send(
            lax.dynamic_slice_in_dim(a, (1 - at) * half, half)
        )

    def join(a, send, at):
        theirs = send(a)
        return jnp.concatenate([jnp.where(at == 0, a, theirs), jnp.where(at == 0, theirs, a)], axis=0)

    def over_rows(a):
        for bit in (1, 2):
            a = a + over_row(a, bit)
        return a

    early = jnp.concatenate([g_out, g_gate, g_a, g_b[0] + g_b[1] + g_b[2]], axis=1)
    early = over_rows(exchange(exchange(early, over_core, core), over_x, x_at))
    early = join(join(early, over_x, x_at), over_core, core)
    late = exchange(g_b[3], over_core, core)
    late = join(over_rows(late + over_x(late)), over_core, core)
    g_proj = jnp.concatenate([early[:, 2 * width : 4 * width], early[:, 4 * width :] + late], axis=1)
    return d_pair, g_proj / crop_len, early[:, width : 2 * width] / crop_len, early[:, :width] / crop_len


def local(pair_tiles, *rest, rows_over, cols_over):
    if pair_tiles.shape == (HALF, HALF, WIDTH) and rows_over == cols_over == 4:
        return blocked(pair_tiles, *rest)
    return plain(pair_tiles, *rest)


def solution(mesh):
    return jax.shard_map(
        functools.partial(local, rows_over=mesh.shape["row"], cols_over=mesh.shape["col"]),
        mesh=mesh,
        in_specs=(
            P(("crop", "row"), "col", None),
            P(("crop", "row"), "col", None),
            P(("crop", "row"), "col"),
            P("crop"),
            P(),
            P(),
            P(),
            P(),
            P(),
        ),
        out_specs=(
            P(("crop", "row"), "col", None),
            P("crop", None),
            P("crop", None),
            P("crop", None),
        ),
        check_vma=False,
    )
```

```python
import functools

import jax
import jax.numpy as jnp
from jax import lax
from jax.experimental import pallas as pl
from jax.experimental.pallas import tpu as pltpu
from jax.sharding import PartitionSpec as P

EPS = 1e-05


def layer_norm(values, gain):
    center = jnp.mean(values, axis=-1, keepdims=True)
    spread = jnp.mean((values - center) ** 2, axis=-1, keepdims=True)
    inverse = lax.rsqrt(spread + EPS)
    centred = (values - center) * inverse
    return (centred * gain, centred, inverse)


def norm_back(upstream, centred, inverse, gain):
    scaled = upstream * gain
    first = jnp.mean(scaled, axis=-1, keepdims=True)
    second = jnp.mean(scaled * centred, axis=-1, keepdims=True)
    return inverse * (scaled - first - centred * second)


def plain(pair_tiles, grad_out, exponents, token_mask, gain_in, w_proj, w_gate, gain_out, w_out):
    f32 = jnp.float32
    bf16 = jnp.bfloat16
    rows, cols, width = pair_tiles.shape
    crop_len = token_mask.shape[0]
    row_at = lax.axis_index("row")
    col_at = lax.axis_index("col")
    maskf = token_mask.astype(f32)
    mask_rows = lax.dynamic_slice_in_dim(maskf, row_at * rows, rows)
    mask_cols = lax.dynamic_slice_in_dim(maskf, col_at * cols, cols)
    pair_mask = (mask_rows[:, None] * mask_cols[None, :])[..., None]
    normed_f, centred, inverse = layer_norm(pair_tiles.astype(f32), gain_in)
    normed = normed_f.astype(bf16)
    flat = normed.reshape(-1, width)
    projected = jnp.dot(flat, w_proj, preferred_element_type=f32).reshape(rows, cols, 4 * width)
    gate_a = projected[..., :width]
    value_a = projected[..., width : 2 * width]
    gate_b = projected[..., 2 * width : 3 * width]
    value_b = projected[..., 3 * width :]
    sig_a = jax.nn.sigmoid(gate_a)
    sig_b = jax.nn.sigmoid(gate_b)
    left = (pair_mask * sig_a * value_a).astype(bf16)
    right_raw = pair_mask * sig_b * value_b
    bound = (448.0 * jnp.exp2(exponents.astype(f32)))[..., None]
    right = jnp.clip(right_raw, -bound, bound).astype(bf16)
    inside = (jnp.abs(right_raw) <= bound).astype(f32)
    panel = lax.all_gather(right, "row", axis=0, tiled=True)
    tri_cols = lax.psum_scatter(
        jnp.einsum("jkc,ikc->jic", panel, left, preferred_element_type=f32).astype(jnp.bfloat16),
        "col",
        scatter_dimension=0,
        tiled=True,
    ).astype(jnp.float32)
    tri = jnp.transpose(tri_cols, (1, 0, 2))
    tnorm_f, tcentred, tinverse = layer_norm(tri, gain_out)
    tnorm = tnorm_f.astype(bf16)
    tflat = tnorm.reshape(-1, width)
    opened = jax.nn.sigmoid(jnp.dot(flat, w_gate, preferred_element_type=f32)).reshape(
        rows, cols, width
    )
    outproj = jnp.dot(tflat, w_out, preferred_element_type=f32).reshape(rows, cols, width)
    upstream = grad_out.astype(f32)
    d_open = upstream * outproj
    d_outproj = (upstream * opened).astype(bf16).reshape(-1, width)
    g_out = jnp.dot(tflat.T, d_outproj, preferred_element_type=f32)
    d_tnorm = jnp.dot(d_outproj, w_out.T, preferred_element_type=f32).reshape(rows, cols, width)
    d_tri = norm_back(d_tnorm, tcentred, tinverse, gain_out).astype(bf16)
    d_gatepre = (d_open * opened * (1.0 - opened)).astype(bf16).reshape(-1, width)
    g_gate = jnp.dot(flat.T, d_gatepre, preferred_element_type=f32)
    grad_full = lax.all_gather(d_tri, "col", axis=1, tiled=True)
    d_left = jnp.einsum("ijc,jkc->ikc", grad_full, panel, preferred_element_type=f32)
    d_right = (
        lax.psum_scatter(
            jnp.einsum("ijc,ikc->jkc", grad_full, left, preferred_element_type=f32).astype(
                jnp.bfloat16
            ),
            "row",
            scatter_dimension=0,
            tiled=True,
        ).astype(jnp.float32)
        * inside
    )
    d_gate_a = d_left * pair_mask * value_a * sig_a * (1.0 - sig_a)
    d_value_a = d_left * pair_mask * sig_a
    d_gate_b = d_right * pair_mask * value_b * sig_b * (1.0 - sig_b)
    d_value_b = d_right * pair_mask * sig_b
    d_proj = (
        jnp.concatenate([d_gate_a, d_value_a, d_gate_b, d_value_b], axis=-1)
        .astype(bf16)
        .reshape(-1, 4 * width)
    )
    g_proj = jnp.dot(flat.T, d_proj, preferred_element_type=f32)
    d_normed = jnp.dot(d_proj, w_proj.T, preferred_element_type=f32) + jnp.dot(
        d_gatepre, w_gate.T, preferred_element_type=f32
    )
    d_pair = norm_back(d_normed.reshape(rows, cols, width), centred, inverse, gain_in).astype(bf16)
    sum_proj, sum_gate, sum_out = lax.psum((g_proj, g_gate, g_out), ("row", "col"))
    return (d_pair, sum_proj / crop_len, sum_gate / crop_len, sum_out / crop_len)


SUB = 16
PART = 32
HALF = 64
WIDTH = 128
LANES = SUB * HALF
GROUP = 16
NT = (((1,), (1,)), ((), ()))
NN = (((1,), (0,)), ((), ()))
TN = (((0,), (0,)), ((), ()))
F32 = jnp.float32
BF16 = jnp.bfloat16


def mm(a, b, dims):
    return lax.dot_general(a, b, dims, preferred_element_type=F32)


def params():
    return pltpu.CompilerParams(vmem_limit_bytes=16 * 1024 * 1024)


def cost(flops, size, exps=0):
    return pl.CostEstimate(flops=flops, bytes_accessed=size, transcendentals=exps)


def first_half(rows):
    return lax.broadcasted_iota(jnp.int32, (rows, WIDTH), 1) < HALF


def swap_halves(a, b):
    first = first_half(HALF)
    return (
        jnp.where(first, a, pltpu.roll(b, HALF, 1)),
        jnp.where(first, pltpu.roll(a, HALF, 1), b),
    )


def eye():
    row = lax.broadcasted_iota(jnp.int32, (WIDTH, WIDTH), 0)
    lane = lax.broadcasted_iota(jnp.int32, (WIDTH, WIDTH), 1)
    return (row == lane).astype(F32).astype(BF16)


def to_channels(cells):
    return mm(eye(), cells, NT)


def to_cells(channels):
    return mm(channels, eye(), TN)


def stage_rows(channels, buf):
    for t in range(SUB // 2):
        part = channels[:, t * WIDTH : (t + 1) * WIDTH]
        one, two = swap_halves(part[:HALF], part[HALF:])
        buf[(2 * t) * HALF : (2 * t + 1) * HALF, :] = one
        buf[(2 * t + 1) * HALF : (2 * t + 2) * HALF, :] = two


def panel_row(buf, p):
    return buf[pl.ds(p, SUB, stride=HALF), :]


def channels_of(panels, buf, out):
    buf[...] = panels.reshape(LANES, WIDTH)
    for t in range(SUB // 2):
        one = buf[pl.ds(2 * t, HALF, stride=SUB), :]
        two = buf[pl.ds(2 * t + 1, HALF, stride=SUB), :]
        low, high = swap_halves(one, two)
        out[:HALF, t * WIDTH : (t + 1) * WIDTH] = low
        out[HALF:, t * WIDTH : (t + 1) * WIDTH] = high
    return out[...]


def norm_channels(values, gain):
    center = jnp.mean(values, axis=0, keepdims=True)
    spread = jnp.mean((values - center) ** 2, axis=0, keepdims=True)
    inverse = lax.rsqrt(spread + EPS)
    centred = (values - center) * inverse
    return centred * gain, centred, inverse


def norm_back_channels(upstream, centred, inverse, gain):
    scaled = upstream * gain
    first = jnp.mean(scaled, axis=0, keepdims=True)
    second = jnp.mean(scaled * centred, axis=0, keepdims=True)
    return inverse * (scaled - first - centred * second)


def column(row):
    at = lax.broadcasted_iota(jnp.int32, (WIDTH, WIDTH), 0)
    lane = lax.broadcasted_iota(jnp.int32, (WIDTH, WIDTH), 1)
    return jnp.sum(jnp.where(at == lane, row, 0.0), axis=1, keepdims=True)


def mask_lanes(token_ref, s):
    valid = jnp.sum(token_ref[...].astype(F32), axis=1, keepdims=True)
    lane = lax.broadcasted_iota(jnp.int32, (1, LANES), 1)
    row = lane // HALF + (lax.axis_index("row") * HALF + s * SUB)
    col = lane % HALF + lax.axis_index("col") * HALF
    return (jnp.maximum(row, col).astype(F32) < valid).astype(F32)


def bound_lanes(exponent_ref):
    bound = 448.0 * jnp.exp2(exponent_ref[...].astype(F32))
    return jnp.concatenate([bound[i : i + 1] for i in range(SUB)], axis=1)


def normed_cells(x_ref, gain_ref):
    gain = column(gain_ref[...])
    normed, centred, inverse = norm_channels(to_channels(x_ref[...].reshape(LANES, WIDTH)), gain)
    return normed.astype(BF16), centred, inverse, gain


def right_kernel(at, x_ref, gain_ref, w_ref, token_ref, exponent_ref, out_ref, buf):
    normed = normed_cells(x_ref, gain_ref)[0]
    proj = mm(w_ref[...], normed, TN)
    raw = mask_lanes(token_ref, at + pl.program_id(0)) * jax.nn.sigmoid(proj[:WIDTH]) * proj[WIDTH:]
    bound = bound_lanes(exponent_ref)
    stage_rows(jnp.clip(raw, -bound, bound), buf)
    for p in range(HALF):
        out_ref[p] = panel_row(buf, p).astype(BF16)


def left_kernel(x_ref, gain_ref, w_ref, token_ref, out_ref, buf):
    normed = normed_cells(x_ref, gain_ref)[0]
    proj = mm(w_ref[...], normed, TN)
    mask = mask_lanes(token_ref, pl.program_id(0))
    stage_rows(mask * jax.nn.sigmoid(proj[:WIDTH]) * proj[WIDTH:], buf)
    first = first_half(SUB)
    for p in range(HALF):
        row = panel_row(buf, p)
        out_ref[p, 0] = jnp.where(first, row, 0.0).astype(BF16)
        out_ref[p, 1] = jnp.where(first, 0.0, row).astype(BF16)


def tri_kernel(s0, s1, s2, s3, left_ref, keep_ref, near_ref, send_ref, panel_ref):
    z, q = lax.axis_index("row"), lax.axis_index("col")
    for m, ref in enumerate((s0, s1, s2, s3)):
        place = ((z ^ (z >> 1)) - m + 4) & 3
        other = place ^ (place >> 1) ^ q
        panel_ref[(other & 1) * 2 + (other >> 1)] = ref[...]
    for p in range(GROUP):
        right = jnp.concatenate([panel_ref[r, p] for r in range(4)], axis=0)
        tri = mm(right, left_ref[p].reshape(WIDTH, WIDTH), NT).astype(BF16)
        keep_ref[p] = tri[:SUB]
        near_ref[p] = tri[SUB : 2 * SUB]
        send_ref[0, p] = tri[2 * SUB : 3 * SUB]
        send_ref[1, p] = tri[3 * SUB :]


def mid_kernel(
    a_ref, b_ref, c_ref, x_ref, grad_ref, gain_in_ref, gain_out_ref, gate_ref, out_w_ref,
    dtri_ref, dgate_ref, g_out_ref, g_gate_ref, buf, wide,
):
    gain_out = column(gain_out_ref[...])
    tri = channels_of(
        a_ref[...].astype(F32) + b_ref[0].astype(F32) + c_ref[...].astype(F32), buf, wide
    )
    tnorm_f, tcentred, tinverse = norm_channels(tri, gain_out)
    tnorm = tnorm_f.astype(BF16)

    def turned(ref):
        buf[...] = ref[...].astype(F32).reshape(LANES, WIDTH)
        rows = [buf[pl.ds(j, HALF, stride=SUB), :] for j in range(SUB)]
        return to_channels(jnp.concatenate(rows, axis=0).astype(BF16))

    normed = norm_channels(turned(x_ref), column(gain_in_ref[...]))[0].astype(BF16)
    upstream = turned(grad_ref)
    opened = jax.nn.sigmoid(mm(gate_ref[...], normed, TN))
    outproj = mm(out_w_ref[...], tnorm, TN)
    d_open = upstream * outproj
    d_outproj = (upstream * opened).astype(BF16)
    g_out_ref[...] = mm(tnorm, d_outproj, NT)
    d_tnorm = mm(out_w_ref[...], d_outproj, NN)
    d_tri = norm_back_channels(d_tnorm, tcentred, tinverse, gain_out)
    d_gatepre = (d_open * opened * (1.0 - opened)).astype(BF16)
    g_gate_ref[...] = mm(normed, d_gatepre, NT)
    stage_rows(d_tri, buf)
    for p in range(HALF):
        dtri_ref[p] = panel_row(buf, p).astype(BF16)
    buf[...] = to_cells(d_gatepre)
    for i in range(HALF):
        dgate_ref[i] = panel_row(buf, i).astype(BF16)


def dright_kernel(*refs):
    *grads_refs, left_ref, p0, p1, p2, p3, held = refs
    z, q = lax.axis_index("row"), lax.axis_index("col")
    for k, ref in enumerate(grads_refs):
        r = k % 4
        block_at = q ^ ((r % 2) * 2 + r // 2)
        slot = ((z ^ (z >> 1)) - (block_at ^ (block_at >> 1)) + 4) & 3
        held[slot, :, (k // 4) * SUB : (k // 4 + 1) * SUB] = ref[...]
    for p in range(GROUP):
        grads = jnp.concatenate([held[m, p] for m in range(4)], axis=0)
        part = mm(grads, left_ref[p].reshape(WIDTH, WIDTH), NN).astype(BF16)
        for m, ref in enumerate((p0, p1, p2, p3)):
            ref[p] = part[m * PART : (m + 1) * PART]


def dleft_kernel(*refs):
    out_ref = refs[-1]
    parts = (len(refs) - 1) // 5
    grad_refs, panel_refs = refs[: 4 * parts], refs[4 * parts : 5 * parts]
    first = first_half(HALF)
    for p in range(GROUP):
        grads = jnp.concatenate([d[p] for d in grad_refs], axis=0)
        right = jnp.concatenate([r[q, p] for r in panel_refs for q in range(4)], axis=0)
        both = mm(grads, right, TN)
        out_ref[p] = jnp.where(first, both[:HALF], both[HALF:])


def gate_grads(upstream, mask, sig, value):
    d_gate = (upstream * mask * value * sig * (1.0 - sig)).astype(BF16)
    d_value = (upstream * mask * sig).astype(BF16)
    return jnp.concatenate([d_gate, d_value], axis=0)


def final_a_kernel(
    x_ref, dleft_ref, token_ref, gain_ref, w_ref, gate_ref, q0, q1, q2, q3, out_ref, g_ref, buf, wide
):
    s = pl.program_id(0)
    normed = normed_cells(x_ref, gain_ref)[0]
    proj = mm(w_ref[...], normed, TN)
    d_left = channels_of(dleft_ref[...], buf, wide)
    d_proj = gate_grads(d_left, mask_lanes(token_ref, s), jax.nn.sigmoid(proj[:WIDTH]), proj[WIDTH:])
    d_gate = jnp.concatenate([q[...] for q in (q0, q1, q2, q3)], axis=1).reshape(LANES, WIDTH)
    out_ref[...] = mm(w_ref[...], d_proj, NN) + mm(gate_ref[...], d_gate, NT)

    @pl.when(s == 0)
    def start():
        g_ref[...] = jnp.zeros_like(g_ref)

    g_ref[...] += mm(normed, d_proj, NT)


def final_b_kernel(
    at, x_ref, part_ref, a_ref, b_ref, token_ref, exponent_ref, gain_ref, w_ref, into_ref,
    out_ref, g_ref, buf, wide,
):
    step = pl.program_id(0)
    normed, centred, inverse, gain = normed_cells(x_ref, gain_ref)
    proj = mm(w_ref[...], normed, TN)
    mask = mask_lanes(token_ref, at + step)
    sig = jax.nn.sigmoid(proj[:WIDTH])
    inside = jnp.abs(mask * sig * proj[WIDTH:]) <= bound_lanes(exponent_ref)
    d_right = channels_of(a_ref[...].astype(F32) + b_ref[...].astype(F32), buf, wide)
    d_proj = gate_grads(jnp.where(inside, d_right, 0.0), mask, sig, proj[WIDTH:])

    @pl.when(step == 0)
    def start():
        g_ref[...] = jnp.zeros_like(g_ref)

    g_ref[...] += mm(normed, d_proj, NT)
    d_normed = part_ref[...] + mm(w_ref[...], d_proj, NN)
    d_pair = norm_back_channels(d_normed, centred, inverse, gain).astype(BF16)
    out_ref[...] = to_cells(d_pair).astype(BF16).reshape(SUB, HALF, WIDTH)


def whole(array):
    return pl.BlockSpec(array.shape, lambda i: (0,) * array.ndim)


def block(shape, at):
    return pl.BlockSpec(shape, lambda i: at)


BUF = pltpu.VMEM((LANES, WIDTH), F32)
WIDE = pltpu.VMEM((WIDTH, LANES), F32)
PANEL = jax.ShapeDtypeStruct((HALF, SUB, WIDTH), BF16)
PANEL_SPEC = pl.BlockSpec((GROUP, SUB, WIDTH), lambda i: (i, 0, 0))
FOUR = jax.ShapeDtypeStruct((4, HALF, SUB, WIDTH), BF16)
FOUR_SPEC = pl.BlockSpec((4, GROUP, SUB, WIDTH), lambda i: (0, i, 0, 0))
TWO = jax.ShapeDtypeStruct((2, HALF, SUB, WIDTH), BF16)
TWO_SPEC = pl.BlockSpec((2, GROUP, SUB, WIDTH), lambda i: (0, i, 0, 0))
LEFT_SPEC = pl.BlockSpec((GROUP, 2, HALF, WIDTH), lambda i: (i, 0, 0, 0))
LONG = jax.ShapeDtypeStruct((HALF, PART, WIDTH), BF16)
LONG_SPEC = pl.BlockSpec((GROUP, PART, WIDTH), lambda i: (i, 0, 0))
WHOLE_PANEL = pl.BlockSpec(PANEL.shape, lambda i: (0, 0, 0))


def right_part(s, pair, gain, w_proj, tokens, exponents):
    steps = PART // SUB
    return pl.pallas_call(
        functools.partial(right_kernel, s * steps),
        grid=(steps,),
        out_shape=LONG,
        in_specs=[
            pl.BlockSpec((SUB, HALF, WIDTH), lambda i: (s * steps + i, 0, 0)),
            whole(gain), block((WIDTH, 2 * WIDTH), (0, 1)), whole(tokens),
            pl.BlockSpec((SUB, HALF), lambda i: (s * steps + i, 0)),
        ],
        out_specs=pl.BlockSpec((HALF, SUB, WIDTH), lambda i: (0, i, 0)),
        scratch_shapes=[BUF],
        compiler_params=params(),
        cost_estimate=cost(8 * LANES * WIDTH * WIDTH, 1 << 20, 2 * LANES * WIDTH),
        name="right_part",
    )(pair, gain, w_proj, tokens, exponents)


def left_part(pair, gain, w_proj, tokens):
    return pl.pallas_call(
        left_kernel,
        grid=(HALF // SUB,),
        out_shape=jax.ShapeDtypeStruct((HALF, 2, HALF, WIDTH), BF16),
        in_specs=[
            pl.BlockSpec((SUB, HALF, WIDTH), lambda i: (i, 0, 0)), whole(gain),
            block((WIDTH, 2 * WIDTH), (0, 0)), whole(tokens),
        ],
        out_specs=pl.BlockSpec((HALF, 2, SUB, WIDTH), lambda i: (0, 0, i, 0)),
        scratch_shapes=[BUF],
        compiler_params=params(),
        cost_estimate=cost(16 * LANES * WIDTH * WIDTH, 3 << 20, 4 * LANES * WIDTH),
        name="left_part",
    )(pair, gain, w_proj, tokens)


def tri_part(at, slots, left):
    return pl.pallas_call(
        tri_kernel,
        grid=(HALF // GROUP,),
        out_shape=(PANEL, PANEL, TWO, FOUR),
        in_specs=[pl.BlockSpec((GROUP, SUB, WIDTH), lambda i: (i, at, 0))] * 4 + [LEFT_SPEC],
        out_specs=(PANEL_SPEC, PANEL_SPEC, TWO_SPEC, FOUR_SPEC),
        compiler_params=params(),
        cost_estimate=cost(2 * HALF * HALF * WIDTH * WIDTH, 5 << 20),
        name="tri_part",
    )(*slots, left)


def mid_part(s, parts, pair, grad, gain_in, gain_out, w_gate, w_out):
    square = jax.ShapeDtypeStruct((WIDTH, WIDTH), F32)
    columns = block((HALF, SUB, WIDTH), (0, s, 0))
    small = [gain_in, gain_out, w_gate, w_out]
    return pl.pallas_call(
        mid_kernel,
        grid=(1,),
        out_shape=(PANEL, PANEL, square, square),
        in_specs=[WHOLE_PANEL, block((1, HALF, SUB, WIDTH), (0, 0, 0, 0)), WHOLE_PANEL]
        + [columns] * 2
        + [whole(a) for a in small],
        out_specs=(WHOLE_PANEL, WHOLE_PANEL, block(square.shape, (0, 0)), block(square.shape, (0, 0))),
        scratch_shapes=[BUF, WIDE],
        compiler_params=params(),
        cost_estimate=cost(12 * LANES * WIDTH * WIDTH, 2 << 20, LANES * WIDTH),
        name="mid_part",
    )(*parts, pair, grad, *small)


def dright_part(blocks, left):
    return pl.pallas_call(
        dright_kernel,
        grid=(HALF // GROUP,),
        out_shape=(LONG,) * 4,
        in_specs=[PANEL_SPEC] * len(blocks) + [LEFT_SPEC],
        out_specs=(LONG_SPEC,) * 4,
        scratch_shapes=[pltpu.VMEM((4, GROUP, PART, WIDTH), BF16)],
        compiler_params=params(),
        cost_estimate=cost(4 * HALF * HALF * WIDTH * WIDTH, 6 << 20),
        name="dright_part",
    )(*blocks, left)


def dleft_part(grads, panels):
    return pl.pallas_call(
        dleft_kernel,
        grid=(HALF // GROUP,),
        out_shape=jax.ShapeDtypeStruct((HALF, HALF, WIDTH), F32),
        in_specs=[PANEL_SPEC] * len(grads) + [FOUR_SPEC] * len(panels),
        out_specs=pl.BlockSpec((GROUP, HALF, WIDTH), lambda i: (i, 0, 0)),
        compiler_params=params(),
        cost_estimate=cost(8 * HALF * HALF * WIDTH * WIDTH, 10 << 20),
        name="dleft_part",
    )(*grads, *panels)


def final_a_part(pair, dleft, tokens, gain, w_proj, w_gate, gates):
    return pl.pallas_call(
        final_a_kernel,
        grid=(HALF // SUB,),
        out_shape=(
            jax.ShapeDtypeStruct((WIDTH, HALF * HALF), F32),
            jax.ShapeDtypeStruct((WIDTH, 2 * WIDTH), F32),
        ),
        in_specs=[
            pl.BlockSpec((SUB, HALF, WIDTH), lambda i: (i, 0, 0)),
            pl.BlockSpec((HALF, SUB, WIDTH), lambda i: (0, i, 0)),
            whole(tokens), whole(gain), block((WIDTH, 2 * WIDTH), (0, 0)), whole(w_gate),
        ]
        + [pl.BlockSpec((SUB, SUB, WIDTH), lambda i: (i, 0, 0))] * 4,
        out_specs=(
            pl.BlockSpec((WIDTH, LANES), lambda i: (0, i)),
            block((WIDTH, 2 * WIDTH), (0, 0)),
        ),
        scratch_shapes=[BUF, WIDE],
        compiler_params=params(),
        cost_estimate=cost(56 * LANES * WIDTH * WIDTH, 8 << 20, 4 * LANES * WIDTH),
        name="final_a_part",
    )(pair, dleft, tokens, gain, w_proj, w_gate, *gates)


def final_b_part(s, pair, part, sums, tokens, exponents, gain, w_proj, into):
    steps = PART // SUB
    rows = pl.BlockSpec((SUB, HALF, WIDTH), lambda i: (s * steps + i, 0, 0))
    panel = pl.BlockSpec((HALF, SUB, WIDTH), lambda i: (0, i, 0))
    return pl.pallas_call(
        functools.partial(final_b_kernel, s * steps),
        grid=(steps,),
        out_shape=(
            jax.ShapeDtypeStruct((HALF, HALF, WIDTH), BF16),
            jax.ShapeDtypeStruct((WIDTH, 2 * WIDTH), F32),
        ),
        in_specs=[
            rows,
            pl.BlockSpec((WIDTH, LANES), lambda i: (0, s * steps + i)),
            panel, panel, whole(tokens),
            pl.BlockSpec((SUB, HALF), lambda i: (s * steps + i, 0)),
            whole(gain), block((WIDTH, 2 * WIDTH), (0, 1)),
            pl.BlockSpec(memory_space=pl.ANY),
        ],
        out_specs=(rows, block((WIDTH, 2 * WIDTH), (0, 0))),
        scratch_shapes=[BUF, WIDE],
        input_output_aliases={8: 0} if into.shape == pair.shape else {},
        compiler_params=params(),
        cost_estimate=cost(28 * LANES * WIDTH * WIDTH, 4 << 20, 2 * LANES * WIDTH),
        name="final_b_part",
    )(pair, part, *sums, tokens, exponents, gain, w_proj, into)


def after(array, *others):
    return lax.optimization_barrier((array, *others))[0]


def blocked(pair_tiles, grad_out, exponents, token_mask, gain_in, w_proj, w_gate, gain_out, w_out):
    width = pair_tiles.shape[-1]
    crop_len = token_mask.shape[0]
    core = lax.axis_index("col") % 2
    x_at = lax.axis_index("col") // 2
    tokens = token_mask.reshape(1, crop_len)
    gain_in = gain_in.reshape(1, width)
    gain_out = gain_out.reshape(1, width)

    def forward(a):
        return lax.ppermute(a, "row", [(0, 1), (1, 3), (3, 2), (2, 0)])

    def over_row(a, bit):
        return lax.ppermute(a, "row", [(k, k ^ bit) for k in range(4)])

    def over_x(a):
        return lax.ppermute(a, "col", [(k, k ^ 2) for k in range(4)])

    def over_core(a):
        return lax.ppermute(a, "col", [(k, k ^ 1) for k in range(4)])

    def plus(a, b):
        return (a.astype(F32) + b.astype(F32)).astype(BF16)

    def gather(own):
        held = [own]
        for _ in range(3):
            held.append(forward(held[-1]))
        return held

    own = [right_part(s, pair_tiles, gain_in, w_proj, tokens, exponents) for s in range(2)]
    left = left_part(pair_tiles, gain_in, w_proj, tokens)
    slots = [gather(own[0])]
    slots.append(gather(after(own[1], slots[0][3])))

    def triangles(s):
        out = []
        for at in range(PART // SUB):
            keep, near, send, panel = tri_part(at, slots[s], left)
            got = over_core(send)
            out.append((keep, got, over_x(plus(near, got[1])), panel))
        return out

    def middle(s, at, parts):
        return mid_part(
            s * (PART // SUB) + at, parts, pair_tiles, grad_out, gain_in, gain_out, w_gate, w_out
        )

    def spread(d_tri):
        far = over_x(d_tri)
        return [d_tri, far, over_core(d_tri), over_core(far)]

    tri = triangles(0)
    mids = []
    for at, (keep, got, mine, _) in enumerate(tri):
        mids.append(middle(0, at, (keep, got, after(mine, slots[1][1]))))
    panels = [t[3] for t in tri]
    blocks = [b for m in mids for b in spread(m[0])]
    first = dright_part([after(blocks[0], slots[1][2])] + blocks[1:], left)

    total = plus(forward(first[1]), first[2])
    tri = triangles(1)
    for at, (keep, got, mine, _) in enumerate(tri):
        mids.append(middle(1, at, (keep, got, after(mine, total) if at else mine)))
    panels += [t[3] for t in tri]
    total = plus(forward(total), first[3])
    more = [b for m in mids[2:] for b in spread(m[0])]
    second = dright_part([after(more[0], total)] + more[1:], left)
    sums_a = (first[0], forward(total))

    total = plus(forward(second[1]), second[2])
    total = plus(forward(total), second[3])
    d_left = dleft_part([after(blocks[0], second[0])] + blocks[1:] + more, panels)
    partial, g_a = final_a_part(pair_tiles, d_left, tokens, gain_in, w_proj, w_gate, [m[1] for m in mids])
    d_pair, g_first = final_b_part(
        0, pair_tiles, partial, sums_a, tokens, exponents, gain_in, w_proj, gain_in
    )
    g_out = sum(m[2] for m in mids)
    g_gate = sum(m[3] for m in mids)

    def exchange(a, send, at):
        half = a.shape[0] // 2
        return lax.dynamic_slice_in_dim(a, at * half, half) + send(
            lax.dynamic_slice_in_dim(a, (1 - at) * half, half)
        )

    def join(a, send, at):
        theirs = send(a)
        return jnp.concatenate([jnp.where(at == 0, a, theirs), jnp.where(at == 0, theirs, a)], axis=0)

    def over_rows(a):
        for bit in (1, 2):
            a = a + over_row(a, bit)
        return a

    early = jnp.concatenate([g_out, g_gate, g_a, g_first], axis=1)
    early = over_rows(exchange(exchange(early, over_core, core), over_x, x_at))
    early = join(join(early, over_x, x_at), over_core, core)
    sums_b = (second[0], after(forward(total), early))
    d_pair, late = final_b_part(
        1, pair_tiles, partial, sums_b, tokens, exponents, gain_in, w_proj, d_pair
    )
    late = exchange(late, over_core, core)
    late = join(over_rows(late + over_x(late)), over_core, core)
    g_proj = jnp.concatenate([early[:, 2 * width : 4 * width], early[:, 4 * width :] + late], axis=1)
    return d_pair, g_proj / crop_len, early[:, width : 2 * width] / crop_len, early[:, :width] / crop_len


def local(pair_tiles, *rest, rows_over, cols_over):
    if pair_tiles.shape == (HALF, HALF, WIDTH) and rows_over == cols_over == 4:
        return blocked(pair_tiles, *rest)
    return plain(pair_tiles, *rest)


def solution(mesh):
    return jax.shard_map(
        functools.partial(local, rows_over=mesh.shape["row"], cols_over=mesh.shape["col"]),
        mesh=mesh,
        in_specs=(
            P(("crop", "row"), "col", None),
            P(("crop", "row"), "col", None),
            P(("crop", "row"), "col"),
            P("crop"),
            P(),
            P(),
            P(),
            P(),
            P(),
        ),
        out_specs=(
            P(("crop", "row"), "col", None),
            P("crop", None),
            P("crop", None),
            P("crop", None),
        ),
        check_vma=False,
    )
```

```python
import functools

import jax
import jax.numpy as jnp
from jax import lax
from jax.experimental import pallas as pl
from jax.experimental.pallas import tpu as pltpu
from jax.sharding import PartitionSpec as P

EPS = 1e-05


def layer_norm(values, gain):
    center = jnp.mean(values, axis=-1, keepdims=True)
    spread = jnp.mean((values - center) ** 2, axis=-1, keepdims=True)
    inverse = lax.rsqrt(spread + EPS)
    centred = (values - center) * inverse
    return (centred * gain, centred, inverse)


def norm_back(upstream, centred, inverse, gain):
    scaled = upstream * gain
    first = jnp.mean(scaled, axis=-1, keepdims=True)
    second = jnp.mean(scaled * centred, axis=-1, keepdims=True)
    return inverse * (scaled - first - centred * second)


def plain(pair_tiles, grad_out, exponents, token_mask, gain_in, w_proj, w_gate, gain_out, w_out):
    f32 = jnp.float32
    bf16 = jnp.bfloat16
    rows, cols, width = pair_tiles.shape
    crop_len = token_mask.shape[0]
    row_at = lax.axis_index("row")
    col_at = lax.axis_index("col")
    maskf = token_mask.astype(f32)
    mask_rows = lax.dynamic_slice_in_dim(maskf, row_at * rows, rows)
    mask_cols = lax.dynamic_slice_in_dim(maskf, col_at * cols, cols)
    pair_mask = (mask_rows[:, None] * mask_cols[None, :])[..., None]
    normed_f, centred, inverse = layer_norm(pair_tiles.astype(f32), gain_in)
    normed = normed_f.astype(bf16)
    flat = normed.reshape(-1, width)
    projected = jnp.dot(flat, w_proj, preferred_element_type=f32).reshape(rows, cols, 4 * width)
    gate_a = projected[..., :width]
    value_a = projected[..., width : 2 * width]
    gate_b = projected[..., 2 * width : 3 * width]
    value_b = projected[..., 3 * width :]
    sig_a = jax.nn.sigmoid(gate_a)
    sig_b = jax.nn.sigmoid(gate_b)
    left = (pair_mask * sig_a * value_a).astype(bf16)
    right_raw = pair_mask * sig_b * value_b
    bound = (448.0 * jnp.exp2(exponents.astype(f32)))[..., None]
    right = jnp.clip(right_raw, -bound, bound).astype(bf16)
    inside = (jnp.abs(right_raw) <= bound).astype(f32)
    panel = lax.all_gather(right, "row", axis=0, tiled=True)
    tri_cols = lax.psum_scatter(
        jnp.einsum("jkc,ikc->jic", panel, left, preferred_element_type=f32).astype(jnp.bfloat16),
        "col",
        scatter_dimension=0,
        tiled=True,
    ).astype(jnp.float32)
    tri = jnp.transpose(tri_cols, (1, 0, 2))
    tnorm_f, tcentred, tinverse = layer_norm(tri, gain_out)
    tnorm = tnorm_f.astype(bf16)
    tflat = tnorm.reshape(-1, width)
    opened = jax.nn.sigmoid(jnp.dot(flat, w_gate, preferred_element_type=f32)).reshape(
        rows, cols, width
    )
    outproj = jnp.dot(tflat, w_out, preferred_element_type=f32).reshape(rows, cols, width)
    upstream = grad_out.astype(f32)
    d_open = upstream * outproj
    d_outproj = (upstream * opened).astype(bf16).reshape(-1, width)
    g_out = jnp.dot(tflat.T, d_outproj, preferred_element_type=f32)
    d_tnorm = jnp.dot(d_outproj, w_out.T, preferred_element_type=f32).reshape(rows, cols, width)
    d_tri = norm_back(d_tnorm, tcentred, tinverse, gain_out).astype(bf16)
    d_gatepre = (d_open * opened * (1.0 - opened)).astype(bf16).reshape(-1, width)
    g_gate = jnp.dot(flat.T, d_gatepre, preferred_element_type=f32)
    grad_full = lax.all_gather(d_tri, "col", axis=1, tiled=True)
    d_left = jnp.einsum("ijc,jkc->ikc", grad_full, panel, preferred_element_type=f32)
    d_right = (
        lax.psum_scatter(
            jnp.einsum("ijc,ikc->jkc", grad_full, left, preferred_element_type=f32).astype(
                jnp.bfloat16
            ),
            "row",
            scatter_dimension=0,
            tiled=True,
        ).astype(jnp.float32)
        * inside
    )
    d_gate_a = d_left * pair_mask * value_a * sig_a * (1.0 - sig_a)
    d_value_a = d_left * pair_mask * sig_a
    d_gate_b = d_right * pair_mask * value_b * sig_b * (1.0 - sig_b)
    d_value_b = d_right * pair_mask * sig_b
    d_proj = (
        jnp.concatenate([d_gate_a, d_value_a, d_gate_b, d_value_b], axis=-1)
        .astype(bf16)
        .reshape(-1, 4 * width)
    )
    g_proj = jnp.dot(flat.T, d_proj, preferred_element_type=f32)
    d_normed = jnp.dot(d_proj, w_proj.T, preferred_element_type=f32) + jnp.dot(
        d_gatepre, w_gate.T, preferred_element_type=f32
    )
    d_pair = norm_back(d_normed.reshape(rows, cols, width), centred, inverse, gain_in).astype(bf16)
    sum_proj, sum_gate, sum_out = lax.psum((g_proj, g_gate, g_out), ("row", "col"))
    return (d_pair, sum_proj / crop_len, sum_gate / crop_len, sum_out / crop_len)


SUB = 16
PART = 16
HALF = 64
WIDTH = 128
LANES = SUB * HALF
GROUP = 16
NT = (((1,), (1,)), ((), ()))
NN = (((1,), (0,)), ((), ()))
TN = (((0,), (0,)), ((), ()))
F32 = jnp.float32
BF16 = jnp.bfloat16


def mm(a, b, dims):
    return lax.dot_general(a, b, dims, preferred_element_type=F32)


def params():
    return pltpu.CompilerParams(vmem_limit_bytes=16 * 1024 * 1024)


def cost(flops, size, exps=0):
    return pl.CostEstimate(flops=flops, bytes_accessed=size, transcendentals=exps)


def first_half(rows):
    return lax.broadcasted_iota(jnp.int32, (rows, WIDTH), 1) < HALF


def swap_halves(a, b):
    first = first_half(HALF)
    return (
        jnp.where(first, a, pltpu.roll(b, HALF, 1)),
        jnp.where(first, pltpu.roll(a, HALF, 1), b),
    )


def eye():
    row = lax.broadcasted_iota(jnp.int32, (WIDTH, WIDTH), 0)
    lane = lax.broadcasted_iota(jnp.int32, (WIDTH, WIDTH), 1)
    return (row == lane).astype(F32).astype(BF16)


def to_channels(cells):
    return mm(eye(), cells, NT)


def to_cells(channels):
    return mm(channels, eye(), TN)


def stage_rows(channels, buf):
    for t in range(SUB // 2):
        part = channels[:, t * WIDTH : (t + 1) * WIDTH]
        one, two = swap_halves(part[:HALF], part[HALF:])
        buf[(2 * t) * HALF : (2 * t + 1) * HALF, :] = one
        buf[(2 * t + 1) * HALF : (2 * t + 2) * HALF, :] = two


def panel_row(buf, p):
    return buf[pl.ds(p, SUB, stride=HALF), :]


def channels_of(panels, buf, out):
    buf[...] = panels.reshape(LANES, WIDTH)
    for t in range(SUB // 2):
        one = buf[pl.ds(2 * t, HALF, stride=SUB), :]
        two = buf[pl.ds(2 * t + 1, HALF, stride=SUB), :]
        low, high = swap_halves(one, two)
        out[:HALF, t * WIDTH : (t + 1) * WIDTH] = low
        out[HALF:, t * WIDTH : (t + 1) * WIDTH] = high
    return out[...]


def norm_channels(values, gain):
    center = jnp.mean(values, axis=0, keepdims=True)
    spread = jnp.mean((values - center) ** 2, axis=0, keepdims=True)
    inverse = lax.rsqrt(spread + EPS)
    centred = (values - center) * inverse
    return centred * gain, centred, inverse


def norm_back_channels(upstream, centred, inverse, gain):
    scaled = upstream * gain
    first = jnp.mean(scaled, axis=0, keepdims=True)
    second = jnp.mean(scaled * centred, axis=0, keepdims=True)
    return inverse * (scaled - first - centred * second)


def column(row):
    at = lax.broadcasted_iota(jnp.int32, (WIDTH, WIDTH), 0)
    lane = lax.broadcasted_iota(jnp.int32, (WIDTH, WIDTH), 1)
    return jnp.sum(jnp.where(at == lane, row, 0.0), axis=1, keepdims=True)


def mask_lanes(token_ref, s):
    valid = jnp.sum(token_ref[...].astype(F32), axis=1, keepdims=True)
    lane = lax.broadcasted_iota(jnp.int32, (1, LANES), 1)
    row = lane // HALF + (lax.axis_index("row") * HALF + s * SUB)
    col = lane % HALF + lax.axis_index("col") * HALF
    return (jnp.maximum(row, col).astype(F32) < valid).astype(F32)


def bound_lanes(exponent_ref):
    bound = 448.0 * jnp.exp2(exponent_ref[...].astype(F32))
    return jnp.concatenate([bound[i : i + 1] for i in range(SUB)], axis=1)


def normed_cells(x_ref, gain_ref):
    gain = column(gain_ref[...])
    normed, centred, inverse = norm_channels(to_channels(x_ref[...].reshape(LANES, WIDTH)), gain)
    return normed.astype(BF16), centred, inverse, gain


def right_kernel(at, x_ref, gain_ref, w_ref, token_ref, exponent_ref, out_ref, buf):
    normed = normed_cells(x_ref, gain_ref)[0]
    proj = mm(w_ref[...], normed, TN)
    raw = mask_lanes(token_ref, at + pl.program_id(0)) * jax.nn.sigmoid(proj[:WIDTH]) * proj[WIDTH:]
    bound = bound_lanes(exponent_ref)
    stage_rows(jnp.clip(raw, -bound, bound), buf)
    for p in range(HALF):
        out_ref[p] = panel_row(buf, p).astype(BF16)


def left_kernel(x_ref, gain_ref, w_ref, token_ref, out_ref, buf):
    normed = normed_cells(x_ref, gain_ref)[0]
    proj = mm(w_ref[...], normed, TN)
    mask = mask_lanes(token_ref, pl.program_id(0))
    stage_rows(mask * jax.nn.sigmoid(proj[:WIDTH]) * proj[WIDTH:], buf)
    first = first_half(SUB)
    for p in range(HALF):
        row = panel_row(buf, p)
        out_ref[p, 0] = jnp.where(first, row, 0.0).astype(BF16)
        out_ref[p, 1] = jnp.where(first, 0.0, row).astype(BF16)


def tri_kernel(s0, s1, s2, s3, left_ref, keep_ref, near_ref, send_ref, panel_ref):
    z, q = lax.axis_index("row"), lax.axis_index("col")
    for m, ref in enumerate((s0, s1, s2, s3)):
        place = ((z ^ (z >> 1)) - m + 4) & 3
        other = place ^ (place >> 1) ^ q
        panel_ref[(other & 1) * 2 + (other >> 1)] = ref[...]
    for p in range(GROUP):
        right = jnp.concatenate([panel_ref[r, p] for r in range(4)], axis=0)
        tri = mm(right, left_ref[p].reshape(WIDTH, WIDTH), NT).astype(BF16)
        keep_ref[p] = tri[:SUB]
        near_ref[p] = tri[SUB : 2 * SUB]
        send_ref[0, p] = tri[2 * SUB : 3 * SUB]
        send_ref[1, p] = tri[3 * SUB :]


def mid_kernel(
    a_ref, b_ref, c_ref, x_ref, grad_ref, gain_in_ref, gain_out_ref, gate_ref, out_w_ref,
    g_out_so_far, g_gate_so_far, dtri_ref, dgate_ref, g_out_ref, g_gate_ref, buf, wide,
):
    gain_out = column(gain_out_ref[...])
    tri = channels_of(
        a_ref[...].astype(F32) + b_ref[0].astype(F32) + c_ref[...].astype(F32), buf, wide
    )
    tnorm_f, tcentred, tinverse = norm_channels(tri, gain_out)
    tnorm = tnorm_f.astype(BF16)

    def turned(ref):
        buf[...] = ref[...].astype(F32).reshape(LANES, WIDTH)
        rows = [buf[pl.ds(j, HALF, stride=SUB), :] for j in range(SUB)]
        return to_channels(jnp.concatenate(rows, axis=0).astype(BF16))

    normed = norm_channels(turned(x_ref), column(gain_in_ref[...]))[0].astype(BF16)
    upstream = turned(grad_ref)
    opened = jax.nn.sigmoid(mm(gate_ref[...], normed, TN))
    outproj = mm(out_w_ref[...], tnorm, TN)
    d_open = upstream * outproj
    d_outproj = (upstream * opened).astype(BF16)
    g_out_ref[...] = g_out_so_far[...] + mm(tnorm, d_outproj, NT)
    d_tnorm = mm(out_w_ref[...], d_outproj, NN)
    d_tri = norm_back_channels(d_tnorm, tcentred, tinverse, gain_out)
    d_gatepre = (d_open * opened * (1.0 - opened)).astype(BF16)
    g_gate_ref[...] = g_gate_so_far[...] + mm(normed, d_gatepre, NT)
    stage_rows(d_tri, buf)
    for p in range(HALF):
        dtri_ref[p] = panel_row(buf, p).astype(BF16)
    buf[...] = to_cells(d_gatepre)
    for i in range(HALF):
        dgate_ref[i] = panel_row(buf, i).astype(BF16)


def dright_kernel(*refs):
    *grads_refs, left_ref, p0, p1, p2, p3, held = refs
    z, q = lax.axis_index("row"), lax.axis_index("col")
    for k, ref in enumerate(grads_refs):
        r = k % 4
        block_at = q ^ ((r % 2) * 2 + r // 2)
        slot = ((z ^ (z >> 1)) - (block_at ^ (block_at >> 1)) + 4) & 3
        held[slot, :, (k // 4) * SUB : (k // 4 + 1) * SUB] = ref[...]
    for p in range(GROUP):
        grads = jnp.concatenate([held[m, p] for m in range(4)], axis=0)
        part = mm(grads, left_ref[p].reshape(WIDTH, WIDTH), NN).astype(BF16)
        for m, ref in enumerate((p0, p1, p2, p3)):
            ref[p] = part[m * PART : (m + 1) * PART]


def dleft_kernel(*refs):
    so_far, out_ref = refs[-2:]
    parts = (len(refs) - 2) // 5
    grad_refs, panel_refs = refs[: 4 * parts], refs[4 * parts : 5 * parts]
    first = first_half(HALF)
    for p in range(GROUP):
        grads = jnp.concatenate([d[p] for d in grad_refs], axis=0)
        right = jnp.concatenate([r[q, p] for r in panel_refs for q in range(4)], axis=0)
        both = mm(grads, right, TN)
        out_ref[p] = so_far[p] + jnp.where(first, both[:HALF], both[HALF:])


def gate_grads(upstream, mask, sig, value):
    d_gate = (upstream * mask * value * sig * (1.0 - sig)).astype(BF16)
    d_value = (upstream * mask * sig).astype(BF16)
    return jnp.concatenate([d_gate, d_value], axis=0)


def final_a_kernel(
    x_ref, dleft_ref, token_ref, gain_ref, w_ref, gate_ref, q0, q1, q2, q3, out_ref, g_ref, buf, wide
):
    s = pl.program_id(0)
    normed = normed_cells(x_ref, gain_ref)[0]
    proj = mm(w_ref[...], normed, TN)
    d_left = channels_of(dleft_ref[...], buf, wide)
    d_proj = gate_grads(d_left, mask_lanes(token_ref, s), jax.nn.sigmoid(proj[:WIDTH]), proj[WIDTH:])
    d_gate = jnp.concatenate([q[...] for q in (q0, q1, q2, q3)], axis=1).reshape(LANES, WIDTH)
    out_ref[...] = mm(w_ref[...], d_proj, NN) + mm(gate_ref[...], d_gate, NT)

    @pl.when(s == 0)
    def start():
        g_ref[...] = jnp.zeros_like(g_ref)

    g_ref[...] += mm(normed, d_proj, NT)


def final_b_kernel(
    at, x_ref, part_ref, a_ref, b_ref, token_ref, exponent_ref, gain_ref, w_ref, so_far, into_ref,
    out_ref, g_ref, buf, wide,
):
    step = pl.program_id(0)
    normed, centred, inverse, gain = normed_cells(x_ref, gain_ref)
    proj = mm(w_ref[...], normed, TN)
    mask = mask_lanes(token_ref, at + step)
    sig = jax.nn.sigmoid(proj[:WIDTH])
    inside = jnp.abs(mask * sig * proj[WIDTH:]) <= bound_lanes(exponent_ref)
    d_right = channels_of(a_ref[...].astype(F32) + b_ref[...].astype(F32), buf, wide)
    d_proj = gate_grads(jnp.where(inside, d_right, 0.0), mask, sig, proj[WIDTH:])

    @pl.when(step == 0)
    def start():
        g_ref[...] = so_far[...]

    g_ref[...] += mm(normed, d_proj, NT)
    d_normed = part_ref[...] + mm(w_ref[...], d_proj, NN)
    d_pair = norm_back_channels(d_normed, centred, inverse, gain).astype(BF16)
    out_ref[...] = to_cells(d_pair).astype(BF16).reshape(SUB, HALF, WIDTH)


def whole(array):
    return pl.BlockSpec(array.shape, lambda i: (0,) * array.ndim)


def block(shape, at):
    return pl.BlockSpec(shape, lambda i: at)


BUF = pltpu.VMEM((LANES, WIDTH), F32)
WIDE = pltpu.VMEM((WIDTH, LANES), F32)
PANEL = jax.ShapeDtypeStruct((HALF, SUB, WIDTH), BF16)
PANEL_SPEC = pl.BlockSpec((GROUP, SUB, WIDTH), lambda i: (i, 0, 0))
FOUR = jax.ShapeDtypeStruct((4, HALF, SUB, WIDTH), BF16)
FOUR_SPEC = pl.BlockSpec((4, GROUP, SUB, WIDTH), lambda i: (0, i, 0, 0))
TWO = jax.ShapeDtypeStruct((2, HALF, SUB, WIDTH), BF16)
TWO_SPEC = pl.BlockSpec((2, GROUP, SUB, WIDTH), lambda i: (0, i, 0, 0))
LEFT_SPEC = pl.BlockSpec((GROUP, 2, HALF, WIDTH), lambda i: (i, 0, 0, 0))
LONG = jax.ShapeDtypeStruct((HALF, PART, WIDTH), BF16)
LONG_SPEC = pl.BlockSpec((GROUP, PART, WIDTH), lambda i: (i, 0, 0))
WHOLE_PANEL = pl.BlockSpec(PANEL.shape, lambda i: (0, 0, 0))


def right_part(s, pair, gain, w_proj, tokens, exponents):
    steps = PART // SUB
    return pl.pallas_call(
        functools.partial(right_kernel, s * steps),
        grid=(steps,),
        out_shape=LONG,
        in_specs=[
            pl.BlockSpec((SUB, HALF, WIDTH), lambda i: (s * steps + i, 0, 0)),
            whole(gain), block((WIDTH, 2 * WIDTH), (0, 1)), whole(tokens),
            pl.BlockSpec((SUB, HALF), lambda i: (s * steps + i, 0)),
        ],
        out_specs=pl.BlockSpec((HALF, SUB, WIDTH), lambda i: (0, i, 0)),
        scratch_shapes=[BUF],
        compiler_params=params(),
        cost_estimate=cost(8 * LANES * WIDTH * WIDTH, 1 << 20, 2 * LANES * WIDTH),
        name="right_part",
    )(pair, gain, w_proj, tokens, exponents)


def left_part(pair, gain, w_proj, tokens):
    return pl.pallas_call(
        left_kernel,
        grid=(HALF // SUB,),
        out_shape=jax.ShapeDtypeStruct((HALF, 2, HALF, WIDTH), BF16),
        in_specs=[
            pl.BlockSpec((SUB, HALF, WIDTH), lambda i: (i, 0, 0)), whole(gain),
            block((WIDTH, 2 * WIDTH), (0, 0)), whole(tokens),
        ],
        out_specs=pl.BlockSpec((HALF, 2, SUB, WIDTH), lambda i: (0, 0, i, 0)),
        scratch_shapes=[BUF],
        compiler_params=params(),
        cost_estimate=cost(16 * LANES * WIDTH * WIDTH, 3 << 20, 4 * LANES * WIDTH),
        name="left_part",
    )(pair, gain, w_proj, tokens)


def tri_part(at, slots, left):
    return pl.pallas_call(
        tri_kernel,
        grid=(HALF // GROUP,),
        out_shape=(PANEL, PANEL, TWO, FOUR),
        in_specs=[pl.BlockSpec((GROUP, SUB, WIDTH), lambda i: (i, at, 0))] * 4 + [LEFT_SPEC],
        out_specs=(PANEL_SPEC, PANEL_SPEC, TWO_SPEC, FOUR_SPEC),
        compiler_params=params(),
        cost_estimate=cost(2 * HALF * HALF * WIDTH * WIDTH, 5 << 20),
        name="tri_part",
    )(*slots, left)


def mid_part(s, parts, pair, grad, gain_in, gain_out, w_gate, w_out, g_out, g_gate):
    square = jax.ShapeDtypeStruct((WIDTH, WIDTH), F32)
    columns = block((HALF, SUB, WIDTH), (0, s, 0))
    small = [gain_in, gain_out, w_gate, w_out, g_out, g_gate]
    return pl.pallas_call(
        mid_kernel,
        grid=(1,),
        out_shape=(PANEL, pltpu.HBM(PANEL.shape, BF16), square, square),
        in_specs=[WHOLE_PANEL, block((1, HALF, SUB, WIDTH), (0, 0, 0, 0)), WHOLE_PANEL]
        + [columns] * 2
        + [whole(a) for a in small],
        out_specs=(WHOLE_PANEL, WHOLE_PANEL, block(square.shape, (0, 0)), block(square.shape, (0, 0))),
        scratch_shapes=[BUF, WIDE],
        compiler_params=params(),
        cost_estimate=cost(12 * LANES * WIDTH * WIDTH, 2 << 20, LANES * WIDTH),
        name="mid_part",
    )(*parts, pair, grad, *small)


def dright_part(blocks, left):
    return pl.pallas_call(
        dright_kernel,
        grid=(HALF // GROUP,),
        out_shape=(pltpu.HBM(LONG.shape, BF16), LONG, LONG, LONG),
        in_specs=[PANEL_SPEC] * len(blocks) + [LEFT_SPEC],
        out_specs=(LONG_SPEC,) * 4,
        scratch_shapes=[pltpu.VMEM((4, GROUP, PART, WIDTH), BF16)],
        compiler_params=params(),
        cost_estimate=cost(4 * HALF * HALF * WIDTH * WIDTH, 6 << 20),
        name="dright_part",
    )(*blocks, left)


def dleft_part(grads, panels, so_far):
    rows = pl.BlockSpec((GROUP, HALF, WIDTH), lambda i: (i, 0, 0))
    return pl.pallas_call(
        dleft_kernel,
        grid=(HALF // GROUP,),
        out_shape=jax.ShapeDtypeStruct((HALF, HALF, WIDTH), F32),
        in_specs=[PANEL_SPEC] * len(grads) + [FOUR_SPEC] * len(panels) + [rows],
        out_specs=rows,
        compiler_params=params(),
        cost_estimate=cost(4 * HALF * HALF * WIDTH * WIDTH, 8 << 20),
        name="dleft_part",
    )(*grads, *panels, so_far)


def final_a_part(pair, dleft, tokens, gain, w_proj, w_gate, gates):
    return pl.pallas_call(
        final_a_kernel,
        grid=(HALF // SUB,),
        out_shape=(
            jax.ShapeDtypeStruct((WIDTH, HALF * HALF), F32),
            jax.ShapeDtypeStruct((WIDTH, 2 * WIDTH), F32),
        ),
        in_specs=[
            pl.BlockSpec((SUB, HALF, WIDTH), lambda i: (i, 0, 0)),
            pl.BlockSpec((HALF, SUB, WIDTH), lambda i: (0, i, 0)),
            whole(tokens), whole(gain), block((WIDTH, 2 * WIDTH), (0, 0)), whole(w_gate),
        ]
        + [pl.BlockSpec((SUB, SUB, WIDTH), lambda i: (i, 0, 0))] * 4,
        out_specs=(
            pl.BlockSpec((WIDTH, LANES), lambda i: (0, i)),
            block((WIDTH, 2 * WIDTH), (0, 0)),
        ),
        scratch_shapes=[BUF, WIDE],
        compiler_params=params(),
        cost_estimate=cost(56 * LANES * WIDTH * WIDTH, 8 << 20, 4 * LANES * WIDTH),
        name="final_a_part",
    )(pair, dleft, tokens, gain, w_proj, w_gate, *gates)


def final_b_part(s, pair, part, sums, tokens, exponents, gain, w_proj, so_far, into):
    steps = PART // SUB
    rows = pl.BlockSpec((SUB, HALF, WIDTH), lambda i: (s * steps + i, 0, 0))
    panel = pl.BlockSpec((HALF, SUB, WIDTH), lambda i: (0, i, 0))
    return pl.pallas_call(
        functools.partial(final_b_kernel, s * steps),
        grid=(steps,),
        out_shape=(
            jax.ShapeDtypeStruct((HALF, HALF, WIDTH), BF16),
            jax.ShapeDtypeStruct((WIDTH, 2 * WIDTH), F32),
        ),
        in_specs=[
            rows,
            pl.BlockSpec((WIDTH, LANES), lambda i: (0, s * steps + i)),
            panel, panel, whole(tokens),
            pl.BlockSpec((SUB, HALF), lambda i: (s * steps + i, 0)),
            whole(gain), block((WIDTH, 2 * WIDTH), (0, 1)), whole(so_far),
            pl.BlockSpec(memory_space=pl.ANY),
        ],
        out_specs=(rows, block((WIDTH, 2 * WIDTH), (0, 0))),
        scratch_shapes=[BUF, WIDE],
        input_output_aliases={9: 0} if into.shape == pair.shape else {},
        compiler_params=params(),
        cost_estimate=cost(28 * LANES * WIDTH * WIDTH, 4 << 20, 2 * LANES * WIDTH),
        name="final_b_part",
    )(pair, part, *sums, tokens, exponents, gain, w_proj, so_far, into)


def after(array, *others):
    return lax.optimization_barrier((array, *others))[0]


def blocked(pair_tiles, grad_out, exponents, token_mask, gain_in, w_proj, w_gate, gain_out, w_out):
    width = pair_tiles.shape[-1]
    crop_len = token_mask.shape[0]
    core = lax.axis_index("col") % 2
    tokens = token_mask.reshape(1, crop_len)
    gain_in = gain_in.reshape(1, width)
    gain_out = gain_out.reshape(1, width)

    def forward(a):
        return lax.ppermute(a, "row", [(0, 1), (1, 3), (3, 2), (2, 0)])

    def over_row(a, bit):
        return lax.ppermute(a, "row", [(k, k ^ bit) for k in range(4)])

    def over_x(a):
        return lax.ppermute(a, "col", [(k, k ^ 2) for k in range(4)])

    def over_core(a):
        return lax.ppermute(a, "col", [(k, k ^ 1) for k in range(4)])

    def plus(a, b):
        return (a.astype(F32) + b.astype(F32)).astype(BF16)

    def right(s):
        return right_part(s, pair_tiles, gain_in, w_proj, tokens, exponents)

    a0, b0 = right(0), right(1)
    left = left_part(pair_tiles, gain_in, w_proj, tokens)
    a1, b1 = forward(a0), forward(b0)
    a2, b2 = forward(a1), forward(after(b1, left))
    c0, d0 = right(2), right(3)
    a3, b3 = forward(after(a2, c0)), forward(after(b2, d0))
    c1, d1 = forward(after(c0, b2)), forward(after(d0, a3))

    def triangle(slots):
        keep, near, send, panel = tri_part(0, slots, left)
        got = over_core(send)
        return keep, got, plus(near, got[1]), panel

    g_out = g_gate = jnp.zeros((width, width), F32)

    def middle(s, tri, mine):
        return mid_part(
            s, (tri[0], tri[1], mine), pair_tiles, grad_out, gain_in, gain_out, w_gate, w_out, g_out, g_gate
        )

    def spread(d_tri):
        far = over_x(d_tri)
        return [d_tri, far, over_core(d_tri), over_core(far)]

    def dright(blocks, *others):
        return dright_part([blocks[0], blocks[1], blocks[2], after(blocks[3], *others)], left)

    tri_a, tri_b = triangle([a0, a1, a2, a3]), triangle([b0, b1, b2, b3])
    x_a, x_b = over_x(tri_a[2]), over_x(tri_b[2])
    c2, d2 = forward(after(c1, tri_a[2])), forward(after(d1, tri_b[2]))
    dtri_a, gate_a, g_out, g_gate = middle(0, tri_a, after(x_a, d1))
    blocks_a = spread(dtri_a)
    dtri_b, gate_b, g_out, g_gate = middle(1, tri_b, after(x_b, c2))
    blocks_b = spread(dtri_b)
    c3, d3 = forward(after(c2, dtri_a)), forward(after(d2, dtri_b))
    part_a = dright(blocks_a, d2)
    part_b = dright(blocks_b, c3)
    r_a, r_b = forward(part_a[1]), forward(part_b[1])

    tri_c = triangle([c0, c1, c2, after(c3, part_a[1])])
    tri_d = triangle([d0, d1, d2, after(d3, part_b[1])])
    x_c, x_d = over_x(tri_c[2]), over_x(tri_d[2])
    r_a = plus(r_a, part_a[2])
    r_a2 = forward(after(r_a, tri_c[2]))
    r_b = plus(r_b, part_b[2])
    r_b2 = forward(after(r_b, tri_d[2]))
    d_left = dleft_part(
        [after(blocks_a[0], tri_d[2])] + blocks_a[1:] + blocks_b,
        [tri_a[3], tri_b[3]],
        jnp.zeros((HALF, HALF, WIDTH), F32),
    )
    dtri_c, gate_c, g_out, g_gate = middle(2, tri_c, after(x_c, r_a, d_left))
    blocks_c = spread(dtri_c)
    dtri_d, gate_d, g_out, g_gate = middle(3, tri_d, after(x_d, r_b))
    blocks_d = spread(dtri_d)
    r_a2 = plus(r_a2, part_a[3])
    r_a3 = forward(after(r_a2, dtri_c))
    r_b2 = plus(r_b2, part_b[3])
    r_b3 = forward(after(r_b2, dtri_d))
    part_c = dright(blocks_c, r_a2)
    part_d = dright(blocks_d, r_b2)

    r_c, r_d = forward(part_c[1]), forward(part_d[1])
    d_left = dleft_part(
        [after(blocks_c[0], part_d[1])] + blocks_c[1:] + blocks_d, [tri_c[3], tri_d[3]], d_left
    )
    partial, g_a = final_a_part(
        pair_tiles, d_left, tokens, gain_in, w_proj, w_gate, [gate_a, gate_b, gate_c, gate_d]
    )
    r_c = forward(plus(r_c, part_c[2]))
    r_d = forward(plus(r_d, part_d[2]))
    zero = jnp.zeros((width, 2 * width), F32)

    def final(s, sums, so_far, into):
        return final_b_part(
            s, pair_tiles, partial, sums, tokens, exponents, gain_in, w_proj, so_far, into
        )

    d_pair, g_first = final(0, (part_a[0], r_a3), zero, gain_in)
    d_pair, g_first = final(1, (part_b[0], r_b3), g_first, d_pair)
    r_c = forward(plus(r_c, part_c[3]))
    r_d = forward(plus(r_d, part_d[3]))

    def halved(a):
        half = a.shape[0] // 2
        a = lax.dynamic_slice_in_dim(a, core * half, half) + over_core(
            lax.dynamic_slice_in_dim(a, (1 - core) * half, half)
        )
        return a + over_x(a)

    early = halved(jnp.concatenate([g_out, g_gate, g_a, g_first], axis=1))
    d_pair, g_last = final(2, (part_c[0], after(r_c, early)), zero, d_pair)
    d_pair, g_last = final(3, (part_d[0], r_d), g_last, d_pair)
    late = halved(g_last)
    sums = jnp.concatenate([early[:, : 4 * width], early[:, 4 * width :] + late], axis=1)
    for bit in (1, 2):
        mine = sums.astype(BF16)
        sums = mine.astype(F32) + over_row(mine, bit).astype(F32)
    sums = sums / crop_len
    theirs = over_core(sums)
    sums = jnp.concatenate(
        [jnp.where(core == 0, sums, theirs), jnp.where(core == 0, theirs, sums)], axis=0
    )
    return d_pair, sums[:, 2 * width :], sums[:, width : 2 * width], sums[:, :width]


def local(pair_tiles, *rest, rows_over, cols_over):
    if pair_tiles.shape == (HALF, HALF, WIDTH) and rows_over == cols_over == 4:
        return blocked(pair_tiles, *rest)
    return plain(pair_tiles, *rest)


def solution(mesh):
    return jax.shard_map(
        functools.partial(local, rows_over=mesh.shape["row"], cols_over=mesh.shape["col"]),
        mesh=mesh,
        in_specs=(
            P(("crop", "row"), "col", None),
            P(("crop", "row"), "col", None),
            P(("crop", "row"), "col"),
            P("crop"),
            P(),
            P(),
            P(),
            P(),
            P(),
        ),
        out_specs=(
            P(("crop", "row"), "col", None),
            P("crop", None),
            P("crop", None),
            P("crop", None),
        ),
        check_vma=False,
    )
```

```python
import functools

import jax
import jax.numpy as jnp
from jax import lax
from jax.experimental import pallas as pl
from jax.experimental.pallas import tpu as pltpu
from jax.sharding import PartitionSpec as P

EPS = 1e-05


def layer_norm(values, gain):
    center = jnp.mean(values, axis=-1, keepdims=True)
    spread = jnp.mean((values - center) ** 2, axis=-1, keepdims=True)
    inverse = lax.rsqrt(spread + EPS)
    centred = (values - center) * inverse
    return (centred * gain, centred, inverse)


def norm_back(upstream, centred, inverse, gain):
    scaled = upstream * gain
    first = jnp.mean(scaled, axis=-1, keepdims=True)
    second = jnp.mean(scaled * centred, axis=-1, keepdims=True)
    return inverse * (scaled - first - centred * second)


def plain(pair_tiles, grad_out, exponents, token_mask, gain_in, w_proj, w_gate, gain_out, w_out):
    f32 = jnp.float32
    bf16 = jnp.bfloat16
    rows, cols, width = pair_tiles.shape
    crop_len = token_mask.shape[0]
    row_at = lax.axis_index("row")
    col_at = lax.axis_index("col")
    maskf = token_mask.astype(f32)
    mask_rows = lax.dynamic_slice_in_dim(maskf, row_at * rows, rows)
    mask_cols = lax.dynamic_slice_in_dim(maskf, col_at * cols, cols)
    pair_mask = (mask_rows[:, None] * mask_cols[None, :])[..., None]
    normed_f, centred, inverse = layer_norm(pair_tiles.astype(f32), gain_in)
    normed = normed_f.astype(bf16)
    flat = normed.reshape(-1, width)
    projected = jnp.dot(flat, w_proj, preferred_element_type=f32).reshape(rows, cols, 4 * width)
    gate_a = projected[..., :width]
    value_a = projected[..., width : 2 * width]
    gate_b = projected[..., 2 * width : 3 * width]
    value_b = projected[..., 3 * width :]
    sig_a = jax.nn.sigmoid(gate_a)
    sig_b = jax.nn.sigmoid(gate_b)
    left = (pair_mask * sig_a * value_a).astype(bf16)
    right_raw = pair_mask * sig_b * value_b
    bound = (448.0 * jnp.exp2(exponents.astype(f32)))[..., None]
    right = jnp.clip(right_raw, -bound, bound).astype(bf16)
    inside = (jnp.abs(right_raw) <= bound).astype(f32)
    panel = lax.all_gather(right, "row", axis=0, tiled=True)
    tri_cols = lax.psum_scatter(
        jnp.einsum("jkc,ikc->jic", panel, left, preferred_element_type=f32).astype(jnp.bfloat16),
        "col",
        scatter_dimension=0,
        tiled=True,
    ).astype(jnp.float32)
    tri = jnp.transpose(tri_cols, (1, 0, 2))
    tnorm_f, tcentred, tinverse = layer_norm(tri, gain_out)
    tnorm = tnorm_f.astype(bf16)
    tflat = tnorm.reshape(-1, width)
    opened = jax.nn.sigmoid(jnp.dot(flat, w_gate, preferred_element_type=f32)).reshape(
        rows, cols, width
    )
    outproj = jnp.dot(tflat, w_out, preferred_element_type=f32).reshape(rows, cols, width)
    upstream = grad_out.astype(f32)
    d_open = upstream * outproj
    d_outproj = (upstream * opened).astype(bf16).reshape(-1, width)
    g_out = jnp.dot(tflat.T, d_outproj, preferred_element_type=f32)
    d_tnorm = jnp.dot(d_outproj, w_out.T, preferred_element_type=f32).reshape(rows, cols, width)
    d_tri = norm_back(d_tnorm, tcentred, tinverse, gain_out).astype(bf16)
    d_gatepre = (d_open * opened * (1.0 - opened)).astype(bf16).reshape(-1, width)
    g_gate = jnp.dot(flat.T, d_gatepre, preferred_element_type=f32)
    grad_full = lax.all_gather(d_tri, "col", axis=1, tiled=True)
    d_left = jnp.einsum("ijc,jkc->ikc", grad_full, panel, preferred_element_type=f32)
    d_right = (
        lax.psum_scatter(
            jnp.einsum("ijc,ikc->jkc", grad_full, left, preferred_element_type=f32).astype(
                jnp.bfloat16
            ),
            "row",
            scatter_dimension=0,
            tiled=True,
        ).astype(jnp.float32)
        * inside
    )
    d_gate_a = d_left * pair_mask * value_a * sig_a * (1.0 - sig_a)
    d_value_a = d_left * pair_mask * sig_a
    d_gate_b = d_right * pair_mask * value_b * sig_b * (1.0 - sig_b)
    d_value_b = d_right * pair_mask * sig_b
    d_proj = (
        jnp.concatenate([d_gate_a, d_value_a, d_gate_b, d_value_b], axis=-1)
        .astype(bf16)
        .reshape(-1, 4 * width)
    )
    g_proj = jnp.dot(flat.T, d_proj, preferred_element_type=f32)
    d_normed = jnp.dot(d_proj, w_proj.T, preferred_element_type=f32) + jnp.dot(
        d_gatepre, w_gate.T, preferred_element_type=f32
    )
    d_pair = norm_back(d_normed.reshape(rows, cols, width), centred, inverse, gain_in).astype(bf16)
    sum_proj, sum_gate, sum_out = lax.psum((g_proj, g_gate, g_out), ("row", "col"))
    return (d_pair, sum_proj / crop_len, sum_gate / crop_len, sum_out / crop_len)


SUB = 16
PAIR = 32
HALF = 64
WIDTH = 128
LANES = SUB * HALF
GROUP = 16
NT = (((1,), (1,)), ((), ()))
NN = (((1,), (0,)), ((), ()))
TN = (((0,), (0,)), ((), ()))
F32 = jnp.float32
BF16 = jnp.bfloat16


def mm(a, b, dims):
    return lax.dot_general(a, b, dims, preferred_element_type=F32)


def params():
    return pltpu.CompilerParams(vmem_limit_bytes=16 * 1024 * 1024)


def cost(flops, size, exps=0):
    return pl.CostEstimate(flops=flops, bytes_accessed=size, transcendentals=exps)


def first_half(rows):
    return lax.broadcasted_iota(jnp.int32, (rows, WIDTH), 1) < HALF


def swap_halves(a, b):
    first = first_half(HALF)
    return (
        jnp.where(first, a, pltpu.roll(b, HALF, 1)),
        jnp.where(first, pltpu.roll(a, HALF, 1), b),
    )


def eye():
    row = lax.broadcasted_iota(jnp.int32, (WIDTH, WIDTH), 0)
    lane = lax.broadcasted_iota(jnp.int32, (WIDTH, WIDTH), 1)
    return (row == lane).astype(F32).astype(BF16)


def to_channels(cells):
    return mm(eye(), cells, NT)


def to_cells(channels):
    return mm(channels, eye(), TN)


def stage_rows(channels, buf):
    for t in range(SUB // 2):
        part = channels[:, t * WIDTH : (t + 1) * WIDTH]
        one, two = swap_halves(part[:HALF], part[HALF:])
        buf[(2 * t) * HALF : (2 * t + 1) * HALF, :] = one
        buf[(2 * t + 1) * HALF : (2 * t + 2) * HALF, :] = two


def panel_row(buf, p):
    return buf[pl.ds(p, SUB, stride=HALF), :]


def channels_of(panels, buf, out):
    buf[...] = panels.reshape(LANES, WIDTH)
    for t in range(SUB // 2):
        one = buf[pl.ds(2 * t, HALF, stride=SUB), :]
        two = buf[pl.ds(2 * t + 1, HALF, stride=SUB), :]
        low, high = swap_halves(one, two)
        out[:HALF, t * WIDTH : (t + 1) * WIDTH] = low
        out[HALF:, t * WIDTH : (t + 1) * WIDTH] = high
    return out[...]


def norm_channels(values, gain):
    center = jnp.mean(values, axis=0, keepdims=True)
    spread = jnp.mean((values - center) ** 2, axis=0, keepdims=True)
    inverse = lax.rsqrt(spread + EPS)
    centred = (values - center) * inverse
    return centred * gain, centred, inverse


def norm_back_channels(upstream, centred, inverse, gain):
    scaled = upstream * gain
    first = jnp.mean(scaled, axis=0, keepdims=True)
    second = jnp.mean(scaled * centred, axis=0, keepdims=True)
    return inverse * (scaled - first - centred * second)


def column(row):
    at = lax.broadcasted_iota(jnp.int32, (WIDTH, WIDTH), 0)
    lane = lax.broadcasted_iota(jnp.int32, (WIDTH, WIDTH), 1)
    return jnp.sum(jnp.where(at == lane, row, 0.0), axis=1, keepdims=True)


def mask_lanes(token_ref, s):
    valid = jnp.sum(token_ref[...].astype(F32), axis=1, keepdims=True)
    lane = lax.broadcasted_iota(jnp.int32, (1, LANES), 1)
    row = lane // HALF + (lax.axis_index("row") * HALF + s * SUB)
    col = lane % HALF + lax.axis_index("col") * HALF
    return (jnp.maximum(row, col).astype(F32) < valid).astype(F32)


def bound_lanes(exponent_ref):
    bound = 448.0 * jnp.exp2(exponent_ref[...].astype(F32))
    return jnp.concatenate([bound[i : i + 1] for i in range(SUB)], axis=1)


def normed_cells(x_ref, gain_ref):
    gain = column(gain_ref[...])
    normed, centred, inverse = norm_channels(to_channels(x_ref[...].reshape(LANES, WIDTH)), gain)
    return normed.astype(BF16), centred, inverse, gain


def right_kernel(at, x_ref, gain_ref, w_ref, token_ref, exponent_ref, out_ref, buf):
    normed = normed_cells(x_ref, gain_ref)[0]
    proj = mm(w_ref[...], normed, TN)
    raw = mask_lanes(token_ref, at) * jax.nn.sigmoid(proj[:WIDTH]) * proj[WIDTH:]
    bound = bound_lanes(exponent_ref)
    stage_rows(jnp.clip(raw, -bound, bound), buf)
    for p in range(HALF):
        out_ref[p] = panel_row(buf, p).astype(BF16)


def left_kernel(x_ref, gain_ref, w_ref, token_ref, out_ref, buf):
    normed = normed_cells(x_ref, gain_ref)[0]
    proj = mm(w_ref[...], normed, TN)
    mask = mask_lanes(token_ref, pl.program_id(0))
    stage_rows(mask * jax.nn.sigmoid(proj[:WIDTH]) * proj[WIDTH:], buf)
    first = first_half(SUB)
    for p in range(HALF):
        row = panel_row(buf, p)
        out_ref[p, 0] = jnp.where(first, row, 0.0).astype(BF16)
        out_ref[p, 1] = jnp.where(first, 0.0, row).astype(BF16)


def tri_kernel(*refs):
    *slot_refs, left_ref, keep_ref, near_ref, send_ref, panel_ref = refs
    z, q = lax.axis_index("row"), lax.axis_index("col")
    for k, ref in enumerate(slot_refs):
        place = ((z ^ (z >> 1)) - (k % 4) + 4) & 3
        other = place ^ (place >> 1) ^ q
        at = (k // 4) * SUB
        panel_ref[(other & 1) * 2 + (other >> 1), :, at : at + SUB] = ref[...]
    for p in range(GROUP):
        right = jnp.concatenate([panel_ref[r, p] for r in range(4)], axis=0)
        tri = mm(right, left_ref[p].reshape(WIDTH, WIDTH), NT).astype(BF16)
        keep_ref[p] = tri[:PAIR]
        near_ref[p] = tri[PAIR : 2 * PAIR]
        send_ref[0, p] = tri[2 * PAIR : 3 * PAIR]
        send_ref[1, p] = tri[3 * PAIR :]


def mid_kernel(
    a_ref, b_ref, c_ref, x_ref, grad_ref, gain_in_ref, gain_out_ref, gate_ref, out_w_ref,
    g_out_so_far, g_gate_so_far, dtri_ref, dgate_ref, g_out_ref, g_gate_ref, buf, wide,
):
    gain_out = column(gain_out_ref[...])
    tri = channels_of(
        a_ref[...].astype(F32) + b_ref[0].astype(F32) + c_ref[...].astype(F32), buf, wide
    )
    tnorm_f, tcentred, tinverse = norm_channels(tri, gain_out)
    tnorm = tnorm_f.astype(BF16)

    def turned(ref):
        buf[...] = ref[...].astype(F32).reshape(LANES, WIDTH)
        rows = [buf[pl.ds(j, HALF, stride=SUB), :] for j in range(SUB)]
        return to_channels(jnp.concatenate(rows, axis=0).astype(BF16))

    normed = norm_channels(turned(x_ref), column(gain_in_ref[...]))[0].astype(BF16)
    upstream = turned(grad_ref)
    opened = jax.nn.sigmoid(mm(gate_ref[...], normed, TN))
    outproj = mm(out_w_ref[...], tnorm, TN)
    d_open = upstream * outproj
    d_outproj = (upstream * opened).astype(BF16)

    @pl.when(pl.program_id(0) == 0)
    def start():
        g_out_ref[...] = g_out_so_far[...]
        g_gate_ref[...] = g_gate_so_far[...]

    g_out_ref[...] += mm(tnorm, d_outproj, NT)
    d_tnorm = mm(out_w_ref[...], d_outproj, NN)
    d_tri = norm_back_channels(d_tnorm, tcentred, tinverse, gain_out)
    d_gatepre = (d_open * opened * (1.0 - opened)).astype(BF16)
    g_gate_ref[...] += mm(normed, d_gatepre, NT)
    stage_rows(d_tri, buf)
    for p in range(HALF):
        dtri_ref[p] = panel_row(buf, p).astype(BF16)
    buf[...] = to_cells(d_gatepre)
    for i in range(HALF):
        dgate_ref[i] = panel_row(buf, i).astype(BF16)


def dright_kernel(d0, d1, d2, d3, left_ref, *refs):
    *part_refs, held = refs
    z, q = lax.axis_index("row"), lax.axis_index("col")
    for r, ref in enumerate((d0, d1, d2, d3)):
        block_at = q ^ ((r % 2) * 2 + r // 2)
        held[((z ^ (z >> 1)) - (block_at ^ (block_at >> 1)) + 4) & 3] = ref[...]
    for p in range(GROUP):
        grads = jnp.concatenate([held[m, p] for m in range(4)], axis=0)
        part = mm(grads, left_ref[p].reshape(WIDTH, WIDTH), NN).astype(BF16)
        for k, ref in enumerate(part_refs):
            at = (k % 4) * PAIR + (k // 4) * SUB
            ref[p] = part[at : at + SUB]


def dleft_kernel(d0, d1, d2, d3, panel_ref, so_far, out_ref):
    first = first_half(HALF)
    for p in range(GROUP):
        grads = jnp.concatenate([d[p] for d in (d0, d1, d2, d3)], axis=0)
        right = jnp.concatenate([panel_ref[r, p] for r in range(4)], axis=0)
        both = mm(grads, right, TN)
        out_ref[p] = so_far[p] + jnp.where(first, both[:HALF], both[HALF:])


def gate_grads(upstream, mask, sig, value):
    d_gate = (upstream * mask * value * sig * (1.0 - sig)).astype(BF16)
    d_value = (upstream * mask * sig).astype(BF16)
    return jnp.concatenate([d_gate, d_value], axis=0)


def final_a_kernel(
    x_ref, dleft_ref, token_ref, gain_ref, w_ref, gate_ref, q0, q1, out_ref, g_ref, buf, wide
):
    s = pl.program_id(0)
    normed = normed_cells(x_ref, gain_ref)[0]
    proj = mm(w_ref[...], normed, TN)
    d_left = channels_of(dleft_ref[...], buf, wide)
    d_proj = gate_grads(d_left, mask_lanes(token_ref, s), jax.nn.sigmoid(proj[:WIDTH]), proj[WIDTH:])
    d_gate = jnp.concatenate([q0[...], q1[...]], axis=1).reshape(LANES, WIDTH)
    out_ref[...] = mm(w_ref[...], d_proj, NN) + mm(gate_ref[...], d_gate, NT)

    @pl.when(s == 0)
    def start():
        g_ref[...] = jnp.zeros_like(g_ref)

    g_ref[...] += mm(normed, d_proj, NT)


def final_b_kernel(
    at, x_ref, part_ref, a_ref, b_ref, token_ref, exponent_ref, gain_ref, w_ref, so_far, into_ref,
    out_ref, g_ref, buf, wide,
):
    normed, centred, inverse, gain = normed_cells(x_ref, gain_ref)
    proj = mm(w_ref[...], normed, TN)
    mask = mask_lanes(token_ref, at)
    sig = jax.nn.sigmoid(proj[:WIDTH])
    inside = jnp.abs(mask * sig * proj[WIDTH:]) <= bound_lanes(exponent_ref)
    d_right = channels_of(a_ref[...].astype(F32) + b_ref[...].astype(F32), buf, wide)
    d_proj = gate_grads(jnp.where(inside, d_right, 0.0), mask, sig, proj[WIDTH:])

    g_ref[...] = so_far[...] + mm(normed, d_proj, NT)
    d_normed = part_ref[...] + mm(w_ref[...], d_proj, NN)
    d_pair = norm_back_channels(d_normed, centred, inverse, gain).astype(BF16)
    out_ref[...] = to_cells(d_pair).astype(BF16).reshape(SUB, HALF, WIDTH)


def whole(array):
    return pl.BlockSpec(array.shape, lambda i: (0,) * array.ndim)


def block(shape, at):
    return pl.BlockSpec(shape, lambda i: at)


BUF = pltpu.VMEM((LANES, WIDTH), F32)
WIDE = pltpu.VMEM((WIDTH, LANES), F32)
PANEL = jax.ShapeDtypeStruct((HALF, SUB, WIDTH), BF16)
PANEL_SPEC = pl.BlockSpec((GROUP, SUB, WIDTH), lambda i: (i, 0, 0))
FOUR = jax.ShapeDtypeStruct((4, HALF, PAIR, WIDTH), BF16)
FOUR_SPEC = pl.BlockSpec((4, GROUP, PAIR, WIDTH), lambda i: (0, i, 0, 0))
TWO = jax.ShapeDtypeStruct((2, HALF, PAIR, WIDTH), BF16)
TWO_SPEC = pl.BlockSpec((2, GROUP, PAIR, WIDTH), lambda i: (0, i, 0, 0))
LEFT_SPEC = pl.BlockSpec((GROUP, 2, HALF, WIDTH), lambda i: (i, 0, 0, 0))
LONG = jax.ShapeDtypeStruct((HALF, PAIR, WIDTH), BF16)
LONG_SPEC = pl.BlockSpec((GROUP, PAIR, WIDTH), lambda i: (i, 0, 0))
WHOLE_PANEL = pl.BlockSpec(PANEL.shape, lambda i: (0, 0, 0))


def right_part(s, pair, gain, w_proj, tokens, exponents):
    return pl.pallas_call(
        functools.partial(right_kernel, s),
        grid=(1,),
        out_shape=PANEL,
        in_specs=[
            block((SUB, HALF, WIDTH), (s, 0, 0)), whole(gain), block((WIDTH, 2 * WIDTH), (0, 1)),
            whole(tokens), block((SUB, HALF), (s, 0)),
        ],
        out_specs=WHOLE_PANEL,
        scratch_shapes=[BUF],
        compiler_params=params(),
        cost_estimate=cost(4 * LANES * WIDTH * WIDTH, 1 << 19, LANES * WIDTH),
        name="right_part",
    )(pair, gain, w_proj, tokens, exponents)


def left_part(pair, gain, w_proj, tokens):
    return pl.pallas_call(
        left_kernel,
        grid=(HALF // SUB,),
        out_shape=jax.ShapeDtypeStruct((HALF, 2, HALF, WIDTH), BF16),
        in_specs=[
            pl.BlockSpec((SUB, HALF, WIDTH), lambda i: (i, 0, 0)), whole(gain),
            block((WIDTH, 2 * WIDTH), (0, 0)), whole(tokens),
        ],
        out_specs=pl.BlockSpec((HALF, 2, SUB, WIDTH), lambda i: (0, 0, i, 0)),
        scratch_shapes=[BUF],
        compiler_params=params(),
        cost_estimate=cost(16 * LANES * WIDTH * WIDTH, 3 << 20, 4 * LANES * WIDTH),
        name="left_part",
    )(pair, gain, w_proj, tokens)


def tri_part(slots, left):
    return pl.pallas_call(
        tri_kernel,
        grid=(HALF // GROUP,),
        out_shape=(LONG, LONG, TWO, FOUR),
        in_specs=[PANEL_SPEC] * 8 + [LEFT_SPEC],
        out_specs=(LONG_SPEC, LONG_SPEC, TWO_SPEC, FOUR_SPEC),
        compiler_params=params(),
        cost_estimate=cost(4 * HALF * HALF * WIDTH * WIDTH, 8 << 20),
        name="tri_part",
    )(*slots, left)


def mid_part(s, parts, pair, grad, gain_in, gain_out, w_gate, w_out, g_out, g_gate):
    square = jax.ShapeDtypeStruct((WIDTH, WIDTH), F32)
    steps = PAIR // SUB
    columns = pl.BlockSpec((HALF, SUB, WIDTH), lambda i: (0, s * steps + i, 0))
    panel = pl.BlockSpec((HALF, SUB, WIDTH), lambda i: (0, i, 0))
    small = [gain_in, gain_out, w_gate, w_out, g_out, g_gate]
    return pl.pallas_call(
        mid_kernel,
        grid=(steps,),
        out_shape=(LONG, LONG, square, square),
        in_specs=[panel, pl.BlockSpec((1, HALF, SUB, WIDTH), lambda i: (0, 0, i, 0)), panel]
        + [columns] * 2
        + [whole(a) for a in small],
        out_specs=(panel, panel, block(square.shape, (0, 0)), block(square.shape, (0, 0))),
        scratch_shapes=[BUF, WIDE],
        compiler_params=params(),
        cost_estimate=cost(24 * LANES * WIDTH * WIDTH, 4 << 20, 2 * LANES * WIDTH),
        name="mid_part",
    )(*parts, pair, grad, *small)


def dright_part(blocks, left):
    return pl.pallas_call(
        dright_kernel,
        grid=(HALF // GROUP,),
        out_shape=(PANEL,) * 8,
        in_specs=[LONG_SPEC] * 4 + [LEFT_SPEC],
        out_specs=(PANEL_SPEC,) * 8,
        scratch_shapes=[pltpu.VMEM((4, GROUP, PAIR, WIDTH), BF16)],
        compiler_params=params(),
        cost_estimate=cost(4 * HALF * HALF * WIDTH * WIDTH, 6 << 20),
        name="dright_part",
    )(*blocks, left)


def dleft_part(grads, panel, so_far):
    rows = pl.BlockSpec((GROUP, HALF, WIDTH), lambda i: (i, 0, 0))
    return pl.pallas_call(
        dleft_kernel,
        grid=(HALF // GROUP,),
        out_shape=jax.ShapeDtypeStruct((HALF, HALF, WIDTH), F32),
        in_specs=[LONG_SPEC] * 4 + [FOUR_SPEC, rows],
        out_specs=rows,
        compiler_params=params(),
        cost_estimate=cost(4 * HALF * HALF * WIDTH * WIDTH, 8 << 20),
        name="dleft_part",
    )(*grads, panel, so_far)


def final_a_part(pair, dleft, tokens, gain, w_proj, w_gate, gates):
    return pl.pallas_call(
        final_a_kernel,
        grid=(HALF // SUB,),
        out_shape=(
            jax.ShapeDtypeStruct((WIDTH, HALF * HALF), F32),
            jax.ShapeDtypeStruct((WIDTH, 2 * WIDTH), F32),
        ),
        in_specs=[
            pl.BlockSpec((SUB, HALF, WIDTH), lambda i: (i, 0, 0)),
            pl.BlockSpec((HALF, SUB, WIDTH), lambda i: (0, i, 0)),
            whole(tokens), whole(gain), block((WIDTH, 2 * WIDTH), (0, 0)), whole(w_gate),
        ]
        + [pl.BlockSpec((SUB, PAIR, WIDTH), lambda i: (i, 0, 0))] * 2,
        out_specs=(
            pl.BlockSpec((WIDTH, LANES), lambda i: (0, i)),
            block((WIDTH, 2 * WIDTH), (0, 0)),
        ),
        scratch_shapes=[BUF, WIDE],
        compiler_params=params(),
        cost_estimate=cost(56 * LANES * WIDTH * WIDTH, 8 << 20, 4 * LANES * WIDTH),
        name="final_a_part",
    )(pair, dleft, tokens, gain, w_proj, w_gate, *gates)


def final_b_part(s, pair, part, sums, tokens, exponents, gain, w_proj, so_far, into):
    rows = block((SUB, HALF, WIDTH), (s, 0, 0))
    return pl.pallas_call(
        functools.partial(final_b_kernel, s),
        grid=(1,),
        out_shape=(
            jax.ShapeDtypeStruct((HALF, HALF, WIDTH), BF16),
            jax.ShapeDtypeStruct((WIDTH, 2 * WIDTH), F32),
        ),
        in_specs=[
            rows, block((WIDTH, LANES), (0, s)), WHOLE_PANEL, WHOLE_PANEL, whole(tokens),
            block((SUB, HALF), (s, 0)), whole(gain), block((WIDTH, 2 * WIDTH), (0, 1)), whole(so_far),
            pl.BlockSpec(memory_space=pl.ANY),
        ],
        out_specs=(rows, block((WIDTH, 2 * WIDTH), (0, 0))),
        scratch_shapes=[BUF, WIDE],
        input_output_aliases={9: 0} if into.shape == pair.shape else {},
        compiler_params=params(),
        cost_estimate=cost(14 * LANES * WIDTH * WIDTH, 2 << 20, LANES * WIDTH),
        name="final_b_part",
    )(pair, part, *sums, tokens, exponents, gain, w_proj, so_far, into)


def after(array, *others):
    return lax.optimization_barrier((array, *others))[0]


def blocked(pair_tiles, grad_out, exponents, token_mask, gain_in, w_proj, w_gate, gain_out, w_out):
    width = pair_tiles.shape[-1]
    crop_len = token_mask.shape[0]
    core = lax.axis_index("col") % 2
    tokens = token_mask.reshape(1, crop_len)
    gain_in = gain_in.reshape(1, width)
    gain_out = gain_out.reshape(1, width)

    def forward(a):
        return lax.ppermute(a, "row", [(0, 1), (1, 3), (3, 2), (2, 0)])

    def over_row(a, bit):
        return lax.ppermute(a, "row", [(k, k ^ bit) for k in range(4)])

    def over_x(a):
        return lax.ppermute(a, "col", [(k, k ^ 2) for k in range(4)])

    def over_core(a):
        return lax.ppermute(a, "col", [(k, k ^ 1) for k in range(4)])

    def plus(a, b):
        return (a.astype(F32) + b.astype(F32)).astype(BF16)

    def right(s):
        operands = (pair_tiles, gain_in, w_proj, tokens, exponents)
        if s == 0:
            operands = [pltpu.with_memory_space_constraint(a, pltpu.HBM) for a in operands]
        return right_part(s, *operands)

    a0, b0 = right(0), right(1)
    left = left_part(pair_tiles, gain_in, w_proj, tokens)
    a1, b1 = forward(a0), forward(b0)
    a2, b2 = forward(a1), forward(after(b1, left))
    c0, d0 = right(2), right(3)
    a3, b3 = forward(after(a2, c0)), forward(after(b2, d0))
    c1, d1 = forward(after(c0, b2)), forward(after(d0, a3))

    g_out = g_gate = jnp.zeros((width, width), F32)
    d_left = jnp.zeros((HALF, HALF, WIDTH), F32)

    def triangle(slots):
        keep, near, send, panel = tri_part(slots, left)
        got = over_core(send)
        return keep, got, plus(near, got[1]), panel

    def middle(s, tri, mine):
        return mid_part(
            s, (tri[0], tri[1], mine), pair_tiles, grad_out, gain_in, gain_out, w_gate, w_out, g_out, g_gate
        )

    def spread(d_tri):
        far = over_x(d_tri)
        return [d_tri, far, over_core(d_tri), over_core(far)]

    ab = triangle([a0, a1, a2, a3, b0, b1, b2, b3])
    x_ab = over_x(ab[2])
    c2, d2 = forward(after(c1, ab[0])), forward(after(d1, ab[2]))
    dtri_ab, gate_ab, g_out, g_gate = middle(0, ab, after(x_ab, c2))
    blocks_ab = spread(dtri_ab)
    c3, d3 = forward(c2), forward(after(d2, dtri_ab))

    cd = triangle([c0, c1, c2, c3, d0, d1, d2, d3])
    x_cd = over_x(cd[2])
    part = dright_part([after(blocks_ab[0], cd[2])] + blocks_ab[1:], left)
    part_a, part_b = part[:4], part[4:]
    r_a, r_b = forward(part_a[1]), forward(part_b[1])
    d_left = dleft_part([after(blocks_ab[0], part_b[1])] + blocks_ab[1:], ab[3], d_left)
    r_a = plus(r_a, part_a[2])
    r_a2 = forward(r_a)
    r_b = plus(r_b, part_b[2])
    dtri_cd, gate_cd, g_out, g_gate = middle(1, cd, after(x_cd, r_a, d_left))
    blocks_cd = spread(dtri_cd)
    r_b2 = forward(after(r_b, dtri_cd))
    r_a2 = plus(r_a2, part_a[3])
    r_a3 = forward(r_a2)
    r_b2 = plus(r_b2, part_b[3])
    r_b3 = forward(r_b2)
    part = dright_part([after(blocks_cd[0], r_a2, r_b2)] + blocks_cd[1:], left)
    part_c, part_d = part[:4], part[4:]

    r_c, r_d = forward(part_c[1]), forward(part_d[1])
    d_left = dleft_part([after(blocks_cd[0], part_d[1])] + blocks_cd[1:], cd[3], d_left)
    partial, g_a = final_a_part(pair_tiles, d_left, tokens, gain_in, w_proj, w_gate, [gate_ab, gate_cd])
    r_c = forward(plus(r_c, part_c[2]))
    r_d = forward(plus(r_d, part_d[2]))
    zero = jnp.zeros((width, 2 * width), F32)

    def final(s, sums, so_far, into):
        return final_b_part(
            s, pair_tiles, partial, sums, tokens, exponents, gain_in, w_proj, so_far, into
        )

    d_pair, g_first = final(0, (part_a[0], r_a3), zero, gain_in)
    d_pair, g_first = final(1, (part_b[0], r_b3), g_first, d_pair)
    r_c = forward(plus(r_c, part_c[3]))
    r_d = forward(plus(r_d, part_d[3]))

    def halved(a):
        half = a.shape[0] // 2
        a = lax.dynamic_slice_in_dim(a, core * half, half) + over_core(
            lax.dynamic_slice_in_dim(a, (1 - core) * half, half)
        )
        return a + over_x(a)

    early = halved(jnp.concatenate([g_out, g_gate, g_a, g_first], axis=1))
    d_pair, g_last = final(2, (part_c[0], after(r_c, early)), zero, d_pair)
    d_pair, g_last = final(3, (part_d[0], r_d), g_last, d_pair)
    late = halved(g_last)
    sums = jnp.concatenate([early[:, : 4 * width], early[:, 4 * width :] + late], axis=1)
    for bit in (1, 2):
        mine = sums.astype(BF16)
        sums = mine.astype(F32) + over_row(mine, bit).astype(F32)
    sums = sums / crop_len
    theirs = over_core(sums)
    sums = jnp.concatenate(
        [jnp.where(core == 0, sums, theirs), jnp.where(core == 0, theirs, sums)], axis=0
    )
    return d_pair, sums[:, 2 * width :], sums[:, width : 2 * width], sums[:, :width]


def local(pair_tiles, *rest, rows_over, cols_over):
    if pair_tiles.shape == (HALF, HALF, WIDTH) and rows_over == cols_over == 4:
        return blocked(pair_tiles, *rest)
    return plain(pair_tiles, *rest)


def solution(mesh):
    return jax.shard_map(
        functools.partial(local, rows_over=mesh.shape["row"], cols_over=mesh.shape["col"]),
        mesh=mesh,
        in_specs=(
            P(("crop", "row"), "col", None),
            P(("crop", "row"), "col", None),
            P(("crop", "row"), "col"),
            P("crop"),
            P(),
            P(),
            P(),
            P(),
            P(),
        ),
        out_specs=(
            P(("crop", "row"), "col", None),
            P("crop", None),
            P("crop", None),
            P("crop", None),
        ),
        check_vma=False,
    )
```

```python
import functools

import jax
import jax.numpy as jnp
from jax import lax
from jax.experimental import pallas as pl
from jax.experimental.pallas import tpu as pltpu
from jax.sharding import PartitionSpec as P

EPS = 1e-05


def layer_norm(values, gain):
    center = jnp.mean(values, axis=-1, keepdims=True)
    spread = jnp.mean((values - center) ** 2, axis=-1, keepdims=True)
    inverse = lax.rsqrt(spread + EPS)
    centred = (values - center) * inverse
    return (centred * gain, centred, inverse)


def norm_back(upstream, centred, inverse, gain):
    scaled = upstream * gain
    first = jnp.mean(scaled, axis=-1, keepdims=True)
    second = jnp.mean(scaled * centred, axis=-1, keepdims=True)
    return inverse * (scaled - first - centred * second)


def plain(pair_tiles, grad_out, exponents, token_mask, gain_in, w_proj, w_gate, gain_out, w_out):
    f32 = jnp.float32
    bf16 = jnp.bfloat16
    rows, cols, width = pair_tiles.shape
    crop_len = token_mask.shape[0]
    row_at = lax.axis_index("row")
    col_at = lax.axis_index("col")
    maskf = token_mask.astype(f32)
    mask_rows = lax.dynamic_slice_in_dim(maskf, row_at * rows, rows)
    mask_cols = lax.dynamic_slice_in_dim(maskf, col_at * cols, cols)
    pair_mask = (mask_rows[:, None] * mask_cols[None, :])[..., None]
    normed_f, centred, inverse = layer_norm(pair_tiles.astype(f32), gain_in)
    normed = normed_f.astype(bf16)
    flat = normed.reshape(-1, width)
    projected = jnp.dot(flat, w_proj, preferred_element_type=f32).reshape(rows, cols, 4 * width)
    gate_a = projected[..., :width]
    value_a = projected[..., width : 2 * width]
    gate_b = projected[..., 2 * width : 3 * width]
    value_b = projected[..., 3 * width :]
    sig_a = jax.nn.sigmoid(gate_a)
    sig_b = jax.nn.sigmoid(gate_b)
    left = (pair_mask * sig_a * value_a).astype(bf16)
    right_raw = pair_mask * sig_b * value_b
    bound = (448.0 * jnp.exp2(exponents.astype(f32)))[..., None]
    right = jnp.clip(right_raw, -bound, bound).astype(bf16)
    inside = (jnp.abs(right_raw) <= bound).astype(f32)
    panel = lax.all_gather(right, "row", axis=0, tiled=True)
    tri_cols = lax.psum_scatter(
        jnp.einsum("jkc,ikc->jic", panel, left, preferred_element_type=f32).astype(jnp.bfloat16),
        "col",
        scatter_dimension=0,
        tiled=True,
    ).astype(jnp.float32)
    tri = jnp.transpose(tri_cols, (1, 0, 2))
    tnorm_f, tcentred, tinverse = layer_norm(tri, gain_out)
    tnorm = tnorm_f.astype(bf16)
    tflat = tnorm.reshape(-1, width)
    opened = jax.nn.sigmoid(jnp.dot(flat, w_gate, preferred_element_type=f32)).reshape(
        rows, cols, width
    )
    outproj = jnp.dot(tflat, w_out, preferred_element_type=f32).reshape(rows, cols, width)
    upstream = grad_out.astype(f32)
    d_open = upstream * outproj
    d_outproj = (upstream * opened).astype(bf16).reshape(-1, width)
    g_out = jnp.dot(tflat.T, d_outproj, preferred_element_type=f32)
    d_tnorm = jnp.dot(d_outproj, w_out.T, preferred_element_type=f32).reshape(rows, cols, width)
    d_tri = norm_back(d_tnorm, tcentred, tinverse, gain_out).astype(bf16)
    d_gatepre = (d_open * opened * (1.0 - opened)).astype(bf16).reshape(-1, width)
    g_gate = jnp.dot(flat.T, d_gatepre, preferred_element_type=f32)
    grad_full = lax.all_gather(d_tri, "col", axis=1, tiled=True)
    d_left = jnp.einsum("ijc,jkc->ikc", grad_full, panel, preferred_element_type=f32)
    d_right = (
        lax.psum_scatter(
            jnp.einsum("ijc,ikc->jkc", grad_full, left, preferred_element_type=f32).astype(
                jnp.bfloat16
            ),
            "row",
            scatter_dimension=0,
            tiled=True,
        ).astype(jnp.float32)
        * inside
    )
    d_gate_a = d_left * pair_mask * value_a * sig_a * (1.0 - sig_a)
    d_value_a = d_left * pair_mask * sig_a
    d_gate_b = d_right * pair_mask * value_b * sig_b * (1.0 - sig_b)
    d_value_b = d_right * pair_mask * sig_b
    d_proj = (
        jnp.concatenate([d_gate_a, d_value_a, d_gate_b, d_value_b], axis=-1)
        .astype(bf16)
        .reshape(-1, 4 * width)
    )
    g_proj = jnp.dot(flat.T, d_proj, preferred_element_type=f32)
    d_normed = jnp.dot(d_proj, w_proj.T, preferred_element_type=f32) + jnp.dot(
        d_gatepre, w_gate.T, preferred_element_type=f32
    )
    d_pair = norm_back(d_normed.reshape(rows, cols, width), centred, inverse, gain_in).astype(bf16)
    sum_proj, sum_gate, sum_out = lax.psum((g_proj, g_gate, g_out), ("row", "col"))
    return (d_pair, sum_proj / crop_len, sum_gate / crop_len, sum_out / crop_len)


SUB = 16
PAIR = 32
HALF = 64
WIDTH = 128
LANES = SUB * HALF
GROUP = 16
NT = (((1,), (1,)), ((), ()))
NN = (((1,), (0,)), ((), ()))
TN = (((0,), (0,)), ((), ()))
F32 = jnp.float32
BF16 = jnp.bfloat16


def mm(a, b, dims):
    return lax.dot_general(a, b, dims, preferred_element_type=F32)


def params():
    return pltpu.CompilerParams(vmem_limit_bytes=16 * 1024 * 1024)


def cost(flops, size, exps=0):
    return pl.CostEstimate(flops=flops, bytes_accessed=size, transcendentals=exps)


def first_half(rows):
    return lax.broadcasted_iota(jnp.int32, (rows, WIDTH), 1) < HALF


def swap_halves(a, b):
    first = first_half(HALF)
    return (
        jnp.where(first, a, pltpu.roll(b, HALF, 1)),
        jnp.where(first, pltpu.roll(a, HALF, 1), b),
    )


def eye():
    row = lax.broadcasted_iota(jnp.int32, (WIDTH, WIDTH), 0)
    lane = lax.broadcasted_iota(jnp.int32, (WIDTH, WIDTH), 1)
    return (row == lane).astype(F32).astype(BF16)


def to_channels(cells):
    return mm(eye(), cells, NT)


def to_cells(channels):
    return mm(channels, eye(), TN)


def stage_rows(channels, buf):
    for t in range(SUB // 2):
        part = channels[:, t * WIDTH : (t + 1) * WIDTH]
        one, two = swap_halves(part[:HALF], part[HALF:])
        buf[(2 * t) * HALF : (2 * t + 1) * HALF, :] = one
        buf[(2 * t + 1) * HALF : (2 * t + 2) * HALF, :] = two


def panel_row(buf, p):
    return buf[pl.ds(p, SUB, stride=HALF), :]


def channels_of(panels, buf, out):
    buf[...] = panels.reshape(LANES, WIDTH)
    for t in range(SUB // 2):
        one = buf[pl.ds(2 * t, HALF, stride=SUB), :]
        two = buf[pl.ds(2 * t + 1, HALF, stride=SUB), :]
        low, high = swap_halves(one, two)
        out[:HALF, t * WIDTH : (t + 1) * WIDTH] = low
        out[HALF:, t * WIDTH : (t + 1) * WIDTH] = high
    return out[...]


def norm_channels(values, gain):
    center = jnp.mean(values, axis=0, keepdims=True)
    spread = jnp.mean((values - center) ** 2, axis=0, keepdims=True)
    inverse = lax.rsqrt(spread + EPS)
    centred = (values - center) * inverse
    return centred * gain, centred, inverse


def norm_back_channels(upstream, centred, inverse, gain):
    scaled = upstream * gain
    first = jnp.mean(scaled, axis=0, keepdims=True)
    second = jnp.mean(scaled * centred, axis=0, keepdims=True)
    return inverse * (scaled - first - centred * second)


def column(row):
    at = lax.broadcasted_iota(jnp.int32, (WIDTH, WIDTH), 0)
    lane = lax.broadcasted_iota(jnp.int32, (WIDTH, WIDTH), 1)
    return jnp.sum(jnp.where(at == lane, row, 0.0), axis=1, keepdims=True)


def mask_lanes(token_ref, s):
    valid = jnp.sum(token_ref[...].astype(F32), axis=1, keepdims=True)
    lane = lax.broadcasted_iota(jnp.int32, (1, LANES), 1)
    row = lane // HALF + (lax.axis_index("row") * HALF + s * SUB)
    col = lane % HALF + lax.axis_index("col") * HALF
    return (jnp.maximum(row, col).astype(F32) < valid).astype(F32)


def bound_lanes(exponent_ref):
    bound = 448.0 * jnp.exp2(exponent_ref[...].astype(F32))
    return jnp.concatenate([bound[i : i + 1] for i in range(SUB)], axis=1)


def normed_cells(x_ref, gain_ref):
    gain = column(gain_ref[...])
    normed, centred, inverse = norm_channels(to_channels(x_ref[...].reshape(LANES, WIDTH)), gain)
    return normed.astype(BF16), centred, inverse, gain


def right_kernel(at, x_ref, gain_ref, w_ref, token_ref, exponent_ref, out_ref, buf):
    normed = normed_cells(x_ref, gain_ref)[0]
    proj = mm(w_ref[...], normed, TN)
    raw = mask_lanes(token_ref, at) * jax.nn.sigmoid(proj[:WIDTH]) * proj[WIDTH:]
    bound = bound_lanes(exponent_ref)
    stage_rows(jnp.clip(raw, -bound, bound), buf)
    for p in range(HALF):
        out_ref[p] = panel_row(buf, p).astype(BF16)


def left_kernel(x_ref, gain_ref, w_ref, token_ref, out_ref, buf):
    normed = normed_cells(x_ref, gain_ref)[0]
    proj = mm(w_ref[...], normed, TN)
    mask = mask_lanes(token_ref, pl.program_id(0))
    stage_rows(mask * jax.nn.sigmoid(proj[:WIDTH]) * proj[WIDTH:], buf)
    first = first_half(SUB)
    for p in range(HALF):
        row = panel_row(buf, p)
        out_ref[p, 0] = jnp.where(first, row, 0.0).astype(BF16)
        out_ref[p, 1] = jnp.where(first, 0.0, row).astype(BF16)


def tri_kernel(*refs):
    *slot_refs, left_ref, keep_ref, near_ref, send_ref, panel_ref = refs
    z, q = lax.axis_index("row"), lax.axis_index("col")
    for k, ref in enumerate(slot_refs):
        place = ((z ^ (z >> 1)) - (k % 4) + 4) & 3
        other = place ^ (place >> 1) ^ q
        at = (k // 4) * SUB
        panel_ref[(other & 1) * 2 + (other >> 1), :, at : at + SUB] = ref[...]
    for p in range(GROUP):
        right = jnp.concatenate([panel_ref[r, p] for r in range(4)], axis=0)
        tri = mm(right, left_ref[p].reshape(WIDTH, WIDTH), NT).astype(BF16)
        keep_ref[p] = tri[:PAIR]
        near_ref[p] = tri[PAIR : 2 * PAIR]
        send_ref[0, p] = tri[2 * PAIR : 3 * PAIR]
        send_ref[1, p] = tri[3 * PAIR :]


def mid_kernel(
    a_ref, b_ref, c_ref, x_ref, grad_ref, gain_in_ref, gain_out_ref, gate_ref, out_w_ref,
    g_out_so_far, g_gate_so_far, dtri_ref, dgate_ref, g_out_ref, g_gate_ref, buf, wide,
):
    gain_out = column(gain_out_ref[...])
    tri = channels_of(
        a_ref[...].astype(F32) + b_ref[0].astype(F32) + c_ref[...].astype(F32), buf, wide
    )
    tnorm_f, tcentred, tinverse = norm_channels(tri, gain_out)
    tnorm = tnorm_f.astype(BF16)

    def turned(ref):
        buf[...] = ref[...].astype(F32).reshape(LANES, WIDTH)
        rows = [buf[pl.ds(j, HALF, stride=SUB), :] for j in range(SUB)]
        return to_channels(jnp.concatenate(rows, axis=0).astype(BF16))

    normed = norm_channels(turned(x_ref), column(gain_in_ref[...]))[0].astype(BF16)
    upstream = turned(grad_ref)
    opened = jax.nn.sigmoid(mm(gate_ref[...], normed, TN))
    outproj = mm(out_w_ref[...], tnorm, TN)
    d_open = upstream * outproj
    d_outproj = (upstream * opened).astype(BF16)

    @pl.when(pl.program_id(0) == 0)
    def start():
        g_out_ref[...] = g_out_so_far[...]
        g_gate_ref[...] = g_gate_so_far[...]

    g_out_ref[...] += mm(tnorm, d_outproj, NT)
    d_tnorm = mm(out_w_ref[...], d_outproj, NN)
    d_tri = norm_back_channels(d_tnorm, tcentred, tinverse, gain_out)
    d_gatepre = (d_open * opened * (1.0 - opened)).astype(BF16)
    g_gate_ref[...] += mm(normed, d_gatepre, NT)
    stage_rows(d_tri, buf)
    for p in range(HALF):
        dtri_ref[p] = panel_row(buf, p).astype(BF16)
    buf[...] = to_cells(d_gatepre)
    for i in range(HALF):
        dgate_ref[i] = panel_row(buf, i).astype(BF16)


def dright_kernel(d0, d1, d2, d3, left_ref, *refs):
    *part_refs, held = refs
    z, q = lax.axis_index("row"), lax.axis_index("col")
    for r, ref in enumerate((d0, d1, d2, d3)):
        block_at = q ^ ((r % 2) * 2 + r // 2)
        held[((z ^ (z >> 1)) - (block_at ^ (block_at >> 1)) + 4) & 3] = ref[...]
    for p in range(GROUP):
        grads = jnp.concatenate([held[m, p] for m in range(4)], axis=0)
        part = mm(grads, left_ref[p].reshape(WIDTH, WIDTH), NN).astype(BF16)
        for k, ref in enumerate(part_refs):
            at = (k % 4) * PAIR + (k // 4) * SUB
            ref[p] = part[at : at + SUB]


def dleft_kernel(d0, d1, d2, d3, panel_ref, so_far, out_ref):
    first = first_half(HALF)
    for p in range(GROUP):
        grads = jnp.concatenate([d[p] for d in (d0, d1, d2, d3)], axis=0)
        right = jnp.concatenate([panel_ref[r, p] for r in range(4)], axis=0)
        both = mm(grads, right, TN)
        out_ref[p] = so_far[p] + jnp.where(first, both[:HALF], both[HALF:])


def gate_grads(upstream, mask, sig, value):
    d_gate = (upstream * mask * value * sig * (1.0 - sig)).astype(BF16)
    d_value = (upstream * mask * sig).astype(BF16)
    return jnp.concatenate([d_gate, d_value], axis=0)


def final_a_kernel(
    x_ref, dleft_ref, token_ref, gain_ref, w_ref, gate_ref, q0, q1, out_ref, g_ref, buf, wide
):
    s = pl.program_id(0)
    normed = normed_cells(x_ref, gain_ref)[0]
    proj = mm(w_ref[...], normed, TN)
    d_left = channels_of(dleft_ref[...], buf, wide)
    d_proj = gate_grads(d_left, mask_lanes(token_ref, s), jax.nn.sigmoid(proj[:WIDTH]), proj[WIDTH:])
    d_gate = jnp.concatenate([q0[...], q1[...]], axis=1).reshape(LANES, WIDTH)
    out_ref[...] = mm(w_ref[...], d_proj, NN) + mm(gate_ref[...], d_gate, NT)

    @pl.when(s == 0)
    def start():
        g_ref[...] = jnp.zeros_like(g_ref)

    g_ref[...] += mm(normed, d_proj, NT)


def final_b_kernel(
    at, x_ref, part_ref, a_ref, b_ref, token_ref, exponent_ref, gain_ref, w_ref, so_far, into_ref,
    out_ref, g_ref, buf, wide,
):
    normed, centred, inverse, gain = normed_cells(x_ref, gain_ref)
    proj = mm(w_ref[...], normed, TN)
    mask = mask_lanes(token_ref, at)
    sig = jax.nn.sigmoid(proj[:WIDTH])
    inside = jnp.abs(mask * sig * proj[WIDTH:]) <= bound_lanes(exponent_ref)
    d_right = channels_of(a_ref[...].astype(F32) + b_ref[...].astype(F32), buf, wide)
    d_proj = gate_grads(jnp.where(inside, d_right, 0.0), mask, sig, proj[WIDTH:])

    g_ref[...] = so_far[...] + mm(normed, d_proj, NT)
    d_normed = part_ref[...] + mm(w_ref[...], d_proj, NN)
    d_pair = norm_back_channels(d_normed, centred, inverse, gain).astype(BF16)
    out_ref[...] = to_cells(d_pair).astype(BF16).reshape(SUB, HALF, WIDTH)


def whole(array):
    return pl.BlockSpec(array.shape, lambda i: (0,) * array.ndim)


def block(shape, at):
    return pl.BlockSpec(shape, lambda i: at)


BUF = pltpu.VMEM((LANES, WIDTH), F32)
WIDE = pltpu.VMEM((WIDTH, LANES), F32)
PANEL = jax.ShapeDtypeStruct((HALF, SUB, WIDTH), BF16)
PANEL_SPEC = pl.BlockSpec((GROUP, SUB, WIDTH), lambda i: (i, 0, 0))
FOUR = jax.ShapeDtypeStruct((4, HALF, PAIR, WIDTH), BF16)
FOUR_SPEC = pl.BlockSpec((4, GROUP, PAIR, WIDTH), lambda i: (0, i, 0, 0))
TWO = jax.ShapeDtypeStruct((2, HALF, PAIR, WIDTH), BF16)
TWO_SPEC = pl.BlockSpec((2, GROUP, PAIR, WIDTH), lambda i: (0, i, 0, 0))
LEFT_SPEC = pl.BlockSpec((GROUP, 2, HALF, WIDTH), lambda i: (i, 0, 0, 0))
LONG = jax.ShapeDtypeStruct((HALF, PAIR, WIDTH), BF16)
LONG_SPEC = pl.BlockSpec((GROUP, PAIR, WIDTH), lambda i: (i, 0, 0))
WHOLE_PANEL = pl.BlockSpec(PANEL.shape, lambda i: (0, 0, 0))


def right_part(s, pair, gain, w_proj, tokens, exponents):
    return pl.pallas_call(
        functools.partial(right_kernel, s),
        grid=(1,),
        out_shape=PANEL,
        in_specs=[
            block((SUB, HALF, WIDTH), (s, 0, 0)), whole(gain), block((WIDTH, 2 * WIDTH), (0, 1)),
            whole(tokens), block((SUB, HALF), (s, 0)),
        ],
        out_specs=WHOLE_PANEL,
        scratch_shapes=[BUF],
        compiler_params=params(),
        cost_estimate=cost(4 * LANES * WIDTH * WIDTH, 1 << 19, LANES * WIDTH),
        name="right_part",
    )(pair, gain, w_proj, tokens, exponents)


def left_part(pair, gain, w_proj, tokens):
    return pl.pallas_call(
        left_kernel,
        grid=(HALF // SUB,),
        out_shape=jax.ShapeDtypeStruct((HALF, 2, HALF, WIDTH), BF16),
        in_specs=[
            pl.BlockSpec((SUB, HALF, WIDTH), lambda i: (i, 0, 0)), whole(gain),
            block((WIDTH, 2 * WIDTH), (0, 0)), whole(tokens),
        ],
        out_specs=pl.BlockSpec((HALF, 2, SUB, WIDTH), lambda i: (0, 0, i, 0)),
        scratch_shapes=[BUF],
        compiler_params=params(),
        cost_estimate=cost(16 * LANES * WIDTH * WIDTH, 3 << 20, 4 * LANES * WIDTH),
        name="left_part",
    )(pair, gain, w_proj, tokens)


def tri_part(slots, left):
    return pl.pallas_call(
        tri_kernel,
        grid=(HALF // GROUP,),
        out_shape=(LONG, LONG, TWO, FOUR),
        in_specs=[PANEL_SPEC] * 8 + [LEFT_SPEC],
        out_specs=(LONG_SPEC, LONG_SPEC, TWO_SPEC, FOUR_SPEC),
        compiler_params=params(),
        cost_estimate=cost(4 * HALF * HALF * WIDTH * WIDTH, 8 << 20),
        name="tri_part",
    )(*slots, left)


def mid_part(s, parts, pair, grad, gain_in, gain_out, w_gate, w_out, g_out, g_gate):
    square = jax.ShapeDtypeStruct((WIDTH, WIDTH), F32)
    steps = PAIR // SUB
    columns = pl.BlockSpec((HALF, SUB, WIDTH), lambda i: (0, s * steps + i, 0))
    panel = pl.BlockSpec((HALF, SUB, WIDTH), lambda i: (0, i, 0))
    small = [gain_in, gain_out, w_gate, w_out, g_out, g_gate]
    return pl.pallas_call(
        mid_kernel,
        grid=(steps,),
        out_shape=(LONG, LONG, square, square),
        in_specs=[panel, pl.BlockSpec((1, HALF, SUB, WIDTH), lambda i: (0, 0, i, 0)), panel]
        + [columns] * 2
        + [whole(a) for a in small],
        out_specs=(panel, panel, block(square.shape, (0, 0)), block(square.shape, (0, 0))),
        scratch_shapes=[BUF, WIDE],
        compiler_params=params(),
        cost_estimate=cost(24 * LANES * WIDTH * WIDTH, 4 << 20, 2 * LANES * WIDTH),
        name="mid_part",
    )(*parts, pair, grad, *small)


def dright_part(blocks, left):
    return pl.pallas_call(
        dright_kernel,
        grid=(HALF // GROUP,),
        out_shape=(PANEL,) * 8,
        in_specs=[LONG_SPEC] * 4 + [LEFT_SPEC],
        out_specs=(PANEL_SPEC,) * 8,
        scratch_shapes=[pltpu.VMEM((4, GROUP, PAIR, WIDTH), BF16)],
        compiler_params=params(),
        cost_estimate=cost(4 * HALF * HALF * WIDTH * WIDTH, 6 << 20),
        name="dright_part",
    )(*blocks, left)


def dleft_part(grads, panel, so_far):
    rows = pl.BlockSpec((GROUP, HALF, WIDTH), lambda i: (i, 0, 0))
    return pl.pallas_call(
        dleft_kernel,
        grid=(HALF // GROUP,),
        out_shape=jax.ShapeDtypeStruct((HALF, HALF, WIDTH), F32),
        in_specs=[LONG_SPEC] * 4 + [FOUR_SPEC, rows],
        out_specs=rows,
        compiler_params=params(),
        cost_estimate=cost(4 * HALF * HALF * WIDTH * WIDTH, 8 << 20),
        name="dleft_part",
    )(*grads, panel, so_far)


def final_a_part(pair, dleft, tokens, gain, w_proj, w_gate, gates):
    return pl.pallas_call(
        final_a_kernel,
        grid=(HALF // SUB,),
        out_shape=(
            jax.ShapeDtypeStruct((WIDTH, HALF * HALF), F32),
            jax.ShapeDtypeStruct((WIDTH, 2 * WIDTH), F32),
        ),
        in_specs=[
            pl.BlockSpec((SUB, HALF, WIDTH), lambda i: (i, 0, 0)),
            pl.BlockSpec((HALF, SUB, WIDTH), lambda i: (0, i, 0)),
            whole(tokens), whole(gain), block((WIDTH, 2 * WIDTH), (0, 0)), whole(w_gate),
        ]
        + [pl.BlockSpec((SUB, PAIR, WIDTH), lambda i: (i, 0, 0))] * 2,
        out_specs=(
            pl.BlockSpec((WIDTH, LANES), lambda i: (0, i)),
            block((WIDTH, 2 * WIDTH), (0, 0)),
        ),
        scratch_shapes=[BUF, WIDE],
        compiler_params=params(),
        cost_estimate=cost(56 * LANES * WIDTH * WIDTH, 8 << 20, 4 * LANES * WIDTH),
        name="final_a_part",
    )(pair, dleft, tokens, gain, w_proj, w_gate, *gates)


def final_b_part(s, pair, part, sums, tokens, exponents, gain, w_proj, so_far, into):
    rows = block((SUB, HALF, WIDTH), (s, 0, 0))
    return pl.pallas_call(
        functools.partial(final_b_kernel, s),
        grid=(1,),
        out_shape=(
            jax.ShapeDtypeStruct((HALF, HALF, WIDTH), BF16),
            jax.ShapeDtypeStruct((WIDTH, 2 * WIDTH), F32),
        ),
        in_specs=[
            rows, block((WIDTH, LANES), (0, s)), WHOLE_PANEL, WHOLE_PANEL, whole(tokens),
            block((SUB, HALF), (s, 0)), whole(gain), block((WIDTH, 2 * WIDTH), (0, 1)), whole(so_far),
            pl.BlockSpec(memory_space=pl.ANY),
        ],
        out_specs=(rows, block((WIDTH, 2 * WIDTH), (0, 0))),
        scratch_shapes=[BUF, WIDE],
        input_output_aliases={9: 0} if into.shape == pair.shape else {},
        compiler_params=params(),
        cost_estimate=cost(14 * LANES * WIDTH * WIDTH, 2 << 20, LANES * WIDTH),
        name="final_b_part",
    )(pair, part, *sums, tokens, exponents, gain, w_proj, so_far, into)


def after(array, *others):
    return lax.optimization_barrier((array, *others))[0]


def blocked(pair_tiles, grad_out, exponents, token_mask, gain_in, w_proj, w_gate, gain_out, w_out):
    width = pair_tiles.shape[-1]
    crop_len = token_mask.shape[0]
    core = lax.axis_index("col") % 2
    tokens = token_mask.reshape(1, crop_len)
    gain_in = gain_in.reshape(1, width)
    gain_out = gain_out.reshape(1, width)

    def forward(a):
        return lax.ppermute(a, "row", [(0, 1), (1, 3), (3, 2), (2, 0)])

    def over_row(a, bit):
        return lax.ppermute(a, "row", [(k, k ^ bit) for k in range(4)])

    def over_x(a):
        return lax.ppermute(a, "col", [(k, k ^ 2) for k in range(4)])

    def over_core(a):
        return lax.ppermute(a, "col", [(k, k ^ 1) for k in range(4)])

    def plus(a, b):
        return (a.astype(F32) + b.astype(F32)).astype(BF16)

    def in_hbm(*arrays):
        return [pltpu.with_memory_space_constraint(a, pltpu.HBM) for a in arrays]

    def right(s):
        return right_part(s, *in_hbm(pair_tiles, gain_in, w_proj, tokens, exponents))

    a0, b0 = right(0), right(1)
    left = left_part(*in_hbm(pair_tiles, gain_in, w_proj, tokens))
    a1, b1 = forward(a0), forward(b0)
    a2, b2 = forward(a1), forward(after(b1, left))
    c0, d0 = right(2), right(3)
    a3, b3 = forward(after(a2, c0)), forward(after(b2, d0))
    c1, d1 = forward(after(c0, b2)), forward(after(d0, a3))

    g_out = g_gate = jnp.zeros((width, width), F32)
    d_left = jnp.zeros((HALF, HALF, WIDTH), F32)

    def triangle(slots):
        keep, near, send, panel = tri_part(slots, left)
        got = over_core(send)
        return keep, got, plus(near, got[1]), panel

    def middle(s, tri, mine):
        return mid_part(
            s, (tri[0], tri[1], mine), pair_tiles, grad_out, gain_in, gain_out, w_gate, w_out, g_out, g_gate
        )

    def spread(d_tri):
        far = over_x(d_tri)
        return [d_tri, far, over_core(d_tri), over_core(far)]

    ab = triangle([a0, a1, a2, a3, b0, b1, b2, b3])
    x_ab = over_x(after(ab[2], c1))
    c2, d2 = forward(after(c1, ab[0])), forward(after(d1, ab[2]))
    dtri_ab, gate_ab, g_out, g_gate = middle(0, ab, after(x_ab, c2, d1))
    blocks_ab = spread(dtri_ab)
    c3, d3 = forward(c2), forward(after(d2, dtri_ab))

    cd = triangle([c0, c1, c2, c3, d0, d1, d2, after(d3, blocks_ab[1])])
    x_cd = over_x(cd[2])
    part = dright_part([after(blocks_ab[0], cd[2])] + blocks_ab[1:], left)
    part_a, part_b = part[:4], part[4:]
    r_a, r_b = forward(part_a[1]), forward(part_b[1])
    d_left = dleft_part([after(blocks_ab[0], part_b[1])] + blocks_ab[1:], ab[3], d_left)
    r_a = plus(r_a, part_a[2])
    r_a2 = forward(r_a)
    r_b = plus(r_b, part_b[2])
    dtri_cd, gate_cd, g_out, g_gate = middle(1, cd, after(x_cd, r_a, d_left))
    blocks_cd = spread(dtri_cd)
    r_b2 = forward(after(r_b, dtri_cd))
    r_a2 = plus(r_a2, part_a[3])
    r_a3 = forward(r_a2)
    r_b2 = plus(r_b2, part_b[3])
    r_b3 = forward(r_b2)
    part = dright_part([after(blocks_cd[0], r_a2, r_b2)] + blocks_cd[1:], left)
    part_c, part_d = part[:4], part[4:]

    r_c, r_d = forward(part_c[1]), forward(part_d[1])
    d_left = dleft_part([after(blocks_cd[0], part_d[1])] + blocks_cd[1:], cd[3], d_left)
    r_c = plus(r_c, part_c[2])
    partial, g_a = final_a_part(
        pair_tiles, after(d_left, r_c), tokens, gain_in, w_proj, w_gate, [gate_ab, gate_cd]
    )
    r_c = forward(r_c)
    r_d = plus(r_d, part_d[2])
    zero = jnp.zeros((width, 2 * width), F32)

    def final(s, sums, so_far, into):
        return final_b_part(
            s, pair_tiles, partial, sums, tokens, exponents, gain_in, w_proj, so_far, into
        )

    d_pair, g_first = final(0, (part_a[0], after(r_a3, r_d)), zero, gain_in)
    r_d = forward(r_d)
    r_c = plus(r_c, part_c[3])
    d_pair, g_first = final(1, (part_b[0], after(r_b3, r_c)), g_first, d_pair)
    r_c = forward(r_c)
    r_d = plus(r_d, part_d[3])

    def halved(a):
        half = a.shape[0] // 2
        a = lax.dynamic_slice_in_dim(a, core * half, half) + over_core(
            lax.dynamic_slice_in_dim(a, (1 - core) * half, half)
        )
        return a + over_x(a)

    early = halved(after(jnp.concatenate([g_out, g_gate, g_a, g_first], axis=1), r_d))
    r_d = forward(r_d)
    d_pair, g_last = final(2, (part_c[0], after(r_c, early)), zero, d_pair)
    d_pair, g_last = final(3, (part_d[0], r_d), g_last, d_pair)
    late = halved(g_last)
    sums = jnp.concatenate([early[:, : 4 * width], early[:, 4 * width :] + late], axis=1)
    for bit in (1, 2):
        mine = sums.astype(BF16)
        sums = mine.astype(F32) + over_row(mine, bit).astype(F32)
    sums = sums / crop_len
    theirs = over_core(sums)
    sums = jnp.concatenate(
        [jnp.where(core == 0, sums, theirs), jnp.where(core == 0, theirs, sums)], axis=0
    )
    return d_pair, sums[:, 2 * width :], sums[:, width : 2 * width], sums[:, :width]


def local(pair_tiles, *rest, rows_over, cols_over):
    if pair_tiles.shape == (HALF, HALF, WIDTH) and rows_over == cols_over == 4:
        return blocked(pair_tiles, *rest)
    return plain(pair_tiles, *rest)


def solution(mesh):
    return jax.shard_map(
        functools.partial(local, rows_over=mesh.shape["row"], cols_over=mesh.shape["col"]),
        mesh=mesh,
        in_specs=(
            P(("crop", "row"), "col", None),
            P(("crop", "row"), "col", None),
            P(("crop", "row"), "col"),
            P("crop"),
            P(),
            P(),
            P(),
            P(),
            P(),
        ),
        out_specs=(
            P(("crop", "row"), "col", None),
            P("crop", None),
            P("crop", None),
            P("crop", None),
        ),
        check_vma=False,
    )
```

```python
import functools

import jax
import jax.numpy as jnp
from jax import lax
from jax.experimental import pallas as pl
from jax.experimental.pallas import tpu as pltpu
from jax.sharding import PartitionSpec as P

EPS = 1e-05


def layer_norm(values, gain):
    center = jnp.mean(values, axis=-1, keepdims=True)
    spread = jnp.mean((values - center) ** 2, axis=-1, keepdims=True)
    inverse = lax.rsqrt(spread + EPS)
    centred = (values - center) * inverse
    return (centred * gain, centred, inverse)


def norm_back(upstream, centred, inverse, gain):
    scaled = upstream * gain
    first = jnp.mean(scaled, axis=-1, keepdims=True)
    second = jnp.mean(scaled * centred, axis=-1, keepdims=True)
    return inverse * (scaled - first - centred * second)


def plain(pair_tiles, grad_out, exponents, token_mask, gain_in, w_proj, w_gate, gain_out, w_out):
    f32 = jnp.float32
    bf16 = jnp.bfloat16
    rows, cols, width = pair_tiles.shape
    crop_len = token_mask.shape[0]
    row_at = lax.axis_index("row")
    col_at = lax.axis_index("col")
    maskf = token_mask.astype(f32)
    mask_rows = lax.dynamic_slice_in_dim(maskf, row_at * rows, rows)
    mask_cols = lax.dynamic_slice_in_dim(maskf, col_at * cols, cols)
    pair_mask = (mask_rows[:, None] * mask_cols[None, :])[..., None]
    normed_f, centred, inverse = layer_norm(pair_tiles.astype(f32), gain_in)
    normed = normed_f.astype(bf16)
    flat = normed.reshape(-1, width)
    projected = jnp.dot(flat, w_proj, preferred_element_type=f32).reshape(rows, cols, 4 * width)
    gate_a = projected[..., :width]
    value_a = projected[..., width : 2 * width]
    gate_b = projected[..., 2 * width : 3 * width]
    value_b = projected[..., 3 * width :]
    sig_a = jax.nn.sigmoid(gate_a)
    sig_b = jax.nn.sigmoid(gate_b)
    left = (pair_mask * sig_a * value_a).astype(bf16)
    right_raw = pair_mask * sig_b * value_b
    bound = (448.0 * jnp.exp2(exponents.astype(f32)))[..., None]
    right = jnp.clip(right_raw, -bound, bound).astype(bf16)
    inside = (jnp.abs(right_raw) <= bound).astype(f32)
    panel = lax.all_gather(right, "row", axis=0, tiled=True)
    tri_cols = lax.psum_scatter(
        jnp.einsum("jkc,ikc->jic", panel, left, preferred_element_type=f32).astype(jnp.bfloat16),
        "col",
        scatter_dimension=0,
        tiled=True,
    ).astype(jnp.float32)
    tri = jnp.transpose(tri_cols, (1, 0, 2))
    tnorm_f, tcentred, tinverse = layer_norm(tri, gain_out)
    tnorm = tnorm_f.astype(bf16)
    tflat = tnorm.reshape(-1, width)
    opened = jax.nn.sigmoid(jnp.dot(flat, w_gate, preferred_element_type=f32)).reshape(
        rows, cols, width
    )
    outproj = jnp.dot(tflat, w_out, preferred_element_type=f32).reshape(rows, cols, width)
    upstream = grad_out.astype(f32)
    d_open = upstream * outproj
    d_outproj = (upstream * opened).astype(bf16).reshape(-1, width)
    g_out = jnp.dot(tflat.T, d_outproj, preferred_element_type=f32)
    d_tnorm = jnp.dot(d_outproj, w_out.T, preferred_element_type=f32).reshape(rows, cols, width)
    d_tri = norm_back(d_tnorm, tcentred, tinverse, gain_out).astype(bf16)
    d_gatepre = (d_open * opened * (1.0 - opened)).astype(bf16).reshape(-1, width)
    g_gate = jnp.dot(flat.T, d_gatepre, preferred_element_type=f32)
    grad_full = lax.all_gather(d_tri, "col", axis=1, tiled=True)
    d_left = jnp.einsum("ijc,jkc->ikc", grad_full, panel, preferred_element_type=f32)
    d_right = (
        lax.psum_scatter(
            jnp.einsum("ijc,ikc->jkc", grad_full, left, preferred_element_type=f32).astype(
                jnp.bfloat16
            ),
            "row",
            scatter_dimension=0,
            tiled=True,
        ).astype(jnp.float32)
        * inside
    )
    d_gate_a = d_left * pair_mask * value_a * sig_a * (1.0 - sig_a)
    d_value_a = d_left * pair_mask * sig_a
    d_gate_b = d_right * pair_mask * value_b * sig_b * (1.0 - sig_b)
    d_value_b = d_right * pair_mask * sig_b
    d_proj = (
        jnp.concatenate([d_gate_a, d_value_a, d_gate_b, d_value_b], axis=-1)
        .astype(bf16)
        .reshape(-1, 4 * width)
    )
    g_proj = jnp.dot(flat.T, d_proj, preferred_element_type=f32)
    d_normed = jnp.dot(d_proj, w_proj.T, preferred_element_type=f32) + jnp.dot(
        d_gatepre, w_gate.T, preferred_element_type=f32
    )
    d_pair = norm_back(d_normed.reshape(rows, cols, width), centred, inverse, gain_in).astype(bf16)
    sum_proj, sum_gate, sum_out = lax.psum((g_proj, g_gate, g_out), ("row", "col"))
    return (d_pair, sum_proj / crop_len, sum_gate / crop_len, sum_out / crop_len)


SUB = 16
PART = 16
HALF = 64
WIDTH = 128
LANES = SUB * HALF
GROUP = 16
NT = (((1,), (1,)), ((), ()))
NN = (((1,), (0,)), ((), ()))
TN = (((0,), (0,)), ((), ()))
F32 = jnp.float32
BF16 = jnp.bfloat16


def mm(a, b, dims):
    return lax.dot_general(a, b, dims, preferred_element_type=F32)


def params():
    return pltpu.CompilerParams(vmem_limit_bytes=16 * 1024 * 1024)


def cost(flops, size, exps=0):
    return pl.CostEstimate(flops=flops, bytes_accessed=size, transcendentals=exps)


def first_half(rows):
    return lax.broadcasted_iota(jnp.int32, (rows, WIDTH), 1) < HALF


def swap_halves(a, b):
    first = first_half(HALF)
    return (
        jnp.where(first, a, pltpu.roll(b, HALF, 1)),
        jnp.where(first, pltpu.roll(a, HALF, 1), b),
    )


def eye():
    row = lax.broadcasted_iota(jnp.int32, (WIDTH, WIDTH), 0)
    lane = lax.broadcasted_iota(jnp.int32, (WIDTH, WIDTH), 1)
    return (row == lane).astype(F32).astype(BF16)


def to_channels(cells):
    return mm(eye(), cells, NT)


def to_cells(channels):
    return mm(channels, eye(), TN)


def stage_rows(channels, buf):
    for t in range(SUB // 2):
        part = channels[:, t * WIDTH : (t + 1) * WIDTH]
        one, two = swap_halves(part[:HALF], part[HALF:])
        buf[(2 * t) * HALF : (2 * t + 1) * HALF, :] = one
        buf[(2 * t + 1) * HALF : (2 * t + 2) * HALF, :] = two


def panel_row(buf, p):
    return buf[pl.ds(p, SUB, stride=HALF), :]


def channels_of(panels, buf, out):
    buf[...] = panels.reshape(LANES, WIDTH)
    for t in range(SUB // 2):
        one = buf[pl.ds(2 * t, HALF, stride=SUB), :]
        two = buf[pl.ds(2 * t + 1, HALF, stride=SUB), :]
        low, high = swap_halves(one, two)
        out[:HALF, t * WIDTH : (t + 1) * WIDTH] = low
        out[HALF:, t * WIDTH : (t + 1) * WIDTH] = high
    return out[...]


def norm_channels(values, gain):
    center = jnp.mean(values, axis=0, keepdims=True)
    spread = jnp.mean((values - center) ** 2, axis=0, keepdims=True)
    inverse = lax.rsqrt(spread + EPS)
    centred = (values - center) * inverse
    return centred * gain, centred, inverse


def norm_back_channels(upstream, centred, inverse, gain):
    scaled = upstream * gain
    first = jnp.mean(scaled, axis=0, keepdims=True)
    second = jnp.mean(scaled * centred, axis=0, keepdims=True)
    return inverse * (scaled - first - centred * second)


def column(row):
    at = lax.broadcasted_iota(jnp.int32, (WIDTH, WIDTH), 0)
    lane = lax.broadcasted_iota(jnp.int32, (WIDTH, WIDTH), 1)
    return jnp.sum(jnp.where(at == lane, row, 0.0), axis=1, keepdims=True)


def mask_lanes(token_ref, s):
    valid = jnp.sum(token_ref[...].astype(F32), axis=1, keepdims=True)
    lane = lax.broadcasted_iota(jnp.int32, (1, LANES), 1)
    row = lane // HALF + (lax.axis_index("row") * HALF + s * SUB)
    col = lane % HALF + lax.axis_index("col") * HALF
    return (jnp.maximum(row, col).astype(F32) < valid).astype(F32)


def bound_lanes(exponent_ref):
    bound = 448.0 * jnp.exp2(exponent_ref[...].astype(F32))
    return jnp.concatenate([bound[i : i + 1] for i in range(SUB)], axis=1)


def normed_cells(x_ref, gain_ref):
    gain = column(gain_ref[...])
    normed, centred, inverse = norm_channels(to_channels(x_ref[...].reshape(LANES, WIDTH)), gain)
    return normed.astype(BF16), centred, inverse, gain


def right_kernel(at, x_ref, gain_ref, w_ref, token_ref, exponent_ref, out_ref, buf):
    normed = normed_cells(x_ref, gain_ref)[0]
    proj = mm(w_ref[...], normed, TN)
    raw = mask_lanes(token_ref, at + pl.program_id(0)) * jax.nn.sigmoid(proj[:WIDTH]) * proj[WIDTH:]
    bound = bound_lanes(exponent_ref)
    stage_rows(jnp.clip(raw, -bound, bound), buf)
    for p in range(HALF):
        out_ref[p] = panel_row(buf, p).astype(BF16)


def left_kernel(x_ref, gain_ref, w_ref, token_ref, out_ref, buf):
    normed = normed_cells(x_ref, gain_ref)[0]
    proj = mm(w_ref[...], normed, TN)
    mask = mask_lanes(token_ref, pl.program_id(0))
    stage_rows(mask * jax.nn.sigmoid(proj[:WIDTH]) * proj[WIDTH:], buf)
    first = first_half(SUB)
    for p in range(HALF):
        row = panel_row(buf, p)
        out_ref[p, 0] = jnp.where(first, row, 0.0).astype(BF16)
        out_ref[p, 1] = jnp.where(first, 0.0, row).astype(BF16)


def tri_kernel(s0, s1, s2, s3, left_ref, keep_ref, near_ref, send_ref, panel_ref):
    z, q = lax.axis_index("row"), lax.axis_index("col")
    for m, ref in enumerate((s0, s1, s2, s3)):
        place = ((z ^ (z >> 1)) - m + 4) & 3
        other = place ^ (place >> 1) ^ q
        panel_ref[(other & 1) * 2 + (other >> 1)] = ref[...]
    for p in range(GROUP):
        right = jnp.concatenate([panel_ref[r, p] for r in range(4)], axis=0)
        tri = mm(right, left_ref[p].reshape(WIDTH, WIDTH), NT).astype(BF16)
        keep_ref[p] = tri[:SUB]
        near_ref[p] = tri[SUB : 2 * SUB]
        send_ref[0, p] = tri[2 * SUB : 3 * SUB]
        send_ref[1, p] = tri[3 * SUB :]


def mid_kernel(
    a_ref, b_ref, c_ref, x_ref, grad_ref, gain_in_ref, gain_out_ref, gate_ref, out_w_ref,
    g_out_so_far, g_gate_so_far, dtri_ref, dgate_ref, g_out_ref, g_gate_ref, buf, wide,
):
    gain_out = column(gain_out_ref[...])
    tri = channels_of(
        a_ref[...].astype(F32) + b_ref[0].astype(F32) + c_ref[...].astype(F32), buf, wide
    )
    tnorm_f, tcentred, tinverse = norm_channels(tri, gain_out)
    tnorm = tnorm_f.astype(BF16)

    def turned(ref):
        buf[...] = ref[...].astype(F32).reshape(LANES, WIDTH)
        rows = [buf[pl.ds(j, HALF, stride=SUB), :] for j in range(SUB)]
        return to_channels(jnp.concatenate(rows, axis=0).astype(BF16))

    normed = norm_channels(turned(x_ref), column(gain_in_ref[...]))[0].astype(BF16)
    upstream = turned(grad_ref)
    opened = jax.nn.sigmoid(mm(gate_ref[...], normed, TN))
    outproj = mm(out_w_ref[...], tnorm, TN)
    d_open = upstream * outproj
    d_outproj = (upstream * opened).astype(BF16)
    g_out_ref[...] = g_out_so_far[...] + mm(tnorm, d_outproj, NT)
    d_tnorm = mm(out_w_ref[...], d_outproj, NN)
    d_tri = norm_back_channels(d_tnorm, tcentred, tinverse, gain_out)
    d_gatepre = (d_open * opened * (1.0 - opened)).astype(BF16)
    g_gate_ref[...] = g_gate_so_far[...] + mm(normed, d_gatepre, NT)
    stage_rows(d_tri, buf)
    for p in range(HALF):
        dtri_ref[p] = panel_row(buf, p).astype(BF16)
    buf[...] = to_cells(d_gatepre)
    for i in range(HALF):
        dgate_ref[i] = panel_row(buf, i).astype(BF16)


def dright_kernel(*refs):
    *grads_refs, left_ref, p0, p1, p2, p3, held = refs
    z, q = lax.axis_index("row"), lax.axis_index("col")
    for k, ref in enumerate(grads_refs):
        r = k % 4
        block_at = q ^ ((r % 2) * 2 + r // 2)
        slot = ((z ^ (z >> 1)) - (block_at ^ (block_at >> 1)) + 4) & 3
        held[slot, :, (k // 4) * SUB : (k // 4 + 1) * SUB] = ref[...]
    for p in range(GROUP):
        grads = jnp.concatenate([held[m, p] for m in range(4)], axis=0)
        part = mm(grads, left_ref[p].reshape(WIDTH, WIDTH), NN).astype(BF16)
        for m, ref in enumerate((p0, p1, p2, p3)):
            ref[p] = part[m * PART : (m + 1) * PART]


def dleft_kernel(*refs):
    so_far, out_ref = refs[-2:]
    parts = (len(refs) - 2) // 5
    grad_refs, panel_refs = refs[: 4 * parts], refs[4 * parts : 5 * parts]
    first = first_half(HALF)
    for p in range(GROUP):
        grads = jnp.concatenate([d[p] for d in grad_refs], axis=0)
        right = jnp.concatenate([r[q, p] for r in panel_refs for q in range(4)], axis=0)
        both = mm(grads, right, TN)
        out_ref[p] = so_far[p] + jnp.where(first, both[:HALF], both[HALF:])


def gate_grads(upstream, mask, sig, value):
    d_gate = (upstream * mask * value * sig * (1.0 - sig)).astype(BF16)
    d_value = (upstream * mask * sig).astype(BF16)
    return jnp.concatenate([d_gate, d_value], axis=0)


def final_a_kernel(
    x_ref, dleft_ref, token_ref, gain_ref, w_ref, gate_ref, q0, q1, q2, q3, out_ref, g_ref, buf, wide
):
    s = pl.program_id(0)
    normed = normed_cells(x_ref, gain_ref)[0]
    proj = mm(w_ref[...], normed, TN)
    d_left = channels_of(dleft_ref[...], buf, wide)
    d_proj = gate_grads(d_left, mask_lanes(token_ref, s), jax.nn.sigmoid(proj[:WIDTH]), proj[WIDTH:])
    d_gate = jnp.concatenate([q[...] for q in (q0, q1, q2, q3)], axis=1).reshape(LANES, WIDTH)
    out_ref[...] = mm(w_ref[...], d_proj, NN) + mm(gate_ref[...], d_gate, NT)

    @pl.when(s == 0)
    def start():
        g_ref[...] = jnp.zeros_like(g_ref)

    g_ref[...] += mm(normed, d_proj, NT)


def final_b_kernel(
    at, x_ref, part_ref, a_ref, b_ref, token_ref, exponent_ref, gain_ref, w_ref, so_far, into_ref,
    out_ref, g_ref, buf, wide,
):
    step = pl.program_id(0)
    normed, centred, inverse, gain = normed_cells(x_ref, gain_ref)
    proj = mm(w_ref[...], normed, TN)
    mask = mask_lanes(token_ref, at + step)
    sig = jax.nn.sigmoid(proj[:WIDTH])
    inside = jnp.abs(mask * sig * proj[WIDTH:]) <= bound_lanes(exponent_ref)
    d_right = channels_of(a_ref[...].astype(F32) + b_ref[...].astype(F32), buf, wide)
    d_proj = gate_grads(jnp.where(inside, d_right, 0.0), mask, sig, proj[WIDTH:])

    @pl.when(step == 0)
    def start():
        g_ref[...] = so_far[...]

    g_ref[...] += mm(normed, d_proj, NT)
    d_normed = part_ref[...] + mm(w_ref[...], d_proj, NN)
    d_pair = norm_back_channels(d_normed, centred, inverse, gain).astype(BF16)
    out_ref[...] = to_cells(d_pair).astype(BF16).reshape(SUB, HALF, WIDTH)


def whole(array):
    return pl.BlockSpec(array.shape, lambda i: (0,) * array.ndim)


def block(shape, at):
    return pl.BlockSpec(shape, lambda i: at)


BUF = pltpu.VMEM((LANES, WIDTH), F32)
WIDE = pltpu.VMEM((WIDTH, LANES), F32)
PANEL = jax.ShapeDtypeStruct((HALF, SUB, WIDTH), BF16)
PANEL_SPEC = pl.BlockSpec((GROUP, SUB, WIDTH), lambda i: (i, 0, 0))
FOUR = jax.ShapeDtypeStruct((4, HALF, SUB, WIDTH), BF16)
FOUR_SPEC = pl.BlockSpec((4, GROUP, SUB, WIDTH), lambda i: (0, i, 0, 0))
TWO = jax.ShapeDtypeStruct((2, HALF, SUB, WIDTH), BF16)
TWO_SPEC = pl.BlockSpec((2, GROUP, SUB, WIDTH), lambda i: (0, i, 0, 0))
LEFT_SPEC = pl.BlockSpec((GROUP, 2, HALF, WIDTH), lambda i: (i, 0, 0, 0))
LONG = jax.ShapeDtypeStruct((HALF, PART, WIDTH), BF16)
LONG_SPEC = pl.BlockSpec((GROUP, PART, WIDTH), lambda i: (i, 0, 0))
WHOLE_PANEL = pl.BlockSpec(PANEL.shape, lambda i: (0, 0, 0))


def right_part(s, pair, gain, w_proj, tokens, exponents):
    steps = PART // SUB
    return pl.pallas_call(
        functools.partial(right_kernel, s * steps),
        grid=(steps,),
        out_shape=LONG,
        in_specs=[
            pl.BlockSpec((SUB, HALF, WIDTH), lambda i: (s * steps + i, 0, 0)),
            whole(gain), block((WIDTH, 2 * WIDTH), (0, 1)), whole(tokens),
            pl.BlockSpec((SUB, HALF), lambda i: (s * steps + i, 0)),
        ],
        out_specs=pl.BlockSpec((HALF, SUB, WIDTH), lambda i: (0, i, 0)),
        scratch_shapes=[BUF],
        compiler_params=params(),
        cost_estimate=cost(8 * LANES * WIDTH * WIDTH, 1 << 20, 2 * LANES * WIDTH),
        name="right_part",
    )(pair, gain, w_proj, tokens, exponents)


def left_part(pair, gain, w_proj, tokens):
    return pl.pallas_call(
        left_kernel,
        grid=(HALF // SUB,),
        out_shape=jax.ShapeDtypeStruct((HALF, 2, HALF, WIDTH), BF16),
        in_specs=[
            pl.BlockSpec((SUB, HALF, WIDTH), lambda i: (i, 0, 0)), whole(gain),
            block((WIDTH, 2 * WIDTH), (0, 0)), whole(tokens),
        ],
        out_specs=pl.BlockSpec((HALF, 2, SUB, WIDTH), lambda i: (0, 0, i, 0)),
        scratch_shapes=[BUF],
        compiler_params=params(),
        cost_estimate=cost(16 * LANES * WIDTH * WIDTH, 3 << 20, 4 * LANES * WIDTH),
        name="left_part",
    )(pair, gain, w_proj, tokens)


def tri_part(at, slots, left):
    return pl.pallas_call(
        tri_kernel,
        grid=(HALF // GROUP,),
        out_shape=(PANEL, PANEL, TWO, FOUR),
        in_specs=[pl.BlockSpec((GROUP, SUB, WIDTH), lambda i: (i, at, 0))] * 4 + [LEFT_SPEC],
        out_specs=(PANEL_SPEC, PANEL_SPEC, TWO_SPEC, FOUR_SPEC),
        compiler_params=params(),
        cost_estimate=cost(2 * HALF * HALF * WIDTH * WIDTH, 5 << 20),
        name="tri_part",
    )(*slots, left)


def mid_part(s, parts, pair, grad, gain_in, gain_out, w_gate, w_out, g_out, g_gate):
    square = jax.ShapeDtypeStruct((WIDTH, WIDTH), F32)
    columns = block((HALF, SUB, WIDTH), (0, s, 0))
    small = [gain_in, gain_out, w_gate, w_out, g_out, g_gate]
    return pl.pallas_call(
        mid_kernel,
        grid=(1,),
        out_shape=(PANEL, pltpu.HBM(PANEL.shape, BF16), square, square),
        in_specs=[WHOLE_PANEL, block((1, HALF, SUB, WIDTH), (0, 0, 0, 0)), WHOLE_PANEL]
        + [columns] * 2
        + [whole(a) for a in small],
        out_specs=(WHOLE_PANEL, WHOLE_PANEL, block(square.shape, (0, 0)), block(square.shape, (0, 0))),
        scratch_shapes=[BUF, WIDE],
        compiler_params=params(),
        cost_estimate=cost(12 * LANES * WIDTH * WIDTH, 2 << 20, LANES * WIDTH),
        name="mid_part",
    )(*parts, pair, grad, *small)


def dright_part(blocks, left):
    return pl.pallas_call(
        dright_kernel,
        grid=(HALF // GROUP,),
        out_shape=(pltpu.HBM(LONG.shape, BF16), LONG, LONG, LONG),
        in_specs=[PANEL_SPEC] * len(blocks) + [LEFT_SPEC],
        out_specs=(LONG_SPEC,) * 4,
        scratch_shapes=[pltpu.VMEM((4, GROUP, PART, WIDTH), BF16)],
        compiler_params=params(),
        cost_estimate=cost(4 * HALF * HALF * WIDTH * WIDTH, 6 << 20),
        name="dright_part",
    )(*blocks, left)


def dleft_part(grads, panels, so_far):
    rows = pl.BlockSpec((GROUP, HALF, WIDTH), lambda i: (i, 0, 0))
    return pl.pallas_call(
        dleft_kernel,
        grid=(HALF // GROUP,),
        out_shape=jax.ShapeDtypeStruct((HALF, HALF, WIDTH), F32),
        in_specs=[PANEL_SPEC] * len(grads) + [FOUR_SPEC] * len(panels) + [rows],
        out_specs=rows,
        compiler_params=params(),
        cost_estimate=cost(4 * HALF * HALF * WIDTH * WIDTH, 8 << 20),
        name="dleft_part",
    )(*grads, *panels, so_far)


def final_a_part(pair, dleft, tokens, gain, w_proj, w_gate, gates):
    return pl.pallas_call(
        final_a_kernel,
        grid=(HALF // SUB,),
        out_shape=(
            jax.ShapeDtypeStruct((WIDTH, HALF * HALF), F32),
            jax.ShapeDtypeStruct((WIDTH, 2 * WIDTH), F32),
        ),
        in_specs=[
            pl.BlockSpec((SUB, HALF, WIDTH), lambda i: (i, 0, 0)),
            pl.BlockSpec((HALF, SUB, WIDTH), lambda i: (0, i, 0)),
            whole(tokens), whole(gain), block((WIDTH, 2 * WIDTH), (0, 0)), whole(w_gate),
        ]
        + [pl.BlockSpec((SUB, SUB, WIDTH), lambda i: (i, 0, 0))] * 4,
        out_specs=(
            pl.BlockSpec((WIDTH, LANES), lambda i: (0, i)),
            block((WIDTH, 2 * WIDTH), (0, 0)),
        ),
        scratch_shapes=[BUF, WIDE],
        compiler_params=params(),
        cost_estimate=cost(56 * LANES * WIDTH * WIDTH, 8 << 20, 4 * LANES * WIDTH),
        name="final_a_part",
    )(pair, dleft, tokens, gain, w_proj, w_gate, *gates)


def final_b_part(s, pair, part, sums, tokens, exponents, gain, w_proj, so_far, into):
    steps = PART // SUB
    rows = pl.BlockSpec((SUB, HALF, WIDTH), lambda i: (s * steps + i, 0, 0))
    panel = pl.BlockSpec((HALF, SUB, WIDTH), lambda i: (0, i, 0))
    return pl.pallas_call(
        functools.partial(final_b_kernel, s * steps),
        grid=(steps,),
        out_shape=(
            jax.ShapeDtypeStruct((HALF, HALF, WIDTH), BF16),
            jax.ShapeDtypeStruct((WIDTH, 2 * WIDTH), F32),
        ),
        in_specs=[
            rows,
            pl.BlockSpec((WIDTH, LANES), lambda i: (0, s * steps + i)),
            panel, panel, whole(tokens),
            pl.BlockSpec((SUB, HALF), lambda i: (s * steps + i, 0)),
            whole(gain), block((WIDTH, 2 * WIDTH), (0, 1)), whole(so_far),
            pl.BlockSpec(memory_space=pl.ANY),
        ],
        out_specs=(rows, block((WIDTH, 2 * WIDTH), (0, 0))),
        scratch_shapes=[BUF, WIDE],
        input_output_aliases={9: 0} if into.shape == pair.shape else {},
        compiler_params=params(),
        cost_estimate=cost(28 * LANES * WIDTH * WIDTH, 4 << 20, 2 * LANES * WIDTH),
        name="final_b_part",
    )(pair, part, *sums, tokens, exponents, gain, w_proj, so_far, into)


def after(array, *others):
    return lax.optimization_barrier((array, *others))[0]


def blocked(pair_tiles, grad_out, exponents, token_mask, gain_in, w_proj, w_gate, gain_out, w_out):
    width = pair_tiles.shape[-1]
    crop_len = token_mask.shape[0]
    core = lax.axis_index("col") % 2
    tokens = token_mask.reshape(1, crop_len)
    gain_in = gain_in.reshape(1, width)
    gain_out = gain_out.reshape(1, width)

    def forward(a):
        return lax.ppermute(a, "row", [(0, 1), (1, 3), (3, 2), (2, 0)])

    def over_row(a, bit):
        return lax.ppermute(a, "row", [(k, k ^ bit) for k in range(4)])

    def over_x(a):
        return lax.ppermute(a, "col", [(k, k ^ 2) for k in range(4)])

    def over_core(a):
        return lax.ppermute(a, "col", [(k, k ^ 1) for k in range(4)])

    def plus(a, b):
        return (a.astype(F32) + b.astype(F32)).astype(BF16)

    def in_hbm(*arrays):
        return [pltpu.with_memory_space_constraint(a, pltpu.HBM) for a in arrays]

    def right(s):
        return right_part(s, *in_hbm(pair_tiles, gain_in, w_proj, tokens, exponents))

    a0, b0 = right(0), right(1)
    left = left_part(*in_hbm(pair_tiles, gain_in, w_proj, tokens))
    a1, b1 = forward(a0), forward(b0)
    a2, b2 = forward(a1), forward(after(b1, left))
    c0, d0 = right(2), right(3)
    a3, b3 = forward(after(a2, c0)), forward(after(b2, d0))
    c1, d1 = forward(after(c0, b2)), forward(after(d0, a3))

    def triangle(slots):
        keep, near, send, panel = tri_part(0, slots, left)
        got = over_core(send)
        return keep, got, plus(near, got[1]), panel

    g_out = g_gate = jnp.zeros((width, width), F32)

    def middle(s, tri, mine):
        return mid_part(
            s, (tri[0], tri[1], mine), pair_tiles, grad_out, gain_in, gain_out, w_gate, w_out, g_out, g_gate
        )

    def spread(d_tri):
        far = over_x(d_tri)
        return [d_tri, far, over_core(d_tri), over_core(far)]

    def dright(blocks, *others):
        return dright_part([blocks[0], blocks[1], blocks[2], after(blocks[3], *others)], left)

    tri_a, tri_b = triangle([a0, a1, a2, a3]), triangle([b0, b1, b2, after(b3, c1)])
    x_a, x_b = over_x(tri_a[2]), over_x(after(tri_b[2], d1))
    c2, d2 = forward(after(c1, tri_a[2])), forward(after(d1, tri_b[2]))
    dtri_a, gate_a, g_out, g_gate = middle(0, tri_a, after(x_a, d1))
    blocks_a = spread(dtri_a)
    dtri_b, gate_b, g_out, g_gate = middle(1, tri_b, after(x_b, c2))
    blocks_b = spread(dtri_b)
    c3, d3 = forward(after(c2, dtri_a)), forward(after(d2, dtri_b))
    part_a = dright(blocks_a, d2)
    part_b = dright(blocks_b, c3)
    r_a, r_b = forward(part_a[1]), forward(part_b[1])

    tri_c = triangle([c0, c1, c2, after(c3, part_a[1])])
    tri_d = triangle([d0, d1, d2, after(d3, part_b[1], tri_c[2])])
    x_c, x_d = over_x(tri_c[2]), over_x(tri_d[2])
    r_a = plus(r_a, part_a[2])
    r_a2 = forward(after(r_a, tri_c[2]))
    r_b = plus(r_b, part_b[2])
    r_b2 = forward(after(r_b, tri_d[2]))
    d_left = dleft_part(
        [after(blocks_a[0], tri_d[2])] + blocks_a[1:] + blocks_b,
        [tri_a[3], tri_b[3]],
        jnp.zeros((HALF, HALF, WIDTH), F32),
    )
    dtri_c, gate_c, g_out, g_gate = middle(2, tri_c, after(x_c, r_a, d_left))
    blocks_c = spread(dtri_c)
    dtri_d, gate_d, g_out, g_gate = middle(3, tri_d, after(x_d, r_b))
    blocks_d = spread(dtri_d)
    r_a2 = plus(r_a2, part_a[3])
    r_a3 = forward(after(r_a2, dtri_c))
    r_b2 = plus(r_b2, part_b[3])
    r_b3 = forward(after(r_b2, dtri_d))
    part_c = dright(blocks_c, r_a2)
    part_d = dright(blocks_d, r_b2)

    r_c, r_d = forward(part_c[1]), forward(part_d[1])
    r_c = plus(r_c, part_c[2])
    d_left = dleft_part(
        [after(blocks_c[0], part_d[1], r_c)] + blocks_c[1:] + blocks_d, [tri_c[3], tri_d[3]], d_left
    )
    r_c = forward(r_c)
    r_d = plus(r_d, part_d[2])
    partial, g_a = final_a_part(
        pair_tiles, after(d_left, r_d), tokens, gain_in, w_proj, w_gate, [gate_a, gate_b, gate_c, gate_d]
    )
    r_d = forward(r_d)
    zero = jnp.zeros((width, 2 * width), F32)

    def final(s, sums, so_far, into):
        return final_b_part(
            s, pair_tiles, partial, sums, tokens, exponents, gain_in, w_proj, so_far, into
        )

    r_c = plus(r_c, part_c[3])
    d_pair, g_first = final(0, (part_a[0], after(r_a3, r_c)), zero, gain_in)
    r_c = forward(r_c)
    r_d = plus(r_d, part_d[3])
    d_pair, g_first = final(1, (part_b[0], after(r_b3, r_d)), g_first, d_pair)
    r_d = forward(r_d)

    def halved(a):
        half = a.shape[0] // 2
        a = lax.dynamic_slice_in_dim(a, core * half, half) + over_core(
            lax.dynamic_slice_in_dim(a, (1 - core) * half, half)
        )
        return a + over_x(a)

    early = halved(jnp.concatenate([g_out, g_gate, g_a, g_first], axis=1))
    d_pair, g_last = final(2, (part_c[0], after(r_c, early)), zero, d_pair)
    d_pair, g_last = final(3, (part_d[0], r_d), g_last, d_pair)
    late = halved(g_last)
    sums = jnp.concatenate([early[:, : 4 * width], early[:, 4 * width :] + late], axis=1)
    for bit in (1, 2):
        mine = sums.astype(BF16)
        sums = mine.astype(F32) + over_row(mine, bit).astype(F32)
    sums = sums / crop_len
    theirs = over_core(sums)
    sums = jnp.concatenate(
        [jnp.where(core == 0, sums, theirs), jnp.where(core == 0, theirs, sums)], axis=0
    )
    return d_pair, sums[:, 2 * width :], sums[:, width : 2 * width], sums[:, :width]


def local(pair_tiles, *rest, rows_over, cols_over):
    if pair_tiles.shape == (HALF, HALF, WIDTH) and rows_over == cols_over == 4:
        return blocked(pair_tiles, *rest)
    return plain(pair_tiles, *rest)


def solution(mesh):
    return jax.shard_map(
        functools.partial(local, rows_over=mesh.shape["row"], cols_over=mesh.shape["col"]),
        mesh=mesh,
        in_specs=(
            P(("crop", "row"), "col", None),
            P(("crop", "row"), "col", None),
            P(("crop", "row"), "col"),
            P("crop"),
            P(),
            P(),
            P(),
            P(),
            P(),
        ),
        out_specs=(
            P(("crop", "row"), "col", None),
            P("crop", None),
            P("crop", None),
            P("crop", None),
        ),
        check_vma=False,
    )
```

```python
import functools

import jax
import jax.numpy as jnp
from jax import lax
from jax.experimental import pallas as pl
from jax.experimental.pallas import tpu as pltpu
from jax.sharding import PartitionSpec as P

EPS = 1e-05


def layer_norm(values, gain):
    center = jnp.mean(values, axis=-1, keepdims=True)
    spread = jnp.mean((values - center) ** 2, axis=-1, keepdims=True)
    inverse = lax.rsqrt(spread + EPS)
    centred = (values - center) * inverse
    return (centred * gain, centred, inverse)


def norm_back(upstream, centred, inverse, gain):
    scaled = upstream * gain
    first = jnp.mean(scaled, axis=-1, keepdims=True)
    second = jnp.mean(scaled * centred, axis=-1, keepdims=True)
    return inverse * (scaled - first - centred * second)


def plain(pair_tiles, grad_out, exponents, token_mask, gain_in, w_proj, w_gate, gain_out, w_out):
    f32 = jnp.float32
    bf16 = jnp.bfloat16
    rows, cols, width = pair_tiles.shape
    crop_len = token_mask.shape[0]
    row_at = lax.axis_index("row")
    col_at = lax.axis_index("col")
    maskf = token_mask.astype(f32)
    mask_rows = lax.dynamic_slice_in_dim(maskf, row_at * rows, rows)
    mask_cols = lax.dynamic_slice_in_dim(maskf, col_at * cols, cols)
    pair_mask = (mask_rows[:, None] * mask_cols[None, :])[..., None]
    normed_f, centred, inverse = layer_norm(pair_tiles.astype(f32), gain_in)
    normed = normed_f.astype(bf16)
    flat = normed.reshape(-1, width)
    projected = jnp.dot(flat, w_proj, preferred_element_type=f32).reshape(rows, cols, 4 * width)
    gate_a = projected[..., :width]
    value_a = projected[..., width : 2 * width]
    gate_b = projected[..., 2 * width : 3 * width]
    value_b = projected[..., 3 * width :]
    sig_a = jax.nn.sigmoid(gate_a)
    sig_b = jax.nn.sigmoid(gate_b)
    left = (pair_mask * sig_a * value_a).astype(bf16)
    right_raw = pair_mask * sig_b * value_b
    bound = (448.0 * jnp.exp2(exponents.astype(f32)))[..., None]
    right = jnp.clip(right_raw, -bound, bound).astype(bf16)
    inside = (jnp.abs(right_raw) <= bound).astype(f32)
    panel = lax.all_gather(right, "row", axis=0, tiled=True)
    tri_cols = lax.psum_scatter(
        jnp.einsum("jkc,ikc->jic", panel, left, preferred_element_type=f32).astype(jnp.bfloat16),
        "col",
        scatter_dimension=0,
        tiled=True,
    ).astype(jnp.float32)
    tri = jnp.transpose(tri_cols, (1, 0, 2))
    tnorm_f, tcentred, tinverse = layer_norm(tri, gain_out)
    tnorm = tnorm_f.astype(bf16)
    tflat = tnorm.reshape(-1, width)
    opened = jax.nn.sigmoid(jnp.dot(flat, w_gate, preferred_element_type=f32)).reshape(
        rows, cols, width
    )
    outproj = jnp.dot(tflat, w_out, preferred_element_type=f32).reshape(rows, cols, width)
    upstream = grad_out.astype(f32)
    d_open = upstream * outproj
    d_outproj = (upstream * opened).astype(bf16).reshape(-1, width)
    g_out = jnp.dot(tflat.T, d_outproj, preferred_element_type=f32)
    d_tnorm = jnp.dot(d_outproj, w_out.T, preferred_element_type=f32).reshape(rows, cols, width)
    d_tri = norm_back(d_tnorm, tcentred, tinverse, gain_out).astype(bf16)
    d_gatepre = (d_open * opened * (1.0 - opened)).astype(bf16).reshape(-1, width)
    g_gate = jnp.dot(flat.T, d_gatepre, preferred_element_type=f32)
    grad_full = lax.all_gather(d_tri, "col", axis=1, tiled=True)
    d_left = jnp.einsum("ijc,jkc->ikc", grad_full, panel, preferred_element_type=f32)
    d_right = (
        lax.psum_scatter(
            jnp.einsum("ijc,ikc->jkc", grad_full, left, preferred_element_type=f32).astype(
                jnp.bfloat16
            ),
            "row",
            scatter_dimension=0,
            tiled=True,
        ).astype(jnp.float32)
        * inside
    )
    d_gate_a = d_left * pair_mask * value_a * sig_a * (1.0 - sig_a)
    d_value_a = d_left * pair_mask * sig_a
    d_gate_b = d_right * pair_mask * value_b * sig_b * (1.0 - sig_b)
    d_value_b = d_right * pair_mask * sig_b
    d_proj = (
        jnp.concatenate([d_gate_a, d_value_a, d_gate_b, d_value_b], axis=-1)
        .astype(bf16)
        .reshape(-1, 4 * width)
    )
    g_proj = jnp.dot(flat.T, d_proj, preferred_element_type=f32)
    d_normed = jnp.dot(d_proj, w_proj.T, preferred_element_type=f32) + jnp.dot(
        d_gatepre, w_gate.T, preferred_element_type=f32
    )
    d_pair = norm_back(d_normed.reshape(rows, cols, width), centred, inverse, gain_in).astype(bf16)
    sum_proj, sum_gate, sum_out = lax.psum((g_proj, g_gate, g_out), ("row", "col"))
    return (d_pair, sum_proj / crop_len, sum_gate / crop_len, sum_out / crop_len)


SUB = 16
PART = 16
HALF = 64
WIDTH = 128
LANES = SUB * HALF
GROUP = 16
NT = (((1,), (1,)), ((), ()))
NN = (((1,), (0,)), ((), ()))
TN = (((0,), (0,)), ((), ()))
F32 = jnp.float32
BF16 = jnp.bfloat16


def mm(a, b, dims):
    return lax.dot_general(a, b, dims, preferred_element_type=F32)


def params():
    return pltpu.CompilerParams(vmem_limit_bytes=16 * 1024 * 1024)


def cost(flops, size, exps=0):
    return pl.CostEstimate(flops=flops // 1024, bytes_accessed=size // 1024, transcendentals=exps // 1024)


def first_half(rows):
    return lax.broadcasted_iota(jnp.int32, (rows, WIDTH), 1) < HALF


def swap_halves(a, b):
    first = first_half(HALF)
    return (
        jnp.where(first, a, pltpu.roll(b, HALF, 1)),
        jnp.where(first, pltpu.roll(a, HALF, 1), b),
    )


def eye():
    row = lax.broadcasted_iota(jnp.int32, (WIDTH, WIDTH), 0)
    lane = lax.broadcasted_iota(jnp.int32, (WIDTH, WIDTH), 1)
    return (row == lane).astype(F32).astype(BF16)


def to_channels(cells):
    return mm(eye(), cells, NT)


def to_cells(channels):
    return mm(channels, eye(), TN)


def stage_rows(channels, buf):
    for t in range(SUB // 2):
        part = channels[:, t * WIDTH : (t + 1) * WIDTH]
        one, two = swap_halves(part[:HALF], part[HALF:])
        buf[(2 * t) * HALF : (2 * t + 1) * HALF, :] = one
        buf[(2 * t + 1) * HALF : (2 * t + 2) * HALF, :] = two


def panel_row(buf, p):
    return buf[pl.ds(p, SUB, stride=HALF), :]


def channels_of(panels, buf, out):
    buf[...] = panels.reshape(LANES, WIDTH)
    for t in range(SUB // 2):
        one = buf[pl.ds(2 * t, HALF, stride=SUB), :]
        two = buf[pl.ds(2 * t + 1, HALF, stride=SUB), :]
        low, high = swap_halves(one, two)
        out[:HALF, t * WIDTH : (t + 1) * WIDTH] = low
        out[HALF:, t * WIDTH : (t + 1) * WIDTH] = high
    return out[...]


def norm_channels(values, gain):
    center = jnp.mean(values, axis=0, keepdims=True)
    spread = jnp.mean((values - center) ** 2, axis=0, keepdims=True)
    inverse = lax.rsqrt(spread + EPS)
    centred = (values - center) * inverse
    return centred * gain, centred, inverse


def norm_back_channels(upstream, centred, inverse, gain):
    scaled = upstream * gain
    first = jnp.mean(scaled, axis=0, keepdims=True)
    second = jnp.mean(scaled * centred, axis=0, keepdims=True)
    return inverse * (scaled - first - centred * second)


def column(row):
    at = lax.broadcasted_iota(jnp.int32, (WIDTH, WIDTH), 0)
    lane = lax.broadcasted_iota(jnp.int32, (WIDTH, WIDTH), 1)
    return jnp.sum(jnp.where(at == lane, row, 0.0), axis=1, keepdims=True)


def mask_lanes(token_ref, s):
    valid = jnp.sum(token_ref[...].astype(F32), axis=1, keepdims=True)
    lane = lax.broadcasted_iota(jnp.int32, (1, LANES), 1)
    row = lane // HALF + (lax.axis_index("row") * HALF + s * SUB)
    col = lane % HALF + lax.axis_index("col") * HALF
    return (jnp.maximum(row, col).astype(F32) < valid).astype(F32)


def bound_lanes(exponent_ref):
    bound = 448.0 * jnp.exp2(exponent_ref[...].astype(F32))
    return jnp.concatenate([bound[i : i + 1] for i in range(SUB)], axis=1)


def normed_cells(x_ref, gain_ref):
    gain = column(gain_ref[...])
    normed, centred, inverse = norm_channels(to_channels(x_ref[...].reshape(LANES, WIDTH)), gain)
    return normed.astype(BF16), centred, inverse, gain


def right_kernel(at, x_ref, gain_ref, w_ref, token_ref, exponent_ref, out_ref, buf):
    normed = normed_cells(x_ref, gain_ref)[0]
    proj = mm(w_ref[...], normed, TN)
    raw = mask_lanes(token_ref, at + pl.program_id(0)) * jax.nn.sigmoid(proj[:WIDTH]) * proj[WIDTH:]
    bound = bound_lanes(exponent_ref)
    stage_rows(jnp.clip(raw, -bound, bound), buf)
    for p in range(HALF):
        out_ref[p] = panel_row(buf, p).astype(BF16)


def left_kernel(x_ref, gain_ref, w_ref, token_ref, out_ref, buf):
    normed = normed_cells(x_ref, gain_ref)[0]
    proj = mm(w_ref[...], normed, TN)
    mask = mask_lanes(token_ref, pl.program_id(0))
    stage_rows(mask * jax.nn.sigmoid(proj[:WIDTH]) * proj[WIDTH:], buf)
    first = first_half(SUB)
    for p in range(HALF):
        row = panel_row(buf, p)
        out_ref[p, 0] = jnp.where(first, row, 0.0).astype(BF16)
        out_ref[p, 1] = jnp.where(first, 0.0, row).astype(BF16)


def tri_kernel(s0, s1, s2, s3, left_ref, keep_ref, near_ref, send_ref, panel_ref):
    z, q = lax.axis_index("row"), lax.axis_index("col")
    for m, ref in enumerate((s0, s1, s2, s3)):
        place = ((z ^ (z >> 1)) - m + 4) & 3
        other = place ^ (place >> 1) ^ q
        panel_ref[(other & 1) * 2 + (other >> 1)] = ref[...]
    for p in range(GROUP):
        right = jnp.concatenate([panel_ref[r, p] for r in range(4)], axis=0)
        tri = mm(right, left_ref[p].reshape(WIDTH, WIDTH), NT).astype(BF16)
        keep_ref[p] = tri[:SUB]
        near_ref[p] = tri[SUB : 2 * SUB]
        send_ref[0, p] = tri[2 * SUB : 3 * SUB]
        send_ref[1, p] = tri[3 * SUB :]


def mid_kernel(
    a_ref, b_ref, c_ref, x_ref, grad_ref, gain_in_ref, gain_out_ref, gate_ref, out_w_ref,
    g_out_so_far, g_gate_so_far, dtri_ref, dgate_ref, g_out_ref, g_gate_ref, buf, wide,
):
    gain_out = column(gain_out_ref[...])
    tri = channels_of(
        a_ref[...].astype(F32) + b_ref[0].astype(F32) + c_ref[...].astype(F32), buf, wide
    )
    tnorm_f, tcentred, tinverse = norm_channels(tri, gain_out)
    tnorm = tnorm_f.astype(BF16)

    def turned(ref):
        buf[...] = ref[...].astype(F32).reshape(LANES, WIDTH)
        rows = [buf[pl.ds(j, HALF, stride=SUB), :] for j in range(SUB)]
        return to_channels(jnp.concatenate(rows, axis=0).astype(BF16))

    normed = norm_channels(turned(x_ref), column(gain_in_ref[...]))[0].astype(BF16)
    upstream = turned(grad_ref)
    opened = jax.nn.sigmoid(mm(gate_ref[...], normed, TN))
    outproj = mm(out_w_ref[...], tnorm, TN)
    d_open = upstream * outproj
    d_outproj = (upstream * opened).astype(BF16)
    g_out_ref[...] = g_out_so_far[...] + mm(tnorm, d_outproj, NT)
    d_tnorm = mm(out_w_ref[...], d_outproj, NN)
    d_tri = norm_back_channels(d_tnorm, tcentred, tinverse, gain_out)
    d_gatepre = (d_open * opened * (1.0 - opened)).astype(BF16)
    g_gate_ref[...] = g_gate_so_far[...] + mm(normed, d_gatepre, NT)
    stage_rows(d_tri, buf)
    for p in range(HALF):
        dtri_ref[p] = panel_row(buf, p).astype(BF16)
    buf[...] = to_cells(d_gatepre)
    for i in range(HALF):
        dgate_ref[i] = panel_row(buf, i).astype(BF16)


def dright_kernel(*refs):
    *grads_refs, left_ref, p0, p1, p2, p3, held = refs
    z, q = lax.axis_index("row"), lax.axis_index("col")
    for k, ref in enumerate(grads_refs):
        r = k % 4
        block_at = q ^ ((r % 2) * 2 + r // 2)
        slot = ((z ^ (z >> 1)) - (block_at ^ (block_at >> 1)) + 4) & 3
        held[slot, :, (k // 4) * SUB : (k // 4 + 1) * SUB] = ref[...]
    for p in range(GROUP):
        grads = jnp.concatenate([held[m, p] for m in range(4)], axis=0)
        part = mm(grads, left_ref[p].reshape(WIDTH, WIDTH), NN).astype(BF16)
        for m, ref in enumerate((p0, p1, p2, p3)):
            ref[p] = part[m * PART : (m + 1) * PART]


def dleft_kernel(*refs):
    so_far, out_ref = refs[-2:]
    parts = (len(refs) - 2) // 5
    grad_refs, panel_refs = refs[: 4 * parts], refs[4 * parts : 5 * parts]
    first = first_half(HALF)
    for p in range(GROUP):
        grads = jnp.concatenate([d[p] for d in grad_refs], axis=0)
        right = jnp.concatenate([r[q, p] for r in panel_refs for q in range(4)], axis=0)
        both = mm(grads, right, TN)
        out_ref[p] = so_far[p] + jnp.where(first, both[:HALF], both[HALF:])


def gate_grads(upstream, mask, sig, value):
    d_gate = (upstream * mask * value * sig * (1.0 - sig)).astype(BF16)
    d_value = (upstream * mask * sig).astype(BF16)
    return jnp.concatenate([d_gate, d_value], axis=0)


def final_a_kernel(
    x_ref, dleft_ref, token_ref, gain_ref, w_ref, gate_ref, q0, q1, q2, q3, out_ref, g_ref, buf, wide
):
    s = pl.program_id(0)
    normed = normed_cells(x_ref, gain_ref)[0]
    proj = mm(w_ref[...], normed, TN)
    d_left = channels_of(dleft_ref[...], buf, wide)
    d_proj = gate_grads(d_left, mask_lanes(token_ref, s), jax.nn.sigmoid(proj[:WIDTH]), proj[WIDTH:])
    d_gate = jnp.concatenate([q[...] for q in (q0, q1, q2, q3)], axis=1).reshape(LANES, WIDTH)
    out_ref[...] = mm(w_ref[...], d_proj, NN) + mm(gate_ref[...], d_gate, NT)

    @pl.when(s == 0)
    def start():
        g_ref[...] = jnp.zeros_like(g_ref)

    g_ref[...] += mm(normed, d_proj, NT)


def final_b_kernel(
    at, x_ref, part_ref, a_ref, b_ref, token_ref, exponent_ref, gain_ref, w_ref, so_far, into_ref,
    out_ref, g_ref, buf, wide,
):
    step = pl.program_id(0)
    normed, centred, inverse, gain = normed_cells(x_ref, gain_ref)
    proj = mm(w_ref[...], normed, TN)
    mask = mask_lanes(token_ref, at + step)
    sig = jax.nn.sigmoid(proj[:WIDTH])
    inside = jnp.abs(mask * sig * proj[WIDTH:]) <= bound_lanes(exponent_ref)
    d_right = channels_of(a_ref[...].astype(F32) + b_ref[...].astype(F32), buf, wide)
    d_proj = gate_grads(jnp.where(inside, d_right, 0.0), mask, sig, proj[WIDTH:])

    @pl.when(step == 0)
    def start():
        g_ref[...] = so_far[...]

    g_ref[...] += mm(normed, d_proj, NT)
    d_normed = part_ref[...] + mm(w_ref[...], d_proj, NN)
    d_pair = norm_back_channels(d_normed, centred, inverse, gain).astype(BF16)
    out_ref[...] = to_cells(d_pair).astype(BF16).reshape(SUB, HALF, WIDTH)


def whole(array):
    return pl.BlockSpec(array.shape, lambda i: (0,) * array.ndim)


def block(shape, at):
    return pl.BlockSpec(shape, lambda i: at)


BUF = pltpu.VMEM((LANES, WIDTH), F32)
WIDE = pltpu.VMEM((WIDTH, LANES), F32)
PANEL = jax.ShapeDtypeStruct((HALF, SUB, WIDTH), BF16)
PANEL_SPEC = pl.BlockSpec((GROUP, SUB, WIDTH), lambda i: (i, 0, 0))
FOUR = jax.ShapeDtypeStruct((4, HALF, SUB, WIDTH), BF16)
FOUR_SPEC = pl.BlockSpec((4, GROUP, SUB, WIDTH), lambda i: (0, i, 0, 0))
TWO = jax.ShapeDtypeStruct((2, HALF, SUB, WIDTH), BF16)
TWO_SPEC = pl.BlockSpec((2, GROUP, SUB, WIDTH), lambda i: (0, i, 0, 0))
LEFT_SPEC = pl.BlockSpec((GROUP, 2, HALF, WIDTH), lambda i: (i, 0, 0, 0))
LONG = jax.ShapeDtypeStruct((HALF, PART, WIDTH), BF16)
LONG_SPEC = pl.BlockSpec((GROUP, PART, WIDTH), lambda i: (i, 0, 0))
WHOLE_PANEL = pl.BlockSpec(PANEL.shape, lambda i: (0, 0, 0))


def right_part(s, pair, gain, w_proj, tokens, exponents):
    steps = PART // SUB
    return pl.pallas_call(
        functools.partial(right_kernel, s * steps),
        grid=(steps,),
        out_shape=LONG,
        in_specs=[
            pl.BlockSpec((SUB, HALF, WIDTH), lambda i: (s * steps + i, 0, 0)),
            whole(gain), block((WIDTH, 2 * WIDTH), (0, 1)), whole(tokens),
            pl.BlockSpec((SUB, HALF), lambda i: (s * steps + i, 0)),
        ],
        out_specs=pl.BlockSpec((HALF, SUB, WIDTH), lambda i: (0, i, 0)),
        scratch_shapes=[BUF],
        compiler_params=params(),
        cost_estimate=cost(8 * LANES * WIDTH * WIDTH, 1 << 20, 2 * LANES * WIDTH),
        name="right_part",
    )(pair, gain, w_proj, tokens, exponents)


def left_part(pair, gain, w_proj, tokens):
    return pl.pallas_call(
        left_kernel,
        grid=(HALF // SUB,),
        out_shape=jax.ShapeDtypeStruct((HALF, 2, HALF, WIDTH), BF16),
        in_specs=[
            pl.BlockSpec((SUB, HALF, WIDTH), lambda i: (i, 0, 0)), whole(gain),
            block((WIDTH, 2 * WIDTH), (0, 0)), whole(tokens),
        ],
        out_specs=pl.BlockSpec((HALF, 2, SUB, WIDTH), lambda i: (0, 0, i, 0)),
        scratch_shapes=[BUF],
        compiler_params=params(),
        cost_estimate=cost(16 * LANES * WIDTH * WIDTH, 3 << 20, 4 * LANES * WIDTH),
        name="left_part",
    )(pair, gain, w_proj, tokens)


def tri_part(at, slots, left):
    return pl.pallas_call(
        tri_kernel,
        grid=(HALF // GROUP,),
        out_shape=(PANEL, PANEL, TWO, FOUR),
        in_specs=[pl.BlockSpec((GROUP, SUB, WIDTH), lambda i: (i, at, 0))] * 4 + [LEFT_SPEC],
        out_specs=(PANEL_SPEC, PANEL_SPEC, TWO_SPEC, FOUR_SPEC),
        compiler_params=params(),
        cost_estimate=cost(2 * HALF * HALF * WIDTH * WIDTH, 5 << 20),
        name="tri_part",
    )(*slots, left)


def mid_part(s, parts, pair, grad, gain_in, gain_out, w_gate, w_out, g_out, g_gate):
    square = jax.ShapeDtypeStruct((WIDTH, WIDTH), F32)
    columns = block((HALF, SUB, WIDTH), (0, s, 0))
    small = [gain_in, gain_out, w_gate, w_out, g_out, g_gate]
    return pl.pallas_call(
        mid_kernel,
        grid=(1,),
        out_shape=(PANEL, pltpu.HBM(PANEL.shape, BF16), square, square),
        in_specs=[WHOLE_PANEL, block((1, HALF, SUB, WIDTH), (0, 0, 0, 0)), WHOLE_PANEL]
        + [columns] * 2
        + [whole(a) for a in small],
        out_specs=(WHOLE_PANEL, WHOLE_PANEL, block(square.shape, (0, 0)), block(square.shape, (0, 0))),
        scratch_shapes=[BUF, WIDE],
        compiler_params=params(),
        cost_estimate=cost(12 * LANES * WIDTH * WIDTH, 2 << 20, LANES * WIDTH),
        name="mid_part",
    )(*parts, pair, grad, *small)


def dright_part(blocks, left):
    return pl.pallas_call(
        dright_kernel,
        grid=(HALF // GROUP,),
        out_shape=(pltpu.HBM(LONG.shape, BF16), LONG, LONG, LONG),
        in_specs=[PANEL_SPEC] * len(blocks) + [LEFT_SPEC],
        out_specs=(LONG_SPEC,) * 4,
        scratch_shapes=[pltpu.VMEM((4, GROUP, PART, WIDTH), BF16)],
        compiler_params=params(),
        cost_estimate=cost(4 * HALF * HALF * WIDTH * WIDTH, 6 << 20),
        name="dright_part",
    )(*blocks, left)


def dleft_part(grads, panels, so_far):
    rows = pl.BlockSpec((GROUP, HALF, WIDTH), lambda i: (i, 0, 0))
    return pl.pallas_call(
        dleft_kernel,
        grid=(HALF // GROUP,),
        out_shape=jax.ShapeDtypeStruct((HALF, HALF, WIDTH), F32),
        in_specs=[PANEL_SPEC] * len(grads) + [FOUR_SPEC] * len(panels) + [rows],
        out_specs=rows,
        compiler_params=params(),
        cost_estimate=cost(4 * HALF * HALF * WIDTH * WIDTH, 8 << 20),
        name="dleft_part",
    )(*grads, *panels, so_far)


def final_a_part(pair, dleft, tokens, gain, w_proj, w_gate, gates):
    return pl.pallas_call(
        final_a_kernel,
        grid=(HALF // SUB,),
        out_shape=(
            jax.ShapeDtypeStruct((WIDTH, HALF * HALF), F32),
            jax.ShapeDtypeStruct((WIDTH, 2 * WIDTH), F32),
        ),
        in_specs=[
            pl.BlockSpec((SUB, HALF, WIDTH), lambda i: (i, 0, 0)),
            pl.BlockSpec((HALF, SUB, WIDTH), lambda i: (0, i, 0)),
            whole(tokens), whole(gain), block((WIDTH, 2 * WIDTH), (0, 0)), whole(w_gate),
        ]
        + [pl.BlockSpec((SUB, SUB, WIDTH), lambda i: (i, 0, 0))] * 4,
        out_specs=(
            pl.BlockSpec((WIDTH, LANES), lambda i: (0, i)),
            block((WIDTH, 2 * WIDTH), (0, 0)),
        ),
        scratch_shapes=[BUF, WIDE],
        compiler_params=params(),
        cost_estimate=cost(56 * LANES * WIDTH * WIDTH, 8 << 20, 4 * LANES * WIDTH),
        name="final_a_part",
    )(pair, dleft, tokens, gain, w_proj, w_gate, *gates)


def final_b_part(s, pair, part, sums, tokens, exponents, gain, w_proj, so_far, into):
    steps = PART // SUB
    rows = pl.BlockSpec((SUB, HALF, WIDTH), lambda i: (s * steps + i, 0, 0))
    panel = pl.BlockSpec((HALF, SUB, WIDTH), lambda i: (0, i, 0))
    return pl.pallas_call(
        functools.partial(final_b_kernel, s * steps),
        grid=(steps,),
        out_shape=(
            jax.ShapeDtypeStruct((HALF, HALF, WIDTH), BF16),
            jax.ShapeDtypeStruct((WIDTH, 2 * WIDTH), F32),
        ),
        in_specs=[
            rows,
            pl.BlockSpec((WIDTH, LANES), lambda i: (0, s * steps + i)),
            panel, panel, whole(tokens),
            pl.BlockSpec((SUB, HALF), lambda i: (s * steps + i, 0)),
            whole(gain), block((WIDTH, 2 * WIDTH), (0, 1)), whole(so_far),
            pl.BlockSpec(memory_space=pl.ANY),
        ],
        out_specs=(rows, block((WIDTH, 2 * WIDTH), (0, 0))),
        scratch_shapes=[BUF, WIDE],
        input_output_aliases={9: 0} if into.shape == pair.shape else {},
        compiler_params=params(),
        cost_estimate=cost(28 * LANES * WIDTH * WIDTH, 4 << 20, 2 * LANES * WIDTH),
        name="final_b_part",
    )(pair, part, *sums, tokens, exponents, gain, w_proj, so_far, into)


def after(array, *others):
    return lax.optimization_barrier((array, *others))[0]


def blocked(pair_tiles, grad_out, exponents, token_mask, gain_in, w_proj, w_gate, gain_out, w_out):
    width = pair_tiles.shape[-1]
    crop_len = token_mask.shape[0]
    core = lax.axis_index("col") % 2
    tokens = token_mask.reshape(1, crop_len)
    gain_in = gain_in.reshape(1, width)
    gain_out = gain_out.reshape(1, width)

    def forward(a):
        return lax.ppermute(a, "row", [(0, 1), (1, 3), (3, 2), (2, 0)])

    def over_row(a, bit):
        return lax.ppermute(a, "row", [(k, k ^ bit) for k in range(4)])

    def over_x(a):
        return lax.ppermute(a, "col", [(k, k ^ 2) for k in range(4)])

    def over_core(a):
        return lax.ppermute(a, "col", [(k, k ^ 1) for k in range(4)])

    def plus(a, b):
        return (a.astype(F32) + b.astype(F32)).astype(BF16)

    def in_hbm(*arrays):
        return [pltpu.with_memory_space_constraint(a, pltpu.HBM) for a in arrays]

    def right(s):
        return right_part(s, *in_hbm(pair_tiles, gain_in, w_proj, tokens, exponents))

    a0, b0 = right(0), right(1)
    left = left_part(*in_hbm(pair_tiles, gain_in, w_proj, tokens))
    a1, b1 = forward(a0), forward(b0)
    a2, b2 = forward(a1), forward(after(b1, left))
    c0, d0 = right(2), right(3)
    a3, b3 = forward(after(a2, b1, c0)), forward(after(b2, d0))
    c1, d1 = forward(after(c0, b2)), forward(after(d0, a3))

    def triangle(slots):
        keep, near, send, panel = tri_part(0, slots, left)
        got = over_core(send)
        return keep, got, plus(near, got[1]), panel

    g_out = g_gate = jnp.zeros((width, width), F32)

    def middle(s, tri, mine):
        return mid_part(
            s, (tri[0], tri[1], mine), pair_tiles, grad_out, gain_in, gain_out, w_gate, w_out, g_out, g_gate
        )

    def spread(d_tri):
        far = over_x(d_tri)
        return [d_tri, far, over_core(d_tri), over_core(far)]

    def dright(blocks, *others):
        return dright_part([blocks[0], blocks[1], blocks[2], after(blocks[3], *others)], left)

    tri_a, tri_b = triangle([a0, a1, a2, after(a3, b3)]), triangle([b0, b1, b2, b3])
    x_a, x_b = over_x(after(tri_a[2], c1)), over_x(tri_b[2])
    c2, d2 = forward(after(c1, tri_a[2])), forward(after(d1, tri_b[2]))
    dtri_a, gate_a, g_out, g_gate = middle(0, tri_a, after(x_a, d1))
    blocks_a = spread(dtri_a)
    dtri_b, gate_b, g_out, g_gate = middle(1, tri_b, after(x_b, c2))
    blocks_b = spread(dtri_b)
    c3, d3 = forward(after(c2, dtri_a)), forward(after(d2, dtri_b))
    part_a = dright(blocks_a, d2)
    part_b = dright(blocks_b, c3)
    r_a, r_b = forward(part_a[1]), forward(part_b[1])

    tri_c = triangle([c0, c1, c2, after(c3, part_a[1])])
    r_a = plus(r_a, part_a[2])
    tri_d = triangle([d0, d1, d2, after(d3, part_b[1], r_a, tri_c[2])])
    x_c, x_d = over_x(tri_c[2]), over_x(tri_d[2])
    r_a = plus(forward(r_a), part_a[3])
    r_b = plus(r_b, part_b[2])
    d_left = dleft_part(
        [after(blocks_a[0], tri_d[2], r_b)] + blocks_a[1:] + blocks_b,
        [tri_a[3], tri_b[3]],
        jnp.zeros((HALF, HALF, WIDTH), F32),
    )
    r_b = plus(forward(r_b), part_b[3])
    dtri_c, gate_c, g_out, g_gate = middle(2, tri_c, after(x_c, r_a, d_left))
    blocks_c = spread(dtri_c)
    dtri_d, gate_d, g_out, g_gate = middle(3, tri_d, after(x_d, r_b))
    blocks_d = spread(dtri_d)
    r_a3, r_b3 = forward(r_a), forward(r_b)
    part_c = dright(blocks_c, r_a3)
    part_d = dright(blocks_d, r_b3, part_c[1])

    r_c, r_d = forward(part_c[1]), forward(part_d[1])
    r_c = plus(r_c, part_c[2])
    d_left = dleft_part(
        [after(blocks_c[0], part_d[1], r_c)] + blocks_c[1:] + blocks_d, [tri_c[3], tri_d[3]], d_left
    )
    r_c = forward(r_c)
    r_d = plus(r_d, part_d[2])
    partial, g_a = final_a_part(
        pair_tiles, after(d_left, r_d), tokens, gain_in, w_proj, w_gate, [gate_a, gate_b, gate_c, gate_d]
    )
    r_d = forward(r_d)
    zero = jnp.zeros((width, 2 * width), F32)

    def final(s, sums, so_far, into):
        return final_b_part(
            s, pair_tiles, partial, sums, tokens, exponents, gain_in, w_proj, so_far, into
        )

    r_c = plus(r_c, part_c[3])
    d_pair, g_first = final(0, (part_a[0], after(r_a3, r_c)), zero, gain_in)
    r_c = forward(r_c)
    r_d = plus(r_d, part_d[3])
    d_pair, g_first = final(1, (part_b[0], after(r_b3, r_d)), g_first, d_pair)
    r_d = forward(r_d)

    d_pair, g_last = final(2, (part_c[0], r_c), g_first, d_pair)
    d_pair, g_last = final(3, (part_d[0], r_d), g_last, d_pair)

    sums = jnp.concatenate([g_out, g_gate, g_a, g_last], axis=1)
    half = width // 2
    sums = lax.dynamic_slice_in_dim(sums, core * half, half) + over_core(
        lax.dynamic_slice_in_dim(sums, (1 - core) * half, half)
    )
    for send in (over_x, lambda a: over_row(a, 1), lambda a: over_row(a, 2)):
        mine = sums.astype(BF16)
        sums = mine.astype(F32) + send(mine).astype(F32)
    sums = sums / crop_len
    theirs = over_core(sums)
    sums = jnp.concatenate(
        [jnp.where(core == 0, sums, theirs), jnp.where(core == 0, theirs, sums)], axis=0
    )
    return d_pair, sums[:, 2 * width :], sums[:, width : 2 * width], sums[:, :width]


def local(pair_tiles, *rest, rows_over, cols_over):
    if pair_tiles.shape == (HALF, HALF, WIDTH) and rows_over == cols_over == 4:
        return blocked(pair_tiles, *rest)
    return plain(pair_tiles, *rest)


def solution(mesh):
    return jax.shard_map(
        functools.partial(local, rows_over=mesh.shape["row"], cols_over=mesh.shape["col"]),
        mesh=mesh,
        in_specs=(
            P(("crop", "row"), "col", None),
            P(("crop", "row"), "col", None),
            P(("crop", "row"), "col"),
            P("crop"),
            P(),
            P(),
            P(),
            P(),
            P(),
        ),
        out_specs=(
            P(("crop", "row"), "col", None),
            P("crop", None),
            P("crop", None),
            P("crop", None),
        ),
        check_vma=False,
    )
```

```python
import functools

import jax
import jax.numpy as jnp
from jax import lax
from jax.experimental import pallas as pl
from jax.experimental.pallas import tpu as pltpu
from jax.sharding import PartitionSpec as P

EPS = 1e-05


def layer_norm(values, gain):
    center = jnp.mean(values, axis=-1, keepdims=True)
    spread = jnp.mean((values - center) ** 2, axis=-1, keepdims=True)
    inverse = lax.rsqrt(spread + EPS)
    centred = (values - center) * inverse
    return (centred * gain, centred, inverse)


def norm_back(upstream, centred, inverse, gain):
    scaled = upstream * gain
    first = jnp.mean(scaled, axis=-1, keepdims=True)
    second = jnp.mean(scaled * centred, axis=-1, keepdims=True)
    return inverse * (scaled - first - centred * second)


def plain(pair_tiles, grad_out, exponents, token_mask, gain_in, w_proj, w_gate, gain_out, w_out):
    f32 = jnp.float32
    bf16 = jnp.bfloat16
    rows, cols, width = pair_tiles.shape
    crop_len = token_mask.shape[0]
    row_at = lax.axis_index("row")
    col_at = lax.axis_index("col")
    maskf = token_mask.astype(f32)
    mask_rows = lax.dynamic_slice_in_dim(maskf, row_at * rows, rows)
    mask_cols = lax.dynamic_slice_in_dim(maskf, col_at * cols, cols)
    pair_mask = (mask_rows[:, None] * mask_cols[None, :])[..., None]
    normed_f, centred, inverse = layer_norm(pair_tiles.astype(f32), gain_in)
    normed = normed_f.astype(bf16)
    flat = normed.reshape(-1, width)
    projected = jnp.dot(flat, w_proj, preferred_element_type=f32).reshape(rows, cols, 4 * width)
    gate_a = projected[..., :width]
    value_a = projected[..., width : 2 * width]
    gate_b = projected[..., 2 * width : 3 * width]
    value_b = projected[..., 3 * width :]
    sig_a = jax.nn.sigmoid(gate_a)
    sig_b = jax.nn.sigmoid(gate_b)
    left = (pair_mask * sig_a * value_a).astype(bf16)
    right_raw = pair_mask * sig_b * value_b
    bound = (448.0 * jnp.exp2(exponents.astype(f32)))[..., None]
    right = jnp.clip(right_raw, -bound, bound).astype(bf16)
    inside = (jnp.abs(right_raw) <= bound).astype(f32)
    panel = lax.all_gather(right, "row", axis=0, tiled=True)
    tri_cols = lax.psum_scatter(
        jnp.einsum("jkc,ikc->jic", panel, left, preferred_element_type=f32).astype(jnp.bfloat16),
        "col",
        scatter_dimension=0,
        tiled=True,
    ).astype(jnp.float32)
    tri = jnp.transpose(tri_cols, (1, 0, 2))
    tnorm_f, tcentred, tinverse = layer_norm(tri, gain_out)
    tnorm = tnorm_f.astype(bf16)
    tflat = tnorm.reshape(-1, width)
    opened = jax.nn.sigmoid(jnp.dot(flat, w_gate, preferred_element_type=f32)).reshape(
        rows, cols, width
    )
    outproj = jnp.dot(tflat, w_out, preferred_element_type=f32).reshape(rows, cols, width)
    upstream = grad_out.astype(f32)
    d_open = upstream * outproj
    d_outproj = (upstream * opened).astype(bf16).reshape(-1, width)
    g_out = jnp.dot(tflat.T, d_outproj, preferred_element_type=f32)
    d_tnorm = jnp.dot(d_outproj, w_out.T, preferred_element_type=f32).reshape(rows, cols, width)
    d_tri = norm_back(d_tnorm, tcentred, tinverse, gain_out).astype(bf16)
    d_gatepre = (d_open * opened * (1.0 - opened)).astype(bf16).reshape(-1, width)
    g_gate = jnp.dot(flat.T, d_gatepre, preferred_element_type=f32)
    grad_full = lax.all_gather(d_tri, "col", axis=1, tiled=True)
    d_left = jnp.einsum("ijc,jkc->ikc", grad_full, panel, preferred_element_type=f32)
    d_right = (
        lax.psum_scatter(
            jnp.einsum("ijc,ikc->jkc", grad_full, left, preferred_element_type=f32).astype(
                jnp.bfloat16
            ),
            "row",
            scatter_dimension=0,
            tiled=True,
        ).astype(jnp.float32)
        * inside
    )
    d_gate_a = d_left * pair_mask * value_a * sig_a * (1.0 - sig_a)
    d_value_a = d_left * pair_mask * sig_a
    d_gate_b = d_right * pair_mask * value_b * sig_b * (1.0 - sig_b)
    d_value_b = d_right * pair_mask * sig_b
    d_proj = (
        jnp.concatenate([d_gate_a, d_value_a, d_gate_b, d_value_b], axis=-1)
        .astype(bf16)
        .reshape(-1, 4 * width)
    )
    g_proj = jnp.dot(flat.T, d_proj, preferred_element_type=f32)
    d_normed = jnp.dot(d_proj, w_proj.T, preferred_element_type=f32) + jnp.dot(
        d_gatepre, w_gate.T, preferred_element_type=f32
    )
    d_pair = norm_back(d_normed.reshape(rows, cols, width), centred, inverse, gain_in).astype(bf16)
    sum_proj, sum_gate, sum_out = lax.psum((g_proj, g_gate, g_out), ("row", "col"))
    return (d_pair, sum_proj / crop_len, sum_gate / crop_len, sum_out / crop_len)


SUB = 16
PART = 16
HALF = 64
WIDTH = 128
LANES = SUB * HALF
GROUP = 16
NT = (((1,), (1,)), ((), ()))
NN = (((1,), (0,)), ((), ()))
TN = (((0,), (0,)), ((), ()))
F32 = jnp.float32
BF16 = jnp.bfloat16


def mm(a, b, dims):
    return lax.dot_general(a, b, dims, preferred_element_type=F32)


def params():
    return pltpu.CompilerParams(vmem_limit_bytes=16 * 1024 * 1024)


def cost(flops, size, exps=0):
    return pl.CostEstimate(flops=flops // 1024, bytes_accessed=size // 1024, transcendentals=exps // 1024)


def first_half(rows):
    return lax.broadcasted_iota(jnp.int32, (rows, WIDTH), 1) < HALF


def swap_halves(a, b):
    first = first_half(HALF)
    return (
        jnp.where(first, a, pltpu.roll(b, HALF, 1)),
        jnp.where(first, pltpu.roll(a, HALF, 1), b),
    )


def eye():
    row = lax.broadcasted_iota(jnp.int32, (WIDTH, WIDTH), 0)
    lane = lax.broadcasted_iota(jnp.int32, (WIDTH, WIDTH), 1)
    return (row == lane).astype(F32).astype(BF16)


def to_channels(cells):
    return mm(eye(), cells, NT)


def to_cells(channels):
    return mm(channels, eye(), TN)


def stage_rows(channels, buf):
    for t in range(SUB // 2):
        part = channels[:, t * WIDTH : (t + 1) * WIDTH]
        one, two = swap_halves(part[:HALF], part[HALF:])
        buf[(2 * t) * HALF : (2 * t + 1) * HALF, :] = one
        buf[(2 * t + 1) * HALF : (2 * t + 2) * HALF, :] = two


def panel_row(buf, p):
    return buf[pl.ds(p, SUB, stride=HALF), :]


def channels_of(panels, buf, out):
    buf[...] = panels.reshape(LANES, WIDTH)
    for t in range(SUB // 2):
        one = buf[pl.ds(2 * t, HALF, stride=SUB), :]
        two = buf[pl.ds(2 * t + 1, HALF, stride=SUB), :]
        low, high = swap_halves(one, two)
        out[:HALF, t * WIDTH : (t + 1) * WIDTH] = low
        out[HALF:, t * WIDTH : (t + 1) * WIDTH] = high
    return out[...]


def norm_channels(values, gain):
    center = jnp.mean(values, axis=0, keepdims=True)
    spread = jnp.mean((values - center) ** 2, axis=0, keepdims=True)
    inverse = lax.rsqrt(spread + EPS)
    centred = (values - center) * inverse
    return centred * gain, centred, inverse


def norm_back_channels(upstream, centred, inverse, gain):
    scaled = upstream * gain
    first = jnp.mean(scaled, axis=0, keepdims=True)
    second = jnp.mean(scaled * centred, axis=0, keepdims=True)
    return inverse * (scaled - first - centred * second)


def column(row):
    at = lax.broadcasted_iota(jnp.int32, (WIDTH, WIDTH), 0)
    lane = lax.broadcasted_iota(jnp.int32, (WIDTH, WIDTH), 1)
    return jnp.sum(jnp.where(at == lane, row, 0.0), axis=1, keepdims=True)


def mask_lanes(token_ref, s):
    valid = jnp.sum(token_ref[...].astype(F32), axis=1, keepdims=True)
    lane = lax.broadcasted_iota(jnp.int32, (1, LANES), 1)
    row = lane // HALF + (lax.axis_index("row") * HALF + s * SUB)
    col = lane % HALF + lax.axis_index("col") * HALF
    return (jnp.maximum(row, col).astype(F32) < valid).astype(F32)


def bound_lanes(exponent_ref):
    bound = 448.0 * jnp.exp2(exponent_ref[...].astype(F32))
    return jnp.concatenate([bound[i : i + 1] for i in range(SUB)], axis=1)


def normed_cells(x_ref, gain_ref):
    gain = column(gain_ref[...])
    normed, centred, inverse = norm_channels(to_channels(x_ref[...].reshape(LANES, WIDTH)), gain)
    return normed.astype(BF16), centred, inverse, gain


def right_kernel(at, x_ref, gain_ref, w_ref, token_ref, exponent_ref, out_ref, buf):
    normed = normed_cells(x_ref, gain_ref)[0]
    proj = mm(w_ref[...], normed, TN)
    raw = mask_lanes(token_ref, at + pl.program_id(0)) * jax.nn.sigmoid(proj[:WIDTH]) * proj[WIDTH:]
    bound = bound_lanes(exponent_ref)
    stage_rows(jnp.clip(raw, -bound, bound), buf)
    for p in range(HALF):
        out_ref[p] = panel_row(buf, p).astype(BF16)


def left_kernel(x_ref, gain_ref, w_ref, token_ref, out_ref, buf):
    normed = normed_cells(x_ref, gain_ref)[0]
    proj = mm(w_ref[...], normed, TN)
    mask = mask_lanes(token_ref, pl.program_id(0))
    stage_rows(mask * jax.nn.sigmoid(proj[:WIDTH]) * proj[WIDTH:], buf)
    first = first_half(SUB)
    for p in range(HALF):
        row = panel_row(buf, p)
        out_ref[p, 0] = jnp.where(first, row, 0.0).astype(BF16)
        out_ref[p, 1] = jnp.where(first, 0.0, row).astype(BF16)


def tri_kernel(s0, s1, s2, s3, left_ref, keep_ref, near_ref, send_ref, panel_ref):
    z, q = lax.axis_index("row"), lax.axis_index("col")
    for m, ref in enumerate((s0, s1, s2, s3)):
        place = ((z ^ (z >> 1)) - m + 4) & 3
        other = place ^ (place >> 1) ^ q
        panel_ref[(other & 1) * 2 + (other >> 1)] = ref[...]
    for p in range(GROUP):
        right = jnp.concatenate([panel_ref[r, p] for r in range(4)], axis=0)
        tri = mm(right, left_ref[p].reshape(WIDTH, WIDTH), NT).astype(BF16)
        keep_ref[p] = tri[:SUB]
        near_ref[p] = tri[SUB : 2 * SUB]
        send_ref[0, p] = tri[2 * SUB : 3 * SUB]
        send_ref[1, p] = tri[3 * SUB :]


def mid_kernel(
    a_ref, b_ref, c_ref, x_ref, grad_ref, gain_in_ref, gain_out_ref, gate_ref, out_w_ref,
    g_out_so_far, g_gate_so_far, dtri_ref, dgate_ref, g_out_ref, g_gate_ref, buf, wide,
):
    gain_out = column(gain_out_ref[...])
    tri = channels_of(
        a_ref[...].astype(F32) + b_ref[0].astype(F32) + c_ref[...].astype(F32), buf, wide
    )
    tnorm_f, tcentred, tinverse = norm_channels(tri, gain_out)
    tnorm = tnorm_f.astype(BF16)

    def turned(ref):
        buf[...] = ref[...].astype(F32).reshape(LANES, WIDTH)
        rows = [buf[pl.ds(j, HALF, stride=SUB), :] for j in range(SUB)]
        return to_channels(jnp.concatenate(rows, axis=0).astype(BF16))

    normed = norm_channels(turned(x_ref), column(gain_in_ref[...]))[0].astype(BF16)
    upstream = turned(grad_ref)
    opened = jax.nn.sigmoid(mm(gate_ref[...], normed, TN))
    outproj = mm(out_w_ref[...], tnorm, TN)
    d_open = upstream * outproj
    d_outproj = (upstream * opened).astype(BF16)
    g_out_ref[...] = g_out_so_far[...] + mm(tnorm, d_outproj, NT)
    d_tnorm = mm(out_w_ref[...], d_outproj, NN)
    d_tri = norm_back_channels(d_tnorm, tcentred, tinverse, gain_out)
    d_gatepre = (d_open * opened * (1.0 - opened)).astype(BF16)
    g_gate_ref[...] = g_gate_so_far[...] + mm(normed, d_gatepre, NT)
    stage_rows(d_tri, buf)
    for p in range(HALF):
        dtri_ref[p] = panel_row(buf, p).astype(BF16)
    buf[...] = to_cells(d_gatepre)
    for i in range(HALF):
        dgate_ref[i] = panel_row(buf, i).astype(BF16)


def dright_kernel(*refs):
    *grads_refs, left_ref, p0, p1, p2, p3, held = refs
    z, q = lax.axis_index("row"), lax.axis_index("col")
    for k, ref in enumerate(grads_refs):
        r = k % 4
        block_at = q ^ ((r % 2) * 2 + r // 2)
        slot = ((z ^ (z >> 1)) - (block_at ^ (block_at >> 1)) + 4) & 3
        held[slot, :, (k // 4) * SUB : (k // 4 + 1) * SUB] = ref[...]
    for p in range(GROUP):
        grads = jnp.concatenate([held[m, p] for m in range(4)], axis=0)
        part = mm(grads, left_ref[p].reshape(WIDTH, WIDTH), NN).astype(BF16)
        for m, ref in enumerate((p0, p1, p2, p3)):
            ref[p] = part[m * PART : (m + 1) * PART]


def dleft_kernel(*refs):
    so_far, out_ref = refs[-2:]
    parts = (len(refs) - 2) // 5
    grad_refs, panel_refs = refs[: 4 * parts], refs[4 * parts : 5 * parts]
    first = first_half(HALF)
    for p in range(GROUP):
        grads = jnp.concatenate([d[p] for d in grad_refs], axis=0)
        right = jnp.concatenate([r[q, p] for r in panel_refs for q in range(4)], axis=0)
        both = mm(grads, right, TN)
        out_ref[p] = so_far[p] + jnp.where(first, both[:HALF], both[HALF:])


def gate_grads(upstream, mask, sig, value):
    d_gate = (upstream * mask * value * sig * (1.0 - sig)).astype(BF16)
    d_value = (upstream * mask * sig).astype(BF16)
    return jnp.concatenate([d_gate, d_value], axis=0)


def final_a_kernel(
    x_ref, dleft_ref, token_ref, gain_ref, w_ref, gate_ref, q0, q1, q2, q3, out_ref, g_ref, buf, wide
):
    s = pl.program_id(0)
    normed = normed_cells(x_ref, gain_ref)[0]
    proj = mm(w_ref[...], normed, TN)
    d_left = channels_of(dleft_ref[...], buf, wide)
    d_proj = gate_grads(d_left, mask_lanes(token_ref, s), jax.nn.sigmoid(proj[:WIDTH]), proj[WIDTH:])
    d_gate = jnp.concatenate([q[...] for q in (q0, q1, q2, q3)], axis=1).reshape(LANES, WIDTH)
    out_ref[...] = mm(w_ref[...], d_proj, NN) + mm(gate_ref[...], d_gate, NT)

    @pl.when(s == 0)
    def start():
        g_ref[...] = jnp.zeros_like(g_ref)

    g_ref[...] += mm(normed, d_proj, NT)


def final_b_kernel(
    at, x_ref, part_ref, a_ref, b_ref, token_ref, exponent_ref, gain_ref, w_ref, so_far, into_ref,
    out_ref, g_ref, buf, wide,
):
    step = pl.program_id(0)
    normed, centred, inverse, gain = normed_cells(x_ref, gain_ref)
    proj = mm(w_ref[...], normed, TN)
    mask = mask_lanes(token_ref, at + step)
    sig = jax.nn.sigmoid(proj[:WIDTH])
    inside = jnp.abs(mask * sig * proj[WIDTH:]) <= bound_lanes(exponent_ref)
    d_right = channels_of(a_ref[...].astype(F32) + b_ref[...].astype(F32), buf, wide)
    d_proj = gate_grads(jnp.where(inside, d_right, 0.0), mask, sig, proj[WIDTH:])

    @pl.when(step == 0)
    def start():
        g_ref[...] = so_far[...]

    g_ref[...] += mm(normed, d_proj, NT)
    d_normed = part_ref[...] + mm(w_ref[...], d_proj, NN)
    d_pair = norm_back_channels(d_normed, centred, inverse, gain).astype(BF16)
    out_ref[...] = to_cells(d_pair).astype(BF16).reshape(SUB, HALF, WIDTH)


def whole(array):
    return pl.BlockSpec(array.shape, lambda i: (0,) * array.ndim)


def block(shape, at):
    return pl.BlockSpec(shape, lambda i: at)


BUF = pltpu.VMEM((LANES, WIDTH), F32)
WIDE = pltpu.VMEM((WIDTH, LANES), F32)
PANEL = jax.ShapeDtypeStruct((HALF, SUB, WIDTH), BF16)
PANEL_SPEC = pl.BlockSpec((GROUP, SUB, WIDTH), lambda i: (i, 0, 0))
FOUR = jax.ShapeDtypeStruct((4, HALF, SUB, WIDTH), BF16)
FOUR_SPEC = pl.BlockSpec((4, GROUP, SUB, WIDTH), lambda i: (0, i, 0, 0))
TWO = jax.ShapeDtypeStruct((2, HALF, SUB, WIDTH), BF16)
TWO_SPEC = pl.BlockSpec((2, GROUP, SUB, WIDTH), lambda i: (0, i, 0, 0))
LEFT_SPEC = pl.BlockSpec((GROUP, 2, HALF, WIDTH), lambda i: (i, 0, 0, 0))
LONG = jax.ShapeDtypeStruct((HALF, PART, WIDTH), BF16)
LONG_SPEC = pl.BlockSpec((GROUP, PART, WIDTH), lambda i: (i, 0, 0))
WHOLE_PANEL = pl.BlockSpec(PANEL.shape, lambda i: (0, 0, 0))


def right_part(s, pair, gain, w_proj, tokens, exponents):
    steps = PART // SUB
    return pl.pallas_call(
        functools.partial(right_kernel, s * steps),
        grid=(steps,),
        out_shape=LONG,
        in_specs=[
            pl.BlockSpec((SUB, HALF, WIDTH), lambda i: (s * steps + i, 0, 0)),
            whole(gain), block((WIDTH, 2 * WIDTH), (0, 1)), whole(tokens),
            pl.BlockSpec((SUB, HALF), lambda i: (s * steps + i, 0)),
        ],
        out_specs=pl.BlockSpec((HALF, SUB, WIDTH), lambda i: (0, i, 0)),
        scratch_shapes=[BUF],
        compiler_params=params(),
        cost_estimate=cost(8 * LANES * WIDTH * WIDTH, 1 << 20, 2 * LANES * WIDTH),
        name="right_part",
    )(pair, gain, w_proj, tokens, exponents)


def left_part(pair, gain, w_proj, tokens):
    return pl.pallas_call(
        left_kernel,
        grid=(HALF // SUB,),
        out_shape=jax.ShapeDtypeStruct((HALF, 2, HALF, WIDTH), BF16),
        in_specs=[
            pl.BlockSpec((SUB, HALF, WIDTH), lambda i: (i, 0, 0)), whole(gain),
            block((WIDTH, 2 * WIDTH), (0, 0)), whole(tokens),
        ],
        out_specs=pl.BlockSpec((HALF, 2, SUB, WIDTH), lambda i: (0, 0, i, 0)),
        scratch_shapes=[BUF],
        compiler_params=params(),
        cost_estimate=cost(16 * LANES * WIDTH * WIDTH, 3 << 20, 4 * LANES * WIDTH),
        name="left_part",
    )(pair, gain, w_proj, tokens)


def tri_part(at, slots, left):
    return pl.pallas_call(
        tri_kernel,
        grid=(HALF // GROUP,),
        out_shape=(PANEL, PANEL, TWO, FOUR),
        in_specs=[pl.BlockSpec((GROUP, SUB, WIDTH), lambda i: (i, at, 0))] * 4 + [LEFT_SPEC],
        out_specs=(PANEL_SPEC, PANEL_SPEC, TWO_SPEC, FOUR_SPEC),
        compiler_params=params(),
        cost_estimate=cost(2 * HALF * HALF * WIDTH * WIDTH, 5 << 20),
        name="tri_part",
    )(*slots, left)


def mid_part(s, parts, pair, grad, gain_in, gain_out, w_gate, w_out, g_out, g_gate):
    square = jax.ShapeDtypeStruct((WIDTH, WIDTH), F32)
    columns = block((HALF, SUB, WIDTH), (0, s, 0))
    small = [gain_in, gain_out, w_gate, w_out, g_out, g_gate]
    return pl.pallas_call(
        mid_kernel,
        grid=(1,),
        out_shape=(PANEL, pltpu.HBM(PANEL.shape, BF16), square, square),
        in_specs=[WHOLE_PANEL, block((1, HALF, SUB, WIDTH), (0, 0, 0, 0)), WHOLE_PANEL]
        + [columns] * 2
        + [whole(a) for a in small],
        out_specs=(WHOLE_PANEL, WHOLE_PANEL, block(square.shape, (0, 0)), block(square.shape, (0, 0))),
        scratch_shapes=[BUF, WIDE],
        compiler_params=params(),
        cost_estimate=cost(12 * LANES * WIDTH * WIDTH, 2 << 20, LANES * WIDTH),
        name="mid_part",
    )(*parts, pair, grad, *small)


def dright_part(blocks, left):
    return pl.pallas_call(
        dright_kernel,
        grid=(HALF // GROUP,),
        out_shape=(pltpu.HBM(LONG.shape, BF16), LONG, LONG, LONG),
        in_specs=[PANEL_SPEC] * len(blocks) + [LEFT_SPEC],
        out_specs=(LONG_SPEC,) * 4,
        scratch_shapes=[pltpu.VMEM((4, GROUP, PART, WIDTH), BF16)],
        compiler_params=params(),
        cost_estimate=cost(4 * HALF * HALF * WIDTH * WIDTH, 6 << 20),
        name="dright_part",
    )(*blocks, left)


def dleft_part(grads, panels, so_far):
    rows = pl.BlockSpec((GROUP, HALF, WIDTH), lambda i: (i, 0, 0))
    return pl.pallas_call(
        dleft_kernel,
        grid=(HALF // GROUP,),
        out_shape=jax.ShapeDtypeStruct((HALF, HALF, WIDTH), F32),
        in_specs=[PANEL_SPEC] * len(grads) + [FOUR_SPEC] * len(panels) + [rows],
        out_specs=rows,
        compiler_params=params(),
        cost_estimate=cost(4 * HALF * HALF * WIDTH * WIDTH, 8 << 20),
        name="dleft_part",
    )(*grads, *panels, so_far)


def final_a_part(pair, dleft, tokens, gain, w_proj, w_gate, gates):
    return pl.pallas_call(
        final_a_kernel,
        grid=(HALF // SUB,),
        out_shape=(
            jax.ShapeDtypeStruct((WIDTH, HALF * HALF), F32),
            jax.ShapeDtypeStruct((WIDTH, 2 * WIDTH), F32),
        ),
        in_specs=[
            pl.BlockSpec((SUB, HALF, WIDTH), lambda i: (i, 0, 0)),
            pl.BlockSpec((HALF, SUB, WIDTH), lambda i: (0, i, 0)),
            whole(tokens), whole(gain), block((WIDTH, 2 * WIDTH), (0, 0)), whole(w_gate),
        ]
        + [pl.BlockSpec((SUB, SUB, WIDTH), lambda i: (i, 0, 0))] * 4,
        out_specs=(
            pl.BlockSpec((WIDTH, LANES), lambda i: (0, i)),
            block((WIDTH, 2 * WIDTH), (0, 0)),
        ),
        scratch_shapes=[BUF, WIDE],
        compiler_params=params(),
        cost_estimate=cost(56 * LANES * WIDTH * WIDTH, 8 << 20, 4 * LANES * WIDTH),
        name="final_a_part",
    )(pair, dleft, tokens, gain, w_proj, w_gate, *gates)


def final_b_part(s, pair, part, sums, tokens, exponents, gain, w_proj, so_far, into):
    steps = PART // SUB
    rows = pl.BlockSpec((SUB, HALF, WIDTH), lambda i: (s * steps + i, 0, 0))
    panel = pl.BlockSpec((HALF, SUB, WIDTH), lambda i: (0, i, 0))
    return pl.pallas_call(
        functools.partial(final_b_kernel, s * steps),
        grid=(steps,),
        out_shape=(
            jax.ShapeDtypeStruct((HALF, HALF, WIDTH), BF16),
            jax.ShapeDtypeStruct((WIDTH, 2 * WIDTH), F32),
        ),
        in_specs=[
            rows,
            pl.BlockSpec((WIDTH, LANES), lambda i: (0, s * steps + i)),
            panel, panel, whole(tokens),
            pl.BlockSpec((SUB, HALF), lambda i: (s * steps + i, 0)),
            whole(gain), block((WIDTH, 2 * WIDTH), (0, 1)), whole(so_far),
            pl.BlockSpec(memory_space=pl.ANY),
        ],
        out_specs=(rows, block((WIDTH, 2 * WIDTH), (0, 0))),
        scratch_shapes=[BUF, WIDE],
        input_output_aliases={9: 0} if into.shape == pair.shape else {},
        compiler_params=params(),
        cost_estimate=cost(28 * LANES * WIDTH * WIDTH, 4 << 20, 2 * LANES * WIDTH),
        name="final_b_part",
    )(pair, part, *sums, tokens, exponents, gain, w_proj, so_far, into)


def after(array, *others):
    return lax.optimization_barrier((array, *others))[0]


def blocked(pair_tiles, grad_out, exponents, token_mask, gain_in, w_proj, w_gate, gain_out, w_out):
    width = pair_tiles.shape[-1]
    crop_len = token_mask.shape[0]
    core = lax.axis_index("col") % 2
    tokens = token_mask.reshape(1, crop_len)
    gain_in = gain_in.reshape(1, width)
    gain_out = gain_out.reshape(1, width)

    def forward(a):
        return lax.ppermute(a, "row", [(0, 1), (1, 3), (3, 2), (2, 0)])

    def over_row(a, bit):
        return lax.ppermute(a, "row", [(k, k ^ bit) for k in range(4)])

    def over_x(a):
        return lax.ppermute(a, "col", [(k, k ^ 2) for k in range(4)])

    def over_core(a):
        return lax.ppermute(a, "col", [(k, k ^ 1) for k in range(4)])

    def plus(a, b):
        return (a.astype(F32) + b.astype(F32)).astype(BF16)

    def in_hbm(*arrays):
        return [pltpu.with_memory_space_constraint(a, pltpu.HBM) for a in arrays]

    def right(s):
        return right_part(s, *in_hbm(pair_tiles, gain_in, w_proj, tokens, exponents))

    a0, b0 = right(0), right(1)
    left = left_part(*in_hbm(pair_tiles, gain_in, w_proj, tokens))
    a1, b1 = forward(a0), forward(b0)
    a2, b2 = forward(a1), forward(after(b1, left))
    c0, d0 = right(2), right(3)
    a3, b3 = forward(after(a2, b1, c0)), forward(after(b2, d0))
    c1, d1 = forward(after(c0, b2)), forward(after(d0, a3))

    def triangle(slots):
        keep, near, send, panel = tri_part(0, slots, left)
        got = over_core(send)
        return keep, got, plus(near, got[1]), panel

    g_out = g_gate = jnp.zeros((width, width), F32)

    def middle(s, tri, mine):
        return mid_part(
            s, (tri[0], tri[1], mine), pair_tiles, grad_out, gain_in, gain_out, w_gate, w_out, g_out, g_gate
        )

    def spread(d_tri):
        far = over_x(d_tri)
        return [d_tri, far, over_core(d_tri), over_core(far)]

    def dright(blocks, *others):
        return dright_part([blocks[0], blocks[1], blocks[2], after(blocks[3], *others)], left)

    tri_a, tri_b = triangle([a0, a1, a2, after(a3, b3)]), triangle([b0, b1, b2, b3])
    x_a = over_x(after(tri_a[2], c1))
    c2, d2 = forward(after(c1, tri_a[2])), forward(after(d1, tri_b[2]))
    x_b = over_x(tri_b[2])
    dtri_a, gate_a, g_out, g_gate = middle(0, tri_a, after(x_a, d1, c2))
    blocks_a = spread(dtri_a)
    dtri_b, gate_b, g_out, g_gate = middle(1, tri_b, after(x_b, d2))
    blocks_b = spread(dtri_b)
    c3, d3 = forward(after(c2, dtri_a)), forward(after(d2, dtri_b))
    part_a = dright(blocks_a, d2)
    part_b = dright(blocks_b, c3)
    r_a, r_b = forward(part_a[1]), forward(part_b[1])

    tri_c = triangle([c0, c1, c2, after(c3, part_a[1])])
    x_c = over_x(tri_c[2])
    dtri_c, gate_c, g_out, g_gate = middle(2, tri_c, after(x_c, d3, part_b[1]))
    blocks_c = spread(dtri_c)
    r_a = plus(r_a, part_a[2])
    tri_d = triangle([d0, d1, d2, after(d3, dtri_c, r_a)])
    r_a2 = forward(r_a)
    x_d = over_x(after(tri_d[2], r_b))
    r_b = plus(r_b, part_b[2])
    r_b2 = forward(r_b)
    r_a2 = plus(r_a2, part_a[3])
    dtri_d, gate_d, g_out, g_gate = middle(3, tri_d, after(x_d, r_a2))
    blocks_d = spread(dtri_d)
    r_a3 = forward(r_a2)
    r_b2 = plus(r_b2, part_b[3])
    d_left = dleft_part(
        [after(blocks_a[0], dtri_d, r_b2)] + blocks_a[1:] + blocks_b,
        [tri_a[3], tri_b[3]],
        jnp.zeros((HALF, HALF, WIDTH), F32),
    )
    r_b3 = forward(r_b2)
    part_c = dright(blocks_c, r_a3, d_left)
    part_d = dright(blocks_d, r_b3, part_c[1])

    zero = jnp.zeros((width, 2 * width), F32)

    def final(s, sums, so_far, into):
        return final_b_part(
            s, pair_tiles, partial, sums, tokens, exponents, gain_in, w_proj, so_far, into
        )

    r_c, r_d = forward(part_c[1]), forward(part_d[1])
    d_left = dleft_part(
        [after(blocks_c[0], part_d[1])] + blocks_c[1:] + blocks_d, [tri_c[3], tri_d[3]], d_left
    )
    r_c = plus(r_c, after(part_c[2], d_left))
    partial, g_a = final_a_part(
        pair_tiles, after(d_left, r_c), tokens, gain_in, w_proj, w_gate, [gate_a, gate_b, gate_c, gate_d]
    )
    r_c = forward(r_c)
    r_d = plus(r_d, after(part_d[2], g_a))
    d_pair, g_first = final(0, (part_a[0], after(r_a3, r_d)), zero, gain_in)
    r_d = forward(r_d)
    r_c = plus(r_c, after(part_c[3], g_first))
    d_pair, g_first = final(1, (part_b[0], after(r_b3, r_c)), g_first, d_pair)
    r_c = forward(r_c)
    r_d = forward(plus(r_d, after(part_d[3], g_first)))
    d_pair, g_last = final(2, (part_c[0], r_c), g_first, d_pair)
    d_pair, g_last = final(3, (part_d[0], r_d), g_last, d_pair)

    sums = jnp.concatenate([g_out, g_gate, g_a, g_last], axis=1)
    half = width // 2
    sums = lax.dynamic_slice_in_dim(sums, core * half, half) + over_core(
        lax.dynamic_slice_in_dim(sums, (1 - core) * half, half)
    )
    for send in (over_x, lambda a: over_row(a, 1), lambda a: over_row(a, 2)):
        mine = sums.astype(BF16)
        sums = mine.astype(F32) + send(mine).astype(F32)
    sums = sums / crop_len
    theirs = over_core(sums)
    sums = jnp.concatenate(
        [jnp.where(core == 0, sums, theirs), jnp.where(core == 0, theirs, sums)], axis=0
    )
    return d_pair, sums[:, 2 * width :], sums[:, width : 2 * width], sums[:, :width]


def local(pair_tiles, *rest, rows_over, cols_over):
    if pair_tiles.shape == (HALF, HALF, WIDTH) and rows_over == cols_over == 4:
        return blocked(pair_tiles, *rest)
    return plain(pair_tiles, *rest)


def solution(mesh):
    return jax.shard_map(
        functools.partial(local, rows_over=mesh.shape["row"], cols_over=mesh.shape["col"]),
        mesh=mesh,
        in_specs=(
            P(("crop", "row"), "col", None),
            P(("crop", "row"), "col", None),
            P(("crop", "row"), "col"),
            P("crop"),
            P(),
            P(),
            P(),
            P(),
            P(),
        ),
        out_specs=(
            P(("crop", "row"), "col", None),
            P("crop", None),
            P("crop", None),
            P("crop", None),
        ),
        check_vma=False,
    )
```

```python
import functools

import jax
import jax.numpy as jnp
from jax import lax
from jax.experimental import pallas as pl
from jax.experimental.pallas import tpu as pltpu
from jax.sharding import PartitionSpec as P

EPS = 1e-05


def layer_norm(values, gain):
    center = jnp.mean(values, axis=-1, keepdims=True)
    spread = jnp.mean((values - center) ** 2, axis=-1, keepdims=True)
    inverse = lax.rsqrt(spread + EPS)
    centred = (values - center) * inverse
    return (centred * gain, centred, inverse)


def norm_back(upstream, centred, inverse, gain):
    scaled = upstream * gain
    first = jnp.mean(scaled, axis=-1, keepdims=True)
    second = jnp.mean(scaled * centred, axis=-1, keepdims=True)
    return inverse * (scaled - first - centred * second)


def plain(pair_tiles, grad_out, exponents, token_mask, gain_in, w_proj, w_gate, gain_out, w_out):
    f32 = jnp.float32
    bf16 = jnp.bfloat16
    rows, cols, width = pair_tiles.shape
    crop_len = token_mask.shape[0]
    row_at = lax.axis_index("row")
    col_at = lax.axis_index("col")
    maskf = token_mask.astype(f32)
    mask_rows = lax.dynamic_slice_in_dim(maskf, row_at * rows, rows)
    mask_cols = lax.dynamic_slice_in_dim(maskf, col_at * cols, cols)
    pair_mask = (mask_rows[:, None] * mask_cols[None, :])[..., None]
    normed_f, centred, inverse = layer_norm(pair_tiles.astype(f32), gain_in)
    normed = normed_f.astype(bf16)
    flat = normed.reshape(-1, width)
    projected = jnp.dot(flat, w_proj, preferred_element_type=f32).reshape(rows, cols, 4 * width)
    gate_a = projected[..., :width]
    value_a = projected[..., width : 2 * width]
    gate_b = projected[..., 2 * width : 3 * width]
    value_b = projected[..., 3 * width :]
    sig_a = jax.nn.sigmoid(gate_a)
    sig_b = jax.nn.sigmoid(gate_b)
    left = (pair_mask * sig_a * value_a).astype(bf16)
    right_raw = pair_mask * sig_b * value_b
    bound = (448.0 * jnp.exp2(exponents.astype(f32)))[..., None]
    right = jnp.clip(right_raw, -bound, bound).astype(bf16)
    inside = (jnp.abs(right_raw) <= bound).astype(f32)
    panel = lax.all_gather(right, "row", axis=0, tiled=True)
    tri_cols = lax.psum_scatter(
        jnp.einsum("jkc,ikc->jic", panel, left, preferred_element_type=f32).astype(jnp.bfloat16),
        "col",
        scatter_dimension=0,
        tiled=True,
    ).astype(jnp.float32)
    tri = jnp.transpose(tri_cols, (1, 0, 2))
    tnorm_f, tcentred, tinverse = layer_norm(tri, gain_out)
    tnorm = tnorm_f.astype(bf16)
    tflat = tnorm.reshape(-1, width)
    opened = jax.nn.sigmoid(jnp.dot(flat, w_gate, preferred_element_type=f32)).reshape(
        rows, cols, width
    )
    outproj = jnp.dot(tflat, w_out, preferred_element_type=f32).reshape(rows, cols, width)
    upstream = grad_out.astype(f32)
    d_open = upstream * outproj
    d_outproj = (upstream * opened).astype(bf16).reshape(-1, width)
    g_out = jnp.dot(tflat.T, d_outproj, preferred_element_type=f32)
    d_tnorm = jnp.dot(d_outproj, w_out.T, preferred_element_type=f32).reshape(rows, cols, width)
    d_tri = norm_back(d_tnorm, tcentred, tinverse, gain_out).astype(bf16)
    d_gatepre = (d_open * opened * (1.0 - opened)).astype(bf16).reshape(-1, width)
    g_gate = jnp.dot(flat.T, d_gatepre, preferred_element_type=f32)
    grad_full = lax.all_gather(d_tri, "col", axis=1, tiled=True)
    d_left = jnp.einsum("ijc,jkc->ikc", grad_full, panel, preferred_element_type=f32)
    d_right = (
        lax.psum_scatter(
            jnp.einsum("ijc,ikc->jkc", grad_full, left, preferred_element_type=f32).astype(
                jnp.bfloat16
            ),
            "row",
            scatter_dimension=0,
            tiled=True,
        ).astype(jnp.float32)
        * inside
    )
    d_gate_a = d_left * pair_mask * value_a * sig_a * (1.0 - sig_a)
    d_value_a = d_left * pair_mask * sig_a
    d_gate_b = d_right * pair_mask * value_b * sig_b * (1.0 - sig_b)
    d_value_b = d_right * pair_mask * sig_b
    d_proj = (
        jnp.concatenate([d_gate_a, d_value_a, d_gate_b, d_value_b], axis=-1)
        .astype(bf16)
        .reshape(-1, 4 * width)
    )
    g_proj = jnp.dot(flat.T, d_proj, preferred_element_type=f32)
    d_normed = jnp.dot(d_proj, w_proj.T, preferred_element_type=f32) + jnp.dot(
        d_gatepre, w_gate.T, preferred_element_type=f32
    )
    d_pair = norm_back(d_normed.reshape(rows, cols, width), centred, inverse, gain_in).astype(bf16)
    sum_proj, sum_gate, sum_out = lax.psum((g_proj, g_gate, g_out), ("row", "col"))
    return (d_pair, sum_proj / crop_len, sum_gate / crop_len, sum_out / crop_len)


SUB = 16
PART = 16
HALF = 64
WIDTH = 128
LANES = SUB * HALF
GROUP = 16
NT = (((1,), (1,)), ((), ()))
NN = (((1,), (0,)), ((), ()))
TN = (((0,), (0,)), ((), ()))
F32 = jnp.float32
BF16 = jnp.bfloat16


def mm(a, b, dims):
    return lax.dot_general(a, b, dims, preferred_element_type=F32)


def params():
    return pltpu.CompilerParams(vmem_limit_bytes=16 * 1024 * 1024)


def cost(flops, size, exps=0):
    return pl.CostEstimate(flops=flops, bytes_accessed=size, transcendentals=exps)


def first_half(rows):
    return lax.broadcasted_iota(jnp.int32, (rows, WIDTH), 1) < HALF


def swap_halves(a, b):
    first = first_half(HALF)
    return (
        jnp.where(first, a, pltpu.roll(b, HALF, 1)),
        jnp.where(first, pltpu.roll(a, HALF, 1), b),
    )


def eye():
    row = lax.broadcasted_iota(jnp.int32, (WIDTH, WIDTH), 0)
    lane = lax.broadcasted_iota(jnp.int32, (WIDTH, WIDTH), 1)
    return (row == lane).astype(F32).astype(BF16)


def to_channels(cells):
    return mm(eye(), cells, NT)


def to_cells(channels):
    return mm(channels, eye(), TN)


def stage_rows(channels, buf):
    for t in range(SUB // 2):
        part = channels[:, t * WIDTH : (t + 1) * WIDTH]
        one, two = swap_halves(part[:HALF], part[HALF:])
        buf[(2 * t) * HALF : (2 * t + 1) * HALF, :] = one
        buf[(2 * t + 1) * HALF : (2 * t + 2) * HALF, :] = two


def panel_row(buf, p):
    return buf[pl.ds(p, SUB, stride=HALF), :]


def channels_of(panels, buf, out):
    buf[...] = panels.reshape(LANES, WIDTH)
    for t in range(SUB // 2):
        one = buf[pl.ds(2 * t, HALF, stride=SUB), :]
        two = buf[pl.ds(2 * t + 1, HALF, stride=SUB), :]
        low, high = swap_halves(one, two)
        out[:HALF, t * WIDTH : (t + 1) * WIDTH] = low
        out[HALF:, t * WIDTH : (t + 1) * WIDTH] = high
    return out[...]


def norm_channels(values, gain):
    center = jnp.mean(values, axis=0, keepdims=True)
    spread = jnp.mean((values - center) ** 2, axis=0, keepdims=True)
    inverse = lax.rsqrt(spread + EPS)
    centred = (values - center) * inverse
    return centred * gain, centred, inverse


def norm_back_channels(upstream, centred, inverse, gain):
    scaled = upstream * gain
    first = jnp.mean(scaled, axis=0, keepdims=True)
    second = jnp.mean(scaled * centred, axis=0, keepdims=True)
    return inverse * (scaled - first - centred * second)


def column(row):
    at = lax.broadcasted_iota(jnp.int32, (WIDTH, WIDTH), 0)
    lane = lax.broadcasted_iota(jnp.int32, (WIDTH, WIDTH), 1)
    return jnp.sum(jnp.where(at == lane, row, 0.0), axis=1, keepdims=True)


def mask_lanes(token_ref, s):
    valid = jnp.sum(token_ref[...].astype(F32), axis=1, keepdims=True)
    lane = lax.broadcasted_iota(jnp.int32, (1, LANES), 1)
    row = lane // HALF + (lax.axis_index("row") * HALF + s * SUB)
    col = lane % HALF + lax.axis_index("col") * HALF
    return (jnp.maximum(row, col).astype(F32) < valid).astype(F32)


def bound_lanes(exponent_ref):
    bound = 448.0 * jnp.exp2(exponent_ref[...].astype(F32))
    return jnp.concatenate([bound[i : i + 1] for i in range(SUB)], axis=1)


def normed_cells(x_ref, gain_ref):
    gain = column(gain_ref[...])
    normed, centred, inverse = norm_channels(to_channels(x_ref[...].reshape(LANES, WIDTH)), gain)
    return normed.astype(BF16), centred, inverse, gain


def right_kernel(at, x_ref, gain_ref, w_ref, token_ref, exponent_ref, out_ref, buf):
    normed = normed_cells(x_ref, gain_ref)[0]
    proj = mm(w_ref[...], normed, TN)
    raw = mask_lanes(token_ref, at + pl.program_id(0)) * jax.nn.sigmoid(proj[:WIDTH]) * proj[WIDTH:]
    bound = bound_lanes(exponent_ref)
    stage_rows(jnp.clip(raw, -bound, bound), buf)
    for p in range(HALF):
        out_ref[p] = panel_row(buf, p).astype(BF16)


def left_kernel(x_ref, gain_ref, w_ref, token_ref, out_ref, buf):
    normed = normed_cells(x_ref, gain_ref)[0]
    proj = mm(w_ref[...], normed, TN)
    mask = mask_lanes(token_ref, pl.program_id(0))
    stage_rows(mask * jax.nn.sigmoid(proj[:WIDTH]) * proj[WIDTH:], buf)
    first = first_half(SUB)
    for p in range(HALF):
        row = panel_row(buf, p)
        out_ref[p, 0] = jnp.where(first, row, 0.0).astype(BF16)
        out_ref[p, 1] = jnp.where(first, 0.0, row).astype(BF16)


def tri_kernel(s0, s1, s2, s3, left_ref, keep_ref, near_ref, send_ref, panel_ref):
    z, q = lax.axis_index("row"), lax.axis_index("col")
    for m, ref in enumerate((s0, s1, s2, s3)):
        place = ((z ^ (z >> 1)) - m + 4) & 3
        other = place ^ (place >> 1) ^ q
        panel_ref[(other & 1) * 2 + (other >> 1)] = ref[...]
    for p in range(GROUP):
        right = jnp.concatenate([panel_ref[r, p] for r in range(4)], axis=0)
        tri = mm(right, left_ref[p].reshape(WIDTH, WIDTH), NT).astype(BF16)
        keep_ref[p] = tri[:SUB]
        near_ref[p] = tri[SUB : 2 * SUB]
        send_ref[0, p] = tri[2 * SUB : 3 * SUB]
        send_ref[1, p] = tri[3 * SUB :]


def mid_kernel(
    a_ref, b_ref, c_ref, x_ref, grad_ref, gain_in_ref, gain_out_ref, gate_ref, out_w_ref,
    g_out_so_far, g_gate_so_far, dtri_ref, dgate_ref, g_out_ref, g_gate_ref, buf, wide,
):
    gain_out = column(gain_out_ref[...])
    tri = channels_of(
        a_ref[...].astype(F32) + b_ref[0].astype(F32) + c_ref[...].astype(F32), buf, wide
    )
    tnorm_f, tcentred, tinverse = norm_channels(tri, gain_out)
    tnorm = tnorm_f.astype(BF16)

    def turned(ref):
        buf[...] = ref[...].astype(F32).reshape(LANES, WIDTH)
        rows = [buf[pl.ds(j, HALF, stride=SUB), :] for j in range(SUB)]
        return to_channels(jnp.concatenate(rows, axis=0).astype(BF16))

    normed = norm_channels(turned(x_ref), column(gain_in_ref[...]))[0].astype(BF16)
    upstream = turned(grad_ref)
    opened = jax.nn.sigmoid(mm(gate_ref[...], normed, TN))
    outproj = mm(out_w_ref[...], tnorm, TN)
    d_open = upstream * outproj
    d_outproj = (upstream * opened).astype(BF16)
    g_out_ref[...] = g_out_so_far[...] + mm(tnorm, d_outproj, NT)
    d_tnorm = mm(out_w_ref[...], d_outproj, NN)
    d_tri = norm_back_channels(d_tnorm, tcentred, tinverse, gain_out)
    d_gatepre = (d_open * opened * (1.0 - opened)).astype(BF16)
    g_gate_ref[...] = g_gate_so_far[...] + mm(normed, d_gatepre, NT)
    stage_rows(d_tri, buf)
    for p in range(HALF):
        dtri_ref[p] = panel_row(buf, p).astype(BF16)
    buf[...] = to_cells(d_gatepre)
    for i in range(HALF):
        dgate_ref[i] = panel_row(buf, i).astype(BF16)


def dright_kernel(*refs):
    *grads_refs, left_ref, p0, p1, p2, p3, held = refs
    z, q = lax.axis_index("row"), lax.axis_index("col")
    for k, ref in enumerate(grads_refs):
        r = k % 4
        block_at = q ^ ((r % 2) * 2 + r // 2)
        slot = ((z ^ (z >> 1)) - (block_at ^ (block_at >> 1)) + 4) & 3
        held[slot, :, (k // 4) * SUB : (k // 4 + 1) * SUB] = ref[...]
    for p in range(GROUP):
        grads = jnp.concatenate([held[m, p] for m in range(4)], axis=0)
        part = mm(grads, left_ref[p].reshape(WIDTH, WIDTH), NN).astype(BF16)
        for m, ref in enumerate((p0, p1, p2, p3)):
            ref[p] = part[m * PART : (m + 1) * PART]


def dleft_kernel(*refs):
    so_far, out_ref = refs[-2:]
    parts = (len(refs) - 2) // 5
    grad_refs, panel_refs = refs[: 4 * parts], refs[4 * parts : 5 * parts]
    first = first_half(HALF)
    for p in range(GROUP):
        grads = jnp.concatenate([d[p] for d in grad_refs], axis=0)
        right = jnp.concatenate([r[q, p] for r in panel_refs for q in range(4)], axis=0)
        both = mm(grads, right, TN)
        out_ref[p] = so_far[p] + jnp.where(first, both[:HALF], both[HALF:])


def gate_grads(upstream, mask, sig, value):
    d_gate = (upstream * mask * value * sig * (1.0 - sig)).astype(BF16)
    d_value = (upstream * mask * sig).astype(BF16)
    return jnp.concatenate([d_gate, d_value], axis=0)


def final_a_kernel(
    x_ref, dleft_ref, token_ref, gain_ref, w_ref, gate_ref, q0, q1, q2, q3, out_ref, g_ref, buf, wide
):
    s = pl.program_id(0)
    normed = normed_cells(x_ref, gain_ref)[0]
    proj = mm(w_ref[...], normed, TN)
    d_left = channels_of(dleft_ref[...], buf, wide)
    d_proj = gate_grads(d_left, mask_lanes(token_ref, s), jax.nn.sigmoid(proj[:WIDTH]), proj[WIDTH:])
    d_gate = jnp.concatenate([q[...] for q in (q0, q1, q2, q3)], axis=1).reshape(LANES, WIDTH)
    out_ref[...] = mm(w_ref[...], d_proj, NN) + mm(gate_ref[...], d_gate, NT)

    @pl.when(s == 0)
    def start():
        g_ref[...] = jnp.zeros_like(g_ref)

    g_ref[...] += mm(normed, d_proj, NT)


def final_b_kernel(
    at, x_ref, part_ref, a_ref, b_ref, token_ref, exponent_ref, gain_ref, w_ref, so_far, into_ref,
    out_ref, g_ref, buf, wide,
):
    step = pl.program_id(0)
    normed, centred, inverse, gain = normed_cells(x_ref, gain_ref)
    proj = mm(w_ref[...], normed, TN)
    mask = mask_lanes(token_ref, at + step)
    sig = jax.nn.sigmoid(proj[:WIDTH])
    inside = jnp.abs(mask * sig * proj[WIDTH:]) <= bound_lanes(exponent_ref)
    d_right = channels_of(a_ref[...].astype(F32) + b_ref[...].astype(F32), buf, wide)
    d_proj = gate_grads(jnp.where(inside, d_right, 0.0), mask, sig, proj[WIDTH:])

    @pl.when(step == 0)
    def start():
        g_ref[...] = so_far[...]

    g_ref[...] += mm(normed, d_proj, NT)
    d_normed = part_ref[...] + mm(w_ref[...], d_proj, NN)
    d_pair = norm_back_channels(d_normed, centred, inverse, gain).astype(BF16)
    out_ref[...] = to_cells(d_pair).astype(BF16).reshape(SUB, HALF, WIDTH)


def whole(array):
    return pl.BlockSpec(array.shape, lambda i: (0,) * array.ndim)


def block(shape, at):
    return pl.BlockSpec(shape, lambda i: at)


BUF = pltpu.VMEM((LANES, WIDTH), F32)
WIDE = pltpu.VMEM((WIDTH, LANES), F32)
PANEL = jax.ShapeDtypeStruct((HALF, SUB, WIDTH), BF16)
PANEL_SPEC = pl.BlockSpec((GROUP, SUB, WIDTH), lambda i: (i, 0, 0))
FOUR = jax.ShapeDtypeStruct((4, HALF, SUB, WIDTH), BF16)
FOUR_SPEC = pl.BlockSpec((4, GROUP, SUB, WIDTH), lambda i: (0, i, 0, 0))
TWO = jax.ShapeDtypeStruct((2, HALF, SUB, WIDTH), BF16)
TWO_SPEC = pl.BlockSpec((2, GROUP, SUB, WIDTH), lambda i: (0, i, 0, 0))
LEFT_SPEC = pl.BlockSpec((GROUP, 2, HALF, WIDTH), lambda i: (i, 0, 0, 0))
LONG = jax.ShapeDtypeStruct((HALF, PART, WIDTH), BF16)
LONG_SPEC = pl.BlockSpec((GROUP, PART, WIDTH), lambda i: (i, 0, 0))
WHOLE_PANEL = pl.BlockSpec(PANEL.shape, lambda i: (0, 0, 0))


def right_part(s, pair, gain, w_proj, tokens, exponents):
    steps = PART // SUB
    return pl.pallas_call(
        functools.partial(right_kernel, s * steps),
        grid=(steps,),
        out_shape=LONG,
        in_specs=[
            pl.BlockSpec((SUB, HALF, WIDTH), lambda i: (s * steps + i, 0, 0)),
            whole(gain), block((WIDTH, 2 * WIDTH), (0, 1)), whole(tokens),
            pl.BlockSpec((SUB, HALF), lambda i: (s * steps + i, 0)),
        ],
        out_specs=pl.BlockSpec((HALF, SUB, WIDTH), lambda i: (0, i, 0)),
        scratch_shapes=[BUF],
        compiler_params=params(),
        cost_estimate=cost(8 * LANES * WIDTH * WIDTH, 1 << 20, 2 * LANES * WIDTH),
        name="right_part",
    )(pair, gain, w_proj, tokens, exponents)


def left_part(pair, gain, w_proj, tokens):
    return pl.pallas_call(
        left_kernel,
        grid=(HALF // SUB,),
        out_shape=jax.ShapeDtypeStruct((HALF, 2, HALF, WIDTH), BF16),
        in_specs=[
            pl.BlockSpec((SUB, HALF, WIDTH), lambda i: (i, 0, 0)), whole(gain),
            block((WIDTH, 2 * WIDTH), (0, 0)), whole(tokens),
        ],
        out_specs=pl.BlockSpec((HALF, 2, SUB, WIDTH), lambda i: (0, 0, i, 0)),
        scratch_shapes=[BUF],
        compiler_params=params(),
        cost_estimate=cost(16 * LANES * WIDTH * WIDTH, 3 << 20, 4 * LANES * WIDTH),
        name="left_part",
    )(pair, gain, w_proj, tokens)


def tri_part(at, slots, left):
    return pl.pallas_call(
        tri_kernel,
        grid=(HALF // GROUP,),
        out_shape=(PANEL, PANEL, TWO, FOUR),
        in_specs=[pl.BlockSpec((GROUP, SUB, WIDTH), lambda i: (i, at, 0))] * 4 + [LEFT_SPEC],
        out_specs=(PANEL_SPEC, PANEL_SPEC, TWO_SPEC, FOUR_SPEC),
        compiler_params=params(),
        cost_estimate=cost(2 * HALF * HALF * WIDTH * WIDTH, 5 << 20),
        name="tri_part",
    )(*slots, left)


def mid_part(s, parts, pair, grad, gain_in, gain_out, w_gate, w_out, g_out, g_gate):
    square = jax.ShapeDtypeStruct((WIDTH, WIDTH), F32)
    columns = block((HALF, SUB, WIDTH), (0, s, 0))
    small = [gain_in, gain_out, w_gate, w_out, g_out, g_gate]
    return pl.pallas_call(
        mid_kernel,
        grid=(1,),
        out_shape=(PANEL, pltpu.HBM(PANEL.shape, BF16), square, square),
        in_specs=[WHOLE_PANEL, block((1, HALF, SUB, WIDTH), (0, 0, 0, 0)), WHOLE_PANEL]
        + [columns] * 2
        + [whole(a) for a in small],
        out_specs=(WHOLE_PANEL, WHOLE_PANEL, block(square.shape, (0, 0)), block(square.shape, (0, 0))),
        scratch_shapes=[BUF, WIDE],
        compiler_params=params(),
        cost_estimate=cost(12 * LANES * WIDTH * WIDTH, 2 << 20, LANES * WIDTH),
        name="mid_part",
    )(*parts, pair, grad, *small)


def dright_part(blocks, left):
    return pl.pallas_call(
        dright_kernel,
        grid=(HALF // GROUP,),
        out_shape=(pltpu.HBM(LONG.shape, BF16), LONG, LONG, LONG),
        in_specs=[PANEL_SPEC] * len(blocks) + [LEFT_SPEC],
        out_specs=(LONG_SPEC,) * 4,
        scratch_shapes=[pltpu.VMEM((4, GROUP, PART, WIDTH), BF16)],
        compiler_params=params(),
        cost_estimate=cost(4 * HALF * HALF * WIDTH * WIDTH, 6 << 20),
        name="dright_part",
    )(*blocks, left)


def dleft_part(grads, panels, so_far):
    rows = pl.BlockSpec((GROUP, HALF, WIDTH), lambda i: (i, 0, 0))
    return pl.pallas_call(
        dleft_kernel,
        grid=(HALF // GROUP,),
        out_shape=jax.ShapeDtypeStruct((HALF, HALF, WIDTH), F32),
        in_specs=[PANEL_SPEC] * len(grads) + [FOUR_SPEC] * len(panels) + [rows],
        out_specs=rows,
        compiler_params=params(),
        cost_estimate=cost(4 * HALF * HALF * WIDTH * WIDTH, 8 << 20),
        name="dleft_part",
    )(*grads, *panels, so_far)


def final_a_part(pair, dleft, tokens, gain, w_proj, w_gate, gates):
    return pl.pallas_call(
        final_a_kernel,
        grid=(HALF // SUB,),
        out_shape=(
            jax.ShapeDtypeStruct((WIDTH, HALF * HALF), F32),
            jax.ShapeDtypeStruct((WIDTH, 2 * WIDTH), F32),
        ),
        in_specs=[
            pl.BlockSpec((SUB, HALF, WIDTH), lambda i: (i, 0, 0)),
            pl.BlockSpec((HALF, SUB, WIDTH), lambda i: (0, i, 0)),
            whole(tokens), whole(gain), block((WIDTH, 2 * WIDTH), (0, 0)), whole(w_gate),
        ]
        + [pl.BlockSpec((SUB, SUB, WIDTH), lambda i: (i, 0, 0))] * 4,
        out_specs=(
            pl.BlockSpec((WIDTH, LANES), lambda i: (0, i)),
            block((WIDTH, 2 * WIDTH), (0, 0)),
        ),
        scratch_shapes=[BUF, WIDE],
        compiler_params=params(),
        cost_estimate=cost(56 * LANES * WIDTH * WIDTH, 8 << 20, 4 * LANES * WIDTH),
        name="final_a_part",
    )(pair, dleft, tokens, gain, w_proj, w_gate, *gates)


def final_b_part(s, pair, part, sums, tokens, exponents, gain, w_proj, so_far, into):
    steps = PART // SUB
    rows = pl.BlockSpec((SUB, HALF, WIDTH), lambda i: (s * steps + i, 0, 0))
    panel = pl.BlockSpec((HALF, SUB, WIDTH), lambda i: (0, i, 0))
    return pl.pallas_call(
        functools.partial(final_b_kernel, s * steps),
        grid=(steps,),
        out_shape=(
            jax.ShapeDtypeStruct((HALF, HALF, WIDTH), BF16),
            jax.ShapeDtypeStruct((WIDTH, 2 * WIDTH), F32),
        ),
        in_specs=[
            rows,
            pl.BlockSpec((WIDTH, LANES), lambda i: (0, s * steps + i)),
            panel, panel, whole(tokens),
            pl.BlockSpec((SUB, HALF), lambda i: (s * steps + i, 0)),
            whole(gain), block((WIDTH, 2 * WIDTH), (0, 1)), whole(so_far),
            pl.BlockSpec(memory_space=pl.ANY),
        ],
        out_specs=(rows, block((WIDTH, 2 * WIDTH), (0, 0))),
        scratch_shapes=[BUF, WIDE],
        input_output_aliases={9: 0} if into.shape == pair.shape else {},
        compiler_params=params(),
        cost_estimate=cost(28 * LANES * WIDTH * WIDTH, 4 << 20, 2 * LANES * WIDTH),
        name="final_b_part",
    )(pair, part, *sums, tokens, exponents, gain, w_proj, so_far, into)


def after(array, *others):
    return lax.optimization_barrier((array, *others))[0]


def blocked(pair_tiles, grad_out, exponents, token_mask, gain_in, w_proj, w_gate, gain_out, w_out):
    width = pair_tiles.shape[-1]
    crop_len = token_mask.shape[0]
    core = lax.axis_index("col") % 2
    tokens = token_mask.reshape(1, crop_len)
    gain_in = gain_in.reshape(1, width)
    gain_out = gain_out.reshape(1, width)

    def forward(a):
        return lax.ppermute(a, "row", [(0, 1), (1, 3), (3, 2), (2, 0)])

    def over_row(a, bit):
        return lax.ppermute(a, "row", [(k, k ^ bit) for k in range(4)])

    def over_x(a):
        return lax.ppermute(a, "col", [(k, k ^ 2) for k in range(4)])

    def over_core(a):
        return lax.ppermute(a, "col", [(k, k ^ 1) for k in range(4)])

    def plus(a, b):
        return (a.astype(F32) + b.astype(F32)).astype(BF16)

    def in_hbm(*arrays):
        return [pltpu.with_memory_space_constraint(a, pltpu.HBM) for a in arrays]

    def right(s):
        return right_part(s, *in_hbm(pair_tiles, gain_in, w_proj, tokens, exponents))

    a0, b0 = right(0), right(1)
    left = left_part(*in_hbm(pair_tiles, gain_in, w_proj, tokens))
    a1, b1 = forward(a0), forward(b0)
    a2, b2 = forward(a1), forward(after(b1, left))
    c0, d0 = right(2), right(3)
    a3, b3 = forward(after(a2, c0)), forward(after(b2, d0))
    c1, d1 = forward(after(c0, b2)), forward(after(d0, a3))

    def triangle(slots):
        keep, near, send, panel = tri_part(0, slots, left)
        got = over_core(send)
        return keep, got, plus(near, got[1]), panel

    g_out = g_gate = jnp.zeros((width, width), F32)

    def middle(s, tri, mine):
        return mid_part(
            s, (tri[0], tri[1], mine), pair_tiles, grad_out, gain_in, gain_out, w_gate, w_out, g_out, g_gate
        )

    def spread(d_tri):
        far = over_x(d_tri)
        return [d_tri, far, over_core(d_tri), over_core(far)]

    def dright(blocks, *others):
        return dright_part([blocks[0], blocks[1], blocks[2], after(blocks[3], *others)], left)

    tri_a, tri_b = triangle([a0, a1, a2, a3]), triangle([b0, b1, b2, b3])
    x_a, x_b = over_x(tri_a[2]), over_x(tri_b[2])
    c2, d2 = forward(after(c1, tri_a[2])), forward(after(d1, tri_b[2]))
    dtri_a, gate_a, g_out, g_gate = middle(0, tri_a, after(x_a, d1))
    blocks_a = spread(dtri_a)
    dtri_b, gate_b, g_out, g_gate = middle(1, tri_b, after(x_b, c2))
    blocks_b = spread(dtri_b)
    c3, d3 = forward(after(c2, dtri_a)), forward(after(d2, dtri_b))
    part_a = dright(blocks_a, d2)
    part_b = dright(blocks_b, c3)
    r_a, r_b = forward(part_a[1]), forward(part_b[1])

    tri_c = triangle([c0, c1, c2, after(c3, part_a[1])])
    tri_d = triangle([d0, d1, d2, after(d3, part_b[1])])
    x_c, x_d = over_x(tri_c[2]), over_x(tri_d[2])
    r_a = plus(r_a, part_a[2])
    r_a2 = forward(after(r_a, tri_c[2]))
    r_b = plus(r_b, part_b[2])
    r_b2 = forward(after(r_b, tri_d[2]))
    d_left = dleft_part(
        [after(blocks_a[0], tri_d[2])] + blocks_a[1:] + blocks_b,
        [tri_a[3], tri_b[3]],
        jnp.zeros((HALF, HALF, WIDTH), F32),
    )
    dtri_c, gate_c, g_out, g_gate = middle(2, tri_c, after(x_c, r_a, d_left))
    blocks_c = spread(dtri_c)
    dtri_d, gate_d, g_out, g_gate = middle(3, tri_d, after(x_d, r_b))
    blocks_d = spread(dtri_d)
    r_a2 = plus(r_a2, part_a[3])
    r_a3 = forward(after(r_a2, dtri_c))
    r_b2 = plus(r_b2, part_b[3])
    r_b3 = forward(after(r_b2, dtri_d))
    part_c = dright(blocks_c, r_a2)
    part_d = dright(blocks_d, r_b2)

    zero = jnp.zeros((width, 2 * width), F32)

    def final(s, sums, so_far, into):
        return final_b_part(
            s, pair_tiles, partial, sums, tokens, exponents, gain_in, w_proj, so_far, into
        )

    r_c, r_d = forward(part_c[1]), forward(part_d[1])
    d_left = dleft_part(
        [after(blocks_c[0], part_d[1])] + blocks_c[1:] + blocks_d, [tri_c[3], tri_d[3]], d_left
    )
    r_c = plus(r_c, after(part_c[2], d_left))
    partial, g_a = final_a_part(
        pair_tiles, after(d_left, r_c), tokens, gain_in, w_proj, w_gate, [gate_a, gate_b, gate_c, gate_d]
    )
    r_c = forward(r_c)
    r_d = plus(r_d, after(part_d[2], g_a))
    d_pair, g_first = final(0, (part_a[0], after(r_a3, r_d)), zero, gain_in)
    r_d = forward(r_d)
    r_c = plus(r_c, after(part_c[3], g_first))
    d_pair, g_first = final(1, (part_b[0], after(r_b3, r_c)), g_first, d_pair)
    r_c = forward(r_c)
    r_d = forward(plus(r_d, after(part_d[3], g_first)))
    d_pair, g_last = final(2, (part_c[0], r_c), g_first, d_pair)
    d_pair, g_last = final(3, (part_d[0], r_d), g_last, d_pair)

    sums = jnp.concatenate([g_out, g_gate, g_a, g_last], axis=1)
    half = width // 2
    sums = lax.dynamic_slice_in_dim(sums, core * half, half) + over_core(
        lax.dynamic_slice_in_dim(sums, (1 - core) * half, half)
    )
    for send in (over_x, lambda a: over_row(a, 1), lambda a: over_row(a, 2)):
        mine = sums.astype(BF16)
        sums = mine.astype(F32) + send(mine).astype(F32)
    sums = sums / crop_len
    theirs = over_core(sums)
    sums = jnp.concatenate(
        [jnp.where(core == 0, sums, theirs), jnp.where(core == 0, theirs, sums)], axis=0
    )
    return d_pair, sums[:, 2 * width :], sums[:, width : 2 * width], sums[:, :width]


def local(pair_tiles, *rest, rows_over, cols_over):
    if pair_tiles.shape == (HALF, HALF, WIDTH) and rows_over == cols_over == 4:
        return blocked(pair_tiles, *rest)
    return plain(pair_tiles, *rest)


def solution(mesh):
    return jax.shard_map(
        functools.partial(local, rows_over=mesh.shape["row"], cols_over=mesh.shape["col"]),
        mesh=mesh,
        in_specs=(
            P(("crop", "row"), "col", None),
            P(("crop", "row"), "col", None),
            P(("crop", "row"), "col"),
            P("crop"),
            P(),
            P(),
            P(),
            P(),
            P(),
        ),
        out_specs=(
            P(("crop", "row"), "col", None),
            P("crop", None),
            P("crop", None),
            P("crop", None),
        ),
        check_vma=False,
    )
```

```python
import functools

import jax
import jax.numpy as jnp
from jax import lax
from jax.experimental import pallas as pl
from jax.experimental.pallas import tpu as pltpu
from jax.sharding import PartitionSpec as P

EPS = 1e-05


def layer_norm(values, gain):
    center = jnp.mean(values, axis=-1, keepdims=True)
    spread = jnp.mean((values - center) ** 2, axis=-1, keepdims=True)
    inverse = lax.rsqrt(spread + EPS)
    centred = (values - center) * inverse
    return (centred * gain, centred, inverse)


def norm_back(upstream, centred, inverse, gain):
    scaled = upstream * gain
    first = jnp.mean(scaled, axis=-1, keepdims=True)
    second = jnp.mean(scaled * centred, axis=-1, keepdims=True)
    return inverse * (scaled - first - centred * second)


def plain(pair_tiles, grad_out, exponents, token_mask, gain_in, w_proj, w_gate, gain_out, w_out):
    f32 = jnp.float32
    bf16 = jnp.bfloat16
    rows, cols, width = pair_tiles.shape
    crop_len = token_mask.shape[0]
    row_at = lax.axis_index("row")
    col_at = lax.axis_index("col")
    maskf = token_mask.astype(f32)
    mask_rows = lax.dynamic_slice_in_dim(maskf, row_at * rows, rows)
    mask_cols = lax.dynamic_slice_in_dim(maskf, col_at * cols, cols)
    pair_mask = (mask_rows[:, None] * mask_cols[None, :])[..., None]
    normed_f, centred, inverse = layer_norm(pair_tiles.astype(f32), gain_in)
    normed = normed_f.astype(bf16)
    flat = normed.reshape(-1, width)
    projected = jnp.dot(flat, w_proj, preferred_element_type=f32).reshape(rows, cols, 4 * width)
    gate_a = projected[..., :width]
    value_a = projected[..., width : 2 * width]
    gate_b = projected[..., 2 * width : 3 * width]
    value_b = projected[..., 3 * width :]
    sig_a = jax.nn.sigmoid(gate_a)
    sig_b = jax.nn.sigmoid(gate_b)
    left = (pair_mask * sig_a * value_a).astype(bf16)
    right_raw = pair_mask * sig_b * value_b
    bound = (448.0 * jnp.exp2(exponents.astype(f32)))[..., None]
    right = jnp.clip(right_raw, -bound, bound).astype(bf16)
    inside = (jnp.abs(right_raw) <= bound).astype(f32)
    panel = lax.all_gather(right, "row", axis=0, tiled=True)
    tri_cols = lax.psum_scatter(
        jnp.einsum("jkc,ikc->jic", panel, left, preferred_element_type=f32).astype(jnp.bfloat16),
        "col",
        scatter_dimension=0,
        tiled=True,
    ).astype(jnp.float32)
    tri = jnp.transpose(tri_cols, (1, 0, 2))
    tnorm_f, tcentred, tinverse = layer_norm(tri, gain_out)
    tnorm = tnorm_f.astype(bf16)
    tflat = tnorm.reshape(-1, width)
    opened = jax.nn.sigmoid(jnp.dot(flat, w_gate, preferred_element_type=f32)).reshape(
        rows, cols, width
    )
    outproj = jnp.dot(tflat, w_out, preferred_element_type=f32).reshape(rows, cols, width)
    upstream = grad_out.astype(f32)
    d_open = upstream * outproj
    d_outproj = (upstream * opened).astype(bf16).reshape(-1, width)
    g_out = jnp.dot(tflat.T, d_outproj, preferred_element_type=f32)
    d_tnorm = jnp.dot(d_outproj, w_out.T, preferred_element_type=f32).reshape(rows, cols, width)
    d_tri = norm_back(d_tnorm, tcentred, tinverse, gain_out).astype(bf16)
    d_gatepre = (d_open * opened * (1.0 - opened)).astype(bf16).reshape(-1, width)
    g_gate = jnp.dot(flat.T, d_gatepre, preferred_element_type=f32)
    grad_full = lax.all_gather(d_tri, "col", axis=1, tiled=True)
    d_left = jnp.einsum("ijc,jkc->ikc", grad_full, panel, preferred_element_type=f32)
    d_right = (
        lax.psum_scatter(
            jnp.einsum("ijc,ikc->jkc", grad_full, left, preferred_element_type=f32).astype(
                jnp.bfloat16
            ),
            "row",
            scatter_dimension=0,
            tiled=True,
        ).astype(jnp.float32)
        * inside
    )
    d_gate_a = d_left * pair_mask * value_a * sig_a * (1.0 - sig_a)
    d_value_a = d_left * pair_mask * sig_a
    d_gate_b = d_right * pair_mask * value_b * sig_b * (1.0 - sig_b)
    d_value_b = d_right * pair_mask * sig_b
    d_proj = (
        jnp.concatenate([d_gate_a, d_value_a, d_gate_b, d_value_b], axis=-1)
        .astype(bf16)
        .reshape(-1, 4 * width)
    )
    g_proj = jnp.dot(flat.T, d_proj, preferred_element_type=f32)
    d_normed = jnp.dot(d_proj, w_proj.T, preferred_element_type=f32) + jnp.dot(
        d_gatepre, w_gate.T, preferred_element_type=f32
    )
    d_pair = norm_back(d_normed.reshape(rows, cols, width), centred, inverse, gain_in).astype(bf16)
    sum_proj, sum_gate, sum_out = lax.psum((g_proj, g_gate, g_out), ("row", "col"))
    return (d_pair, sum_proj / crop_len, sum_gate / crop_len, sum_out / crop_len)


SUB = 16
PART = 16
HALF = 64
WIDTH = 128
LANES = SUB * HALF
GROUP = 16
NT = (((1,), (1,)), ((), ()))
NN = (((1,), (0,)), ((), ()))
TN = (((0,), (0,)), ((), ()))
F32 = jnp.float32
BF16 = jnp.bfloat16


def mm(a, b, dims):
    return lax.dot_general(a, b, dims, preferred_element_type=F32)


def params():
    return pltpu.CompilerParams(vmem_limit_bytes=16 * 1024 * 1024)


def cost(flops, size, exps=0):
    return pl.CostEstimate(flops=flops, bytes_accessed=size, transcendentals=exps)


def first_half(rows):
    return lax.broadcasted_iota(jnp.int32, (rows, WIDTH), 1) < HALF


def swap_halves(a, b):
    first = first_half(HALF)
    return (
        jnp.where(first, a, pltpu.roll(b, HALF, 1)),
        jnp.where(first, pltpu.roll(a, HALF, 1), b),
    )


def eye():
    row = lax.broadcasted_iota(jnp.int32, (WIDTH, WIDTH), 0)
    lane = lax.broadcasted_iota(jnp.int32, (WIDTH, WIDTH), 1)
    return (row == lane).astype(F32).astype(BF16)


def to_channels(cells):
    return mm(eye(), cells, NT)


def to_cells(channels):
    return mm(channels, eye(), TN)


def stage_rows(channels, buf):
    for t in range(SUB // 2):
        part = channels[:, t * WIDTH : (t + 1) * WIDTH]
        one, two = swap_halves(part[:HALF], part[HALF:])
        buf[(2 * t) * HALF : (2 * t + 1) * HALF, :] = one
        buf[(2 * t + 1) * HALF : (2 * t + 2) * HALF, :] = two


def panel_row(buf, p):
    return buf[pl.ds(p, SUB, stride=HALF), :]


def channels_of(panels, buf, out):
    buf[...] = panels.reshape(LANES, WIDTH)
    for t in range(SUB // 2):
        one = buf[pl.ds(2 * t, HALF, stride=SUB), :]
        two = buf[pl.ds(2 * t + 1, HALF, stride=SUB), :]
        low, high = swap_halves(one, two)
        out[:HALF, t * WIDTH : (t + 1) * WIDTH] = low
        out[HALF:, t * WIDTH : (t + 1) * WIDTH] = high
    return out[...]


def norm_channels(values, gain):
    center = jnp.mean(values, axis=0, keepdims=True)
    spread = jnp.mean((values - center) ** 2, axis=0, keepdims=True)
    inverse = lax.rsqrt(spread + EPS)
    centred = (values - center) * inverse
    return centred * gain, centred, inverse


def norm_back_channels(upstream, centred, inverse, gain):
    scaled = upstream * gain
    first = jnp.mean(scaled, axis=0, keepdims=True)
    second = jnp.mean(scaled * centred, axis=0, keepdims=True)
    return inverse * (scaled - first - centred * second)


def column(row):
    at = lax.broadcasted_iota(jnp.int32, (WIDTH, WIDTH), 0)
    lane = lax.broadcasted_iota(jnp.int32, (WIDTH, WIDTH), 1)
    return jnp.sum(jnp.where(at == lane, row, 0.0), axis=1, keepdims=True)


def mask_lanes(token_ref, s):
    valid = jnp.sum(token_ref[...].astype(F32), axis=1, keepdims=True)
    lane = lax.broadcasted_iota(jnp.int32, (1, LANES), 1)
    row = lane // HALF + (lax.axis_index("row") * HALF + s * SUB)
    col = lane % HALF + lax.axis_index("col") * HALF
    return (jnp.maximum(row, col).astype(F32) < valid).astype(F32)


def bound_lanes(exponent_ref):
    bound = 448.0 * jnp.exp2(exponent_ref[...].astype(F32))
    return jnp.concatenate([bound[i : i + 1] for i in range(SUB)], axis=1)


def normed_cells(x_ref, gain_ref):
    gain = column(gain_ref[...])
    normed, centred, inverse = norm_channels(to_channels(x_ref[...].reshape(LANES, WIDTH)), gain)
    return normed.astype(BF16), centred, inverse, gain


def right_kernel(at, x_ref, gain_ref, w_ref, token_ref, exponent_ref, out_ref, buf):
    normed = normed_cells(x_ref, gain_ref)[0]
    proj = mm(w_ref[...], normed, TN)
    raw = mask_lanes(token_ref, at + pl.program_id(0)) * jax.nn.sigmoid(proj[:WIDTH]) * proj[WIDTH:]
    bound = bound_lanes(exponent_ref)
    stage_rows(jnp.clip(raw, -bound, bound), buf)
    for p in range(HALF):
        out_ref[p] = panel_row(buf, p).astype(BF16)


def left_kernel(x_ref, gain_ref, w_ref, token_ref, out_ref, buf):
    normed = normed_cells(x_ref, gain_ref)[0]
    proj = mm(w_ref[...], normed, TN)
    mask = mask_lanes(token_ref, pl.program_id(0))
    stage_rows(mask * jax.nn.sigmoid(proj[:WIDTH]) * proj[WIDTH:], buf)
    first = first_half(SUB)
    for p in range(HALF):
        row = panel_row(buf, p)
        out_ref[p, 0] = jnp.where(first, row, 0.0).astype(BF16)
        out_ref[p, 1] = jnp.where(first, 0.0, row).astype(BF16)


def tri_kernel(s0, s1, s2, s3, left_ref, keep_ref, near_ref, send_ref, panel_ref):
    z, q = lax.axis_index("row"), lax.axis_index("col")
    for m, ref in enumerate((s0, s1, s2, s3)):
        place = ((z ^ (z >> 1)) - m + 4) & 3
        other = place ^ (place >> 1) ^ q
        panel_ref[(other & 1) * 2 + (other >> 1)] = ref[...]
    for p in range(GROUP):
        right = jnp.concatenate([panel_ref[r, p] for r in range(4)], axis=0)
        tri = mm(right, left_ref[p].reshape(WIDTH, WIDTH), NT).astype(BF16)
        keep_ref[p] = tri[:SUB]
        near_ref[p] = tri[SUB : 2 * SUB]
        send_ref[0, p] = tri[2 * SUB : 3 * SUB]
        send_ref[1, p] = tri[3 * SUB :]


def mid_kernel(
    a_ref, b_ref, c_ref, x_ref, grad_ref, gain_in_ref, gain_out_ref, gate_ref, out_w_ref,
    g_out_so_far, g_gate_so_far, dtri_ref, dgate_ref, g_out_ref, g_gate_ref, buf, wide,
):
    gain_out = column(gain_out_ref[...])
    tri = channels_of(
        a_ref[...].astype(F32) + b_ref[0].astype(F32) + c_ref[...].astype(F32), buf, wide
    )
    tnorm_f, tcentred, tinverse = norm_channels(tri, gain_out)
    tnorm = tnorm_f.astype(BF16)

    def turned(ref):
        buf[...] = ref[...].astype(F32).reshape(LANES, WIDTH)
        rows = [buf[pl.ds(j, HALF, stride=SUB), :] for j in range(SUB)]
        return to_channels(jnp.concatenate(rows, axis=0).astype(BF16))

    normed = norm_channels(turned(x_ref), column(gain_in_ref[...]))[0].astype(BF16)
    upstream = turned(grad_ref)
    opened = jax.nn.sigmoid(mm(gate_ref[...], normed, TN))
    outproj = mm(out_w_ref[...], tnorm, TN)
    d_open = upstream * outproj
    d_outproj = (upstream * opened).astype(BF16)
    g_out_ref[...] = g_out_so_far[...] + mm(tnorm, d_outproj, NT)
    d_tnorm = mm(out_w_ref[...], d_outproj, NN)
    d_tri = norm_back_channels(d_tnorm, tcentred, tinverse, gain_out)
    d_gatepre = (d_open * opened * (1.0 - opened)).astype(BF16)
    g_gate_ref[...] = g_gate_so_far[...] + mm(normed, d_gatepre, NT)
    stage_rows(d_tri, buf)
    for p in range(HALF):
        dtri_ref[p] = panel_row(buf, p).astype(BF16)
    buf[...] = to_cells(d_gatepre)
    for i in range(HALF):
        dgate_ref[i] = panel_row(buf, i).astype(BF16)


def dright_kernel(*refs):
    *grads_refs, left_ref, p0, p1, p2, p3, held = refs
    z, q = lax.axis_index("row"), lax.axis_index("col")
    for k, ref in enumerate(grads_refs):
        r = k % 4
        block_at = q ^ ((r % 2) * 2 + r // 2)
        slot = ((z ^ (z >> 1)) - (block_at ^ (block_at >> 1)) + 4) & 3
        held[slot, :, (k // 4) * SUB : (k // 4 + 1) * SUB] = ref[...]
    for p in range(GROUP):
        grads = jnp.concatenate([held[m, p] for m in range(4)], axis=0)
        part = mm(grads, left_ref[p].reshape(WIDTH, WIDTH), NN).astype(BF16)
        for m, ref in enumerate((p0, p1, p2, p3)):
            ref[p] = part[m * PART : (m + 1) * PART]


def dleft_kernel(*refs):
    so_far, out_ref = refs[-2:]
    parts = (len(refs) - 2) // 5
    grad_refs, panel_refs = refs[: 4 * parts], refs[4 * parts : 5 * parts]
    first = first_half(HALF)
    for p in range(GROUP):
        grads = jnp.concatenate([d[p] for d in grad_refs], axis=0)
        right = jnp.concatenate([r[q, p] for r in panel_refs for q in range(4)], axis=0)
        both = mm(grads, right, TN)
        out_ref[p] = so_far[p] + jnp.where(first, both[:HALF], both[HALF:])


def gate_grads(upstream, mask, sig, value):
    d_gate = (upstream * mask * value * sig * (1.0 - sig)).astype(BF16)
    d_value = (upstream * mask * sig).astype(BF16)
    return jnp.concatenate([d_gate, d_value], axis=0)


def final_a_kernel(
    x_ref, dleft_ref, token_ref, gain_ref, w_ref, gate_ref, q0, q1, q2, q3, out_ref, g_ref, buf, wide
):
    s = pl.program_id(0)
    normed = normed_cells(x_ref, gain_ref)[0]
    proj = mm(w_ref[...], normed, TN)
    d_left = channels_of(dleft_ref[...], buf, wide)
    d_proj = gate_grads(d_left, mask_lanes(token_ref, s), jax.nn.sigmoid(proj[:WIDTH]), proj[WIDTH:])
    d_gate = jnp.concatenate([q[...] for q in (q0, q1, q2, q3)], axis=1).reshape(LANES, WIDTH)
    out_ref[...] = mm(w_ref[...], d_proj, NN) + mm(gate_ref[...], d_gate, NT)

    @pl.when(s == 0)
    def start():
        g_ref[...] = jnp.zeros_like(g_ref)

    g_ref[...] += mm(normed, d_proj, NT)


def final_b_kernel(
    at, x_ref, part_ref, a_ref, b_ref, token_ref, exponent_ref, gain_ref, w_ref, so_far, into_ref,
    out_ref, g_ref, buf, wide,
):
    step = pl.program_id(0)
    normed, centred, inverse, gain = normed_cells(x_ref, gain_ref)
    proj = mm(w_ref[...], normed, TN)
    mask = mask_lanes(token_ref, at + step)
    sig = jax.nn.sigmoid(proj[:WIDTH])
    inside = jnp.abs(mask * sig * proj[WIDTH:]) <= bound_lanes(exponent_ref)
    d_right = channels_of(a_ref[...].astype(F32) + b_ref[...].astype(F32), buf, wide)
    d_proj = gate_grads(jnp.where(inside, d_right, 0.0), mask, sig, proj[WIDTH:])

    @pl.when(step == 0)
    def start():
        g_ref[...] = so_far[...]

    g_ref[...] += mm(normed, d_proj, NT)
    d_normed = part_ref[...] + mm(w_ref[...], d_proj, NN)
    d_pair = norm_back_channels(d_normed, centred, inverse, gain).astype(BF16)
    out_ref[...] = to_cells(d_pair).astype(BF16).reshape(SUB, HALF, WIDTH)


def whole(array):
    return pl.BlockSpec(array.shape, lambda i: (0,) * array.ndim)


def block(shape, at):
    return pl.BlockSpec(shape, lambda i: at)


BUF = pltpu.VMEM((LANES, WIDTH), F32)
WIDE = pltpu.VMEM((WIDTH, LANES), F32)
PANEL = jax.ShapeDtypeStruct((HALF, SUB, WIDTH), BF16)
PANEL_SPEC = pl.BlockSpec((GROUP, SUB, WIDTH), lambda i: (i, 0, 0))
FOUR = jax.ShapeDtypeStruct((4, HALF, SUB, WIDTH), BF16)
FOUR_SPEC = pl.BlockSpec((4, GROUP, SUB, WIDTH), lambda i: (0, i, 0, 0))
TWO = jax.ShapeDtypeStruct((2, HALF, SUB, WIDTH), BF16)
TWO_SPEC = pl.BlockSpec((2, GROUP, SUB, WIDTH), lambda i: (0, i, 0, 0))
LEFT_SPEC = pl.BlockSpec((GROUP, 2, HALF, WIDTH), lambda i: (i, 0, 0, 0))
LONG = jax.ShapeDtypeStruct((HALF, PART, WIDTH), BF16)
LONG_SPEC = pl.BlockSpec((GROUP, PART, WIDTH), lambda i: (i, 0, 0))
WHOLE_PANEL = pl.BlockSpec(PANEL.shape, lambda i: (0, 0, 0))


def right_part(s, pair, gain, w_proj, tokens, exponents):
    steps = PART // SUB
    return pl.pallas_call(
        functools.partial(right_kernel, s * steps),
        grid=(steps,),
        out_shape=LONG,
        in_specs=[
            pl.BlockSpec((SUB, HALF, WIDTH), lambda i: (s * steps + i, 0, 0)),
            whole(gain), block((WIDTH, 2 * WIDTH), (0, 1)), whole(tokens),
            pl.BlockSpec((SUB, HALF), lambda i: (s * steps + i, 0)),
        ],
        out_specs=pl.BlockSpec((HALF, SUB, WIDTH), lambda i: (0, i, 0)),
        scratch_shapes=[BUF],
        compiler_params=params(),
        cost_estimate=cost(8 * LANES * WIDTH * WIDTH, 1 << 20, 2 * LANES * WIDTH),
        name="right_part",
    )(pair, gain, w_proj, tokens, exponents)


def left_part(pair, gain, w_proj, tokens):
    return pl.pallas_call(
        left_kernel,
        grid=(HALF // SUB,),
        out_shape=jax.ShapeDtypeStruct((HALF, 2, HALF, WIDTH), BF16),
        in_specs=[
            pl.BlockSpec((SUB, HALF, WIDTH), lambda i: (i, 0, 0)), whole(gain),
            block((WIDTH, 2 * WIDTH), (0, 0)), whole(tokens),
        ],
        out_specs=pl.BlockSpec((HALF, 2, SUB, WIDTH), lambda i: (0, 0, i, 0)),
        scratch_shapes=[BUF],
        compiler_params=params(),
        cost_estimate=cost(16 * LANES * WIDTH * WIDTH, 3 << 20, 4 * LANES * WIDTH),
        name="left_part",
    )(pair, gain, w_proj, tokens)


def tri_part(at, slots, left):
    return pl.pallas_call(
        tri_kernel,
        grid=(HALF // GROUP,),
        out_shape=(PANEL, PANEL, TWO, FOUR),
        in_specs=[pl.BlockSpec((GROUP, SUB, WIDTH), lambda i: (i, at, 0))] * 4 + [LEFT_SPEC],
        out_specs=(PANEL_SPEC, PANEL_SPEC, TWO_SPEC, FOUR_SPEC),
        compiler_params=params(),
        cost_estimate=cost(2 * HALF * HALF * WIDTH * WIDTH, 5 << 20),
        name="tri_part",
    )(*slots, left)


def mid_part(s, parts, pair, grad, gain_in, gain_out, w_gate, w_out, g_out, g_gate):
    square = jax.ShapeDtypeStruct((WIDTH, WIDTH), F32)
    columns = block((HALF, SUB, WIDTH), (0, s, 0))
    small = [gain_in, gain_out, w_gate, w_out, g_out, g_gate]
    return pl.pallas_call(
        mid_kernel,
        grid=(1,),
        out_shape=(PANEL, pltpu.HBM(PANEL.shape, BF16), square, square),
        in_specs=[WHOLE_PANEL, block((1, HALF, SUB, WIDTH), (0, 0, 0, 0)), WHOLE_PANEL]
        + [columns] * 2
        + [whole(a) for a in small],
        out_specs=(WHOLE_PANEL, WHOLE_PANEL, block(square.shape, (0, 0)), block(square.shape, (0, 0))),
        scratch_shapes=[BUF, WIDE],
        compiler_params=params(),
        cost_estimate=cost(12 * LANES * WIDTH * WIDTH, 2 << 20, LANES * WIDTH),
        name="mid_part",
    )(*parts, pair, grad, *small)


def dright_part(blocks, left):
    return pl.pallas_call(
        dright_kernel,
        grid=(HALF // GROUP,),
        out_shape=(pltpu.HBM(LONG.shape, BF16), LONG, LONG, LONG),
        in_specs=[PANEL_SPEC] * len(blocks) + [LEFT_SPEC],
        out_specs=(LONG_SPEC,) * 4,
        scratch_shapes=[pltpu.VMEM((4, GROUP, PART, WIDTH), BF16)],
        compiler_params=params(),
        cost_estimate=cost(4 * HALF * HALF * WIDTH * WIDTH, 6 << 20),
        name="dright_part",
    )(*blocks, left)


def dleft_part(grads, panels, so_far):
    rows = pl.BlockSpec((GROUP, HALF, WIDTH), lambda i: (i, 0, 0))
    return pl.pallas_call(
        dleft_kernel,
        grid=(HALF // GROUP,),
        out_shape=jax.ShapeDtypeStruct((HALF, HALF, WIDTH), F32),
        in_specs=[PANEL_SPEC] * len(grads) + [FOUR_SPEC] * len(panels) + [rows],
        out_specs=rows,
        compiler_params=params(),
        cost_estimate=cost(4 * HALF * HALF * WIDTH * WIDTH, 8 << 20),
        name="dleft_part",
    )(*grads, *panels, so_far)


def final_a_part(pair, dleft, tokens, gain, w_proj, w_gate, gates):
    return pl.pallas_call(
        final_a_kernel,
        grid=(HALF // SUB,),
        out_shape=(
            jax.ShapeDtypeStruct((WIDTH, HALF * HALF), F32),
            jax.ShapeDtypeStruct((WIDTH, 2 * WIDTH), F32),
        ),
        in_specs=[
            pl.BlockSpec((SUB, HALF, WIDTH), lambda i: (i, 0, 0)),
            pl.BlockSpec((HALF, SUB, WIDTH), lambda i: (0, i, 0)),
            whole(tokens), whole(gain), block((WIDTH, 2 * WIDTH), (0, 0)), whole(w_gate),
        ]
        + [pl.BlockSpec((SUB, SUB, WIDTH), lambda i: (i, 0, 0))] * 4,
        out_specs=(
            pl.BlockSpec((WIDTH, LANES), lambda i: (0, i)),
            block((WIDTH, 2 * WIDTH), (0, 0)),
        ),
        scratch_shapes=[BUF, WIDE],
        compiler_params=params(),
        cost_estimate=cost(56 * LANES * WIDTH * WIDTH, 8 << 20, 4 * LANES * WIDTH),
        name="final_a_part",
    )(pair, dleft, tokens, gain, w_proj, w_gate, *gates)


def final_b_part(s, pair, part, sums, tokens, exponents, gain, w_proj, so_far, into):
    steps = PART // SUB
    rows = pl.BlockSpec((SUB, HALF, WIDTH), lambda i: (s * steps + i, 0, 0))
    panel = pl.BlockSpec((HALF, SUB, WIDTH), lambda i: (0, i, 0))
    return pl.pallas_call(
        functools.partial(final_b_kernel, s * steps),
        grid=(steps,),
        out_shape=(
            jax.ShapeDtypeStruct((HALF, HALF, WIDTH), BF16),
            jax.ShapeDtypeStruct((WIDTH, 2 * WIDTH), F32),
        ),
        in_specs=[
            rows,
            pl.BlockSpec((WIDTH, LANES), lambda i: (0, s * steps + i)),
            panel, panel, whole(tokens),
            pl.BlockSpec((SUB, HALF), lambda i: (s * steps + i, 0)),
            whole(gain), block((WIDTH, 2 * WIDTH), (0, 1)), whole(so_far),
            pl.BlockSpec(memory_space=pl.ANY),
        ],
        out_specs=(rows, block((WIDTH, 2 * WIDTH), (0, 0))),
        scratch_shapes=[BUF, WIDE],
        input_output_aliases={9: 0} if into.shape == pair.shape else {},
        compiler_params=params(),
        cost_estimate=cost(28 * LANES * WIDTH * WIDTH, 4 << 20, 2 * LANES * WIDTH),
        name="final_b_part",
    )(pair, part, *sums, tokens, exponents, gain, w_proj, so_far, into)


def after(array, *others):
    return lax.optimization_barrier((array, *others))[0]


def blocked(pair_tiles, grad_out, exponents, token_mask, gain_in, w_proj, w_gate, gain_out, w_out):
    width = pair_tiles.shape[-1]
    crop_len = token_mask.shape[0]
    core = lax.axis_index("col") % 2
    tokens = token_mask.reshape(1, crop_len)
    gain_in = gain_in.reshape(1, width)
    gain_out = gain_out.reshape(1, width)

    def forward(a):
        return lax.ppermute(a, "row", [(0, 1), (1, 3), (3, 2), (2, 0)])

    def over_row(a, bit):
        return lax.ppermute(a, "row", [(k, k ^ bit) for k in range(4)])

    def over_x(a):
        return lax.ppermute(a, "col", [(k, k ^ 2) for k in range(4)])

    def over_core(a):
        return lax.ppermute(a, "col", [(k, k ^ 1) for k in range(4)])

    def plus(a, b):
        return (a.astype(F32) + b.astype(F32)).astype(BF16)

    def in_hbm(*arrays):
        return [pltpu.with_memory_space_constraint(a, pltpu.HBM) for a in arrays]

    def right(s):
        return right_part(s, *in_hbm(pair_tiles, gain_in, w_proj, tokens, exponents))

    a0, b0 = right(0), right(1)
    left = left_part(*in_hbm(pair_tiles, gain_in, w_proj, tokens))
    a1, b1 = forward(a0), forward(b0)
    a2, b2 = forward(a1), forward(after(b1, left))
    c0, d0 = right(2), right(3)
    a3, b3 = forward(after(a2, c0)), forward(after(b2, d0))
    c1, d1 = forward(after(c0, b2)), forward(after(d0, a3))

    def triangle(slots):
        keep, near, send, panel = tri_part(0, slots, left)
        got = over_core(send)
        return keep, got, plus(near, got[1]), panel

    g_out = g_gate = jnp.zeros((width, width), F32)

    def middle(s, tri, mine):
        return mid_part(
            s, (tri[0], tri[1], mine), pair_tiles, grad_out, gain_in, gain_out, w_gate, w_out, g_out, g_gate
        )

    def spread(d_tri):
        far = over_x(d_tri)
        return [d_tri, far, over_core(d_tri), over_core(far)]

    def dright(blocks, *others):
        return dright_part([blocks[0], blocks[1], blocks[2], after(blocks[3], *others)], left)

    tri_a, tri_b = triangle([a0, a1, a2, a3]), triangle([b0, b1, b2, b3])
    x_a, x_b = over_x(tri_a[2]), over_x(tri_b[2])
    c2, d2 = forward(after(c1, tri_a[2])), forward(after(d1, tri_b[2]))
    dtri_a, gate_a, g_out, g_gate = middle(0, tri_a, after(x_a, d1))
    blocks_a = spread(dtri_a)
    dtri_b, gate_b, g_out, g_gate = middle(1, tri_b, after(x_b, c2))
    blocks_b = spread(dtri_b)
    c3, d3 = forward(after(c2, dtri_a)), forward(after(d2, dtri_b))
    part_a = dright(blocks_a, d2)
    part_b = dright(blocks_b, c3)
    r_a, r_b = forward(part_a[1]), forward(part_b[1])

    tri_c = triangle([c0, c1, c2, after(c3, part_a[1])])
    tri_d = triangle([d0, d1, d2, after(d3, part_b[1])])
    x_c, x_d = over_x(tri_c[2]), over_x(tri_d[2])
    r_a = plus(r_a, part_a[2])
    r_a2 = forward(after(r_a, tri_c[2]))
    r_b = plus(r_b, part_b[2])
    r_b2 = forward(after(r_b, tri_d[2]))
    d_left = dleft_part(
        [after(blocks_a[0], tri_d[2])] + blocks_a[1:] + blocks_b,
        [tri_a[3], tri_b[3]],
        jnp.zeros((HALF, HALF, WIDTH), F32),
    )
    dtri_c, gate_c, g_out, g_gate = middle(2, tri_c, after(x_c, r_a, d_left))
    blocks_c = spread(dtri_c)
    dtri_d, gate_d, g_out, g_gate = middle(3, tri_d, after(x_d, r_b))
    blocks_d = spread(dtri_d)
    r_a2 = plus(r_a2, part_a[3])
    r_a3 = forward(after(r_a2, dtri_c))
    r_b2 = plus(r_b2, part_b[3])
    r_b3 = forward(after(r_b2, dtri_d))
    part_c = dright(blocks_c, r_a2)
    part_d = dright(blocks_d, r_b2, r_a3)

    zero = jnp.zeros((width, 2 * width), F32)

    def final(s, sums, so_far, into):
        return final_b_part(
            s, pair_tiles, partial, sums, tokens, exponents, gain_in, w_proj, so_far, into
        )

    r_c, r_d = forward(part_c[1]), forward(part_d[1])
    d_left = dleft_part(
        [after(blocks_c[0], part_d[1])] + blocks_c[1:] + blocks_d, [tri_c[3], tri_d[3]], d_left
    )
    r_c = forward(plus(r_c, after(part_c[2], d_left)))
    r_d = plus(r_d, after(part_d[2], d_left))
    partial, g_a = final_a_part(
        pair_tiles, after(d_left, r_d), tokens, gain_in, w_proj, w_gate, [gate_a, gate_b, gate_c, gate_d]
    )
    r_d = forward(r_d)
    r_c = plus(r_c, after(part_c[3], g_a))
    d_pair, g_first = final(0, (part_a[0], after(r_a3, r_c)), zero, gain_in)
    r_c = forward(r_c)
    r_d = plus(r_d, after(part_d[3], g_first))
    d_pair, g_first = final(1, (part_b[0], after(r_b3, r_d)), g_first, d_pair)
    r_d = forward(r_d)
    d_pair, g_last = final(2, (part_c[0], r_c), g_first, d_pair)
    d_pair, g_last = final(3, (part_d[0], r_d), g_last, d_pair)

    sums = jnp.concatenate([g_out, g_gate, g_a, g_last], axis=1)
    half = width // 2
    sums = lax.dynamic_slice_in_dim(sums, core * half, half) + over_core(
        lax.dynamic_slice_in_dim(sums, (1 - core) * half, half)
    )
    for send in (over_x, lambda a: over_row(a, 1), lambda a: over_row(a, 2)):
        mine = sums.astype(BF16)
        sums = mine.astype(F32) + send(mine).astype(F32)
    sums = sums / crop_len
    theirs = over_core(sums)
    sums = jnp.concatenate(
        [jnp.where(core == 0, sums, theirs), jnp.where(core == 0, theirs, sums)], axis=0
    )
    return d_pair, sums[:, 2 * width :], sums[:, width : 2 * width], sums[:, :width]


def local(pair_tiles, *rest, rows_over, cols_over):
    if pair_tiles.shape == (HALF, HALF, WIDTH) and rows_over == cols_over == 4:
        return blocked(pair_tiles, *rest)
    return plain(pair_tiles, *rest)


def solution(mesh):
    return jax.shard_map(
        functools.partial(local, rows_over=mesh.shape["row"], cols_over=mesh.shape["col"]),
        mesh=mesh,
        in_specs=(
            P(("crop", "row"), "col", None),
            P(("crop", "row"), "col", None),
            P(("crop", "row"), "col"),
            P("crop"),
            P(),
            P(),
            P(),
            P(),
            P(),
        ),
        out_specs=(
            P(("crop", "row"), "col", None),
            P("crop", None),
            P("crop", None),
            P("crop", None),
        ),
        check_vma=False,
    )
```

```python
import functools

import jax
import jax.numpy as jnp
from jax import lax
from jax.experimental import pallas as pl
from jax.experimental.pallas import tpu as pltpu
from jax.sharding import PartitionSpec as P

EPS = 1e-05


def layer_norm(values, gain):
    center = jnp.mean(values, axis=-1, keepdims=True)
    spread = jnp.mean((values - center) ** 2, axis=-1, keepdims=True)
    inverse = lax.rsqrt(spread + EPS)
    centred = (values - center) * inverse
    return (centred * gain, centred, inverse)


def norm_back(upstream, centred, inverse, gain):
    scaled = upstream * gain
    first = jnp.mean(scaled, axis=-1, keepdims=True)
    second = jnp.mean(scaled * centred, axis=-1, keepdims=True)
    return inverse * (scaled - first - centred * second)


def plain(pair_tiles, grad_out, exponents, token_mask, gain_in, w_proj, w_gate, gain_out, w_out):
    f32 = jnp.float32
    bf16 = jnp.bfloat16
    rows, cols, width = pair_tiles.shape
    crop_len = token_mask.shape[0]
    row_at = lax.axis_index("row")
    col_at = lax.axis_index("col")
    maskf = token_mask.astype(f32)
    mask_rows = lax.dynamic_slice_in_dim(maskf, row_at * rows, rows)
    mask_cols = lax.dynamic_slice_in_dim(maskf, col_at * cols, cols)
    pair_mask = (mask_rows[:, None] * mask_cols[None, :])[..., None]
    normed_f, centred, inverse = layer_norm(pair_tiles.astype(f32), gain_in)
    normed = normed_f.astype(bf16)
    flat = normed.reshape(-1, width)
    projected = jnp.dot(flat, w_proj, preferred_element_type=f32).reshape(rows, cols, 4 * width)
    gate_a = projected[..., :width]
    value_a = projected[..., width : 2 * width]
    gate_b = projected[..., 2 * width : 3 * width]
    value_b = projected[..., 3 * width :]
    sig_a = jax.nn.sigmoid(gate_a)
    sig_b = jax.nn.sigmoid(gate_b)
    left = (pair_mask * sig_a * value_a).astype(bf16)
    right_raw = pair_mask * sig_b * value_b
    bound = (448.0 * jnp.exp2(exponents.astype(f32)))[..., None]
    right = jnp.clip(right_raw, -bound, bound).astype(bf16)
    inside = (jnp.abs(right_raw) <= bound).astype(f32)
    panel = lax.all_gather(right, "row", axis=0, tiled=True)
    tri_cols = lax.psum_scatter(
        jnp.einsum("jkc,ikc->jic", panel, left, preferred_element_type=f32).astype(jnp.bfloat16),
        "col",
        scatter_dimension=0,
        tiled=True,
    ).astype(jnp.float32)
    tri = jnp.transpose(tri_cols, (1, 0, 2))
    tnorm_f, tcentred, tinverse = layer_norm(tri, gain_out)
    tnorm = tnorm_f.astype(bf16)
    tflat = tnorm.reshape(-1, width)
    opened = jax.nn.sigmoid(jnp.dot(flat, w_gate, preferred_element_type=f32)).reshape(
        rows, cols, width
    )
    outproj = jnp.dot(tflat, w_out, preferred_element_type=f32).reshape(rows, cols, width)
    upstream = grad_out.astype(f32)
    d_open = upstream * outproj
    d_outproj = (upstream * opened).astype(bf16).reshape(-1, width)
    g_out = jnp.dot(tflat.T, d_outproj, preferred_element_type=f32)
    d_tnorm = jnp.dot(d_outproj, w_out.T, preferred_element_type=f32).reshape(rows, cols, width)
    d_tri = norm_back(d_tnorm, tcentred, tinverse, gain_out).astype(bf16)
    d_gatepre = (d_open * opened * (1.0 - opened)).astype(bf16).reshape(-1, width)
    g_gate = jnp.dot(flat.T, d_gatepre, preferred_element_type=f32)
    grad_full = lax.all_gather(d_tri, "col", axis=1, tiled=True)
    d_left = jnp.einsum("ijc,jkc->ikc", grad_full, panel, preferred_element_type=f32)
    d_right = (
        lax.psum_scatter(
            jnp.einsum("ijc,ikc->jkc", grad_full, left, preferred_element_type=f32).astype(
                jnp.bfloat16
            ),
            "row",
            scatter_dimension=0,
            tiled=True,
        ).astype(jnp.float32)
        * inside
    )
    d_gate_a = d_left * pair_mask * value_a * sig_a * (1.0 - sig_a)
    d_value_a = d_left * pair_mask * sig_a
    d_gate_b = d_right * pair_mask * value_b * sig_b * (1.0 - sig_b)
    d_value_b = d_right * pair_mask * sig_b
    d_proj = (
        jnp.concatenate([d_gate_a, d_value_a, d_gate_b, d_value_b], axis=-1)
        .astype(bf16)
        .reshape(-1, 4 * width)
    )
    g_proj = jnp.dot(flat.T, d_proj, preferred_element_type=f32)
    d_normed = jnp.dot(d_proj, w_proj.T, preferred_element_type=f32) + jnp.dot(
        d_gatepre, w_gate.T, preferred_element_type=f32
    )
    d_pair = norm_back(d_normed.reshape(rows, cols, width), centred, inverse, gain_in).astype(bf16)
    sum_proj, sum_gate, sum_out = lax.psum((g_proj, g_gate, g_out), ("row", "col"))
    return (d_pair, sum_proj / crop_len, sum_gate / crop_len, sum_out / crop_len)


SUB = 16
PART = 16
HALF = 64
WIDTH = 128
LANES = SUB * HALF
GROUP = 16
NT = (((1,), (1,)), ((), ()))
NN = (((1,), (0,)), ((), ()))
TN = (((0,), (0,)), ((), ()))
F32 = jnp.float32
BF16 = jnp.bfloat16


def mm(a, b, dims):
    return lax.dot_general(a, b, dims, preferred_element_type=F32)


def params():
    return pltpu.CompilerParams(vmem_limit_bytes=16 * 1024 * 1024)


def cost(flops, size, exps=0):
    return pl.CostEstimate(flops=flops, bytes_accessed=size, transcendentals=exps)


def first_half(rows):
    return lax.broadcasted_iota(jnp.int32, (rows, WIDTH), 1) < HALF


def swap_halves(a, b):
    first = first_half(HALF)
    return (
        jnp.where(first, a, pltpu.roll(b, HALF, 1)),
        jnp.where(first, pltpu.roll(a, HALF, 1), b),
    )


def eye():
    row = lax.broadcasted_iota(jnp.int32, (WIDTH, WIDTH), 0)
    lane = lax.broadcasted_iota(jnp.int32, (WIDTH, WIDTH), 1)
    return (row == lane).astype(F32).astype(BF16)


def to_channels(cells):
    return mm(eye(), cells, NT)


def to_cells(channels):
    return mm(channels, eye(), TN)


def stage_rows(channels, buf):
    for t in range(SUB // 2):
        part = channels[:, t * WIDTH : (t + 1) * WIDTH]
        one, two = swap_halves(part[:HALF], part[HALF:])
        buf[(2 * t) * HALF : (2 * t + 1) * HALF, :] = one
        buf[(2 * t + 1) * HALF : (2 * t + 2) * HALF, :] = two


def panel_row(buf, p):
    return buf[pl.ds(p, SUB, stride=HALF), :]


def channels_of(panels, buf, out):
    buf[...] = panels.reshape(LANES, WIDTH)
    for t in range(SUB // 2):
        one = buf[pl.ds(2 * t, HALF, stride=SUB), :]
        two = buf[pl.ds(2 * t + 1, HALF, stride=SUB), :]
        low, high = swap_halves(one, two)
        out[:HALF, t * WIDTH : (t + 1) * WIDTH] = low
        out[HALF:, t * WIDTH : (t + 1) * WIDTH] = high
    return out[...]


def norm_channels(values, gain):
    center = jnp.mean(values, axis=0, keepdims=True)
    spread = jnp.mean((values - center) ** 2, axis=0, keepdims=True)
    inverse = lax.rsqrt(spread + EPS)
    centred = (values - center) * inverse
    return centred * gain, centred, inverse


def norm_back_channels(upstream, centred, inverse, gain):
    scaled = upstream * gain
    first = jnp.mean(scaled, axis=0, keepdims=True)
    second = jnp.mean(scaled * centred, axis=0, keepdims=True)
    return inverse * (scaled - first - centred * second)


def column(row):
    at = lax.broadcasted_iota(jnp.int32, (WIDTH, WIDTH), 0)
    lane = lax.broadcasted_iota(jnp.int32, (WIDTH, WIDTH), 1)
    return jnp.sum(jnp.where(at == lane, row, 0.0), axis=1, keepdims=True)


def mask_lanes(token_ref, s):
    valid = jnp.sum(token_ref[...].astype(F32), axis=1, keepdims=True)
    lane = lax.broadcasted_iota(jnp.int32, (1, LANES), 1)
    row = lane // HALF + (lax.axis_index("row") * HALF + s * SUB)
    col = lane % HALF + lax.axis_index("col") * HALF
    return (jnp.maximum(row, col).astype(F32) < valid).astype(F32)


def bound_lanes(exponent_ref):
    bound = 448.0 * jnp.exp2(exponent_ref[...].astype(F32))
    return jnp.concatenate([bound[i : i + 1] for i in range(SUB)], axis=1)


def normed_cells(x_ref, gain_ref):
    gain = column(gain_ref[...])
    normed, centred, inverse = norm_channels(to_channels(x_ref[...].reshape(LANES, WIDTH)), gain)
    return normed.astype(BF16), centred, inverse, gain


def right_kernel(at, x_ref, gain_ref, w_ref, token_ref, exponent_ref, out_ref, buf):
    normed = normed_cells(x_ref, gain_ref)[0]
    proj = mm(w_ref[...], normed, TN)
    raw = mask_lanes(token_ref, at + pl.program_id(0)) * jax.nn.sigmoid(proj[:WIDTH]) * proj[WIDTH:]
    bound = bound_lanes(exponent_ref)
    stage_rows(jnp.clip(raw, -bound, bound), buf)
    for p in range(HALF):
        out_ref[p] = panel_row(buf, p).astype(BF16)


def left_kernel(x_ref, gain_ref, w_ref, token_ref, out_ref, buf):
    normed = normed_cells(x_ref, gain_ref)[0]
    proj = mm(w_ref[...], normed, TN)
    mask = mask_lanes(token_ref, pl.program_id(0))
    stage_rows(mask * jax.nn.sigmoid(proj[:WIDTH]) * proj[WIDTH:], buf)
    first = first_half(SUB)
    for p in range(HALF):
        row = panel_row(buf, p)
        out_ref[p, 0] = jnp.where(first, row, 0.0).astype(BF16)
        out_ref[p, 1] = jnp.where(first, 0.0, row).astype(BF16)


def tri_kernel(s0, s1, s2, s3, left_ref, keep_ref, near_ref, send_ref, panel_ref):
    z, q = lax.axis_index("row"), lax.axis_index("col")
    for m, ref in enumerate((s0, s1, s2, s3)):
        place = ((z ^ (z >> 1)) - m + 4) & 3
        other = place ^ (place >> 1) ^ q
        panel_ref[(other & 1) * 2 + (other >> 1)] = ref[...]
    for p in range(GROUP):
        right = jnp.concatenate([panel_ref[r, p] for r in range(4)], axis=0)
        tri = mm(right, left_ref[p].reshape(WIDTH, WIDTH), NT).astype(BF16)
        keep_ref[p] = tri[:SUB]
        near_ref[p] = tri[SUB : 2 * SUB]
        send_ref[0, p] = tri[2 * SUB : 3 * SUB]
        send_ref[1, p] = tri[3 * SUB :]


def mid_kernel(
    a_ref, b_ref, c_ref, x_ref, grad_ref, gain_in_ref, gain_out_ref, gate_ref, out_w_ref,
    g_out_so_far, g_gate_so_far, dtri_ref, dgate_ref, g_out_ref, g_gate_ref, buf, wide,
):
    gain_out = column(gain_out_ref[...])
    tri = channels_of(
        a_ref[...].astype(F32) + b_ref[0].astype(F32) + c_ref[...].astype(F32), buf, wide
    )
    tnorm_f, tcentred, tinverse = norm_channels(tri, gain_out)
    tnorm = tnorm_f.astype(BF16)

    def turned(ref):
        buf[...] = ref[...].astype(F32).reshape(LANES, WIDTH)
        rows = [buf[pl.ds(j, HALF, stride=SUB), :] for j in range(SUB)]
        return to_channels(jnp.concatenate(rows, axis=0).astype(BF16))

    normed = norm_channels(turned(x_ref), column(gain_in_ref[...]))[0].astype(BF16)
    upstream = turned(grad_ref)
    opened = jax.nn.sigmoid(mm(gate_ref[...], normed, TN))
    outproj = mm(out_w_ref[...], tnorm, TN)
    d_open = upstream * outproj
    d_outproj = (upstream * opened).astype(BF16)
    g_out_ref[...] = g_out_so_far[...] + mm(tnorm, d_outproj, NT)
    d_tnorm = mm(out_w_ref[...], d_outproj, NN)
    d_tri = norm_back_channels(d_tnorm, tcentred, tinverse, gain_out)
    d_gatepre = (d_open * opened * (1.0 - opened)).astype(BF16)
    g_gate_ref[...] = g_gate_so_far[...] + mm(normed, d_gatepre, NT)
    stage_rows(d_tri, buf)
    for p in range(HALF):
        dtri_ref[p] = panel_row(buf, p).astype(BF16)
    buf[...] = to_cells(d_gatepre)
    for i in range(HALF):
        dgate_ref[i] = panel_row(buf, i).astype(BF16)


def dright_kernel(*refs):
    *grads_refs, left_ref, p0, p1, p2, p3, held = refs
    z, q = lax.axis_index("row"), lax.axis_index("col")
    for k, ref in enumerate(grads_refs):
        r = k % 4
        block_at = q ^ ((r % 2) * 2 + r // 2)
        slot = ((z ^ (z >> 1)) - (block_at ^ (block_at >> 1)) + 4) & 3
        held[slot, :, (k // 4) * SUB : (k // 4 + 1) * SUB] = ref[...]
    for p in range(GROUP):
        grads = jnp.concatenate([held[m, p] for m in range(4)], axis=0)
        part = mm(grads, left_ref[p].reshape(WIDTH, WIDTH), NN).astype(BF16)
        for m, ref in enumerate((p0, p1, p2, p3)):
            ref[p] = part[m * PART : (m + 1) * PART]


def dleft_kernel(*refs):
    so_far, out_ref = refs[-2:]
    parts = (len(refs) - 2) // 5
    grad_refs, panel_refs = refs[: 4 * parts], refs[4 * parts : 5 * parts]
    first = first_half(HALF)
    for p in range(GROUP):
        grads = jnp.concatenate([d[p] for d in grad_refs], axis=0)
        right = jnp.concatenate([r[q, p] for r in panel_refs for q in range(4)], axis=0)
        both = mm(grads, right, TN)
        out_ref[p] = so_far[p] + jnp.where(first, both[:HALF], both[HALF:])


def gate_grads(upstream, mask, sig, value):
    d_gate = (upstream * mask * value * sig * (1.0 - sig)).astype(BF16)
    d_value = (upstream * mask * sig).astype(BF16)
    return jnp.concatenate([d_gate, d_value], axis=0)


def final_a_kernel(
    x_ref, dleft_ref, token_ref, gain_ref, w_ref, gate_ref, q0, q1, q2, q3, out_ref, g_ref, buf, wide
):
    s = pl.program_id(0)
    normed = normed_cells(x_ref, gain_ref)[0]
    proj = mm(w_ref[...], normed, TN)
    d_left = channels_of(dleft_ref[...], buf, wide)
    d_proj = gate_grads(d_left, mask_lanes(token_ref, s), jax.nn.sigmoid(proj[:WIDTH]), proj[WIDTH:])
    d_gate = jnp.concatenate([q[...] for q in (q0, q1, q2, q3)], axis=1).reshape(LANES, WIDTH)
    out_ref[...] = mm(w_ref[...], d_proj, NN) + mm(gate_ref[...], d_gate, NT)

    @pl.when(s == 0)
    def start():
        g_ref[...] = jnp.zeros_like(g_ref)

    g_ref[...] += mm(normed, d_proj, NT)


def final_b_kernel(
    at, x_ref, part_ref, a_ref, b_ref, token_ref, exponent_ref, gain_ref, w_ref, so_far, into_ref,
    out_ref, g_ref, buf, wide,
):
    step = pl.program_id(0)
    normed, centred, inverse, gain = normed_cells(x_ref, gain_ref)
    proj = mm(w_ref[...], normed, TN)
    mask = mask_lanes(token_ref, at + step)
    sig = jax.nn.sigmoid(proj[:WIDTH])
    inside = jnp.abs(mask * sig * proj[WIDTH:]) <= bound_lanes(exponent_ref)
    d_right = channels_of(a_ref[...].astype(F32) + b_ref[...].astype(F32), buf, wide)
    d_proj = gate_grads(jnp.where(inside, d_right, 0.0), mask, sig, proj[WIDTH:])

    @pl.when(step == 0)
    def start():
        g_ref[...] = so_far[...]

    g_ref[...] += mm(normed, d_proj, NT)
    d_normed = part_ref[...] + mm(w_ref[...], d_proj, NN)
    d_pair = norm_back_channels(d_normed, centred, inverse, gain).astype(BF16)
    out_ref[...] = to_cells(d_pair).astype(BF16).reshape(SUB, HALF, WIDTH)


def whole(array):
    return pl.BlockSpec(array.shape, lambda i: (0,) * array.ndim)


def block(shape, at):
    return pl.BlockSpec(shape, lambda i: at)


BUF = pltpu.VMEM((LANES, WIDTH), F32)
WIDE = pltpu.VMEM((WIDTH, LANES), F32)
PANEL = jax.ShapeDtypeStruct((HALF, SUB, WIDTH), BF16)
PANEL_SPEC = pl.BlockSpec((GROUP, SUB, WIDTH), lambda i: (i, 0, 0))
FOUR = jax.ShapeDtypeStruct((4, HALF, SUB, WIDTH), BF16)
FOUR_SPEC = pl.BlockSpec((4, GROUP, SUB, WIDTH), lambda i: (0, i, 0, 0))
TWO = jax.ShapeDtypeStruct((2, HALF, SUB, WIDTH), BF16)
TWO_SPEC = pl.BlockSpec((2, GROUP, SUB, WIDTH), lambda i: (0, i, 0, 0))
LEFT_SPEC = pl.BlockSpec((GROUP, 2, HALF, WIDTH), lambda i: (i, 0, 0, 0))
LONG = jax.ShapeDtypeStruct((HALF, PART, WIDTH), BF16)
LONG_SPEC = pl.BlockSpec((GROUP, PART, WIDTH), lambda i: (i, 0, 0))
WHOLE_PANEL = pl.BlockSpec(PANEL.shape, lambda i: (0, 0, 0))


def right_part(s, pair, gain, w_proj, tokens, exponents):
    steps = PART // SUB
    return pl.pallas_call(
        functools.partial(right_kernel, s * steps),
        grid=(steps,),
        out_shape=LONG,
        in_specs=[
            pl.BlockSpec((SUB, HALF, WIDTH), lambda i: (s * steps + i, 0, 0)),
            whole(gain), block((WIDTH, 2 * WIDTH), (0, 1)), whole(tokens),
            pl.BlockSpec((SUB, HALF), lambda i: (s * steps + i, 0)),
        ],
        out_specs=pl.BlockSpec((HALF, SUB, WIDTH), lambda i: (0, i, 0)),
        scratch_shapes=[BUF],
        compiler_params=params(),
        cost_estimate=cost(8 * LANES * WIDTH * WIDTH, 1 << 20, 2 * LANES * WIDTH),
        name="right_part",
    )(pair, gain, w_proj, tokens, exponents)


def left_part(pair, gain, w_proj, tokens):
    return pl.pallas_call(
        left_kernel,
        grid=(HALF // SUB,),
        out_shape=jax.ShapeDtypeStruct((HALF, 2, HALF, WIDTH), BF16),
        in_specs=[
            pl.BlockSpec((SUB, HALF, WIDTH), lambda i: (i, 0, 0)), whole(gain),
            block((WIDTH, 2 * WIDTH), (0, 0)), whole(tokens),
        ],
        out_specs=pl.BlockSpec((HALF, 2, SUB, WIDTH), lambda i: (0, 0, i, 0)),
        scratch_shapes=[BUF],
        compiler_params=params(),
        cost_estimate=cost(16 * LANES * WIDTH * WIDTH, 3 << 20, 4 * LANES * WIDTH),
        name="left_part",
    )(pair, gain, w_proj, tokens)


def tri_part(at, slots, left):
    return pl.pallas_call(
        tri_kernel,
        grid=(HALF // GROUP,),
        out_shape=(PANEL, PANEL, TWO, FOUR),
        in_specs=[pl.BlockSpec((GROUP, SUB, WIDTH), lambda i: (i, at, 0))] * 4 + [LEFT_SPEC],
        out_specs=(PANEL_SPEC, PANEL_SPEC, TWO_SPEC, FOUR_SPEC),
        compiler_params=params(),
        cost_estimate=cost(2 * HALF * HALF * WIDTH * WIDTH, 5 << 20),
        name="tri_part",
    )(*slots, left)


def mid_part(s, parts, pair, grad, gain_in, gain_out, w_gate, w_out, g_out, g_gate):
    square = jax.ShapeDtypeStruct((WIDTH, WIDTH), F32)
    columns = block((HALF, SUB, WIDTH), (0, s, 0))
    small = [gain_in, gain_out, w_gate, w_out, g_out, g_gate]
    return pl.pallas_call(
        mid_kernel,
        grid=(1,),
        out_shape=(PANEL, pltpu.HBM(PANEL.shape, BF16), square, square),
        in_specs=[WHOLE_PANEL, block((1, HALF, SUB, WIDTH), (0, 0, 0, 0)), WHOLE_PANEL]
        + [columns] * 2
        + [whole(a) for a in small],
        out_specs=(WHOLE_PANEL, WHOLE_PANEL, block(square.shape, (0, 0)), block(square.shape, (0, 0))),
        scratch_shapes=[BUF, WIDE],
        compiler_params=params(),
        cost_estimate=cost(12 * LANES * WIDTH * WIDTH, 2 << 20, LANES * WIDTH),
        name="mid_part",
    )(*parts, pair, grad, *small)


def dright_part(blocks, left):
    return pl.pallas_call(
        dright_kernel,
        grid=(HALF // GROUP,),
        out_shape=(pltpu.HBM(LONG.shape, BF16), LONG, LONG, LONG),
        in_specs=[PANEL_SPEC] * len(blocks) + [LEFT_SPEC],
        out_specs=(LONG_SPEC,) * 4,
        scratch_shapes=[pltpu.VMEM((4, GROUP, PART, WIDTH), BF16)],
        compiler_params=params(),
        cost_estimate=cost(4 * HALF * HALF * WIDTH * WIDTH, 6 << 20),
        name="dright_part",
    )(*blocks, left)


def dleft_part(grads, panels, so_far):
    rows = pl.BlockSpec((GROUP, HALF, WIDTH), lambda i: (i, 0, 0))
    return pl.pallas_call(
        dleft_kernel,
        grid=(HALF // GROUP,),
        out_shape=jax.ShapeDtypeStruct((HALF, HALF, WIDTH), F32),
        in_specs=[PANEL_SPEC] * len(grads) + [FOUR_SPEC] * len(panels) + [rows],
        out_specs=rows,
        compiler_params=params(),
        cost_estimate=cost(4 * HALF * HALF * WIDTH * WIDTH, 8 << 20),
        name="dleft_part",
    )(*grads, *panels, so_far)


def final_a_part(pair, dleft, tokens, gain, w_proj, w_gate, gates):
    return pl.pallas_call(
        final_a_kernel,
        grid=(HALF // SUB,),
        out_shape=(
            jax.ShapeDtypeStruct((WIDTH, HALF * HALF), F32),
            jax.ShapeDtypeStruct((WIDTH, 2 * WIDTH), F32),
        ),
        in_specs=[
            pl.BlockSpec((SUB, HALF, WIDTH), lambda i: (i, 0, 0)),
            pl.BlockSpec((HALF, SUB, WIDTH), lambda i: (0, i, 0)),
            whole(tokens), whole(gain), block((WIDTH, 2 * WIDTH), (0, 0)), whole(w_gate),
        ]
        + [pl.BlockSpec((SUB, SUB, WIDTH), lambda i: (i, 0, 0))] * 4,
        out_specs=(
            pl.BlockSpec((WIDTH, LANES), lambda i: (0, i)),
            block((WIDTH, 2 * WIDTH), (0, 0)),
        ),
        scratch_shapes=[BUF, WIDE],
        compiler_params=params(),
        cost_estimate=cost(56 * LANES * WIDTH * WIDTH, 8 << 20, 4 * LANES * WIDTH),
        name="final_a_part",
    )(pair, dleft, tokens, gain, w_proj, w_gate, *gates)


def final_b_part(s, pair, part, sums, tokens, exponents, gain, w_proj, so_far, into):
    steps = PART // SUB
    rows = pl.BlockSpec((SUB, HALF, WIDTH), lambda i: (s * steps + i, 0, 0))
    panel = pl.BlockSpec((HALF, SUB, WIDTH), lambda i: (0, i, 0))
    return pl.pallas_call(
        functools.partial(final_b_kernel, s * steps),
        grid=(steps,),
        out_shape=(
            jax.ShapeDtypeStruct((HALF, HALF, WIDTH), BF16),
            jax.ShapeDtypeStruct((WIDTH, 2 * WIDTH), F32),
        ),
        in_specs=[
            rows,
            pl.BlockSpec((WIDTH, LANES), lambda i: (0, s * steps + i)),
            panel, panel, whole(tokens),
            pl.BlockSpec((SUB, HALF), lambda i: (s * steps + i, 0)),
            whole(gain), block((WIDTH, 2 * WIDTH), (0, 1)), whole(so_far),
            pl.BlockSpec(memory_space=pl.ANY),
        ],
        out_specs=(rows, block((WIDTH, 2 * WIDTH), (0, 0))),
        scratch_shapes=[BUF, WIDE],
        input_output_aliases={9: 0} if into.shape == pair.shape else {},
        compiler_params=params(),
        cost_estimate=cost(28 * LANES * WIDTH * WIDTH, 4 << 20, 2 * LANES * WIDTH),
        name="final_b_part",
    )(pair, part, *sums, tokens, exponents, gain, w_proj, so_far, into)


def after(array, *others):
    return lax.optimization_barrier((array, *others))[0]


def blocked(pair_tiles, grad_out, exponents, token_mask, gain_in, w_proj, w_gate, gain_out, w_out):
    width = pair_tiles.shape[-1]
    crop_len = token_mask.shape[0]
    core = lax.axis_index("col") % 2
    tokens = token_mask.reshape(1, crop_len)
    gain_in = gain_in.reshape(1, width)
    gain_out = gain_out.reshape(1, width)

    def forward(a):
        return lax.ppermute(a, "row", [(0, 1), (1, 3), (3, 2), (2, 0)])

    def over_row(a, bit):
        return lax.ppermute(a, "row", [(k, k ^ bit) for k in range(4)])

    def over_x(a):
        return lax.ppermute(a, "col", [(k, k ^ 2) for k in range(4)])

    def over_core(a):
        return lax.ppermute(a, "col", [(k, k ^ 1) for k in range(4)])

    def plus(a, b):
        return (a.astype(F32) + b.astype(F32)).astype(BF16)

    def in_hbm(*arrays):
        return [pltpu.with_memory_space_constraint(a, pltpu.HBM) for a in arrays]

    def right(s):
        return right_part(s, *in_hbm(pair_tiles, gain_in, w_proj, tokens, exponents))

    a0, b0 = right(0), right(1)
    left = left_part(*in_hbm(pair_tiles, gain_in, w_proj, tokens))
    a1, b1 = forward(a0), forward(b0)
    a2, b2 = forward(a1), forward(after(b1, left))
    c0, d0 = right(2), right(3)
    a3, b3 = forward(after(a2, b1, c0)), forward(after(b2, d0))
    c1, d1 = forward(after(c0, b2)), forward(after(d0, a3))

    def triangle(slots):
        keep, near, send, panel = tri_part(0, slots, left)
        got = over_core(send)
        return keep, got, plus(near, got[1]), panel

    g_out = g_gate = jnp.zeros((width, width), F32)

    def middle(s, tri, mine):
        return mid_part(
            s, (tri[0], tri[1], mine), pair_tiles, grad_out, gain_in, gain_out, w_gate, w_out, g_out, g_gate
        )

    def spread(d_tri):
        far = over_x(d_tri)
        return [d_tri, far, over_core(d_tri), over_core(far)]

    def dright(blocks, *others):
        return dright_part([blocks[0], blocks[1], blocks[2], after(blocks[3], *others)], left)

    tri_a, tri_b = triangle([a0, a1, a2, after(a3, b2)]), triangle([b0, b1, b2, after(b3, c1)])
    x_a, x_b = over_x(tri_a[2]), over_x(tri_b[2])
    c2, d2 = forward(after(c1, tri_a[2])), forward(after(d1, tri_b[2]))
    dtri_a, gate_a, g_out, g_gate = middle(0, tri_a, after(x_a, d1))
    blocks_a = spread(dtri_a)
    dtri_b, gate_b, g_out, g_gate = middle(1, tri_b, after(x_b, c2))
    blocks_b = spread(dtri_b)
    c3, d3 = forward(after(c2, dtri_a)), forward(after(d2, dtri_b))
    part_a = dright(blocks_a, d2, c3)
    part_b = dright(blocks_b, c3)
    r_a, r_b = forward(part_a[1]), forward(part_b[1])

    tri_c = triangle([c0, c1, c2, after(c3, part_a[1])])
    tri_d = triangle([d0, d1, d2, after(d3, part_b[1])])
    x_c, x_d = over_x(tri_c[2]), over_x(tri_d[2])
    r_a = plus(r_a, part_a[2])
    r_a2 = forward(after(r_a, tri_c[2]))
    r_b = plus(r_b, part_b[2])
    r_b2 = forward(after(r_b, tri_d[2]))
    d_left = dleft_part(
        [after(blocks_a[0], tri_d[2])] + blocks_a[1:] + blocks_b,
        [tri_a[3], tri_b[3]],
        jnp.zeros((HALF, HALF, WIDTH), F32),
    )
    dtri_c, gate_c, g_out, g_gate = middle(2, tri_c, after(x_c, r_a, d_left))
    blocks_c = spread(dtri_c)
    dtri_d, gate_d, g_out, g_gate = middle(3, tri_d, after(x_d, r_b))
    blocks_d = spread(dtri_d)
    r_a2 = plus(r_a2, part_a[3])
    r_a3 = forward(after(r_a2, dtri_c))
    r_b2 = plus(r_b2, part_b[3])
    r_b3 = forward(after(r_b2, dtri_d))
    part_c = dright(blocks_c, r_a2)
    part_d = dright(blocks_d, r_b2)

    zero = jnp.zeros((width, 2 * width), F32)

    def final(s, sums, so_far, into):
        return final_b_part(
            s, pair_tiles, partial, sums, tokens, exponents, gain_in, w_proj, so_far, into
        )

    r_c, r_d = forward(part_c[1]), forward(part_d[1])
    d_left = dleft_part(
        [after(blocks_c[0], part_d[1])] + blocks_c[1:] + blocks_d, [tri_c[3], tri_d[3]], d_left
    )
    r_c = plus(r_c, after(part_c[2], d_left))
    partial, g_a = final_a_part(
        pair_tiles, after(d_left, r_c), tokens, gain_in, w_proj, w_gate, [gate_a, gate_b, gate_c, gate_d]
    )
    r_c = forward(r_c)
    r_d = plus(r_d, after(part_d[2], g_a))
    d_pair, g_first = final(0, (part_a[0], after(r_a3, r_d)), zero, gain_in)
    r_d = forward(r_d)
    r_c = plus(r_c, after(part_c[3], g_first))
    d_pair, g_first = final(1, (part_b[0], after(r_b3, r_c)), g_first, d_pair)
    r_c = forward(r_c)
    r_d = forward(plus(r_d, after(part_d[3], g_first)))
    d_pair, g_last = final(2, (part_c[0], r_c), g_first, d_pair)
    d_pair, g_last = final(3, (part_d[0], r_d), g_last, d_pair)

    sums = jnp.concatenate([g_out, g_gate, g_a, g_last], axis=1)
    half = width // 2
    sums = lax.dynamic_slice_in_dim(sums, core * half, half) + over_core(
        lax.dynamic_slice_in_dim(sums, (1 - core) * half, half)
    )
    for send in (over_x, lambda a: over_row(a, 1), lambda a: over_row(a, 2)):
        mine = sums.astype(BF16)
        sums = mine.astype(F32) + send(mine).astype(F32)
    sums = sums / crop_len
    theirs = over_core(sums)
    sums = jnp.concatenate(
        [jnp.where(core == 0, sums, theirs), jnp.where(core == 0, theirs, sums)], axis=0
    )
    return d_pair, sums[:, 2 * width :], sums[:, width : 2 * width], sums[:, :width]


def local(pair_tiles, *rest, rows_over, cols_over):
    if pair_tiles.shape == (HALF, HALF, WIDTH) and rows_over == cols_over == 4:
        return blocked(pair_tiles, *rest)
    return plain(pair_tiles, *rest)


def solution(mesh):
    return jax.shard_map(
        functools.partial(local, rows_over=mesh.shape["row"], cols_over=mesh.shape["col"]),
        mesh=mesh,
        in_specs=(
            P(("crop", "row"), "col", None),
            P(("crop", "row"), "col", None),
            P(("crop", "row"), "col"),
            P("crop"),
            P(),
            P(),
            P(),
            P(),
            P(),
        ),
        out_specs=(
            P(("crop", "row"), "col", None),
            P("crop", None),
            P("crop", None),
            P("crop", None),
        ),
        check_vma=False,
    )
```

```python
import functools

import jax
import jax.numpy as jnp
from jax import lax
from jax.experimental import pallas as pl
from jax.experimental.pallas import tpu as pltpu
from jax.sharding import PartitionSpec as P

EPS = 1e-05


def layer_norm(values, gain):
    center = jnp.mean(values, axis=-1, keepdims=True)
    spread = jnp.mean((values - center) ** 2, axis=-1, keepdims=True)
    inverse = lax.rsqrt(spread + EPS)
    centred = (values - center) * inverse
    return (centred * gain, centred, inverse)


def norm_back(upstream, centred, inverse, gain):
    scaled = upstream * gain
    first = jnp.mean(scaled, axis=-1, keepdims=True)
    second = jnp.mean(scaled * centred, axis=-1, keepdims=True)
    return inverse * (scaled - first - centred * second)


def plain(pair_tiles, grad_out, exponents, token_mask, gain_in, w_proj, w_gate, gain_out, w_out):
    f32 = jnp.float32
    bf16 = jnp.bfloat16
    rows, cols, width = pair_tiles.shape
    crop_len = token_mask.shape[0]
    row_at = lax.axis_index("row")
    col_at = lax.axis_index("col")
    maskf = token_mask.astype(f32)
    mask_rows = lax.dynamic_slice_in_dim(maskf, row_at * rows, rows)
    mask_cols = lax.dynamic_slice_in_dim(maskf, col_at * cols, cols)
    pair_mask = (mask_rows[:, None] * mask_cols[None, :])[..., None]
    normed_f, centred, inverse = layer_norm(pair_tiles.astype(f32), gain_in)
    normed = normed_f.astype(bf16)
    flat = normed.reshape(-1, width)
    projected = jnp.dot(flat, w_proj, preferred_element_type=f32).reshape(rows, cols, 4 * width)
    gate_a = projected[..., :width]
    value_a = projected[..., width : 2 * width]
    gate_b = projected[..., 2 * width : 3 * width]
    value_b = projected[..., 3 * width :]
    sig_a = jax.nn.sigmoid(gate_a)
    sig_b = jax.nn.sigmoid(gate_b)
    left = (pair_mask * sig_a * value_a).astype(bf16)
    right_raw = pair_mask * sig_b * value_b
    bound = (448.0 * jnp.exp2(exponents.astype(f32)))[..., None]
    right = jnp.clip(right_raw, -bound, bound).astype(bf16)
    inside = (jnp.abs(right_raw) <= bound).astype(f32)
    panel = lax.all_gather(right, "row", axis=0, tiled=True)
    tri_cols = lax.psum_scatter(
        jnp.einsum("jkc,ikc->jic", panel, left, preferred_element_type=f32).astype(jnp.bfloat16),
        "col",
        scatter_dimension=0,
        tiled=True,
    ).astype(jnp.float32)
    tri = jnp.transpose(tri_cols, (1, 0, 2))
    tnorm_f, tcentred, tinverse = layer_norm(tri, gain_out)
    tnorm = tnorm_f.astype(bf16)
    tflat = tnorm.reshape(-1, width)
    opened = jax.nn.sigmoid(jnp.dot(flat, w_gate, preferred_element_type=f32)).reshape(
        rows, cols, width
    )
    outproj = jnp.dot(tflat, w_out, preferred_element_type=f32).reshape(rows, cols, width)
    upstream = grad_out.astype(f32)
    d_open = upstream * outproj
    d_outproj = (upstream * opened).astype(bf16).reshape(-1, width)
    g_out = jnp.dot(tflat.T, d_outproj, preferred_element_type=f32)
    d_tnorm = jnp.dot(d_outproj, w_out.T, preferred_element_type=f32).reshape(rows, cols, width)
    d_tri = norm_back(d_tnorm, tcentred, tinverse, gain_out).astype(bf16)
    d_gatepre = (d_open * opened * (1.0 - opened)).astype(bf16).reshape(-1, width)
    g_gate = jnp.dot(flat.T, d_gatepre, preferred_element_type=f32)
    grad_full = lax.all_gather(d_tri, "col", axis=1, tiled=True)
    d_left = jnp.einsum("ijc,jkc->ikc", grad_full, panel, preferred_element_type=f32)
    d_right = (
        lax.psum_scatter(
            jnp.einsum("ijc,ikc->jkc", grad_full, left, preferred_element_type=f32).astype(
                jnp.bfloat16
            ),
            "row",
            scatter_dimension=0,
            tiled=True,
        ).astype(jnp.float32)
        * inside
    )
    d_gate_a = d_left * pair_mask * value_a * sig_a * (1.0 - sig_a)
    d_value_a = d_left * pair_mask * sig_a
    d_gate_b = d_right * pair_mask * value_b * sig_b * (1.0 - sig_b)
    d_value_b = d_right * pair_mask * sig_b
    d_proj = (
        jnp.concatenate([d_gate_a, d_value_a, d_gate_b, d_value_b], axis=-1)
        .astype(bf16)
        .reshape(-1, 4 * width)
    )
    g_proj = jnp.dot(flat.T, d_proj, preferred_element_type=f32)
    d_normed = jnp.dot(d_proj, w_proj.T, preferred_element_type=f32) + jnp.dot(
        d_gatepre, w_gate.T, preferred_element_type=f32
    )
    d_pair = norm_back(d_normed.reshape(rows, cols, width), centred, inverse, gain_in).astype(bf16)
    sum_proj, sum_gate, sum_out = lax.psum((g_proj, g_gate, g_out), ("row", "col"))
    return (d_pair, sum_proj / crop_len, sum_gate / crop_len, sum_out / crop_len)


SUB = 16
PART = 16
HALF = 64
WIDTH = 128
LANES = SUB * HALF
GROUP = 16
NT = (((1,), (1,)), ((), ()))
NN = (((1,), (0,)), ((), ()))
TN = (((0,), (0,)), ((), ()))
F32 = jnp.float32
BF16 = jnp.bfloat16


def mm(a, b, dims):
    return lax.dot_general(a, b, dims, preferred_element_type=F32)


def params():
    return pltpu.CompilerParams(vmem_limit_bytes=16 * 1024 * 1024)


def cost(flops, size, exps=0):
    return pl.CostEstimate(flops=flops, bytes_accessed=size, transcendentals=exps)


def first_half(rows):
    return lax.broadcasted_iota(jnp.int32, (rows, WIDTH), 1) < HALF


def swap_halves(a, b):
    first = first_half(HALF)
    return (
        jnp.where(first, a, pltpu.roll(b, HALF, 1)),
        jnp.where(first, pltpu.roll(a, HALF, 1), b),
    )


def eye():
    row = lax.broadcasted_iota(jnp.int32, (WIDTH, WIDTH), 0)
    lane = lax.broadcasted_iota(jnp.int32, (WIDTH, WIDTH), 1)
    return (row == lane).astype(F32).astype(BF16)


def to_channels(cells):
    return mm(eye(), cells, NT)


def to_cells(channels):
    return mm(channels, eye(), TN)


def stage_rows(channels, buf):
    for t in range(SUB // 2):
        part = channels[:, t * WIDTH : (t + 1) * WIDTH]
        one, two = swap_halves(part[:HALF], part[HALF:])
        buf[(2 * t) * HALF : (2 * t + 1) * HALF, :] = one
        buf[(2 * t + 1) * HALF : (2 * t + 2) * HALF, :] = two


def panel_row(buf, p):
    return buf[pl.ds(p, SUB, stride=HALF), :]


def channels_of(panels, buf, out):
    buf[...] = panels.reshape(LANES, WIDTH)
    for t in range(SUB // 2):
        one = buf[pl.ds(2 * t, HALF, stride=SUB), :]
        two = buf[pl.ds(2 * t + 1, HALF, stride=SUB), :]
        low, high = swap_halves(one, two)
        out[:HALF, t * WIDTH : (t + 1) * WIDTH] = low
        out[HALF:, t * WIDTH : (t + 1) * WIDTH] = high
    return out[...]


def norm_channels(values, gain):
    center = jnp.mean(values, axis=0, keepdims=True)
    spread = jnp.mean((values - center) ** 2, axis=0, keepdims=True)
    inverse = lax.rsqrt(spread + EPS)
    centred = (values - center) * inverse
    return centred * gain, centred, inverse


def norm_back_channels(upstream, centred, inverse, gain):
    scaled = upstream * gain
    first = jnp.mean(scaled, axis=0, keepdims=True)
    second = jnp.mean(scaled * centred, axis=0, keepdims=True)
    return inverse * (scaled - first - centred * second)


def column(row):
    at = lax.broadcasted_iota(jnp.int32, (WIDTH, WIDTH), 0)
    lane = lax.broadcasted_iota(jnp.int32, (WIDTH, WIDTH), 1)
    return jnp.sum(jnp.where(at == lane, row, 0.0), axis=1, keepdims=True)


def mask_lanes(token_ref, s):
    valid = jnp.sum(token_ref[...].astype(F32), axis=1, keepdims=True)
    lane = lax.broadcasted_iota(jnp.int32, (1, LANES), 1)
    row = lane // HALF + (lax.axis_index("row") * HALF + s * SUB)
    col = lane % HALF + lax.axis_index("col") * HALF
    return (jnp.maximum(row, col).astype(F32) < valid).astype(F32)


def bound_lanes(exponent_ref):
    bound = 448.0 * jnp.exp2(exponent_ref[...].astype(F32))
    return jnp.concatenate([bound[i : i + 1] for i in range(SUB)], axis=1)


def normed_cells(x_ref, gain_ref):
    gain = column(gain_ref[...])
    normed, centred, inverse = norm_channels(to_channels(x_ref[...].reshape(LANES, WIDTH)), gain)
    return normed.astype(BF16), centred, inverse, gain


def right_kernel(at, x_ref, gain_ref, w_ref, token_ref, exponent_ref, out_ref, buf):
    normed = normed_cells(x_ref, gain_ref)[0]
    proj = mm(w_ref[...], normed, TN)
    raw = mask_lanes(token_ref, at + pl.program_id(0)) * jax.nn.sigmoid(proj[:WIDTH]) * proj[WIDTH:]
    bound = bound_lanes(exponent_ref)
    stage_rows(jnp.clip(raw, -bound, bound), buf)
    for p in range(HALF):
        out_ref[p] = panel_row(buf, p).astype(BF16)


def left_kernel(x_ref, gain_ref, w_ref, token_ref, out_ref, buf):
    normed = normed_cells(x_ref, gain_ref)[0]
    proj = mm(w_ref[...], normed, TN)
    mask = mask_lanes(token_ref, pl.program_id(0))
    stage_rows(mask * jax.nn.sigmoid(proj[:WIDTH]) * proj[WIDTH:], buf)
    first = first_half(SUB)
    for p in range(HALF):
        row = panel_row(buf, p)
        out_ref[p, 0] = jnp.where(first, row, 0.0).astype(BF16)
        out_ref[p, 1] = jnp.where(first, 0.0, row).astype(BF16)


def tri_kernel(s0, s1, s2, s3, left_ref, keep_ref, near_ref, send_ref, panel_ref):
    z, q = lax.axis_index("row"), lax.axis_index("col")
    for m, ref in enumerate((s0, s1, s2, s3)):
        place = ((z ^ (z >> 1)) - m + 4) & 3
        other = place ^ (place >> 1) ^ q
        panel_ref[(other & 1) * 2 + (other >> 1)] = ref[...]
    for p in range(GROUP):
        right = jnp.concatenate([panel_ref[r, p] for r in range(4)], axis=0)
        tri = mm(right, left_ref[p].reshape(WIDTH, WIDTH), NT).astype(BF16)
        keep_ref[p] = tri[:SUB]
        near_ref[p] = tri[SUB : 2 * SUB]
        send_ref[0, p] = tri[2 * SUB : 3 * SUB]
        send_ref[1, p] = tri[3 * SUB :]


def mid_kernel(
    a_ref, b_ref, c_ref, x_ref, grad_ref, gain_in_ref, gain_out_ref, gate_ref, out_w_ref,
    g_out_so_far, g_gate_so_far, dtri_ref, dgate_ref, g_out_ref, g_gate_ref, buf, wide,
):
    gain_out = column(gain_out_ref[...])
    tri = channels_of(
        a_ref[...].astype(F32) + b_ref[0].astype(F32) + c_ref[...].astype(F32), buf, wide
    )
    tnorm_f, tcentred, tinverse = norm_channels(tri, gain_out)
    tnorm = tnorm_f.astype(BF16)

    def turned(ref):
        buf[...] = ref[...].astype(F32).reshape(LANES, WIDTH)
        rows = [buf[pl.ds(j, HALF, stride=SUB), :] for j in range(SUB)]
        return to_channels(jnp.concatenate(rows, axis=0).astype(BF16))

    normed = norm_channels(turned(x_ref), column(gain_in_ref[...]))[0].astype(BF16)
    upstream = turned(grad_ref)
    opened = jax.nn.sigmoid(mm(gate_ref[...], normed, TN))
    outproj = mm(out_w_ref[...], tnorm, TN)
    d_open = upstream * outproj
    d_outproj = (upstream * opened).astype(BF16)
    g_out_ref[...] = g_out_so_far[...] + mm(tnorm, d_outproj, NT)
    d_tnorm = mm(out_w_ref[...], d_outproj, NN)
    d_tri = norm_back_channels(d_tnorm, tcentred, tinverse, gain_out)
    d_gatepre = (d_open * opened * (1.0 - opened)).astype(BF16)
    g_gate_ref[...] = g_gate_so_far[...] + mm(normed, d_gatepre, NT)
    stage_rows(d_tri, buf)
    for p in range(HALF):
        dtri_ref[p] = panel_row(buf, p).astype(BF16)
    buf[...] = to_cells(d_gatepre)
    for i in range(HALF):
        dgate_ref[i] = panel_row(buf, i).astype(BF16)


def dright_kernel(*refs):
    *grads_refs, left_ref, p0, p1, p2, p3, held = refs
    z, q = lax.axis_index("row"), lax.axis_index("col")
    for k, ref in enumerate(grads_refs):
        r = k % 4
        block_at = q ^ ((r % 2) * 2 + r // 2)
        slot = ((z ^ (z >> 1)) - (block_at ^ (block_at >> 1)) + 4) & 3
        held[slot, :, (k // 4) * SUB : (k // 4 + 1) * SUB] = ref[...]
    for p in range(GROUP):
        grads = jnp.concatenate([held[m, p] for m in range(4)], axis=0)
        part = mm(grads, left_ref[p].reshape(WIDTH, WIDTH), NN).astype(BF16)
        for m, ref in enumerate((p0, p1, p2, p3)):
            ref[p] = part[m * PART : (m + 1) * PART]


def dleft_kernel(*refs):
    so_far, out_ref = refs[-2:]
    parts = (len(refs) - 2) // 5
    grad_refs, panel_refs = refs[: 4 * parts], refs[4 * parts : 5 * parts]
    first = first_half(HALF)
    for p in range(GROUP):
        grads = jnp.concatenate([d[p] for d in grad_refs], axis=0)
        right = jnp.concatenate([r[q, p] for r in panel_refs for q in range(4)], axis=0)
        both = mm(grads, right, TN)
        out_ref[p] = so_far[p] + jnp.where(first, both[:HALF], both[HALF:])


def gate_grads(upstream, mask, sig, value):
    d_gate = (upstream * mask * value * sig * (1.0 - sig)).astype(BF16)
    d_value = (upstream * mask * sig).astype(BF16)
    return jnp.concatenate([d_gate, d_value], axis=0)


def final_a_kernel(
    x_ref, dleft_ref, token_ref, gain_ref, w_ref, gate_ref, q0, q1, q2, q3, out_ref, g_ref, buf, wide
):
    s = pl.program_id(0)
    normed = normed_cells(x_ref, gain_ref)[0]
    proj = mm(w_ref[...], normed, TN)
    d_left = channels_of(dleft_ref[...], buf, wide)
    d_proj = gate_grads(d_left, mask_lanes(token_ref, s), jax.nn.sigmoid(proj[:WIDTH]), proj[WIDTH:])
    d_gate = jnp.concatenate([q[...] for q in (q0, q1, q2, q3)], axis=1).reshape(LANES, WIDTH)
    out_ref[...] = mm(w_ref[...], d_proj, NN) + mm(gate_ref[...], d_gate, NT)

    @pl.when(s == 0)
    def start():
        g_ref[...] = jnp.zeros_like(g_ref)

    g_ref[...] += mm(normed, d_proj, NT)


def final_b_kernel(
    at, x_ref, part_ref, a_ref, b_ref, token_ref, exponent_ref, gain_ref, w_ref, so_far, into_ref,
    out_ref, g_ref, buf, wide,
):
    step = pl.program_id(0)
    normed, centred, inverse, gain = normed_cells(x_ref, gain_ref)
    proj = mm(w_ref[...], normed, TN)
    mask = mask_lanes(token_ref, at + step)
    sig = jax.nn.sigmoid(proj[:WIDTH])
    inside = jnp.abs(mask * sig * proj[WIDTH:]) <= bound_lanes(exponent_ref)
    d_right = channels_of(a_ref[...].astype(F32) + b_ref[...].astype(F32), buf, wide)
    d_proj = gate_grads(jnp.where(inside, d_right, 0.0), mask, sig, proj[WIDTH:])

    @pl.when(step == 0)
    def start():
        g_ref[...] = so_far[...]

    g_ref[...] += mm(normed, d_proj, NT)
    d_normed = part_ref[...] + mm(w_ref[...], d_proj, NN)
    d_pair = norm_back_channels(d_normed, centred, inverse, gain).astype(BF16)
    out_ref[...] = to_cells(d_pair).astype(BF16).reshape(SUB, HALF, WIDTH)


def whole(array):
    return pl.BlockSpec(array.shape, lambda i: (0,) * array.ndim)


def block(shape, at):
    return pl.BlockSpec(shape, lambda i: at)


BUF = pltpu.VMEM((LANES, WIDTH), F32)
WIDE = pltpu.VMEM((WIDTH, LANES), F32)
PANEL = jax.ShapeDtypeStruct((HALF, SUB, WIDTH), BF16)
PANEL_SPEC = pl.BlockSpec((GROUP, SUB, WIDTH), lambda i: (i, 0, 0))
FOUR = jax.ShapeDtypeStruct((4, HALF, SUB, WIDTH), BF16)
FOUR_SPEC = pl.BlockSpec((4, GROUP, SUB, WIDTH), lambda i: (0, i, 0, 0))
TWO = jax.ShapeDtypeStruct((2, HALF, SUB, WIDTH), BF16)
TWO_SPEC = pl.BlockSpec((2, GROUP, SUB, WIDTH), lambda i: (0, i, 0, 0))
LEFT_SPEC = pl.BlockSpec((GROUP, 2, HALF, WIDTH), lambda i: (i, 0, 0, 0))
LONG = jax.ShapeDtypeStruct((HALF, PART, WIDTH), BF16)
LONG_SPEC = pl.BlockSpec((GROUP, PART, WIDTH), lambda i: (i, 0, 0))
WHOLE_PANEL = pl.BlockSpec(PANEL.shape, lambda i: (0, 0, 0))


def right_part(s, pair, gain, w_proj, tokens, exponents):
    steps = PART // SUB
    return pl.pallas_call(
        functools.partial(right_kernel, s * steps),
        grid=(steps,),
        out_shape=LONG,
        in_specs=[
            pl.BlockSpec((SUB, HALF, WIDTH), lambda i: (s * steps + i, 0, 0)),
            whole(gain), block((WIDTH, 2 * WIDTH), (0, 1)), whole(tokens),
            pl.BlockSpec((SUB, HALF), lambda i: (s * steps + i, 0)),
        ],
        out_specs=pl.BlockSpec((HALF, SUB, WIDTH), lambda i: (0, i, 0)),
        scratch_shapes=[BUF],
        compiler_params=params(),
        cost_estimate=cost(8 * LANES * WIDTH * WIDTH, 1 << 20, 2 * LANES * WIDTH),
        name="right_part",
    )(pair, gain, w_proj, tokens, exponents)


def left_part(pair, gain, w_proj, tokens):
    return pl.pallas_call(
        left_kernel,
        grid=(HALF // SUB,),
        out_shape=jax.ShapeDtypeStruct((HALF, 2, HALF, WIDTH), BF16),
        in_specs=[
            pl.BlockSpec((SUB, HALF, WIDTH), lambda i: (i, 0, 0)), whole(gain),
            block((WIDTH, 2 * WIDTH), (0, 0)), whole(tokens),
        ],
        out_specs=pl.BlockSpec((HALF, 2, SUB, WIDTH), lambda i: (0, 0, i, 0)),
        scratch_shapes=[BUF],
        compiler_params=params(),
        cost_estimate=cost(16 * LANES * WIDTH * WIDTH, 3 << 20, 4 * LANES * WIDTH),
        name="left_part",
    )(pair, gain, w_proj, tokens)


def tri_part(at, slots, left):
    return pl.pallas_call(
        tri_kernel,
        grid=(HALF // GROUP,),
        out_shape=(PANEL, PANEL, TWO, FOUR),
        in_specs=[pl.BlockSpec((GROUP, SUB, WIDTH), lambda i: (i, at, 0))] * 4 + [LEFT_SPEC],
        out_specs=(PANEL_SPEC, PANEL_SPEC, TWO_SPEC, FOUR_SPEC),
        compiler_params=params(),
        cost_estimate=cost(2 * HALF * HALF * WIDTH * WIDTH, 5 << 20),
        name="tri_part",
    )(*slots, left)


def mid_part(s, parts, pair, grad, gain_in, gain_out, w_gate, w_out, g_out, g_gate):
    square = jax.ShapeDtypeStruct((WIDTH, WIDTH), F32)
    columns = block((HALF, SUB, WIDTH), (0, s, 0))
    small = [gain_in, gain_out, w_gate, w_out, g_out, g_gate]
    return pl.pallas_call(
        mid_kernel,
        grid=(1,),
        out_shape=(PANEL, pltpu.HBM(PANEL.shape, BF16), square, square),
        in_specs=[WHOLE_PANEL, block((1, HALF, SUB, WIDTH), (0, 0, 0, 0)), WHOLE_PANEL]
        + [columns] * 2
        + [whole(a) for a in small],
        out_specs=(WHOLE_PANEL, WHOLE_PANEL, block(square.shape, (0, 0)), block(square.shape, (0, 0))),
        scratch_shapes=[BUF, WIDE],
        compiler_params=params(),
        cost_estimate=cost(12 * LANES * WIDTH * WIDTH, 2 << 20, LANES * WIDTH),
        name="mid_part",
    )(*parts, pair, grad, *small)


def dright_part(blocks, left):
    return pl.pallas_call(
        dright_kernel,
        grid=(HALF // GROUP,),
        out_shape=(pltpu.HBM(LONG.shape, BF16), LONG, LONG, LONG),
        in_specs=[PANEL_SPEC] * len(blocks) + [LEFT_SPEC],
        out_specs=(LONG_SPEC,) * 4,
        scratch_shapes=[pltpu.VMEM((4, GROUP, PART, WIDTH), BF16)],
        compiler_params=params(),
        cost_estimate=cost(4 * HALF * HALF * WIDTH * WIDTH, 6 << 20),
        name="dright_part",
    )(*blocks, left)


def dleft_part(grads, panels, so_far):
    rows = pl.BlockSpec((GROUP, HALF, WIDTH), lambda i: (i, 0, 0))
    return pl.pallas_call(
        dleft_kernel,
        grid=(HALF // GROUP,),
        out_shape=jax.ShapeDtypeStruct((HALF, HALF, WIDTH), F32),
        in_specs=[PANEL_SPEC] * len(grads) + [FOUR_SPEC] * len(panels) + [rows],
        out_specs=rows,
        compiler_params=params(),
        cost_estimate=cost(4 * HALF * HALF * WIDTH * WIDTH, 8 << 20),
        name="dleft_part",
    )(*grads, *panels, so_far)


def final_a_part(pair, dleft, tokens, gain, w_proj, w_gate, gates):
    return pl.pallas_call(
        final_a_kernel,
        grid=(HALF // SUB,),
        out_shape=(
            jax.ShapeDtypeStruct((WIDTH, HALF * HALF), F32),
            jax.ShapeDtypeStruct((WIDTH, 2 * WIDTH), F32),
        ),
        in_specs=[
            pl.BlockSpec((SUB, HALF, WIDTH), lambda i: (i, 0, 0)),
            pl.BlockSpec((HALF, SUB, WIDTH), lambda i: (0, i, 0)),
            whole(tokens), whole(gain), block((WIDTH, 2 * WIDTH), (0, 0)), whole(w_gate),
        ]
        + [pl.BlockSpec((SUB, SUB, WIDTH), lambda i: (i, 0, 0))] * 4,
        out_specs=(
            pl.BlockSpec((WIDTH, LANES), lambda i: (0, i)),
            block((WIDTH, 2 * WIDTH), (0, 0)),
        ),
        scratch_shapes=[BUF, WIDE],
        compiler_params=params(),
        cost_estimate=cost(56 * LANES * WIDTH * WIDTH, 8 << 20, 4 * LANES * WIDTH),
        name="final_a_part",
    )(pair, dleft, tokens, gain, w_proj, w_gate, *gates)


def final_b_part(s, pair, part, sums, tokens, exponents, gain, w_proj, so_far, into):
    steps = PART // SUB
    rows = pl.BlockSpec((SUB, HALF, WIDTH), lambda i: (s * steps + i, 0, 0))
    panel = pl.BlockSpec((HALF, SUB, WIDTH), lambda i: (0, i, 0))
    return pl.pallas_call(
        functools.partial(final_b_kernel, s * steps),
        grid=(steps,),
        out_shape=(
            jax.ShapeDtypeStruct((HALF, HALF, WIDTH), BF16),
            jax.ShapeDtypeStruct((WIDTH, 2 * WIDTH), F32),
        ),
        in_specs=[
            rows,
            pl.BlockSpec((WIDTH, LANES), lambda i: (0, s * steps + i)),
            panel, panel, whole(tokens),
            pl.BlockSpec((SUB, HALF), lambda i: (s * steps + i, 0)),
            whole(gain), block((WIDTH, 2 * WIDTH), (0, 1)), whole(so_far),
            pl.BlockSpec(memory_space=pl.ANY),
        ],
        out_specs=(rows, block((WIDTH, 2 * WIDTH), (0, 0))),
        scratch_shapes=[BUF, WIDE],
        input_output_aliases={9: 0} if into.shape == pair.shape else {},
        compiler_params=params(),
        cost_estimate=cost(28 * LANES * WIDTH * WIDTH, 4 << 20, 2 * LANES * WIDTH),
        name="final_b_part",
    )(pair, part, *sums, tokens, exponents, gain, w_proj, so_far, into)


def after(array, *others):
    return lax.optimization_barrier((array, *others))[0]


def blocked(pair_tiles, grad_out, exponents, token_mask, gain_in, w_proj, w_gate, gain_out, w_out):
    width = pair_tiles.shape[-1]
    crop_len = token_mask.shape[0]
    core = lax.axis_index("col") % 2
    tokens = token_mask.reshape(1, crop_len)
    gain_in = gain_in.reshape(1, width)
    gain_out = gain_out.reshape(1, width)

    def forward(a):
        return lax.ppermute(a, "row", [(0, 1), (1, 3), (3, 2), (2, 0)])

    def over_row(a, bit):
        return lax.ppermute(a, "row", [(k, k ^ bit) for k in range(4)])

    def over_x(a):
        return lax.ppermute(a, "col", [(k, k ^ 2) for k in range(4)])

    def over_core(a):
        return lax.ppermute(a, "col", [(k, k ^ 1) for k in range(4)])

    def plus(a, b):
        return (a.astype(F32) + b.astype(F32)).astype(BF16)

    def in_hbm(*arrays):
        return [pltpu.with_memory_space_constraint(a, pltpu.HBM) for a in arrays]

    def right(s):
        return right_part(s, *in_hbm(pair_tiles, gain_in, w_proj, tokens, exponents))

    a0, b0 = right(0), right(1)
    left = left_part(*in_hbm(pair_tiles, gain_in, w_proj, tokens))
    a1, b1 = forward(a0), forward(b0)
    a2, b2 = forward(a1), forward(after(b1, left))
    c0, d0 = right(2), right(3)
    a3, b3 = forward(after(a2, c0)), forward(after(b2, d0))
    c1, d1 = forward(after(c0, b2)), forward(after(d0, a3))

    def triangle(slots):
        keep, near, send, panel = tri_part(0, slots, left)
        got = over_core(send)
        return keep, got, plus(near, got[1]), panel

    g_out = g_gate = jnp.zeros((width, width), F32)

    def middle(s, tri, mine):
        return mid_part(
            s, (tri[0], tri[1], mine), pair_tiles, grad_out, gain_in, gain_out, w_gate, w_out, g_out, g_gate
        )

    def spread(d_tri):
        far = over_x(d_tri)
        return [d_tri, far, over_core(d_tri), over_core(far)]

    def dright(blocks, *others):
        return dright_part([blocks[0], blocks[1], blocks[2], after(blocks[3], *others)], left)

    tri_a, tri_b = triangle([a0, a1, a2, a3]), triangle([b0, b1, b2, b3])
    x_a, x_b = over_x(tri_a[2]), over_x(tri_b[2])
    c2, d2 = forward(after(c1, tri_a[2])), forward(after(d1, tri_b[2]))
    dtri_a, gate_a, g_out, g_gate = middle(0, tri_a, after(x_a, d1))
    blocks_a = spread(dtri_a)
    dtri_b, gate_b, g_out, g_gate = middle(1, tri_b, after(x_b, c2))
    blocks_b = spread(dtri_b)
    c3, d3 = forward(after(c2, dtri_a)), forward(after(d2, dtri_b))
    part_a = dright(blocks_a, d2)
    part_b = dright(blocks_b, c3)
    r_a, r_b = forward(part_a[1]), forward(part_b[1])

    tri_c = triangle([c0, c1, c2, after(c3, part_a[1])])
    tri_d = triangle([d0, d1, d2, after(d3, part_b[1])])
    x_c, x_d = over_x(tri_c[2]), over_x(tri_d[2])
    r_a = plus(r_a, part_a[2])
    r_a2 = forward(after(r_a, tri_c[2]))
    r_b = plus(r_b, part_b[2])
    r_b2 = forward(after(r_b, tri_d[2]))
    d_left = dleft_part(
        [after(blocks_a[0], tri_d[2])] + blocks_a[1:] + blocks_b,
        [tri_a[3], tri_b[3]],
        jnp.zeros((HALF, HALF, WIDTH), F32),
    )
    dtri_c, gate_c, g_out, g_gate = middle(2, tri_c, after(x_c, r_a, d_left))
    blocks_c = spread(dtri_c)
    r_a2 = plus(r_a2, part_a[3])
    dtri_d, gate_d, g_out, g_gate = middle(3, tri_d, after(x_d, r_b, r_a2))
    blocks_d = spread(dtri_d)
    r_a3 = forward(after(r_a2, dtri_c))
    r_b2 = plus(r_b2, part_b[3])
    r_b3 = forward(after(r_b2, dtri_d))
    part_c = dright(blocks_c, r_a3)
    part_d = dright(blocks_d, r_b2)

    zero = jnp.zeros((width, 2 * width), F32)

    def final(s, sums, so_far, into):
        return final_b_part(
            s, pair_tiles, partial, sums, tokens, exponents, gain_in, w_proj, so_far, into
        )

    r_c, r_d = forward(part_c[1]), forward(part_d[1])
    d_left = dleft_part(
        [after(blocks_c[0], part_d[1])] + blocks_c[1:] + blocks_d, [tri_c[3], tri_d[3]], d_left
    )
    r_c = plus(r_c, after(part_c[2], d_left))
    partial, g_a = final_a_part(
        pair_tiles, after(d_left, r_c), tokens, gain_in, w_proj, w_gate, [gate_a, gate_b, gate_c, gate_d]
    )
    r_c = forward(r_c)
    r_d = plus(r_d, after(part_d[2], g_a))
    d_pair, g_first = final(0, (part_a[0], after(r_a3, r_d)), zero, gain_in)
    r_d = forward(r_d)
    r_c = plus(r_c, after(part_c[3], g_first))
    d_pair, g_first = final(1, (part_b[0], after(r_b3, r_c)), g_first, d_pair)
    r_c = forward(r_c)
    r_d = forward(plus(r_d, after(part_d[3], g_first)))
    d_pair, g_last = final(2, (part_c[0], r_c), g_first, d_pair)
    d_pair, g_last = final(3, (part_d[0], r_d), g_last, d_pair)

    sums = jnp.concatenate([g_out, g_gate, g_a, g_last], axis=1)
    half = width // 2
    sums = lax.dynamic_slice_in_dim(sums, core * half, half) + over_core(
        lax.dynamic_slice_in_dim(sums, (1 - core) * half, half)
    )
    for send in (over_x, lambda a: over_row(a, 1), lambda a: over_row(a, 2)):
        mine = sums.astype(BF16)
        sums = mine.astype(F32) + send(mine).astype(F32)
    sums = sums / crop_len
    theirs = over_core(sums)
    sums = jnp.concatenate(
        [jnp.where(core == 0, sums, theirs), jnp.where(core == 0, theirs, sums)], axis=0
    )
    return d_pair, sums[:, 2 * width :], sums[:, width : 2 * width], sums[:, :width]


def local(pair_tiles, *rest, rows_over, cols_over):
    if pair_tiles.shape == (HALF, HALF, WIDTH) and rows_over == cols_over == 4:
        return blocked(pair_tiles, *rest)
    return plain(pair_tiles, *rest)


def solution(mesh):
    return jax.shard_map(
        functools.partial(local, rows_over=mesh.shape["row"], cols_over=mesh.shape["col"]),
        mesh=mesh,
        in_specs=(
            P(("crop", "row"), "col", None),
            P(("crop", "row"), "col", None),
            P(("crop", "row"), "col"),
            P("crop"),
            P(),
            P(),
            P(),
            P(),
            P(),
        ),
        out_specs=(
            P(("crop", "row"), "col", None),
            P("crop", None),
            P("crop", None),
            P("crop", None),
        ),
        check_vma=False,
    )
```
